32 devices in a mesh: dp: 16 (over z, y, core), tensor: 2 (over x).
Axes of the slice: x: 2, y: 2, z: 4, core: 2. Of those that a mesh axis runs over, the one named last changes fastest.
Arguments:
- tokens: bfloat16 [32768, 1024], P(('dp', 'tensor')), may hold values from -6 to 6
- segment_ids: int32 [16, 2048], P('dp'), may hold values from 0 to 7, never falling along the last dimension, each value on 1 to 800 neighbouring positions
- key_mask: int32 [16, 2048], P('dp'), may hold values 0 or 1
- owners: int32 [48, 1], replicated, may hold values from 0 to 15; in each aligned block of 48 rows (0 to 47, 48 to 95, ...) at most 6 rows name the same one
- master_slots: float32 [2, 96, 128, 1024], P('tensor', 'dp'), may hold values from -0.25 to 0.25
- slot_first: float32 [2, 96, 128, 1024], P('tensor', 'dp'), may hold values from -384 to 384
- slot_second: float32 [2, 96, 128, 1024], P('tensor', 'dp'), may hold values from 2048 to 16384
- vectors: float32 [12, 1024], replicated, may hold values from -0.8 to 1.65, as said below
- vector_first: float32 [12, 1024], replicated, may hold values from -384 to 384
- vector_second: float32 [12, 1024], replicated, may hold values from 2048 to 16384
- out_grad: bfloat16 [32768, 1024], P(('dp', 'tensor')), may hold values from -6 to 6
Outputs:
- layer_out: bfloat16 [32768, 1024], P(('dp', 'tensor'))
- input_grad: bfloat16 [32768, 1024], P(('dp', 'tensor'))
- slot_new: float32 [2, 96, 128, 1024], P('tensor', 'dp')
- slot_first_new: float32 [2, 96, 128, 1024], P('tensor', 'dp')
- slot_second_new: float32 [2, 96, 128, 1024], P('tensor', 'dp')
- vector_new: float32 [12, 1024], replicated
- vector_first_new: float32 [12, 1024], replicated
- vector_second_new: float32 [12, 1024], replicated
The draws below stay inside these ranges and needn't reach their ends.
Inputs may be any that keep to these rules, and one draw needn't show every extreme that they name: `owners`: no owner holds more than 6 pieces, and some owner holds exactly 6. `segment_ids`: within a sequence the numbers never fall; a document has 1 to 800 tokens, one exactly 800. `vectors`: rows 8 and 10 are positive.
All inputs are finite; a program needn't handle non-finite values. No bound on the sum of `key_mask` on one device may be relied on, other than what follows from the above.
Results may differ from the reference program's by a relative error of at most 0.025.
Values may be sent and summed in bfloat16 or wider, within the bound.
A program may use at most 384 MiB of HBM per device.

```python
import math
import jax
import jax.numpy as jnp
import numpy as np
from jax import lax

D = 1024
HEADS = 16
HD = 64
FF = 4096
LEN = 2048
QBLK = 512
DOCS = 8
DOC_MAX = 800
STEP = 10
TOKENS = 32768
ROWS_T = 6144
PIECES = 48
PR = 128
CAP = 6
GSQ = 4096
N_DP = 16
N_TENSOR = 2


def draw_vectors(key, part):
    key = jax.random.fold_in(key, 7)
    bias_key, gain_key = jax.random.split(key)
    row_index = jnp.arange(12, dtype=jnp.int32)[:, None]
    gain_rows = (row_index == 8) | (row_index == 10)
    gains = jnp.exp(jax.random.uniform(gain_key, (12, D), jnp.float32, -0.35, 0.35))
    biases = jnp.clip(0.2 * jax.random.normal(bias_key, (12, D), jnp.float32), -0.8, 0.8)
    return jnp.where(gain_rows, gains, biases)


def set_ends(values, stream_key, smallest, top_value):
    extent = values.shape
    index_at = [jax.random.randint(jax.random.fold_in(stream_key, axis), (), 0, extent[axis]) for axis in range(len(extent))]
    values = values.at[tuple(index_at)].set(smallest)
    longest = extent.index(max(extent))
    index_at[longest] = (index_at[longest] + 1) % extent[longest]
    return values.at[tuple(index_at)].set(top_value)


def levels(stream_key, shape, cuts, least, top_value):
    factor_of = 1.0
    for dim, blocks in cuts:
        heights = jax.random.uniform(jax.random.fold_in(jax.random.fold_in(stream_key, 6), dim), (blocks,), jnp.float32, least / len(cuts), top_value / len(cuts))
        factor_of = factor_of * jnp.repeat(jnp.exp(heights), shape[dim] // blocks).reshape((-1,) + (1,) * (len(shape) - 1 - dim))
    return factor_of


def split_up(amount, total, reach, slope):
    loads = [(1 << 20) // math.isqrt(rank ** slope) + 1 for rank in range(2, amount + 1)]
    rest, counts = total - reach - (amount - 1), [1] * (amount - 1)
    while rest > 0:
        candidates = [i for i in range(amount - 1) if counts[i] < reach]
        pool, remaining = sum([loads[i] for i in candidates]), rest
        for i in candidates:
            addition = min(reach - counts[i], max(1, remaining * loads[i] // pool), rest)
            counts[i] = counts[i] + addition
            rest = rest - addition
    return np.array([reach] + counts)


def ragged(own_key, amount, total, reach, slope):
    if amount == 2:
        one = jax.random.randint(own_key, (), max(1, total - reach), min(reach, total - 1) + 1)
        return jnp.stack([one, total - one])
    lengths = jnp.asarray(split_up(amount, total, reach, slope), jnp.int32)
    twos = (amount - 1) // 2
    source_of, receiver = lengths[1:1 + 2 * twos:2], lengths[2:2 + 2 * twos:2]
    margin = jnp.minimum(source_of - 1, reach - receiver)
    moved = jax.random.randint(jax.random.fold_in(own_key, 1), (twos,), 0, 1 << 20) % (margin + 1)
    lengths = lengths.at[1:1 + 2 * twos:2].set(source_of - moved).at[2:2 + 2 * twos:2].set(receiver + moved)
    return lengths[jax.random.permutation(jax.random.fold_in(own_key, 2), amount)]


def routed_block(key, own, number, rows, count, top, limit, skew):
    order = jax.random.permutation(key, count)
    packed, common = load_shares(count, rows * top, limit, skew, True), load_shares(count, rows * top, limit, skew, False)
    places = jnp.arange(count)

    def named(tallies, turn):
        used = int((tallies > 0).sum())
        fixed = max(1, used // 4)
        moved = fixed + (places - fixed + turn * (used - fixed)) % max(1, count - fixed)
        return jnp.zeros((count,), jnp.int32).at[order[jnp.where(places < fixed, places, moved)]].set(jnp.asarray(tallies, jnp.int32))

    tallies = jnp.where(number % 4 == 0, named(packed, number // 4), named(common, number - number // 4 - 1))
    mixed = jax.random.permutation(jax.random.fold_in(own, 3), count)
    giver, sink = mixed[0:count // 2 * 2:2], mixed[1:count // 2 * 2:2]
    margin = jnp.minimum(tallies[giver] - 1, limit - tallies[sink]) // 2
    margin = jnp.where((giver == order[0]) | (sink == order[0]) | (tallies[sink] == 0), 0, jnp.maximum(margin, 0))
    moved = jax.random.randint(jax.random.fold_in(own, 4), (count // 2,), 0, 1 << 20) % (margin + 1)
    tallies = tallies.at[giver].add(-moved).at[sink].add(moved)
    items = jnp.searchsorted(jnp.cumsum(tallies), jnp.arange(rows * top), side="right").astype(jnp.int32)
    grid = items.reshape(top, rows).T
    grid = grid[jax.random.permutation(jax.random.fold_in(own, 1), rows)]
    turn = jax.random.randint(jax.random.fold_in(own, 2), (rows, 1), 0, top)
    return jnp.take_along_axis(grid, (jnp.arange(top)[None, :] + turn) % top, axis=1)


def load_shares(amount, total, limit, skew, full):
    portions = [(1 << 20) // math.isqrt(grade ** skew) + 1 for grade in range(1, amount + 1)]
    largest = limit if full else min(limit, max(-(-total // amount), total * portions[0] // sum(portions)))
    least = 1 if total - largest >= amount - 1 else 0
    holding, rest = [largest] + [least] * (amount - 1), total - largest - least * (amount - 1)
    while rest > 0:
        candidates = [i for i in range(1, amount) if holding[i] < largest] or [i for i in range(1, amount) if holding[i] < limit]
        whole, remaining = sum([portions[i] for i in candidates]), rest
        for i in candidates:
            addition = min(limit - holding[i], max(1, remaining * portions[i] // whole), rest)
            holding[i] = holding[i] + addition
            rest = rest - addition
    return np.array(holding)


def scatter_about(rng, extent, deviation, bound, pieces=(), kind=jnp.bfloat16):
    values = deviation * jax.random.normal(rng, extent, jnp.float32)
    if pieces:
        values = values * levels(rng, extent, pieces, -0.22, 0.18)
    return jnp.clip(values, -bound, bound).astype(kind)


def setup_inputs(seed: int = 0) -> dict:
    keys = jax.random.split(jax.random.key(seed), 12)
    tokens = scatter_about(keys[0], (TOKENS, D), 1.0, 6.0, ((0, 32),))
    segment_ids = jax.vmap(lambda own: jnp.searchsorted(jnp.cumsum(ragged(own, DOCS, LEN, DOC_MAX, 2)), jnp.arange(LEN), side="right"))(jax.random.split(keys[1], (TOKENS // LEN))).reshape((TOKENS // LEN, LEN)).astype(jnp.int32)
    key_mask = set_ends((jax.random.randint(keys[2], (TOKENS // LEN, LEN), 0, 8) < 7).astype(jnp.int32), jax.random.fold_in(keys[2], 1), 0, 1)
    owners_keys = jax.random.split(jax.random.fold_in(keys[3], 1), PIECES // PIECES)
    owners_turns = jax.random.permutation(jax.random.fold_in(keys[3], 3), PIECES // PIECES)
    owners = jax.vmap(lambda own, number: routed_block(jax.random.fold_in(keys[3], 2), own, number, PIECES, N_DP, 1, CAP, 2))(owners_keys, owners_turns).reshape((PIECES, 1))
    master_slots = scatter_about(keys[4], (N_TENSOR, N_DP * CAP, PR, D), (D // 2) ** -0.5, 0.25, ((0, 2), (1, 16)), jnp.float32)
    slot_first = scatter_about(keys[5], (N_TENSOR, N_DP * CAP, PR, D), (GSQ ** 0.5), 384.0, ((0, 2), (1, 16)), jnp.float32)
    slot_second = jnp.clip(jnp.exp(math.log(16384.0) - 2.0794415 * jax.random.uniform(keys[6], (N_TENSOR, N_DP * CAP, PR, D), jnp.float32) ** levels(keys[6], (N_TENSOR, N_DP * CAP, PR, D), ((0, 2), (1, 16)), -0.2, 0.2)), 2048.0, 16384.0)
    vectors = draw_vectors(jax.random.fold_in(keys[11], 71), 0)
    vector_first = scatter_about(keys[8], (12, D), (GSQ ** 0.5), 384.0, (), jnp.float32)
    vector_second = jnp.clip(jnp.exp(jax.random.uniform(keys[9], (12, D), jnp.float32, math.log(2048.0), math.log(16384.0))), 2048.0, 16384.0)
    out_grad = scatter_about(keys[10], (TOKENS, D), 1.0, 6.0, ((0, 32),))
    return dict(tokens=tokens, segment_ids=segment_ids, key_mask=key_mask, owners=owners, master_slots=master_slots, slot_first=slot_first, slot_second=slot_second, vectors=vectors, vector_first=vector_first, vector_second=vector_second, out_grad=out_grad)


@jax.custom_vjp
def low(v):
    return lax.optimization_barrier(v.astype(jnp.bfloat16)).astype(jnp.float32)

@jax.custom_vjp
def low_back(v):
    return v

def low_keep(v):
    return (low(v), None)

def low_pass(kept, grad):
    return (grad,)

def back_keep(v):
    return (v, None)

def back_low(kept, grad):
    return (low(grad),)
low.defvjp(low_keep, low_pass)
low_back.defvjp(back_keep, back_low)
norm_eps = 1e-05
mask_fill = -1000000000.0
beta_one = 0.5
beta_two = 0.5
rate_matrix = 0.03
rate_vector = 0.1
weight_decay = 0.01
adam_eps = 1e-08
highest = lax.Precision.HIGHEST

def slot_index(owners):
    owner_of = owners[:, 0].astype(jnp.int32)
    positions = jnp.arange(owner_of.shape[0], dtype=jnp.int32)
    earlier = (positions[None, :] < positions[:, None]) & (owner_of[None, :] == owner_of[:, None])
    within = lax.optimization_barrier(jnp.sum(earlier.astype(jnp.int32), axis=1)).astype(jnp.int32)
    return (owner_of * CAP + within).astype(jnp.int32)

def layer_norm(residual, gains, offset):
    center = residual - lax.optimization_barrier(jnp.mean(residual, axis=-1, keepdims=True))
    spread = lax.optimization_barrier(jnp.mean(center * center, axis=-1, keepdims=True))
    return center * lax.rsqrt(spread + norm_eps) * gains + offset

def unpack(stacks):
    head_cols = D // N_TENSOR
    unit_cols = FF // N_TENSOR
    w_query = stacks[:, 0:head_cols].reshape(D, D).T
    w_key = stacks[:, head_cols:2 * head_cols].reshape(D, D).T
    w_value = stacks[:, 2 * head_cols:3 * head_cols].reshape(D, D).T
    w_out = stacks[:, 3 * head_cols:4 * head_cols].reshape(D, D)
    w_up = stacks[:, 4 * head_cols:4 * head_cols + unit_cols].reshape(FF, D).T
    w_down = stacks[:, 4 * head_cols + unit_cols:].reshape(FF, D)
    return (w_query, w_key, w_value, w_out, w_up, w_down)

def allowed_pairs(segment, valid):
    position = jnp.arange(LEN, dtype=jnp.int32)
    same = segment[:, None] == segment[None, :]
    return same & ((valid[None, :] == 1) | (position[:, None] == position[None, :]))

def attend_block(queries, key_rows, value_rows, allowed):
    scores = jnp.einsum('hqd,hkd->hqk', queries, key_rows, precision=highest)
    scores = jnp.where(allowed[None], low_back(scores), mask_fill)
    row_max = lax.optimization_barrier(jnp.max(scores, axis=-1, keepdims=True))
    raised = jnp.exp(scores - row_max)
    weights = raised / lax.optimization_barrier(jnp.sum(raised, axis=-1, keepdims=True))
    return jnp.einsum('hqk,hkd->hqd', low(weights), value_rows, precision=highest)

def attention(queries, key_rows, value_rows, allowed):
    blocks = LEN // QBLK
    grouped = queries.reshape(HEADS, blocks, QBLK, HD).transpose(1, 0, 2, 3)
    masks = allowed.reshape(blocks, QBLK, LEN)
    block_fn = jax.checkpoint(attend_block)

    def one_block(element):
        return block_fn(element[0], key_rows, value_rows, element[1])
    context = lax.map(one_block, (grouped, masks))
    return context.transpose(1, 0, 2, 3).reshape(HEADS, LEN, HD)

def split_heads(values):
    return values.reshape(LEN, HEADS, HD).transpose(1, 0, 2)

def group_product(copies, weights, cols):
    parts = jnp.einsum('tld,dtk->ltk', copies, weights.reshape(D, N_TENSOR, cols), precision=highest)
    return parts.reshape(LEN, N_TENSOR * cols)

def forward_one(stacks, vectors, tokens, allowed):
    w_query, w_key, w_value, w_out, w_up, w_down = unpack(stacks)
    head_cols = D // N_TENSOR
    unit_cols = FF // N_TENSOR
    query_scale = HD ** (-0.5)
    token_copies = low_back(jnp.broadcast_to(tokens, (N_TENSOR, LEN, D)))
    queries = low(low_back((group_product(token_copies, w_query, head_cols) + vectors[0]) * query_scale))
    key_rows = low(low_back(group_product(token_copies, w_key, head_cols)))
    value_rows = low(low_back(group_product(token_copies, w_value, head_cols) + vectors[1]))
    context = attention(split_heads(queries), split_heads(key_rows), split_heads(value_rows), allowed)
    context = low(low_back(context.transpose(1, 0, 2).reshape(LEN, D)))
    attn_terms = jnp.einsum('ltk,tkd->tld', context.reshape(LEN, N_TENSOR, head_cols), w_out.reshape(N_TENSOR, head_cols, D), precision=highest)
    mixed = low_back(lax.optimization_barrier(jnp.sum(low(attn_terms), axis=0))) + vectors[6]
    normed = layer_norm(tokens + mixed, vectors[8], vectors[9])
    norm_copies = low_back(jnp.broadcast_to(low(normed), (N_TENSOR, LEN, D)))
    hidden_pre = low_back(group_product(norm_copies, w_up, unit_cols) + vectors[2:6].reshape(FF))
    hidden = low(jax.nn.gelu(hidden_pre, approximate=False))
    mlp_terms = jnp.einsum('ltk,tkd->tld', hidden.reshape(LEN, N_TENSOR, unit_cols), w_down.reshape(N_TENSOR, unit_cols, D), precision=highest)
    branch = low_back(lax.optimization_barrier(jnp.sum(low(mlp_terms), axis=0))) + vectors[7]
    return layer_norm(normed + branch, vectors[10], vectors[11])

def adam_update(weights, first, second, grads, rate, decay):
    first_new = beta_one * first + (1.0 - beta_one) * grads
    second_new = beta_two * second + (1.0 - beta_two) * grads * grads
    first_hat = first_new / (1.0 - beta_one ** STEP)
    second_hat = second_new / (1.0 - beta_two ** STEP)
    updated = weights - rate * (first_hat / (jnp.sqrt(second_hat) + adam_eps) + decay * weights)
    return (updated, first_new, second_new)

def reference(tokens, segment_ids, key_mask, owners, master_slots, slot_first, slot_second, vectors, vector_first, vector_second, out_grad):
    slots = slot_index(owners)
    stacks = low(master_slots[:, slots].reshape(N_TENSOR, ROWS_T, D))
    seq_total = TOKENS // LEN
    inputs = (tokens.reshape(seq_total, LEN, D), segment_ids, key_mask, out_grad.reshape(seq_total, LEN, D))

    def one_sequence(carry, element):
        seq_tokens, seq_segments, seq_mask, seq_grad = element
        allowed = allowed_pairs(seq_segments, seq_mask)

        def forward(stack_arg, vector_arg, token_arg):
            return forward_one(stack_arg, vector_arg, token_arg, allowed)
        result, pullback = jax.vjp(forward, stacks, vectors, seq_tokens.astype(jnp.float32))
        grad_stacks, grad_vectors, grad_tokens = pullback(seq_grad.astype(jnp.float32))
        return ((carry[0] + grad_stacks, carry[1] + grad_vectors), (result.astype(jnp.bfloat16), grad_tokens.astype(jnp.bfloat16)))
    start = (jnp.zeros((N_TENSOR, ROWS_T, D), jnp.float32), jnp.zeros((12, D), jnp.float32))
    (grad_stacks, grad_vectors), (outputs, input_grads) = lax.scan(one_sequence, start, inputs)
    grad_slots = jnp.zeros_like(master_slots).at[:, slots].set(grad_stacks.reshape(N_TENSOR, PIECES, PR, D))
    slot_new, slot_first_new, slot_second_new = adam_update(master_slots, slot_first, slot_second, grad_slots, rate_matrix, weight_decay)
    vector_new, vector_first_new, vector_second_new = adam_update(vectors, vector_first, vector_second, grad_vectors, rate_vector, 0.0)
    return (outputs.reshape(TOKENS, D), input_grads.reshape(TOKENS, D), slot_new, slot_first_new, slot_second_new, vector_new, vector_first_new, vector_second_new)
```

```python
import functools

import jax
import jax.numpy as jnp
from jax import lax
from jax.experimental import pallas as pl
from jax.experimental.pallas import tpu as pltpu
from jax.sharding import PartitionSpec as P

D = 1024
HD = 64
FF = 4096
QBLK = 512
STEP = 10
CAP = 6


norm_eps = 1e-05
mask_fill = -1000000000.0
beta_one = 0.5
beta_two = 0.5
rate_matrix = 0.03
rate_vector = 0.1
weight_decay = 0.01
adam_eps = 1e-08


def slot_index(owners):
    owner_of = owners[:, 0]
    positions = jnp.arange(owner_of.shape[0], dtype=jnp.int32)
    earlier = (positions[None, :] < positions[:, None]) & (owner_of[None, :] == owner_of[:, None])
    within = jnp.sum(earlier.astype(jnp.int32), axis=1)
    return owner_of * CAP + within


def layer_stats(residual):
    center = residual - jnp.mean(residual, axis=-1, keepdims=True)
    spread = jnp.mean(center * center, axis=-1, keepdims=True)
    inverse = lax.rsqrt(spread + norm_eps)
    return (center * inverse, inverse)


def norm_back(grads, normal, inverse, gains):
    scaled = grads * gains
    return inverse * (
        scaled
        - jnp.mean(scaled, axis=-1, keepdims=True)
        - normal * jnp.mean(scaled * normal, axis=-1, keepdims=True)
    )


def gelu_exact(values):
    return jax.nn.gelu(values, approximate=False)


def block_mask(segment, valid, start):
    length = segment.shape[0]
    query_pos = start + jnp.arange(QBLK, dtype=jnp.int32)
    key_pos = jnp.arange(length, dtype=jnp.int32)
    query_seg = lax.dynamic_slice_in_dim(segment, start, QBLK, 0)
    same = query_seg[:, None] == segment[None, :]
    return same & ((valid[None, :] == 1) | (query_pos[:, None] == key_pos[None, :]))


def block_scores(block_q, key_rows, segment, valid, start):
    scores = jnp.einsum("qhd,khd->hqk", block_q, key_rows, preferred_element_type=jnp.float32)
    return jnp.where(block_mask(segment, valid, start)[None], scores, mask_fill)


def attend_forward(queries, key_rows, value_rows, segment, valid):
    length = queries.shape[0]

    def one_block(index):
        start = index * QBLK
        block_q = lax.dynamic_slice_in_dim(queries, start, QBLK, 0)
        scores = block_scores(block_q, key_rows, segment, valid, start)
        row_max = jnp.max(scores, axis=2, keepdims=True)
        raised = jnp.exp(scores - row_max)
        totals = jnp.sum(raised, axis=2, keepdims=True)
        weights = (raised / totals).astype(jnp.bfloat16)
        context = jnp.einsum(
            "hqk,khd->qhd", weights, value_rows, preferred_element_type=jnp.float32
        )
        return (context, (row_max + jnp.log(totals))[:, :, 0])

    context, log_sums = lax.map(one_block, jnp.arange(length // QBLK, dtype=jnp.int32))
    return (context.reshape(length, -1), log_sums)


def attend_backward(queries, key_rows, value_rows, segment, valid, log_sums, grad_context):
    length = queries.shape[0]

    def one_block(carry, index):
        key_acc, value_acc = carry
        start = index * QBLK
        block_q = lax.dynamic_slice_in_dim(queries, start, QBLK, 0)
        block_g = lax.dynamic_slice_in_dim(grad_context, start, QBLK, 0)
        scores = block_scores(block_q, key_rows, segment, valid, start)
        weights = jnp.exp(scores - log_sums[index][:, :, None])
        value_acc = value_acc + jnp.einsum(
            "hqk,qhd->khd",
            weights.astype(jnp.bfloat16),
            block_g,
            preferred_element_type=jnp.float32,
        )
        grad_weights = jnp.einsum(
            "qhd,khd->hqk", block_g, value_rows, preferred_element_type=jnp.float32
        )
        inner = jnp.sum(weights * grad_weights, axis=2, keepdims=True)
        grad_scores = (weights * (grad_weights - inner)).astype(jnp.bfloat16)
        grad_q = jnp.einsum(
            "hqk,khd->qhd", grad_scores, key_rows, preferred_element_type=jnp.float32
        )
        key_acc = key_acc + jnp.einsum(
            "hqk,qhd->khd", grad_scores, block_q, preferred_element_type=jnp.float32
        )
        return ((key_acc, value_acc), grad_q)

    zeros_kv = jnp.zeros(key_rows.shape, jnp.float32)
    (grad_keys, grad_values), grad_queries = lax.scan(
        one_block, (zeros_kv, zeros_kv), jnp.arange(length // QBLK, dtype=jnp.int32)
    )
    return (
        grad_queries.reshape(length, -1),
        grad_keys.reshape(length, -1),
        grad_values.reshape(length, -1),
    )


def adam_update(weights, first, second, grads, rate, decay):
    first_new = beta_one * first + (1.0 - beta_one) * grads
    second_new = beta_two * second + (1.0 - beta_two) * grads * grads
    first_hat = first_new / (1.0 - beta_one**STEP)
    second_hat = second_new / (1.0 - beta_two**STEP)
    updated = weights - rate * (first_hat / (jnp.sqrt(second_hat) + adam_eps) + decay * weights)
    return (updated, first_new, second_new)


def on_device_generic(
    tokens,
    segment_ids,
    key_mask,
    owners,
    master_slots,
    slot_first,
    slot_second,
    vectors,
    vector_first,
    vector_second,
    out_grad,
):
    n_tensor = lax.axis_size("tensor")
    group = lax.axis_index("tensor")
    head_cols = D // n_tensor
    unit_cols = FF // n_tensor
    heads_here = head_cols // HD
    seq_count = segment_ids.shape[0]
    length = segment_ids.shape[1]
    query_scale = HD ** (-0.5)
    slots = slot_index(owners)
    gathered_slots = lax.all_gather(master_slots[0].astype(jnp.bfloat16), "dp", axis=0, tiled=True)
    stack = jnp.take(gathered_slots, slots, axis=0).reshape(-1, D)
    w_mix = stack[0 : 3 * head_cols]
    w_out = stack[3 * head_cols : 4 * head_cols]
    w_up = stack[4 * head_cols : 4 * head_cols + unit_cols]
    w_down = stack[4 * head_cols + unit_cols :]
    bias_query = lax.dynamic_slice_in_dim(vectors[0], group * head_cols, head_cols, 0)
    bias_value = lax.dynamic_slice_in_dim(vectors[1], group * head_cols, head_cols, 0)
    bias_up = lax.dynamic_slice_in_dim(vectors[2:6].reshape(FF), group * unit_cols, unit_cols, 0)
    gathered = lax.all_gather(tokens, "tensor", axis=0, tiled=True)
    mixed = jnp.einsum("ld,kd->lk", gathered, w_mix, preferred_element_type=jnp.float32)
    queries = ((mixed[:, :head_cols] + bias_query) * query_scale).astype(jnp.bfloat16)
    key_rows = mixed[:, head_cols : 2 * head_cols].astype(jnp.bfloat16)
    value_rows = (mixed[:, 2 * head_cols :] + bias_value).astype(jnp.bfloat16)
    head_shape = (seq_count, length, heads_here, HD)
    queries_h = queries.reshape(head_shape)
    keys_h = key_rows.reshape(head_shape)
    values_h = value_rows.reshape(head_shape)

    def forward_seq(element):
        return attend_forward(element[0], element[1], element[2], element[3], element[4])

    context, log_sums = lax.map(forward_seq, (queries_h, keys_h, values_h, segment_ids, key_mask))
    context = context.reshape(-1, head_cols).astype(jnp.bfloat16)
    attn_sum = lax.psum_scatter(
        jnp.einsum("lk,kd->ld", context, w_out, preferred_element_type=jnp.float32).astype(
            jnp.bfloat16
        ),
        "tensor",
        scatter_dimension=0,
        tiled=True,
    ).astype(jnp.float32)
    residual_one = tokens.astype(jnp.float32) + (attn_sum + vectors[6])
    normal_one, inverse_one = layer_stats(residual_one)
    normed = normal_one * vectors[8] + vectors[9]
    normed_low = normed.astype(jnp.bfloat16)
    norm_rows = lax.all_gather(normed_low, "tensor", axis=0, tiled=True)
    hidden_pre = (
        jnp.einsum("ld,kd->lk", norm_rows, w_up, preferred_element_type=jnp.float32) + bias_up
    )
    hidden_full, gelu_pull = jax.vjp(gelu_exact, hidden_pre)
    hidden = hidden_full.astype(jnp.bfloat16)
    mlp_sum = lax.psum_scatter(
        jnp.einsum("lk,kd->ld", hidden, w_down, preferred_element_type=jnp.float32).astype(
            jnp.bfloat16
        ),
        "tensor",
        scatter_dimension=0,
        tiled=True,
    ).astype(jnp.float32)
    residual_two = normed + (mlp_sum + vectors[7])
    normal_two, inverse_two = layer_stats(residual_two)
    layer_out = (normal_two * vectors[10] + vectors[11]).astype(jnp.bfloat16)
    grad_out = out_grad.astype(jnp.float32)
    grad_two = norm_back(grad_out, normal_two, inverse_two, vectors[10])
    grad_down_in = lax.all_gather(grad_two.astype(jnp.bfloat16), "tensor", axis=0, tiled=True)
    grad_hidden = jnp.einsum("ld,kd->lk", grad_down_in, w_down, preferred_element_type=jnp.float32)
    grad_w_down = jnp.einsum("lk,ld->kd", hidden, grad_down_in, preferred_element_type=jnp.float32)
    grad_pre = gelu_pull(grad_hidden)[0].astype(jnp.bfloat16)
    norm_back_rows = lax.all_gather(normed_low, "tensor", axis=0, tiled=True)
    grad_w_up = jnp.einsum(
        "lk,ld->kd", grad_pre, norm_back_rows, preferred_element_type=jnp.float32
    )
    grad_norm = grad_two + lax.psum_scatter(
        jnp.einsum("lk,kd->ld", grad_pre, w_up, preferred_element_type=jnp.float32).astype(
            jnp.bfloat16
        ),
        "tensor",
        scatter_dimension=0,
        tiled=True,
    ).astype(jnp.float32)
    grad_one = norm_back(grad_norm, normal_one, inverse_one, vectors[8])
    grad_attn_in = lax.all_gather(grad_one.astype(jnp.bfloat16), "tensor", axis=0, tiled=True)
    grad_context = jnp.einsum(
        "ld,kd->lk", grad_attn_in, w_out, preferred_element_type=jnp.float32
    ).astype(jnp.bfloat16)
    grad_w_out = jnp.einsum("lk,ld->kd", context, grad_attn_in, preferred_element_type=jnp.float32)

    def backward_seq(element):
        return attend_backward(
            element[0], element[1], element[2], element[3], element[4], element[5], element[6]
        )

    grad_q, grad_k, grad_v = lax.map(
        backward_seq,
        (
            queries_h,
            keys_h,
            values_h,
            segment_ids,
            key_mask,
            log_sums,
            grad_context.reshape(head_shape),
        ),
    )
    grad_queries = grad_q.reshape(-1, head_cols).astype(jnp.bfloat16) * query_scale
    grad_keys = grad_k.reshape(-1, head_cols).astype(jnp.bfloat16)
    grad_values = grad_v.reshape(-1, head_cols).astype(jnp.bfloat16)
    grad_mix = jnp.concatenate([grad_queries, grad_keys, grad_values], axis=1)
    mix_back_rows = lax.all_gather(tokens, "tensor", axis=0, tiled=True)
    grad_w_mix = jnp.einsum(
        "lk,ld->kd", grad_mix, mix_back_rows, preferred_element_type=jnp.float32
    )
    input_grad = (
        grad_one
        + lax.psum_scatter(
            jnp.einsum("lk,kd->ld", grad_mix, w_mix, preferred_element_type=jnp.float32).astype(
                jnp.bfloat16
            ),
            "tensor",
            scatter_dimension=0,
            tiled=True,
        ).astype(jnp.float32)
    ).astype(jnp.bfloat16)
    query_full = lax.dynamic_update_slice_in_dim(
        jnp.zeros((D,), jnp.float32),
        jnp.sum(grad_queries.astype(jnp.float32), axis=0),
        group * head_cols,
        0,
    )
    value_full = lax.dynamic_update_slice_in_dim(
        jnp.zeros((D,), jnp.float32),
        jnp.sum(grad_values.astype(jnp.float32), axis=0),
        group * head_cols,
        0,
    )
    up_full = lax.dynamic_update_slice_in_dim(
        jnp.zeros((FF,), jnp.float32),
        jnp.sum(grad_pre.astype(jnp.float32), axis=0),
        group * unit_cols,
        0,
    )
    tail_rows = jnp.stack(
        [
            jnp.sum(grad_one, axis=0),
            jnp.sum(grad_two, axis=0),
            jnp.sum(grad_norm * normal_one, axis=0),
            jnp.sum(grad_norm, axis=0),
            jnp.sum(grad_out * normal_two, axis=0),
            jnp.sum(grad_out, axis=0),
        ]
    )
    vector_terms = jnp.concatenate(
        [jnp.stack([query_full, value_full]), up_full.reshape(FF // D, D), tail_rows], axis=0
    )
    vector_grads = lax.psum(vector_terms, ("dp", "tensor"))
    grad_stack = jnp.concatenate([grad_w_mix, grad_w_out, grad_w_up, grad_w_down], axis=0)
    grad_pieces = grad_stack.reshape(slots.shape[0], -1, D)
    spread_slots = (
        jnp.zeros((lax.axis_size("dp") * CAP,) + grad_pieces.shape[1:], jnp.float32)
        .at[slots]
        .set(grad_pieces)
    )
    own_grads = lax.psum_scatter(
        spread_slots.astype(jnp.bfloat16), "dp", scatter_dimension=0, tiled=True
    ).astype(jnp.float32)
    slot_new, slot_first_new, slot_second_new = adam_update(
        master_slots[0], slot_first[0], slot_second[0], own_grads, rate_matrix, weight_decay
    )
    vector_new, vector_first_new, vector_second_new = adam_update(
        vectors, vector_first, vector_second, vector_grads, rate_vector, 0.0
    )
    return (
        layer_out,
        input_grad,
        slot_new[None],
        slot_first_new[None],
        slot_second_new[None],
        vector_new,
        vector_first_new,
        vector_second_new,
    )


DOC_MAX = 800
EXT_PAD = 512
ABLK = 256
HPG = 4
AUG = 16
neg_big = -1000000000.0
NN = (((1,), (0,)), ((), ()))
NT = (((1,), (1,)), ((), ()))
TN = (((0,), (0,)), ((), ()))


def mm(a, b, dims):
    return lax.dot_general(a, b, dims, preferred_element_type=jnp.float32)


def attn_fwd_kernel(lo_ref, hi_ref, q_ref, k_ref, v_ref, qaug_ref, kaug_ref, hid_ref, o_ref, lse_ref, kn_ref, m_ref, acc_ref):
    ext = q_ref.shape[1]
    ones = jnp.concatenate(
        [jnp.ones((1, ABLK), jnp.float32), jnp.zeros((AUG - 1, ABLK), jnp.float32)], axis=0
    ).astype(jnp.bfloat16)
    for h in range(HPG):
        rows = slice(h * HD, (h + 1) * HD)
        kn_ref[h] = jnp.concatenate([k_ref[rows, :], kaug_ref[...]], axis=0).T

    def query_block(qb, _):
        lo = lo_ref[qb]
        hi = hi_ref[qb]
        qs = pl.ds(pl.multiple_of(qb * ABLK, ABLK), ABLK)

        @pl.when(hi > lo)
        def _work():
            hidden = hid_ref[0:1, qs]
            for h in range(HPG):
                rows = slice(h * HD, (h + 1) * HD)
                q32 = q_ref[rows, qs].astype(jnp.float32)
                k32 = k_ref[rows, qs].astype(jnp.float32)
                own = jnp.sum(q32 * k32, axis=0, keepdims=True)
                m_ref[h] = jnp.where(hidden > 0.0, own, -1e30)
                acc_ref[h, 0:HD, :] = v_ref[rows, qs].astype(jnp.float32) * hidden
                acc_ref[h, HD:, :] = jnp.broadcast_to(hidden, (AUG, ABLK))

            def key_block(kb, _):
                ks = pl.ds(pl.multiple_of(kb * ABLK, ABLK), ABLK)
                for h in range(HPG):
                    rows = slice(h * HD, (h + 1) * HD)
                    qa = jnp.concatenate([q_ref[rows, qs], qaug_ref[:, qs]], axis=0)
                    s = mm(kn_ref[h, ks, :], qa, NN)
                    old = m_ref[h]
                    new = jnp.maximum(old, jnp.max(s, axis=0, keepdims=True))
                    m_ref[h] = new
                    p = jnp.exp(s - new).astype(jnp.bfloat16)
                    va = jnp.concatenate([v_ref[rows, ks], ones], axis=0)
                    acc_ref[h] = acc_ref[h] * jnp.exp(old - new) + mm(va, p, NN)
                return 0

            lax.fori_loop(lo, hi, key_block, 0)
            for h in range(HPG):
                rows = slice(h * HD, (h + 1) * HD)
                total = acc_ref[h, HD : HD + 1, :]
                o_ref[rows, qs] = (acc_ref[h, 0:HD, :] * (1.0 / total)).astype(jnp.bfloat16)
                lse_ref[0, h : h + 1, qs] = m_ref[h] + jnp.log(total)

        @pl.when(hi <= lo)
        def _skip():
            o_ref[:, qs] = jnp.zeros((HPG * HD, ABLK), jnp.bfloat16)
            lse_ref[0, :, qs] = jnp.zeros((8, ABLK), jnp.float32)

        return 0

    lax.fori_loop(0, ext // ABLK, query_block, 0)


def attn_bwd_kernel(
    lo_ref, hi_ref, q_ref, k_ref, v_ref, g_ref, c_ref, lse_ref, qaug_ref, kaug_ref, hid_ref,
    dq_ref, dk_ref, dv_ref, kn_ref, vn_ref, acc_ref, dk_acc, dv_acc,
):
    ext = q_ref.shape[1]
    for h in range(HPG):
        rows = slice(h * HD, (h + 1) * HD)
        kn_ref[h] = jnp.concatenate([k_ref[rows, :], kaug_ref[...]], axis=0).T
        vn_ref[h] = v_ref[rows, :].T
    dk_acc[...] = jnp.zeros_like(dk_acc)
    dv_acc[...] = jnp.zeros_like(dv_acc)

    def query_block(qb, _):
        lo = lo_ref[qb]
        hi = hi_ref[qb]
        qs = pl.ds(pl.multiple_of(qb * ABLK, ABLK), ABLK)

        @pl.when(hi > lo)
        def _work():
            hidden = hid_ref[0:1, qs]
            deltas = []
            logs = []
            for h in range(HPG):
                rows = slice(h * HD, (h + 1) * HD)
                q32 = q_ref[rows, qs].astype(jnp.float32)
                k32 = k_ref[rows, qs].astype(jnp.float32)
                v32 = v_ref[rows, qs].astype(jnp.float32)
                g32 = g_ref[rows, qs].astype(jnp.float32)
                c32 = c_ref[rows, qs].astype(jnp.float32)
                delta = jnp.sum(g32 * c32, axis=0, keepdims=True)
                log = lse_ref[0, h : h + 1, qs]
                own = jnp.sum(q32 * k32, axis=0, keepdims=True)
                p_own = jnp.where(hidden > 0.0, jnp.exp(own - log), 0.0)
                d_own = p_own * (jnp.sum(g32 * v32, axis=0, keepdims=True) - delta)
                acc_ref[h] = d_own * k32
                dk_acc[rows, qs] += d_own * q32
                dv_acc[rows, qs] += p_own * g32
                deltas.append(delta)
                logs.append(log)

            def key_block(kb, _):
                ks = pl.ds(pl.multiple_of(kb * ABLK, ABLK), ABLK)
                for h in range(HPG):
                    rows = slice(h * HD, (h + 1) * HD)
                    q = q_ref[rows, qs]
                    g = g_ref[rows, qs]
                    qa = jnp.concatenate([q, qaug_ref[:, qs]], axis=0)
                    s = mm(kn_ref[h, ks, :], qa, NN)
                    p = jnp.exp(s - logs[h])
                    dp = mm(vn_ref[h, ks, :], g, NN)
                    ds = (p * (dp - deltas[h])).astype(jnp.bfloat16)
                    pb = p.astype(jnp.bfloat16)
                    dv_acc[rows, ks] += mm(g, pb, NT)
                    dk_acc[rows, ks] += mm(q, ds, NT)
                    acc_ref[h] += mm(k_ref[rows, ks], ds, NN)
                return 0

            lax.fori_loop(lo, hi, key_block, 0)
            for h in range(HPG):
                rows = slice(h * HD, (h + 1) * HD)
                dq_ref[rows, qs] = acc_ref[h].astype(jnp.bfloat16) * (HD ** (-0.5))

        @pl.when(hi <= lo)
        def _skip():
            dq_ref[:, qs] = jnp.zeros((HPG * HD, ABLK), jnp.bfloat16)

        return 0

    lax.fori_loop(0, ext // ABLK, query_block, 0)
    dk_ref[...] = dk_acc[...].astype(jnp.bfloat16)
    dv_ref[...] = dv_acc[...].astype(jnp.bfloat16)


def group_block(offset, rows, ext):
    return pl.BlockSpec((rows, ext), lambda g, lo, hi: (offset + g, 0))


def fixed_block(rows, ext):
    return pl.BlockSpec((rows, ext), lambda g, lo, hi: (0, 0))


def attend(lo, hi, qkv, qaug, kaug, hidden):
    ext = qkv.shape[1]
    groups = D // HD // HPG
    rows = HPG * HD
    return pl.pallas_call(
        attn_fwd_kernel,
        out_shape=(
            jax.ShapeDtypeStruct((D, ext), jnp.bfloat16),
            jax.ShapeDtypeStruct((groups, 8, ext), jnp.float32),
        ),
        grid_spec=pltpu.PrefetchScalarGridSpec(
            num_scalar_prefetch=2,
            grid=(groups,),
            in_specs=[
                group_block(0, rows, ext),
                group_block(groups, rows, ext),
                group_block(2 * groups, rows, ext),
                fixed_block(AUG, ext),
                fixed_block(AUG, ext),
                fixed_block(8, ext),
            ],
            out_specs=[
                group_block(0, rows, ext),
                pl.BlockSpec((1, 8, ext), lambda g, lo, hi: (g, 0, 0)),
            ],
            scratch_shapes=[
                pltpu.VMEM((HPG, ext, HD + AUG), jnp.bfloat16),
                pltpu.VMEM((HPG, 1, ABLK), jnp.float32),
                pltpu.VMEM((HPG, HD + AUG, ABLK), jnp.float32),
            ],
        ),
        compiler_params=pltpu.CompilerParams(vmem_limit_bytes=40 * 2**20),
        cost_estimate=pl.CostEstimate(flops=20 * 10**9, bytes_accessed=14 * 10**6, transcendentals=0),
        name="attend",
    )(lo, hi, qkv, qkv, qkv, qaug, kaug, hidden)


def attend_back(lo, hi, qkv, grads, context, logs, qaug, kaug, hidden):
    ext = qkv.shape[1]
    groups = D // HD // HPG
    rows = HPG * HD
    out = jax.ShapeDtypeStruct((D, ext), jnp.bfloat16)
    return pl.pallas_call(
        attn_bwd_kernel,
        out_shape=(out, out, out),
        grid_spec=pltpu.PrefetchScalarGridSpec(
            num_scalar_prefetch=2,
            grid=(groups,),
            in_specs=[
                group_block(0, rows, ext),
                group_block(groups, rows, ext),
                group_block(2 * groups, rows, ext),
                group_block(0, rows, ext),
                group_block(0, rows, ext),
                pl.BlockSpec((1, 8, ext), lambda g, lo, hi: (g, 0, 0)),
                fixed_block(AUG, ext),
                fixed_block(AUG, ext),
                fixed_block(8, ext),
            ],
            out_specs=[group_block(0, rows, ext)] * 3,
            scratch_shapes=[
                pltpu.VMEM((HPG, ext, HD + AUG), jnp.bfloat16),
                pltpu.VMEM((HPG, ext, HD), jnp.bfloat16),
                pltpu.VMEM((HPG, HD, ABLK), jnp.float32),
                pltpu.VMEM((rows, ext), jnp.float32),
                pltpu.VMEM((rows, ext), jnp.float32),
            ],
        ),
        compiler_params=pltpu.CompilerParams(vmem_limit_bytes=48 * 2**20),
        cost_estimate=pl.CostEstimate(flops=50 * 10**9, bytes_accessed=30 * 10**6, transcendentals=0),
        name="attend_back",
    )(lo, hi, qkv, qkv, qkv, grads, context, logs, qaug, kaug, hidden)


def document_plan(segment, valid, half, rows):
    length = segment.shape[0]
    ext = rows + EXT_PAD
    base = half * EXT_PAD
    position = jnp.arange(length, dtype=jnp.int32)
    documents = jnp.arange(8, dtype=jnp.int32)[:, None]
    one_hot = segment[None, :] == documents
    counts = jnp.sum(one_hot.astype(jnp.int32), axis=1, keepdims=True)
    starts = jnp.sum((segment[None, :] < documents).astype(jnp.int32), axis=1, keepdims=True)
    start = jnp.sum(jnp.where(one_hot, starts, 0), axis=0)
    end = jnp.sum(jnp.where(one_hot, starts + counts, 0), axis=0)
    crossing = (start < rows) & (end > rows)
    left = jnp.max(jnp.where(crossing, rows - start, 0))
    right = jnp.max(jnp.where(crossing, end - rows, 0))
    worker = jnp.where(left <= right, half == 1, half == 0)
    own = (position >= half * rows) & (position < (half + 1) * rows)
    handled = jnp.where(crossing, worker, own)
    cut = lambda values: lax.dynamic_slice_in_dim(values, base, ext, 0)
    handled_ext = cut(handled)
    begins = jnp.where(handled_ext, cut(start) - base, ext).reshape(-1, ABLK)
    ends = jnp.where(handled_ext, cut(end) - base, 0).reshape(-1, ABLK)
    lo = jnp.min(begins, axis=1) // ABLK
    hi = (jnp.max(ends, axis=1) + (ABLK - 1)) // ABLK
    blank = jnp.max(ends, axis=1) == 0
    lo = jnp.where(blank, 0, lo)
    hi = jnp.where(blank, 0, hi)
    hot = cut(one_hot.T).T
    masked = cut(valid) == 0
    ones = jnp.ones((1, ext), jnp.bfloat16)
    fill = jnp.zeros((AUG - 9, ext), jnp.bfloat16)
    qaug = jnp.concatenate([hot.astype(jnp.bfloat16), ones, fill], axis=0)
    kaug = jnp.concatenate(
        [
            jnp.where(hot, 0.0, neg_big).astype(jnp.bfloat16),
            jnp.where(masked[None, :], neg_big, 0.0).astype(jnp.bfloat16),
            fill,
        ],
        axis=0,
    )
    hidden = jnp.broadcast_to(masked.astype(jnp.float32)[None, :], (8, ext))
    foreign = lax.dynamic_slice_in_dim(crossing & ~worker, half * rows, rows, 0)
    return lo, hi, qaug, kaug, hidden, handled_ext, foreign


def gelu_pair(values):
    cdf = 0.5 * lax.erfc(values * (-(0.5**0.5)))
    density = jnp.exp(values * values * -0.5) * (0.5 / jnp.pi) ** 0.5
    return (values * cdf, cdf + values * density)


def on_device_rows(
    tokens,
    segment_ids,
    key_mask,
    owners,
    master_slots,
    slot_first,
    slot_second,
    vectors,
    vector_first,
    vector_second,
    out_grad,
):
    n_dp = lax.axis_size("dp")
    n_tensor = lax.axis_size("tensor")
    half = lax.axis_index("tensor")
    every = ("tensor", "dp")
    rows = tokens.shape[0]
    ext = rows + EXT_PAD
    halo = DOC_MAX // 2
    swap = [(0, 1), (1, 0)]
    edge = jnp.where(half == 0, rows - halo, 0)
    halo_at = jnp.where(half == 0, rows, EXT_PAD - halo)
    own_at = half * EXT_PAD

    def extend(own_rows, halo_rows):
        whole = jnp.zeros((ext,) + own_rows.shape[1:], own_rows.dtype)
        whole = lax.dynamic_update_slice_in_dim(whole, halo_rows, halo_at, 0)
        return lax.dynamic_update_slice_in_dim(whole, own_rows, own_at, 0)

    def own_part(values):
        return lax.dynamic_slice_in_dim(values, own_at, rows, 0)

    def halo_part(values):
        return lax.dynamic_slice_in_dim(values, halo_at, halo, 0)

    lo, hi, qaug, kaug, hidden_keys, handled, foreign = document_plan(
        segment_ids[0], key_mask[0], half, rows
    )
    halo_tokens = lax.ppermute(lax.dynamic_slice_in_dim(tokens, edge, halo, 0), "tensor", swap)
    tokens_ext = extend(tokens, halo_tokens)

    slots = slot_index(owners)
    pieces = slots.shape[0]
    piece_rows = master_slots.shape[2]
    chunk = piece_rows // n_dp
    low_slots = master_slots[0].astype(jnp.bfloat16).reshape(CAP, n_dp, chunk, D)
    spread = lax.all_to_all(low_slots.transpose(1, 0, 2, 3), "dp", 0, 0, tiled=False)
    dense = jnp.take(spread.reshape(n_dp * CAP, chunk, D), slots, axis=0)
    mix_pieces = 4 * (D // n_tensor) // piece_rows
    up_pieces = (FF // n_tensor) // piece_rows

    def gather(part):
        return lax.all_gather(part.reshape(-1, D), every, axis=0, tiled=True)

    w_mix = gather(dense[:mix_pieces])
    w_up = gather(dense[mix_pieces : mix_pieces + up_pieces])
    w_down = gather(dense[mix_pieces + up_pieces :])
    per = mix_pieces // 4
    w_mix = (
        w_mix.reshape(n_tensor, n_dp, 4, per, chunk, D).transpose(2, 0, 3, 1, 4, 5).reshape(4 * D, D)
    )
    w_qkv = w_mix[: 3 * D]
    w_out = w_mix[3 * D :]
    bias_up = (
        vectors[2:6].reshape(n_tensor, up_pieces, n_dp, chunk).transpose(0, 2, 1, 3).reshape(FF)
    )

    bias_qkv = jnp.concatenate([vectors[0], jnp.zeros((D,), jnp.float32), vectors[1]])
    scale_qkv = jnp.concatenate([jnp.full((D,), HD ** (-0.5)), jnp.ones((2 * D,))])
    qkv = (
        (mm(w_qkv, tokens_ext, NT) + bias_qkv[:, None]) * scale_qkv.astype(jnp.float32)[:, None]
    ).astype(jnp.bfloat16)
    context, logs = attend(lo, hi, qkv, qaug, kaug, hidden_keys)
    attn_ext = mm(context, w_out, TN).astype(jnp.bfloat16)
    halo_attn = lax.ppermute(halo_part(attn_ext), "tensor", swap)
    attn_back = lax.dynamic_update_slice_in_dim(
        jnp.zeros((rows, D), jnp.bfloat16), halo_attn, edge, 0
    )
    attn_sum = jnp.where(foreign[:, None], attn_back, own_part(attn_ext)).astype(jnp.float32)
    residual_one = tokens.astype(jnp.float32) + (attn_sum + vectors[6])
    normal_one, inverse_one = layer_stats(residual_one)
    normed = normal_one * vectors[8] + vectors[9]
    normed_low = normed.astype(jnp.bfloat16)

    gelu, slope = gelu_pair(mm(normed_low, w_up, NT) + bias_up)
    hidden = gelu.astype(jnp.bfloat16)
    slope = slope.astype(jnp.bfloat16)
    residual_two = normed + (mm(hidden, w_down, NN) + vectors[7])
    normal_two, inverse_two = layer_stats(residual_two)
    layer_out = (normal_two * vectors[10] + vectors[11]).astype(jnp.bfloat16)
    grad_out = out_grad.astype(jnp.float32)
    grad_two = norm_back(grad_out, normal_two, inverse_two, vectors[10])
    grad_two_low = grad_two.astype(jnp.bfloat16)

    def scatter(part):
        return lax.psum_scatter(part, every, scatter_dimension=0, tiled=True)

    grad_w_down = scatter(mm(hidden, grad_two_low, TN).astype(jnp.bfloat16))
    grad_pre32 = mm(grad_two_low, w_down, NT) * slope.astype(jnp.float32)
    grad_pre = grad_pre32.astype(jnp.bfloat16)
    grad_w_up = scatter(mm(grad_pre, normed_low, TN).astype(jnp.bfloat16))
    grad_norm = grad_two + mm(grad_pre, w_up, NN)
    grad_one = norm_back(grad_norm, normal_one, inverse_one, vectors[8])
    grad_one_low = grad_one.astype(jnp.bfloat16)

    halo_grad = lax.ppermute(
        lax.dynamic_slice_in_dim(grad_one_low, edge, halo, 0), "tensor", swap
    )
    grad_ext = jnp.where(handled[:, None], extend(grad_one_low, halo_grad), 0)
    grad_context = mm(w_out, grad_ext, NT).astype(jnp.bfloat16)
    grad_w_out = mm(context, grad_ext, NN)
    grad_q, grad_k, grad_v = attend_back(
        lo, hi, qkv, grad_context, context, logs, qaug, kaug, hidden_keys
    )
    grad_qkv = jnp.concatenate([grad_q, grad_k, grad_v], axis=0)
    grad_w_qkv = mm(grad_qkv, tokens_ext, NN)
    grad_w_mix = jnp.concatenate([grad_w_qkv, grad_w_out], axis=0).astype(jnp.bfloat16)
    grad_w_mix = scatter(
        grad_w_mix.reshape(4, n_tensor, per, n_dp, chunk, D)
        .transpose(1, 3, 0, 2, 4, 5)
        .reshape(4 * D, D)
    )
    input_ext = mm(grad_qkv, w_qkv, TN)
    halo_input = lax.ppermute(halo_part(input_ext).astype(jnp.bfloat16), "tensor", swap)
    input_back = lax.dynamic_update_slice_in_dim(
        jnp.zeros((rows, D), jnp.bfloat16), halo_input, edge, 0
    )
    input_grad = (grad_one + own_part(input_ext) + input_back.astype(jnp.float32)).astype(
        jnp.bfloat16
    )

    up_sum = (
        jnp.sum(grad_pre.astype(jnp.float32), axis=0)
        .reshape(n_tensor, n_dp, up_pieces, chunk)
        .transpose(0, 2, 1, 3)
        .reshape(FF // D, D)
    )
    vector_terms = jnp.concatenate(
        [
            jnp.stack(
                [
                    jnp.sum(grad_q.astype(jnp.float32), axis=1),
                    jnp.sum(grad_v.astype(jnp.float32), axis=1),
                ]
            ),
            up_sum,
            jnp.stack(
                [
                    jnp.sum(grad_one, axis=0),
                    jnp.sum(grad_two, axis=0),
                    jnp.sum(grad_norm * normal_one, axis=0),
                    jnp.sum(grad_norm, axis=0),
                    jnp.sum(grad_out * normal_two, axis=0),
                    jnp.sum(grad_out, axis=0),
                ]
            ),
        ],
        axis=0,
    )
    vector_grads = lax.psum(vector_terms, ("dp", "tensor"))

    grad_chunks = jnp.concatenate([grad_w_mix, grad_w_up, grad_w_down], axis=0).reshape(
        pieces, chunk, D
    )
    piece_of = jnp.full((n_dp * CAP,), pieces, jnp.int32).at[slots].set(
        jnp.arange(pieces, dtype=jnp.int32)
    )
    padded = jnp.concatenate([grad_chunks, jnp.zeros((1, chunk, D), jnp.bfloat16)], axis=0)
    outgoing = jnp.take(padded, piece_of, axis=0).reshape(n_dp, CAP, chunk, D)
    incoming = lax.all_to_all(outgoing, "dp", 0, 0, tiled=False)
    own_grads = incoming.transpose(1, 0, 2, 3).reshape(CAP, piece_rows, D).astype(jnp.float32)
    slot_new, slot_first_new, slot_second_new = adam_update(
        master_slots[0], slot_first[0], slot_second[0], own_grads, rate_matrix, weight_decay
    )
    vector_new, vector_first_new, vector_second_new = adam_update(
        vectors, vector_first, vector_second, vector_grads, rate_vector, 0.0
    )
    return (
        layer_out,
        input_grad,
        slot_new[None],
        slot_first_new[None],
        slot_second_new[None],
        vector_new,
        vector_first_new,
        vector_second_new,
    )


def solution(mesh):
    placed = (
        P(("dp", "tensor"), None),
        P("dp", None),
        P("dp", None),
        P(),
        P("tensor", "dp", None, None),
        P("tensor", "dp", None, None),
        P("tensor", "dp", None, None),
        P(),
        P(),
        P(),
        P(("dp", "tensor"), None),
    )
    two_halves = mesh.shape["tensor"] == 2
    return jax.shard_map(
        on_device_rows if two_halves else on_device_generic,
        mesh=mesh,
        in_specs=placed,
        out_specs=(
            P(("dp", "tensor"), None),
            P(("dp", "tensor"), None),
            P("tensor", "dp", None, None),
            P("tensor", "dp", None, None),
            P("tensor", "dp", None, None),
            P(),
            P(),
            P(),
        ),
        check_vma=False,
    )
```

```python
import functools

import jax
import jax.numpy as jnp
from jax import lax
from jax.experimental import pallas as pl
from jax.experimental.pallas import tpu as pltpu
from jax.sharding import PartitionSpec as P

D = 1024
HD = 64
FF = 4096
QBLK = 512
STEP = 10
CAP = 6


norm_eps = 1e-05
mask_fill = -1000000000.0
beta_one = 0.5
beta_two = 0.5
rate_matrix = 0.03
rate_vector = 0.1
weight_decay = 0.01
adam_eps = 1e-08


def slot_index(owners):
    owner_of = owners[:, 0]
    positions = jnp.arange(owner_of.shape[0], dtype=jnp.int32)
    earlier = (positions[None, :] < positions[:, None]) & (owner_of[None, :] == owner_of[:, None])
    within = jnp.sum(earlier.astype(jnp.int32), axis=1)
    return owner_of * CAP + within


def layer_stats(residual):
    center = residual - jnp.mean(residual, axis=-1, keepdims=True)
    spread = jnp.mean(center * center, axis=-1, keepdims=True)
    inverse = lax.rsqrt(spread + norm_eps)
    return (center * inverse, inverse)


def norm_back(grads, normal, inverse, gains):
    scaled = grads * gains
    return inverse * (
        scaled
        - jnp.mean(scaled, axis=-1, keepdims=True)
        - normal * jnp.mean(scaled * normal, axis=-1, keepdims=True)
    )


def gelu_exact(values):
    return jax.nn.gelu(values, approximate=False)


def block_mask(segment, valid, start):
    length = segment.shape[0]
    query_pos = start + jnp.arange(QBLK, dtype=jnp.int32)
    key_pos = jnp.arange(length, dtype=jnp.int32)
    query_seg = lax.dynamic_slice_in_dim(segment, start, QBLK, 0)
    same = query_seg[:, None] == segment[None, :]
    return same & ((valid[None, :] == 1) | (query_pos[:, None] == key_pos[None, :]))


def block_scores(block_q, key_rows, segment, valid, start):
    scores = jnp.einsum("qhd,khd->hqk", block_q, key_rows, preferred_element_type=jnp.float32)
    return jnp.where(block_mask(segment, valid, start)[None], scores, mask_fill)


def attend_forward(queries, key_rows, value_rows, segment, valid):
    length = queries.shape[0]

    def one_block(index):
        start = index * QBLK
        block_q = lax.dynamic_slice_in_dim(queries, start, QBLK, 0)
        scores = block_scores(block_q, key_rows, segment, valid, start)
        row_max = jnp.max(scores, axis=2, keepdims=True)
        raised = jnp.exp(scores - row_max)
        totals = jnp.sum(raised, axis=2, keepdims=True)
        weights = (raised / totals).astype(jnp.bfloat16)
        context = jnp.einsum(
            "hqk,khd->qhd", weights, value_rows, preferred_element_type=jnp.float32
        )
        return (context, (row_max + jnp.log(totals))[:, :, 0])

    context, log_sums = lax.map(one_block, jnp.arange(length // QBLK, dtype=jnp.int32))
    return (context.reshape(length, -1), log_sums)


def attend_backward(queries, key_rows, value_rows, segment, valid, log_sums, grad_context):
    length = queries.shape[0]

    def one_block(carry, index):
        key_acc, value_acc = carry
        start = index * QBLK
        block_q = lax.dynamic_slice_in_dim(queries, start, QBLK, 0)
        block_g = lax.dynamic_slice_in_dim(grad_context, start, QBLK, 0)
        scores = block_scores(block_q, key_rows, segment, valid, start)
        weights = jnp.exp(scores - log_sums[index][:, :, None])
        value_acc = value_acc + jnp.einsum(
            "hqk,qhd->khd",
            weights.astype(jnp.bfloat16),
            block_g,
            preferred_element_type=jnp.float32,
        )
        grad_weights = jnp.einsum(
            "qhd,khd->hqk", block_g, value_rows, preferred_element_type=jnp.float32
        )
        inner = jnp.sum(weights * grad_weights, axis=2, keepdims=True)
        grad_scores = (weights * (grad_weights - inner)).astype(jnp.bfloat16)
        grad_q = jnp.einsum(
            "hqk,khd->qhd", grad_scores, key_rows, preferred_element_type=jnp.float32
        )
        key_acc = key_acc + jnp.einsum(
            "hqk,qhd->khd", grad_scores, block_q, preferred_element_type=jnp.float32
        )
        return ((key_acc, value_acc), grad_q)

    zeros_kv = jnp.zeros(key_rows.shape, jnp.float32)
    (grad_keys, grad_values), grad_queries = lax.scan(
        one_block, (zeros_kv, zeros_kv), jnp.arange(length // QBLK, dtype=jnp.int32)
    )
    return (
        grad_queries.reshape(length, -1),
        grad_keys.reshape(length, -1),
        grad_values.reshape(length, -1),
    )


def adam_update(weights, first, second, grads, rate, decay):
    first_new = beta_one * first + (1.0 - beta_one) * grads
    second_new = beta_two * second + (1.0 - beta_two) * grads * grads
    first_hat = first_new / (1.0 - beta_one**STEP)
    second_hat = second_new / (1.0 - beta_two**STEP)
    updated = weights - rate * (first_hat / (jnp.sqrt(second_hat) + adam_eps) + decay * weights)
    return (updated, first_new, second_new)


def on_device_generic(
    tokens,
    segment_ids,
    key_mask,
    owners,
    master_slots,
    slot_first,
    slot_second,
    vectors,
    vector_first,
    vector_second,
    out_grad,
):
    n_tensor = lax.axis_size("tensor")
    group = lax.axis_index("tensor")
    head_cols = D // n_tensor
    unit_cols = FF // n_tensor
    heads_here = head_cols // HD
    seq_count = segment_ids.shape[0]
    length = segment_ids.shape[1]
    query_scale = HD ** (-0.5)
    slots = slot_index(owners)
    gathered_slots = lax.all_gather(master_slots[0].astype(jnp.bfloat16), "dp", axis=0, tiled=True)
    stack = jnp.take(gathered_slots, slots, axis=0).reshape(-1, D)
    w_mix = stack[0 : 3 * head_cols]
    w_out = stack[3 * head_cols : 4 * head_cols]
    w_up = stack[4 * head_cols : 4 * head_cols + unit_cols]
    w_down = stack[4 * head_cols + unit_cols :]
    bias_query = lax.dynamic_slice_in_dim(vectors[0], group * head_cols, head_cols, 0)
    bias_value = lax.dynamic_slice_in_dim(vectors[1], group * head_cols, head_cols, 0)
    bias_up = lax.dynamic_slice_in_dim(vectors[2:6].reshape(FF), group * unit_cols, unit_cols, 0)
    gathered = lax.all_gather(tokens, "tensor", axis=0, tiled=True)
    mixed = jnp.einsum("ld,kd->lk", gathered, w_mix, preferred_element_type=jnp.float32)
    queries = ((mixed[:, :head_cols] + bias_query) * query_scale).astype(jnp.bfloat16)
    key_rows = mixed[:, head_cols : 2 * head_cols].astype(jnp.bfloat16)
    value_rows = (mixed[:, 2 * head_cols :] + bias_value).astype(jnp.bfloat16)
    head_shape = (seq_count, length, heads_here, HD)
    queries_h = queries.reshape(head_shape)
    keys_h = key_rows.reshape(head_shape)
    values_h = value_rows.reshape(head_shape)

    def forward_seq(element):
        return attend_forward(element[0], element[1], element[2], element[3], element[4])

    context, log_sums = lax.map(forward_seq, (queries_h, keys_h, values_h, segment_ids, key_mask))
    context = context.reshape(-1, head_cols).astype(jnp.bfloat16)
    attn_sum = lax.psum_scatter(
        jnp.einsum("lk,kd->ld", context, w_out, preferred_element_type=jnp.float32).astype(
            jnp.bfloat16
        ),
        "tensor",
        scatter_dimension=0,
        tiled=True,
    ).astype(jnp.float32)
    residual_one = tokens.astype(jnp.float32) + (attn_sum + vectors[6])
    normal_one, inverse_one = layer_stats(residual_one)
    normed = normal_one * vectors[8] + vectors[9]
    normed_low = normed.astype(jnp.bfloat16)
    norm_rows = lax.all_gather(normed_low, "tensor", axis=0, tiled=True)
    hidden_pre = (
        jnp.einsum("ld,kd->lk", norm_rows, w_up, preferred_element_type=jnp.float32) + bias_up
    )
    hidden_full, gelu_pull = jax.vjp(gelu_exact, hidden_pre)
    hidden = hidden_full.astype(jnp.bfloat16)
    mlp_sum = lax.psum_scatter(
        jnp.einsum("lk,kd->ld", hidden, w_down, preferred_element_type=jnp.float32).astype(
            jnp.bfloat16
        ),
        "tensor",
        scatter_dimension=0,
        tiled=True,
    ).astype(jnp.float32)
    residual_two = normed + (mlp_sum + vectors[7])
    normal_two, inverse_two = layer_stats(residual_two)
    layer_out = (normal_two * vectors[10] + vectors[11]).astype(jnp.bfloat16)
    grad_out = out_grad.astype(jnp.float32)
    grad_two = norm_back(grad_out, normal_two, inverse_two, vectors[10])
    grad_down_in = lax.all_gather(grad_two.astype(jnp.bfloat16), "tensor", axis=0, tiled=True)
    grad_hidden = jnp.einsum("ld,kd->lk", grad_down_in, w_down, preferred_element_type=jnp.float32)
    grad_w_down = jnp.einsum("lk,ld->kd", hidden, grad_down_in, preferred_element_type=jnp.float32)
    grad_pre = gelu_pull(grad_hidden)[0].astype(jnp.bfloat16)
    norm_back_rows = lax.all_gather(normed_low, "tensor", axis=0, tiled=True)
    grad_w_up = jnp.einsum(
        "lk,ld->kd", grad_pre, norm_back_rows, preferred_element_type=jnp.float32
    )
    grad_norm = grad_two + lax.psum_scatter(
        jnp.einsum("lk,kd->ld", grad_pre, w_up, preferred_element_type=jnp.float32).astype(
            jnp.bfloat16
        ),
        "tensor",
        scatter_dimension=0,
        tiled=True,
    ).astype(jnp.float32)
    grad_one = norm_back(grad_norm, normal_one, inverse_one, vectors[8])
    grad_attn_in = lax.all_gather(grad_one.astype(jnp.bfloat16), "tensor", axis=0, tiled=True)
    grad_context = jnp.einsum(
        "ld,kd->lk", grad_attn_in, w_out, preferred_element_type=jnp.float32
    ).astype(jnp.bfloat16)
    grad_w_out = jnp.einsum("lk,ld->kd", context, grad_attn_in, preferred_element_type=jnp.float32)

    def backward_seq(element):
        return attend_backward(
            element[0], element[1], element[2], element[3], element[4], element[5], element[6]
        )

    grad_q, grad_k, grad_v = lax.map(
        backward_seq,
        (
            queries_h,
            keys_h,
            values_h,
            segment_ids,
            key_mask,
            log_sums,
            grad_context.reshape(head_shape),
        ),
    )
    grad_queries = grad_q.reshape(-1, head_cols).astype(jnp.bfloat16) * query_scale
    grad_keys = grad_k.reshape(-1, head_cols).astype(jnp.bfloat16)
    grad_values = grad_v.reshape(-1, head_cols).astype(jnp.bfloat16)
    grad_mix = jnp.concatenate([grad_queries, grad_keys, grad_values], axis=1)
    mix_back_rows = lax.all_gather(tokens, "tensor", axis=0, tiled=True)
    grad_w_mix = jnp.einsum(
        "lk,ld->kd", grad_mix, mix_back_rows, preferred_element_type=jnp.float32
    )
    input_grad = (
        grad_one
        + lax.psum_scatter(
            jnp.einsum("lk,kd->ld", grad_mix, w_mix, preferred_element_type=jnp.float32).astype(
                jnp.bfloat16
            ),
            "tensor",
            scatter_dimension=0,
            tiled=True,
        ).astype(jnp.float32)
    ).astype(jnp.bfloat16)
    query_full = lax.dynamic_update_slice_in_dim(
        jnp.zeros((D,), jnp.float32),
        jnp.sum(grad_queries.astype(jnp.float32), axis=0),
        group * head_cols,
        0,
    )
    value_full = lax.dynamic_update_slice_in_dim(
        jnp.zeros((D,), jnp.float32),
        jnp.sum(grad_values.astype(jnp.float32), axis=0),
        group * head_cols,
        0,
    )
    up_full = lax.dynamic_update_slice_in_dim(
        jnp.zeros((FF,), jnp.float32),
        jnp.sum(grad_pre.astype(jnp.float32), axis=0),
        group * unit_cols,
        0,
    )
    tail_rows = jnp.stack(
        [
            jnp.sum(grad_one, axis=0),
            jnp.sum(grad_two, axis=0),
            jnp.sum(grad_norm * normal_one, axis=0),
            jnp.sum(grad_norm, axis=0),
            jnp.sum(grad_out * normal_two, axis=0),
            jnp.sum(grad_out, axis=0),
        ]
    )
    vector_terms = jnp.concatenate(
        [jnp.stack([query_full, value_full]), up_full.reshape(FF // D, D), tail_rows], axis=0
    )
    vector_grads = lax.psum(vector_terms, ("dp", "tensor"))
    grad_stack = jnp.concatenate([grad_w_mix, grad_w_out, grad_w_up, grad_w_down], axis=0)
    grad_pieces = grad_stack.reshape(slots.shape[0], -1, D)
    spread_slots = (
        jnp.zeros((lax.axis_size("dp") * CAP,) + grad_pieces.shape[1:], jnp.float32)
        .at[slots]
        .set(grad_pieces)
    )
    own_grads = lax.psum_scatter(
        spread_slots.astype(jnp.bfloat16), "dp", scatter_dimension=0, tiled=True
    ).astype(jnp.float32)
    slot_new, slot_first_new, slot_second_new = adam_update(
        master_slots[0], slot_first[0], slot_second[0], own_grads, rate_matrix, weight_decay
    )
    vector_new, vector_first_new, vector_second_new = adam_update(
        vectors, vector_first, vector_second, vector_grads, rate_vector, 0.0
    )
    return (
        layer_out,
        input_grad,
        slot_new[None],
        slot_first_new[None],
        slot_second_new[None],
        vector_new,
        vector_first_new,
        vector_second_new,
    )


DOC_MAX = 800
EXT_PAD = 512
ABLK = 256
HPG = 4
AUG = 16
neg_big = -1000000000.0
NN = (((1,), (0,)), ((), ()))
NT = (((1,), (1,)), ((), ()))
TN = (((0,), (0,)), ((), ()))


def mm(a, b, dims):
    return lax.dot_general(a, b, dims, preferred_element_type=jnp.float32)


def attn_fwd_kernel(lo_ref, hi_ref, q_ref, k_ref, v_ref, qaug_ref, kaug_ref, hid_ref, o_ref, lse_ref, kn_ref, m_ref, acc_ref):
    ext = q_ref.shape[1]
    ones = jnp.concatenate(
        [jnp.ones((1, ABLK), jnp.float32), jnp.zeros((AUG - 1, ABLK), jnp.float32)], axis=0
    ).astype(jnp.bfloat16)
    for h in range(HPG):
        rows = slice(h * HD, (h + 1) * HD)
        kn_ref[h] = jnp.concatenate([k_ref[rows, :], kaug_ref[...]], axis=0).T

    def query_block(qb, _):
        lo = lo_ref[qb]
        hi = hi_ref[qb]
        qs = pl.ds(pl.multiple_of(qb * ABLK, ABLK), ABLK)

        @pl.when(hi > lo)
        def _work():
            hidden = hid_ref[0:1, qs]
            for h in range(HPG):
                rows = slice(h * HD, (h + 1) * HD)
                q32 = q_ref[rows, qs].astype(jnp.float32)
                k32 = k_ref[rows, qs].astype(jnp.float32)
                own = jnp.sum(q32 * k32, axis=0, keepdims=True)
                m_ref[h] = jnp.where(hidden > 0.0, own, -1e30)
                acc_ref[h, 0:HD, :] = v_ref[rows, qs].astype(jnp.float32) * hidden
                acc_ref[h, HD:, :] = jnp.broadcast_to(hidden, (AUG, ABLK))

            def key_block(kb, _):
                ks = pl.ds(pl.multiple_of(kb * ABLK, ABLK), ABLK)
                for h in range(HPG):
                    rows = slice(h * HD, (h + 1) * HD)
                    qa = jnp.concatenate([q_ref[rows, qs], qaug_ref[:, qs]], axis=0)
                    s = mm(kn_ref[h, ks, :], qa, NN)
                    old = m_ref[h]
                    new = jnp.maximum(old, jnp.max(s, axis=0, keepdims=True))
                    m_ref[h] = new
                    p = jnp.exp(s - new).astype(jnp.bfloat16)
                    va = jnp.concatenate([v_ref[rows, ks], ones], axis=0)
                    acc_ref[h] = acc_ref[h] * jnp.exp(old - new) + mm(va, p, NN)
                return 0

            lax.fori_loop(lo, hi, key_block, 0)
            for h in range(HPG):
                rows = slice(h * HD, (h + 1) * HD)
                total = acc_ref[h, HD : HD + 1, :]
                o_ref[rows, qs] = (acc_ref[h, 0:HD, :] * (1.0 / total)).astype(jnp.bfloat16)
                lse_ref[0, h : h + 1, qs] = m_ref[h] + jnp.log(total)

        @pl.when(hi <= lo)
        def _skip():
            o_ref[:, qs] = jnp.zeros((HPG * HD, ABLK), jnp.bfloat16)
            lse_ref[0, :, qs] = jnp.zeros((8, ABLK), jnp.float32)

        return 0

    lax.fori_loop(0, ext // ABLK, query_block, 0)


def attn_bwd_kernel(
    lo_ref, hi_ref, q_ref, k_ref, v_ref, g_ref, c_ref, lse_ref, qaug_ref, kaug_ref, hid_ref,
    dq_ref, dk_ref, dv_ref, kn_ref, vn_ref, acc_ref, dk_acc, dv_acc,
):
    ext = q_ref.shape[1]
    for h in range(HPG):
        rows = slice(h * HD, (h + 1) * HD)
        kn_ref[h] = jnp.concatenate([k_ref[rows, :], kaug_ref[...]], axis=0).T
        vn_ref[h] = v_ref[rows, :].T
    dk_acc[...] = jnp.zeros_like(dk_acc)
    dv_acc[...] = jnp.zeros_like(dv_acc)

    def query_block(qb, _):
        lo = lo_ref[qb]
        hi = hi_ref[qb]
        qs = pl.ds(pl.multiple_of(qb * ABLK, ABLK), ABLK)

        @pl.when(hi > lo)
        def _work():
            hidden = hid_ref[0:1, qs]
            deltas = []
            logs = []
            for h in range(HPG):
                rows = slice(h * HD, (h + 1) * HD)
                q32 = q_ref[rows, qs].astype(jnp.float32)
                k32 = k_ref[rows, qs].astype(jnp.float32)
                v32 = v_ref[rows, qs].astype(jnp.float32)
                g32 = g_ref[rows, qs].astype(jnp.float32)
                c32 = c_ref[rows, qs].astype(jnp.float32)
                delta = jnp.sum(g32 * c32, axis=0, keepdims=True)
                log = lse_ref[0, h : h + 1, qs]
                own = jnp.sum(q32 * k32, axis=0, keepdims=True)
                p_own = jnp.where(hidden > 0.0, jnp.exp(own - log), 0.0)
                d_own = p_own * (jnp.sum(g32 * v32, axis=0, keepdims=True) - delta)
                acc_ref[h] = d_own * k32
                dk_acc[rows, qs] += d_own * q32
                dv_acc[rows, qs] += p_own * g32
                deltas.append(delta)
                logs.append(log)

            def key_block(kb, _):
                ks = pl.ds(pl.multiple_of(kb * ABLK, ABLK), ABLK)
                for h in range(HPG):
                    rows = slice(h * HD, (h + 1) * HD)
                    q = q_ref[rows, qs]
                    g = g_ref[rows, qs]
                    qa = jnp.concatenate([q, qaug_ref[:, qs]], axis=0)
                    s = mm(kn_ref[h, ks, :], qa, NN)
                    p = jnp.exp(s - logs[h])
                    dp = mm(vn_ref[h, ks, :], g, NN)
                    ds = (p * (dp - deltas[h])).astype(jnp.bfloat16)
                    pb = p.astype(jnp.bfloat16)
                    dv_acc[rows, ks] += mm(g, pb, NT)
                    dk_acc[rows, ks] += mm(q, ds, NT)
                    acc_ref[h] += mm(k_ref[rows, ks], ds, NN)
                return 0

            lax.fori_loop(lo, hi, key_block, 0)
            for h in range(HPG):
                rows = slice(h * HD, (h + 1) * HD)
                dq_ref[rows, qs] = acc_ref[h].astype(jnp.bfloat16) * (HD ** (-0.5))

        @pl.when(hi <= lo)
        def _skip():
            dq_ref[:, qs] = jnp.zeros((HPG * HD, ABLK), jnp.bfloat16)

        return 0

    lax.fori_loop(0, ext // ABLK, query_block, 0)
    dk_ref[...] = dk_acc[...].astype(jnp.bfloat16)
    dv_ref[...] = dv_acc[...].astype(jnp.bfloat16)


def group_block(offset, rows, ext):
    return pl.BlockSpec((rows, ext), lambda g, lo, hi: (offset + g, 0))


def fixed_block(rows, ext):
    return pl.BlockSpec((rows, ext), lambda g, lo, hi: (0, 0))


def attend(lo, hi, qkv, qaug, kaug, hidden):
    ext = qkv.shape[1]
    groups = D // HD // HPG
    rows = HPG * HD
    return pl.pallas_call(
        attn_fwd_kernel,
        out_shape=(
            jax.ShapeDtypeStruct((D, ext), jnp.bfloat16),
            jax.ShapeDtypeStruct((groups, 8, ext), jnp.float32),
        ),
        grid_spec=pltpu.PrefetchScalarGridSpec(
            num_scalar_prefetch=2,
            grid=(groups,),
            in_specs=[
                group_block(0, rows, ext),
                group_block(groups, rows, ext),
                group_block(2 * groups, rows, ext),
                fixed_block(AUG, ext),
                fixed_block(AUG, ext),
                fixed_block(8, ext),
            ],
            out_specs=[
                group_block(0, rows, ext),
                pl.BlockSpec((1, 8, ext), lambda g, lo, hi: (g, 0, 0)),
            ],
            scratch_shapes=[
                pltpu.VMEM((HPG, ext, HD + AUG), jnp.bfloat16),
                pltpu.VMEM((HPG, 1, ABLK), jnp.float32),
                pltpu.VMEM((HPG, HD + AUG, ABLK), jnp.float32),
            ],
        ),
        compiler_params=pltpu.CompilerParams(vmem_limit_bytes=40 * 2**20),
        cost_estimate=pl.CostEstimate(flops=20 * 10**9, bytes_accessed=14 * 10**6, transcendentals=0),
        name="attend",
    )(lo, hi, qkv, qkv, qkv, qaug, kaug, hidden)


def attend_back(lo, hi, qkv, grads, context, logs, qaug, kaug, hidden, first, step):
    ext = qkv.shape[1]
    groups = D // HD // HPG
    rows = HPG * HD
    count = len(range(first, groups, step))
    out = jax.ShapeDtypeStruct((count * rows, ext), jnp.bfloat16)

    def taken(offset):
        return pl.BlockSpec((rows, ext), lambda g, lo, hi: (offset + first + step * g, 0))

    return pl.pallas_call(
        attn_bwd_kernel,
        out_shape=(out, out, out),
        grid_spec=pltpu.PrefetchScalarGridSpec(
            num_scalar_prefetch=2,
            grid=(count,),
            in_specs=[
                taken(0),
                taken(groups),
                taken(2 * groups),
                taken(0),
                taken(0),
                pl.BlockSpec((1, 8, ext), lambda g, lo, hi: (first + step * g, 0, 0)),
                fixed_block(AUG, ext),
                fixed_block(AUG, ext),
                fixed_block(8, ext),
            ],
            out_specs=[group_block(0, rows, ext)] * 3,
            scratch_shapes=[
                pltpu.VMEM((HPG, ext, HD + AUG), jnp.bfloat16),
                pltpu.VMEM((HPG, ext, HD), jnp.bfloat16),
                pltpu.VMEM((HPG, HD, ABLK), jnp.float32),
                pltpu.VMEM((rows, ext), jnp.float32),
                pltpu.VMEM((rows, ext), jnp.float32),
            ],
        ),
        compiler_params=pltpu.CompilerParams(vmem_limit_bytes=48 * 2**20),
        cost_estimate=pl.CostEstimate(flops=50 * 10**9, bytes_accessed=30 * 10**6, transcendentals=0),
        name="attend_back",
    )(lo, hi, qkv, qkv, qkv, grads, context, logs, qaug, kaug, hidden)


def document_plan(segment, valid, half, rows):
    length = segment.shape[0]
    ext = rows + EXT_PAD
    base = half * EXT_PAD
    position = jnp.arange(length, dtype=jnp.int32)
    documents = jnp.arange(8, dtype=jnp.int32)[:, None]
    one_hot = segment[None, :] == documents
    counts = jnp.sum(one_hot.astype(jnp.int32), axis=1, keepdims=True)
    starts = jnp.sum((segment[None, :] < documents).astype(jnp.int32), axis=1, keepdims=True)
    start = jnp.sum(jnp.where(one_hot, starts, 0), axis=0)
    end = jnp.sum(jnp.where(one_hot, starts + counts, 0), axis=0)
    crossing = (start < rows) & (end > rows)
    left = jnp.max(jnp.where(crossing, rows - start, 0))
    right = jnp.max(jnp.where(crossing, end - rows, 0))
    worker = jnp.where(left <= right, half == 1, half == 0)
    own = (position >= half * rows) & (position < (half + 1) * rows)
    handled = jnp.where(crossing, worker, own)
    cut = lambda values: lax.dynamic_slice_in_dim(values, base, ext, 0)
    handled_ext = cut(handled)
    begins = jnp.where(handled_ext, cut(start) - base, ext).reshape(-1, ABLK)
    ends = jnp.where(handled_ext, cut(end) - base, 0).reshape(-1, ABLK)
    lo = jnp.min(begins, axis=1) // ABLK
    hi = (jnp.max(ends, axis=1) + (ABLK - 1)) // ABLK
    blank = jnp.max(ends, axis=1) == 0
    lo = jnp.where(blank, 0, lo)
    hi = jnp.where(blank, 0, hi)
    hot = cut(one_hot.T).T
    masked = cut(valid) == 0
    ones = jnp.ones((1, ext), jnp.bfloat16)
    fill = jnp.zeros((AUG - 9, ext), jnp.bfloat16)
    qaug = jnp.concatenate([hot.astype(jnp.bfloat16), ones, fill], axis=0)
    kaug = jnp.concatenate(
        [
            jnp.where(hot, 0.0, neg_big).astype(jnp.bfloat16),
            jnp.where(masked[None, :], neg_big, 0.0).astype(jnp.bfloat16),
            fill,
        ],
        axis=0,
    )
    hidden = jnp.broadcast_to(masked.astype(jnp.float32)[None, :], (8, ext))
    foreign = lax.dynamic_slice_in_dim(crossing & ~worker, half * rows, rows, 0)
    return lo, hi, qaug, kaug, hidden, handled_ext, foreign


MESH = pl.DeviceIdType.MESH
CHUNKS = 3


def neighbours(z, y, core, x):
    def at(z, y, core, x):
        return {"dp": (z * 2 + y) * 2 + core, "tensor": x}

    return {
        "x": at(z, y, core, 1 - x),
        "y": at(z, 1 - y, core, x),
        "core": at(z, y, 1 - core, x),
        "up": at(jnp.minimum(z + 1, 3), y, core, x),
        "down": at(jnp.maximum(z - 1, 0), y, core, x),
    }


def greet(near, z):
    barrier = pltpu.get_barrier_semaphore()
    for name in ("x", "y", "core"):
        pl.semaphore_signal(barrier, inc=1, device_id=near[name], device_id_type=MESH)

    @pl.when(z < 3)
    def _up():
        pl.semaphore_signal(barrier, inc=1, device_id=near["up"], device_id_type=MESH)

    @pl.when(z > 0)
    def _down():
        pl.semaphore_signal(barrier, inc=1, device_id=near["down"], device_id_type=MESH)

    at_end = jnp.where((z == 0) | (z == 3), 1, 0)
    pl.semaphore_wait(barrier, 5 - at_end)


def greet_all(near, me, n_dp):
    barrier = pltpu.get_barrier_semaphore()
    pl.semaphore_signal(barrier, inc=1, device_id=near["x"], device_id_type=MESH)

    def one(i, _):
        other = {"dp": lax.rem(me + i, n_dp), "tensor": lax.axis_index("tensor")}
        pl.semaphore_signal(barrier, inc=1, device_id=other, device_id_type=MESH)
        return 0

    lax.fori_loop(1, n_dp, one, 0)
    pl.semaphore_wait(barrier, n_dp)


def gather_kernel(
    slots_ref, low_ref, mix_ref, up_ref, down_ref,
    spread_ref, dense_ref, local_sem, own_sem, post, mail, send, recv,
):
    z, y, core, x = coordinates()
    near = neighbours(z, y, core, x)
    width = D // 2
    outs = (mix_ref, up_ref, down_ref)
    me = lax.axis_index("dp")
    n_dp = low_ref.shape[0]
    greet_all(near, me, n_dp)

    def letter(to):
        return pltpu.make_async_remote_copy(
            src_ref=low_ref.at[to],
            dst_ref=spread_ref.at[pl.ds(me * CAP, CAP)],
            send_sem=post.at[to],
            recv_sem=mail.at[me],
            device_id={"dp": to, "tensor": x},
            device_id_type=MESH,
        )

    def answer(of):
        return pltpu.make_async_remote_copy(
            src_ref=low_ref.at[of],
            dst_ref=spread_ref.at[pl.ds(of * CAP, CAP)],
            send_sem=post.at[of],
            recv_sem=mail.at[of],
            device_id={"dp": of, "tensor": x},
            device_id_type=MESH,
        )

    def peer(i):
        return lax.rem(me + i, n_dp)

    def post_one(i, _):
        letter(peer(i)).start()
        return 0

    lax.fori_loop(1, n_dp, post_one, 0)
    mine = pltpu.make_async_copy(low_ref.at[me], spread_ref.at[pl.ds(me * CAP, CAP)], local_sem)
    mine.start()
    mine.wait()

    def mail_one(i, _):
        answer(peer(i)).wait_recv()
        letter(peer(i)).wait_send()
        return 0

    lax.fori_loop(1, n_dp, mail_one, 0)

    def place(p, _):
        dense_ref[p // 16, (p // 4) % 4, p % 4] = spread_ref[slots_ref[p]]
        return 0

    lax.fori_loop(0, slots_ref.shape[0], place, 0)

    def block(k, t, zz, yy, cc, part=None):
        groups = slice(None) if part is None else pl.ds(2 * part, 2)
        return outs[k].at[
            groups,
            t,
            :,
            pl.ds(pl.multiple_of((zz * 2 + yy) * 16, 16), 16),
            pl.ds(pl.multiple_of(cc * width, width), width),
        ]

    own = [
        pltpu.make_async_copy(dense_ref.at[k], block(k, x, z, y, core), own_sem.at[k])
        for k in range(CHUNKS)
    ]
    for one in own:
        one.start()

    def copy(kind, link, k, zz, t, yy, cc, part=None, fresh=False):
        view = block(k, t, zz, yy, cc, part)
        return pltpu.make_async_remote_copy(
            src_ref=dense_ref.at[k] if fresh else view,
            dst_ref=view,
            send_sem=send.at[kind, k, zz],
            recv_sem=recv.at[kind, k, zz],
            device_id=near[link],
            device_id_type=MESH,
        )

    def up(k, zz, fresh=False):
        return copy(0, "up", k, zz, x, y, core, fresh=fresh)

    def down(k, zz, fresh=False):
        return copy(1, "down", k, zz, x, y, core, fresh=fresh)

    def spread(k, zz, fresh):
        copy(2, "x", k, zz, x, y, core, fresh=fresh).start()
        copy(3, "y", k, zz, x, y, core, fresh=fresh).start()
        copy(4, "core", k, zz, x, y, core, fresh=fresh).start()

    def each(d, body):
        @pl.when((d > 0) & (z - d >= 0))
        def _below():
            for k in range(CHUNKS):
                body(k, z - d, 0)

        @pl.when((d > 0) & (z + d <= 3))
        def _above():
            for k in range(CHUNKS):
                body(k, z + d, 1)

    def each_or_own(d, body):
        each(d, body)

        @pl.when(d == 0)
        def _own():
            for k in range(CHUNKS):
                body(k, z, None)

    def begin(k):
        @pl.when(z < 3)
        def _up():
            up(k, z, True).start()

        @pl.when(z > 0)
        def _down():
            down(k, z, True).start()

        spread(k, z, True)

    def first(k, zz, side):
        if side == 0:
            up(k, zz).wait_recv()

            @pl.when(z < 3)
            def _up():
                up(k, zz).start()

        else:
            down(k, zz).wait_recv()

            @pl.when(z > 0)
            def _on():
                down(k, zz).start()

        spread(k, zz, False)

    def second(k, zz, side):
        copy(2, "x", k, zz, 1 - x, y, core).wait_recv()
        copy(5, "y", k, zz, 1 - x, y, core, 0).start()
        copy(7, "core", k, zz, 1 - x, y, core).start()
        copy(3, "y", k, zz, x, 1 - y, core).wait_recv()
        copy(6, "x", k, zz, x, 1 - y, core, 1).start()
        copy(8, "core", k, zz, x, 1 - y, core).start()

    def third(k, zz, side):
        copy(5, "y", k, zz, 1 - x, 1 - y, core, 0).wait_recv()
        copy(9, "core", k, zz, 1 - x, 1 - y, core, 0).start()
        copy(6, "x", k, zz, 1 - x, 1 - y, core, 1).wait_recv()
        copy(10, "core", k, zz, 1 - x, 1 - y, core, 1).start()

    def finish(k, zz, side):
        if side != 1:

            @pl.when(z < 3)
            def _up():
                up(k, zz).wait_send()

        if side != 0:

            @pl.when(z > 0)
            def _down():
                down(k, zz).wait_send()

        copy(2, "x", k, zz, x, y, core).wait_send()
        copy(3, "y", k, zz, x, y, core).wait_send()
        copy(5, "y", k, zz, 1 - x, y, core, 0).wait_send()
        copy(6, "x", k, zz, x, 1 - y, core, 1).wait_send()
        copy(4, "core", k, zz, x, y, core).wait_send()
        copy(7, "core", k, zz, 1 - x, y, core).wait_send()
        copy(8, "core", k, zz, x, 1 - y, core).wait_send()
        copy(9, "core", k, zz, 1 - x, 1 - y, core, 0).wait_send()
        copy(10, "core", k, zz, 1 - x, 1 - y, core, 1).wait_send()
        copy(4, "core", k, zz, x, y, 1 - core).wait_recv()
        copy(7, "core", k, zz, 1 - x, y, 1 - core).wait_recv()
        copy(8, "core", k, zz, x, 1 - y, 1 - core).wait_recv()
        copy(9, "core", k, zz, 1 - x, 1 - y, 1 - core, 0).wait_recv()
        copy(10, "core", k, zz, 1 - x, 1 - y, 1 - core, 1).wait_recv()

    for k in range(CHUNKS):
        begin(k)

    def step(d, _):
        @pl.when(d < 4)
        def _one():
            each(d, first)

        @pl.when((d >= 1) & (d < 5))
        def _two():
            each_or_own(d - 1, second)

        @pl.when(d >= 2)
        def _three():
            each_or_own(d - 2, third)

        return 0

    lax.fori_loop(1, 6, step, 0)

    def end(d, _):
        each_or_own(d, finish)
        return 0

    lax.fori_loop(0, 4, end, 0)
    for one in own:
        one.wait()


def gather_weights(slots, low):
    n_dp = low.shape[0]
    stack = jax.ShapeDtypeStruct((4, 2, 4, 128, D), low.dtype)
    return pl.pallas_call(
        gather_kernel,
        out_shape=(stack,) * 3,
        in_specs=[
            pl.BlockSpec(memory_space=pltpu.SMEM),
            pl.BlockSpec(memory_space=pl.ANY),
        ],
        out_specs=(pl.BlockSpec(memory_space=pl.ANY),) * 3,
        scratch_shapes=[
            pltpu.VMEM((n_dp * CAP, 16, D // 2), low.dtype),
            pltpu.VMEM((CHUNKS, 4, 4, 16, D // 2), low.dtype),
            pltpu.SemaphoreType.DMA,
            pltpu.SemaphoreType.DMA((CHUNKS,)),
            pltpu.SemaphoreType.DMA((n_dp,)),
            pltpu.SemaphoreType.DMA((n_dp,)),
            pltpu.SemaphoreType.DMA((11, CHUNKS, 4)),
            pltpu.SemaphoreType.DMA((11, CHUNKS, 4)),
        ],
        compiler_params=pltpu.CompilerParams(
            collective_id=1, has_side_effects=True, vmem_limit_bytes=32 * 2**20
        ),
        cost_estimate=pl.CostEstimate(flops=0, bytes_accessed=50 * 10**6, transcendentals=0),
        name="gather_weights",
    )(slots, low)


def gelu_pair(values):
    cdf = 0.5 * lax.erfc(values * (-(0.5**0.5)))
    density = jnp.exp(values * values * -0.5) * (0.5 / jnp.pi) ** 0.5
    return (values * cdf, cdf + values * density)


def coordinates():
    dp = lax.axis_index("dp")
    return dp // 4, (dp // 2) % 2, dp % 2, lax.axis_index("tensor")


def exchange(values, axis):
    if axis == "x":
        return lax.ppermute(values, "tensor", [(0, 1), (1, 0)])
    flip = {"core": 1, "y": 2, "z_near": 4, "z_far": 8}[axis]
    return lax.ppermute(values, "dp", [(i, i ^ flip) for i in range(lax.axis_size("dp"))])


def pick(values, index, axis):
    return lax.dynamic_index_in_dim(values, index, axis, keepdims=False)


def add_low(one, two):
    return (one.astype(jnp.float32) + two.astype(jnp.float32)).astype(jnp.bfloat16)


def sum_all(values):
    for axis in ("core", "y", "x", "z_near", "z_far"):
        values = values + exchange(values, axis)
    return values


def halve(values, index, axis, link):
    other = exchange(pick(values, 1 - index, axis), link)
    return pick(values, index, axis), other


def scatter_rows(lhs, rhs, dims, shape):
    z, y, core, x = coordinates()
    width = D // 2
    far = lax.dynamic_slice_in_dim(rhs, (1 - core) * width, width, 1)
    near = lax.dynamic_slice_in_dim(rhs, core * width, width, 1)
    arrived = exchange(mm(lhs, far, dims).astype(jnp.bfloat16), "core")
    product = (mm(lhs, near, dims) + arrived.astype(jnp.float32)).astype(jnp.bfloat16)
    product = product.reshape(shape + (width,))
    middle = shape[2] // 2
    one, one_in = halve(product[:, :, :middle], x, 1, "x")
    two, two_in = halve(product[:, :, middle:], y, 4, "y")
    one_send = exchange(add_low(pick(one, 1 - y, 3), pick(one_in, 1 - y, 3)), "y")
    two_send = exchange(add_low(pick(two, 1 - x, 1), pick(two_in, 1 - x, 1)), "x")
    one = pick(one, y, 3).astype(jnp.float32) + pick(one_in, y, 3).astype(jnp.float32) + one_send.astype(jnp.float32)
    two = pick(two, x, 1).astype(jnp.float32) + pick(two_in, x, 1).astype(jnp.float32) + two_send.astype(jnp.float32)
    line = jnp.concatenate([one, two], axis=1).astype(jnp.bfloat16)
    line = line.reshape(shape[0], shape[2], 2, 2, 16, width)
    line, line_in = halve(line, z // 2, 2, "z_far")
    last_in = exchange(add_low(pick(line, 1 - z % 2, 2), pick(line_in, 1 - z % 2, 2)), "z_near")
    last = pick(line, z % 2, 2).astype(jnp.float32) + pick(line_in, z % 2, 2).astype(jnp.float32)
    return (last + last_in.astype(jnp.float32)).astype(jnp.bfloat16).reshape(-1, 16, width)


def on_device_rows(
    tokens,
    segment_ids,
    key_mask,
    owners,
    master_slots,
    slot_first,
    slot_second,
    vectors,
    vector_first,
    vector_second,
    out_grad,
):
    n_dp = lax.axis_size("dp")
    n_tensor = lax.axis_size("tensor")
    half = lax.axis_index("tensor")
    every = ("tensor", "dp")
    rows = tokens.shape[0]
    ext = rows + EXT_PAD
    halo = DOC_MAX // 2
    swap = [(0, 1), (1, 0)]
    edge = jnp.where(half == 0, rows - halo, 0)
    halo_at = jnp.where(half == 0, rows, EXT_PAD - halo)
    own_at = half * EXT_PAD

    def extend(own_rows, halo_rows):
        whole = jnp.zeros((ext,) + own_rows.shape[1:], own_rows.dtype)
        whole = lax.dynamic_update_slice_in_dim(whole, halo_rows, halo_at, 0)
        return lax.dynamic_update_slice_in_dim(whole, own_rows, own_at, 0)

    def own_part(values):
        return lax.dynamic_slice_in_dim(values, own_at, rows, 0)

    def halo_part(values):
        return lax.dynamic_slice_in_dim(values, halo_at, halo, 0)

    lo, hi, qaug, kaug, hidden_keys, handled, foreign = document_plan(
        segment_ids[0], key_mask[0], half, rows
    )
    halo_tokens = lax.ppermute(lax.dynamic_slice_in_dim(tokens, edge, halo, 0), "tensor", swap)
    tokens_ext = extend(tokens, halo_tokens)

    slots = slot_index(owners)
    pieces = slots.shape[0]
    piece_rows = master_slots.shape[2]
    low_slots = master_slots[0].astype(jnp.bfloat16).reshape(CAP, 8, 16, 2, D // 2)
    low_slots = low_slots.transpose(1, 3, 0, 2, 4).reshape(n_dp, CAP, 16, D // 2)
    mix_pieces = 4 * (D // n_tensor) // piece_rows
    up_pieces = (FF // n_tensor) // piece_rows
    per = mix_pieces // 4
    mix, up, down = gather_weights(slots, low_slots)
    w_qkv = mix[:3].reshape(3 * D, D)
    w_out = mix[3].reshape(D, D)
    w_up = up.reshape(FF, D)
    w_down = down.reshape(FF, D)
    bias_up = vectors[2:6].reshape(n_tensor, 4, -1).transpose(1, 0, 2).reshape(FF)

    bias_qkv = jnp.concatenate([vectors[0], jnp.zeros((D,), jnp.float32), vectors[1]])
    scale_qkv = jnp.concatenate([jnp.full((D,), HD ** (-0.5)), jnp.ones((2 * D,))])
    qkv = (
        (mm(w_qkv, tokens_ext, NT) + bias_qkv[:, None]) * scale_qkv.astype(jnp.float32)[:, None]
    ).astype(jnp.bfloat16)
    context, logs = attend(lo, hi, qkv, qaug, kaug, hidden_keys)
    attn_ext = mm(context, w_out, TN).astype(jnp.bfloat16)
    halo_attn = lax.ppermute(halo_part(attn_ext), "tensor", swap)
    attn_back = lax.dynamic_update_slice_in_dim(
        jnp.zeros((rows, D), jnp.bfloat16), halo_attn, edge, 0
    )
    attn_sum = jnp.where(foreign[:, None], attn_back, own_part(attn_ext)).astype(jnp.float32)
    residual_one = tokens.astype(jnp.float32) + (attn_sum + vectors[6])
    normal_one, inverse_one = layer_stats(residual_one)
    normed = normal_one * vectors[8] + vectors[9]
    normed_low = normed.astype(jnp.bfloat16)

    gelu, slope = gelu_pair(mm(normed_low, w_up, NT) + bias_up)
    hidden = gelu.astype(jnp.bfloat16)
    slope = slope.astype(jnp.bfloat16)
    residual_two = normed + (mm(hidden, w_down, NN) + vectors[7])
    normal_two, inverse_two = layer_stats(residual_two)
    layer_out = (normal_two * vectors[10] + vectors[11]).astype(jnp.bfloat16)
    grad_out = out_grad.astype(jnp.float32)
    grad_two = norm_back(grad_out, normal_two, inverse_two, vectors[10])
    grad_two_low = grad_two.astype(jnp.bfloat16)

    wide = (4, n_tensor, up_pieces // 4, 4, 2, 16)
    grad_w_down = scatter_rows(hidden, grad_two_low, TN, wide)
    grad_pre32 = mm(grad_two_low, w_down, NT) * slope.astype(jnp.float32)
    grad_pre = grad_pre32.astype(jnp.bfloat16)
    grad_w_up = scatter_rows(grad_pre, normed_low, TN, wide)
    grad_norm = grad_two + mm(grad_pre, w_up, NN)
    grad_one = norm_back(grad_norm, normal_one, inverse_one, vectors[8])
    grad_one_low = grad_one.astype(jnp.bfloat16)

    halo_grad = lax.ppermute(
        lax.dynamic_slice_in_dim(grad_one_low, edge, halo, 0), "tensor", swap
    )
    grad_ext = jnp.where(handled[:, None], extend(grad_one_low, halo_grad), 0)
    grad_context = mm(w_out, grad_ext, NT).astype(jnp.bfloat16)
    grad_w_out = scatter_rows(context, grad_ext, NN, (1, n_tensor, per, 4, 2, 16))
    half_heads = (3, n_tensor, per // 2, 4, 2, 16)
    parts = []
    grad_w_qkv = []
    for first in range(2):
        part = attend_back(
            lo, hi, qkv, grad_context, context, logs, qaug, kaug, hidden_keys, first, 2
        )
        parts.append(part)
        grad_w_qkv.append(
            scatter_rows(jnp.concatenate(part, axis=0), tokens_ext, NN, half_heads)
        )
    grad_w_qkv = jnp.concatenate(
        [g.reshape(3, per // 2, 16, D // 2) for g in grad_w_qkv], axis=1
    ).reshape(3 * per, 16, D // 2)

    def whole(index):
        pair = [part[index].reshape(n_tensor, -1, ext) for part in parts]
        return jnp.concatenate(pair, axis=1).reshape(D, ext)

    grad_q, grad_k, grad_v = whole(0), whole(1), whole(2)
    grad_qkv = jnp.concatenate([grad_q, grad_k, grad_v], axis=0)
    input_ext = mm(grad_qkv, w_qkv, TN)
    halo_input = lax.ppermute(halo_part(input_ext).astype(jnp.bfloat16), "tensor", swap)
    input_back = lax.dynamic_update_slice_in_dim(
        jnp.zeros((rows, D), jnp.bfloat16), halo_input, edge, 0
    )
    input_grad = (grad_one + own_part(input_ext) + input_back.astype(jnp.float32)).astype(
        jnp.bfloat16
    )

    early_terms = jnp.concatenate(
        [
            jnp.sum(grad_pre.astype(jnp.float32), axis=0)
            .reshape(4, n_tensor, -1)
            .transpose(1, 0, 2)
            .reshape(FF // D, D),
            jnp.stack(
                [
                    jnp.sum(grad_one, axis=0),
                    jnp.sum(grad_two, axis=0),
                    jnp.sum(grad_norm * normal_one, axis=0),
                    jnp.sum(grad_norm, axis=0),
                    jnp.sum(grad_out * normal_two, axis=0),
                    jnp.sum(grad_out, axis=0),
                ]
            ),
        ],
        axis=0,
    )
    late_terms = jnp.stack(
        [
            jnp.sum(grad_q.astype(jnp.float32), axis=1),
            jnp.sum(grad_v.astype(jnp.float32), axis=1),
        ]
    )
    vector_grads = jnp.concatenate([sum_all(late_terms), sum_all(early_terms)], axis=0)

    grad_chunks = jnp.concatenate([grad_w_qkv, grad_w_out, grad_w_up, grad_w_down], axis=0)
    piece_of = jnp.full((n_dp * CAP,), pieces, jnp.int32).at[slots].set(
        jnp.arange(pieces, dtype=jnp.int32)
    )
    padded = jnp.concatenate([grad_chunks, jnp.zeros((1, 16, D // 2), jnp.bfloat16)], axis=0)
    outgoing = jnp.take(padded, piece_of, axis=0).reshape(n_dp, CAP, 16, D // 2)
    incoming = lax.all_to_all(outgoing, "dp", 0, 0, tiled=False)
    own_grads = incoming.reshape(8, 2, CAP, 16, D // 2).transpose(2, 0, 3, 1, 4)
    own_grads = own_grads.reshape(CAP, piece_rows, D).astype(jnp.float32)
    slot_new, slot_first_new, slot_second_new = adam_update(
        master_slots[0], slot_first[0], slot_second[0], own_grads, rate_matrix, weight_decay
    )
    vector_new, vector_first_new, vector_second_new = adam_update(
        vectors, vector_first, vector_second, vector_grads, rate_vector, 0.0
    )
    return (
        layer_out,
        input_grad,
        slot_new[None],
        slot_first_new[None],
        slot_second_new[None],
        vector_new,
        vector_first_new,
        vector_second_new,
    )


def solution(mesh):
    placed = (
        P(("dp", "tensor"), None),
        P("dp", None),
        P("dp", None),
        P(),
        P("tensor", "dp", None, None),
        P("tensor", "dp", None, None),
        P("tensor", "dp", None, None),
        P(),
        P(),
        P(),
        P(("dp", "tensor"), None),
    )
    by_rows = mesh.shape["tensor"] == 2 and mesh.shape["dp"] == 16
    return jax.shard_map(
        on_device_rows if by_rows else on_device_generic,
        mesh=mesh,
        in_specs=placed,
        out_specs=(
            P(("dp", "tensor"), None),
            P(("dp", "tensor"), None),
            P("tensor", "dp", None, None),
            P("tensor", "dp", None, None),
            P("tensor", "dp", None, None),
            P(),
            P(),
            P(),
        ),
        check_vma=False,
    )
```

```python
import functools

import jax
import jax.numpy as jnp
from jax import lax
from jax.experimental import pallas as pl
from jax.experimental.pallas import tpu as pltpu
from jax.sharding import PartitionSpec as P

D = 1024
HD = 64
FF = 4096
QBLK = 512
STEP = 10
CAP = 6


norm_eps = 1e-05
mask_fill = -1000000000.0
beta_one = 0.5
beta_two = 0.5
rate_matrix = 0.03
rate_vector = 0.1
weight_decay = 0.01
adam_eps = 1e-08


def slot_index(owners):
    owner_of = owners[:, 0]
    positions = jnp.arange(owner_of.shape[0], dtype=jnp.int32)
    earlier = (positions[None, :] < positions[:, None]) & (owner_of[None, :] == owner_of[:, None])
    within = jnp.sum(earlier.astype(jnp.int32), axis=1)
    return owner_of * CAP + within


def layer_stats(residual):
    center = residual - jnp.mean(residual, axis=-1, keepdims=True)
    spread = jnp.mean(center * center, axis=-1, keepdims=True)
    inverse = lax.rsqrt(spread + norm_eps)
    return (center * inverse, inverse)


def norm_back(grads, normal, inverse, gains):
    scaled = grads * gains
    return inverse * (
        scaled
        - jnp.mean(scaled, axis=-1, keepdims=True)
        - normal * jnp.mean(scaled * normal, axis=-1, keepdims=True)
    )


def gelu_exact(values):
    return jax.nn.gelu(values, approximate=False)


def block_mask(segment, valid, start):
    length = segment.shape[0]
    query_pos = start + jnp.arange(QBLK, dtype=jnp.int32)
    key_pos = jnp.arange(length, dtype=jnp.int32)
    query_seg = lax.dynamic_slice_in_dim(segment, start, QBLK, 0)
    same = query_seg[:, None] == segment[None, :]
    return same & ((valid[None, :] == 1) | (query_pos[:, None] == key_pos[None, :]))


def block_scores(block_q, key_rows, segment, valid, start):
    scores = jnp.einsum("qhd,khd->hqk", block_q, key_rows, preferred_element_type=jnp.float32)
    return jnp.where(block_mask(segment, valid, start)[None], scores, mask_fill)


def attend_forward(queries, key_rows, value_rows, segment, valid):
    length = queries.shape[0]

    def one_block(index):
        start = index * QBLK
        block_q = lax.dynamic_slice_in_dim(queries, start, QBLK, 0)
        scores = block_scores(block_q, key_rows, segment, valid, start)
        row_max = jnp.max(scores, axis=2, keepdims=True)
        raised = jnp.exp(scores - row_max)
        totals = jnp.sum(raised, axis=2, keepdims=True)
        weights = (raised / totals).astype(jnp.bfloat16)
        context = jnp.einsum(
            "hqk,khd->qhd", weights, value_rows, preferred_element_type=jnp.float32
        )
        return (context, (row_max + jnp.log(totals))[:, :, 0])

    context, log_sums = lax.map(one_block, jnp.arange(length // QBLK, dtype=jnp.int32))
    return (context.reshape(length, -1), log_sums)


def attend_backward(queries, key_rows, value_rows, segment, valid, log_sums, grad_context):
    length = queries.shape[0]

    def one_block(carry, index):
        key_acc, value_acc = carry
        start = index * QBLK
        block_q = lax.dynamic_slice_in_dim(queries, start, QBLK, 0)
        block_g = lax.dynamic_slice_in_dim(grad_context, start, QBLK, 0)
        scores = block_scores(block_q, key_rows, segment, valid, start)
        weights = jnp.exp(scores - log_sums[index][:, :, None])
        value_acc = value_acc + jnp.einsum(
            "hqk,qhd->khd",
            weights.astype(jnp.bfloat16),
            block_g,
            preferred_element_type=jnp.float32,
        )
        grad_weights = jnp.einsum(
            "qhd,khd->hqk", block_g, value_rows, preferred_element_type=jnp.float32
        )
        inner = jnp.sum(weights * grad_weights, axis=2, keepdims=True)
        grad_scores = (weights * (grad_weights - inner)).astype(jnp.bfloat16)
        grad_q = jnp.einsum(
            "hqk,khd->qhd", grad_scores, key_rows, preferred_element_type=jnp.float32
        )
        key_acc = key_acc + jnp.einsum(
            "hqk,qhd->khd", grad_scores, block_q, preferred_element_type=jnp.float32
        )
        return ((key_acc, value_acc), grad_q)

    zeros_kv = jnp.zeros(key_rows.shape, jnp.float32)
    (grad_keys, grad_values), grad_queries = lax.scan(
        one_block, (zeros_kv, zeros_kv), jnp.arange(length // QBLK, dtype=jnp.int32)
    )
    return (
        grad_queries.reshape(length, -1),
        grad_keys.reshape(length, -1),
        grad_values.reshape(length, -1),
    )


def adam_update(weights, first, second, grads, rate, decay):
    first_new = beta_one * first + (1.0 - beta_one) * grads
    second_new = beta_two * second + (1.0 - beta_two) * grads * grads
    first_hat = first_new / (1.0 - beta_one**STEP)
    second_hat = second_new / (1.0 - beta_two**STEP)
    updated = weights - rate * (first_hat / (jnp.sqrt(second_hat) + adam_eps) + decay * weights)
    return (updated, first_new, second_new)


def on_device_generic(
    tokens,
    segment_ids,
    key_mask,
    owners,
    master_slots,
    slot_first,
    slot_second,
    vectors,
    vector_first,
    vector_second,
    out_grad,
):
    n_tensor = lax.axis_size("tensor")
    group = lax.axis_index("tensor")
    head_cols = D // n_tensor
    unit_cols = FF // n_tensor
    heads_here = head_cols // HD
    seq_count = segment_ids.shape[0]
    length = segment_ids.shape[1]
    query_scale = HD ** (-0.5)
    slots = slot_index(owners)
    gathered_slots = lax.all_gather(master_slots[0].astype(jnp.bfloat16), "dp", axis=0, tiled=True)
    stack = jnp.take(gathered_slots, slots, axis=0).reshape(-1, D)
    w_mix = stack[0 : 3 * head_cols]
    w_out = stack[3 * head_cols : 4 * head_cols]
    w_up = stack[4 * head_cols : 4 * head_cols + unit_cols]
    w_down = stack[4 * head_cols + unit_cols :]
    bias_query = lax.dynamic_slice_in_dim(vectors[0], group * head_cols, head_cols, 0)
    bias_value = lax.dynamic_slice_in_dim(vectors[1], group * head_cols, head_cols, 0)
    bias_up = lax.dynamic_slice_in_dim(vectors[2:6].reshape(FF), group * unit_cols, unit_cols, 0)
    gathered = lax.all_gather(tokens, "tensor", axis=0, tiled=True)
    mixed = jnp.einsum("ld,kd->lk", gathered, w_mix, preferred_element_type=jnp.float32)
    queries = ((mixed[:, :head_cols] + bias_query) * query_scale).astype(jnp.bfloat16)
    key_rows = mixed[:, head_cols : 2 * head_cols].astype(jnp.bfloat16)
    value_rows = (mixed[:, 2 * head_cols :] + bias_value).astype(jnp.bfloat16)
    head_shape = (seq_count, length, heads_here, HD)
    queries_h = queries.reshape(head_shape)
    keys_h = key_rows.reshape(head_shape)
    values_h = value_rows.reshape(head_shape)

    def forward_seq(element):
        return attend_forward(element[0], element[1], element[2], element[3], element[4])

    context, log_sums = lax.map(forward_seq, (queries_h, keys_h, values_h, segment_ids, key_mask))
    context = context.reshape(-1, head_cols).astype(jnp.bfloat16)
    attn_sum = lax.psum_scatter(
        jnp.einsum("lk,kd->ld", context, w_out, preferred_element_type=jnp.float32).astype(
            jnp.bfloat16
        ),
        "tensor",
        scatter_dimension=0,
        tiled=True,
    ).astype(jnp.float32)
    residual_one = tokens.astype(jnp.float32) + (attn_sum + vectors[6])
    normal_one, inverse_one = layer_stats(residual_one)
    normed = normal_one * vectors[8] + vectors[9]
    normed_low = normed.astype(jnp.bfloat16)
    norm_rows = lax.all_gather(normed_low, "tensor", axis=0, tiled=True)
    hidden_pre = (
        jnp.einsum("ld,kd->lk", norm_rows, w_up, preferred_element_type=jnp.float32) + bias_up
    )
    hidden_full, gelu_pull = jax.vjp(gelu_exact, hidden_pre)
    hidden = hidden_full.astype(jnp.bfloat16)
    mlp_sum = lax.psum_scatter(
        jnp.einsum("lk,kd->ld", hidden, w_down, preferred_element_type=jnp.float32).astype(
            jnp.bfloat16
        ),
        "tensor",
        scatter_dimension=0,
        tiled=True,
    ).astype(jnp.float32)
    residual_two = normed + (mlp_sum + vectors[7])
    normal_two, inverse_two = layer_stats(residual_two)
    layer_out = (normal_two * vectors[10] + vectors[11]).astype(jnp.bfloat16)
    grad_out = out_grad.astype(jnp.float32)
    grad_two = norm_back(grad_out, normal_two, inverse_two, vectors[10])
    grad_down_in = lax.all_gather(grad_two.astype(jnp.bfloat16), "tensor", axis=0, tiled=True)
    grad_hidden = jnp.einsum("ld,kd->lk", grad_down_in, w_down, preferred_element_type=jnp.float32)
    grad_w_down = jnp.einsum("lk,ld->kd", hidden, grad_down_in, preferred_element_type=jnp.float32)
    grad_pre = gelu_pull(grad_hidden)[0].astype(jnp.bfloat16)
    norm_back_rows = lax.all_gather(normed_low, "tensor", axis=0, tiled=True)
    grad_w_up = jnp.einsum(
        "lk,ld->kd", grad_pre, norm_back_rows, preferred_element_type=jnp.float32
    )
    grad_norm = grad_two + lax.psum_scatter(
        jnp.einsum("lk,kd->ld", grad_pre, w_up, preferred_element_type=jnp.float32).astype(
            jnp.bfloat16
        ),
        "tensor",
        scatter_dimension=0,
        tiled=True,
    ).astype(jnp.float32)
    grad_one = norm_back(grad_norm, normal_one, inverse_one, vectors[8])
    grad_attn_in = lax.all_gather(grad_one.astype(jnp.bfloat16), "tensor", axis=0, tiled=True)
    grad_context = jnp.einsum(
        "ld,kd->lk", grad_attn_in, w_out, preferred_element_type=jnp.float32
    ).astype(jnp.bfloat16)
    grad_w_out = jnp.einsum("lk,ld->kd", context, grad_attn_in, preferred_element_type=jnp.float32)

    def backward_seq(element):
        return attend_backward(
            element[0], element[1], element[2], element[3], element[4], element[5], element[6]
        )

    grad_q, grad_k, grad_v = lax.map(
        backward_seq,
        (
            queries_h,
            keys_h,
            values_h,
            segment_ids,
            key_mask,
            log_sums,
            grad_context.reshape(head_shape),
        ),
    )
    grad_queries = grad_q.reshape(-1, head_cols).astype(jnp.bfloat16) * query_scale
    grad_keys = grad_k.reshape(-1, head_cols).astype(jnp.bfloat16)
    grad_values = grad_v.reshape(-1, head_cols).astype(jnp.bfloat16)
    grad_mix = jnp.concatenate([grad_queries, grad_keys, grad_values], axis=1)
    mix_back_rows = lax.all_gather(tokens, "tensor", axis=0, tiled=True)
    grad_w_mix = jnp.einsum(
        "lk,ld->kd", grad_mix, mix_back_rows, preferred_element_type=jnp.float32
    )
    input_grad = (
        grad_one
        + lax.psum_scatter(
            jnp.einsum("lk,kd->ld", grad_mix, w_mix, preferred_element_type=jnp.float32).astype(
                jnp.bfloat16
            ),
            "tensor",
            scatter_dimension=0,
            tiled=True,
        ).astype(jnp.float32)
    ).astype(jnp.bfloat16)
    query_full = lax.dynamic_update_slice_in_dim(
        jnp.zeros((D,), jnp.float32),
        jnp.sum(grad_queries.astype(jnp.float32), axis=0),
        group * head_cols,
        0,
    )
    value_full = lax.dynamic_update_slice_in_dim(
        jnp.zeros((D,), jnp.float32),
        jnp.sum(grad_values.astype(jnp.float32), axis=0),
        group * head_cols,
        0,
    )
    up_full = lax.dynamic_update_slice_in_dim(
        jnp.zeros((FF,), jnp.float32),
        jnp.sum(grad_pre.astype(jnp.float32), axis=0),
        group * unit_cols,
        0,
    )
    tail_rows = jnp.stack(
        [
            jnp.sum(grad_one, axis=0),
            jnp.sum(grad_two, axis=0),
            jnp.sum(grad_norm * normal_one, axis=0),
            jnp.sum(grad_norm, axis=0),
            jnp.sum(grad_out * normal_two, axis=0),
            jnp.sum(grad_out, axis=0),
        ]
    )
    vector_terms = jnp.concatenate(
        [jnp.stack([query_full, value_full]), up_full.reshape(FF // D, D), tail_rows], axis=0
    )
    vector_grads = lax.psum(vector_terms, ("dp", "tensor"))
    grad_stack = jnp.concatenate([grad_w_mix, grad_w_out, grad_w_up, grad_w_down], axis=0)
    grad_pieces = grad_stack.reshape(slots.shape[0], -1, D)
    spread_slots = (
        jnp.zeros((lax.axis_size("dp") * CAP,) + grad_pieces.shape[1:], jnp.float32)
        .at[slots]
        .set(grad_pieces)
    )
    own_grads = lax.psum_scatter(
        spread_slots.astype(jnp.bfloat16), "dp", scatter_dimension=0, tiled=True
    ).astype(jnp.float32)
    slot_new, slot_first_new, slot_second_new = adam_update(
        master_slots[0], slot_first[0], slot_second[0], own_grads, rate_matrix, weight_decay
    )
    vector_new, vector_first_new, vector_second_new = adam_update(
        vectors, vector_first, vector_second, vector_grads, rate_vector, 0.0
    )
    return (
        layer_out,
        input_grad,
        slot_new[None],
        slot_first_new[None],
        slot_second_new[None],
        vector_new,
        vector_first_new,
        vector_second_new,
    )


DOC_MAX = 800
EXT_PAD = 512
ABLK = 256
HPG = 8
AUG = 16
neg_big = -1000000000.0
NN = (((1,), (0,)), ((), ()))
NT = (((1,), (1,)), ((), ()))
TN = (((0,), (0,)), ((), ()))


def mm(a, b, dims):
    return lax.dot_general(a, b, dims, preferred_element_type=jnp.float32)


def attn_fwd_kernel(lo_ref, hi_ref, q_ref, k_ref, v_ref, qaug_ref, kaug_ref, hid_ref, o_ref, lse_ref, kn_ref, m_ref, acc_ref):
    ext = q_ref.shape[1]
    ones = jnp.concatenate(
        [jnp.ones((1, ABLK), jnp.float32), jnp.zeros((AUG - 1, ABLK), jnp.float32)], axis=0
    ).astype(jnp.bfloat16)
    for h in range(HPG):
        rows = slice(h * HD, (h + 1) * HD)
        kn_ref[h] = jnp.concatenate([k_ref[rows, :], kaug_ref[...]], axis=0).T

    def query_block(qb, _):
        lo = lo_ref[qb]
        hi = hi_ref[qb]
        qs = pl.ds(pl.multiple_of(qb * ABLK, ABLK), ABLK)

        @pl.when(hi > lo)
        def _work():
            hidden = hid_ref[0:1, qs]
            for h in range(HPG):
                rows = slice(h * HD, (h + 1) * HD)
                q32 = q_ref[rows, qs].astype(jnp.float32)
                k32 = k_ref[rows, qs].astype(jnp.float32)
                own = jnp.sum(q32 * k32, axis=0, keepdims=True)
                m_ref[h] = jnp.where(hidden > 0.0, own, -1e30)
                acc_ref[h, 0:HD, :] = v_ref[rows, qs].astype(jnp.float32) * hidden
                acc_ref[h, HD:, :] = jnp.broadcast_to(hidden, (AUG, ABLK))

            def key_block(kb, _):
                ks = pl.ds(pl.multiple_of(kb * ABLK, ABLK), ABLK)
                heads = [slice(h * HD, (h + 1) * HD) for h in range(HPG)]
                scores = [
                    mm(kn_ref[h, ks, :], jnp.concatenate([q_ref[heads[h], qs], qaug_ref[:, qs]], axis=0), NN)
                    for h in range(HPG)
                ]
                olds = [m_ref[h] for h in range(HPG)]
                news = [
                    jnp.maximum(olds[h], jnp.max(scores[h], axis=0, keepdims=True)) for h in range(HPG)
                ]
                raised = [jnp.exp(scores[h] - news[h]).astype(jnp.bfloat16) for h in range(HPG)]
                for h in range(HPG):
                    m_ref[h] = news[h]
                    va = jnp.concatenate([v_ref[heads[h], ks], ones], axis=0)
                    acc_ref[h] = acc_ref[h] * jnp.exp(olds[h] - news[h]) + mm(va, raised[h], NN)
                return 0

            lax.fori_loop(lo, hi, key_block, 0)
            for h in range(HPG):
                rows = slice(h * HD, (h + 1) * HD)
                total = acc_ref[h, HD : HD + 1, :]
                o_ref[rows, qs] = (acc_ref[h, 0:HD, :] * (1.0 / total)).astype(jnp.bfloat16)
                lse_ref[0, h : h + 1, qs] = m_ref[h] + jnp.log(total)

        @pl.when(hi <= lo)
        def _skip():
            o_ref[:, qs] = jnp.zeros((HPG * HD, ABLK), jnp.bfloat16)
            lse_ref[0, :, qs] = jnp.zeros((8, ABLK), jnp.float32)

        return 0

    lax.fori_loop(0, ext // ABLK, query_block, 0)


def attn_bwd_kernel(
    lo_ref, hi_ref, q_ref, k_ref, v_ref, g_ref, c_ref, lse_ref, qaug_ref, kaug_ref, hid_ref,
    dq_ref, dk_ref, dv_ref, kn_ref, vn_ref, acc_ref, dk_acc, dv_acc,
):
    ext = q_ref.shape[1]
    for h in range(HPG):
        rows = slice(h * HD, (h + 1) * HD)
        kn_ref[h] = jnp.concatenate([k_ref[rows, :], kaug_ref[...]], axis=0).T
        vn_ref[h] = v_ref[rows, :].T
    dk_acc[...] = jnp.zeros_like(dk_acc)
    dv_acc[...] = jnp.zeros_like(dv_acc)

    def query_block(qb, _):
        lo = lo_ref[qb]
        hi = hi_ref[qb]
        qs = pl.ds(pl.multiple_of(qb * ABLK, ABLK), ABLK)

        @pl.when(hi > lo)
        def _work():
            hidden = hid_ref[0:1, qs]
            deltas = []
            logs = []
            for h in range(HPG):
                rows = slice(h * HD, (h + 1) * HD)
                q32 = q_ref[rows, qs].astype(jnp.float32)
                k32 = k_ref[rows, qs].astype(jnp.float32)
                v32 = v_ref[rows, qs].astype(jnp.float32)
                g32 = g_ref[rows, qs].astype(jnp.float32)
                c32 = c_ref[rows, qs].astype(jnp.float32)
                delta = jnp.sum(g32 * c32, axis=0, keepdims=True)
                log = lse_ref[0, h : h + 1, qs]
                own = jnp.sum(q32 * k32, axis=0, keepdims=True)
                p_own = jnp.where(hidden > 0.0, jnp.exp(own - log), 0.0)
                d_own = p_own * (jnp.sum(g32 * v32, axis=0, keepdims=True) - delta)
                acc_ref[h] = d_own * k32
                dk_acc[rows, qs] += d_own * q32
                dv_acc[rows, qs] += p_own * g32
                deltas.append(delta)
                logs.append(log)

            def key_block(kb, _):
                ks = pl.ds(pl.multiple_of(kb * ABLK, ABLK), ABLK)
                heads = [slice(h * HD, (h + 1) * HD) for h in range(HPG)]
                every = range(HPG)
                qs_h = [q_ref[heads[h], qs] for h in every]
                gs_h = [g_ref[heads[h], qs] for h in every]
                scores = [
                    mm(kn_ref[h, ks, :], jnp.concatenate([qs_h[h], qaug_ref[:, qs]], axis=0), NN)
                    for h in every
                ]
                grads = [mm(vn_ref[h, ks, :], gs_h[h], NN) for h in every]
                weights = [jnp.exp(scores[h] - logs[h]) for h in every]
                low = [weights[h].astype(jnp.bfloat16) for h in every]
                back = [
                    (weights[h] * (grads[h] - deltas[h])).astype(jnp.bfloat16) for h in every
                ]
                v_new = [mm(gs_h[h], low[h], NT) for h in every]
                k_new = [mm(qs_h[h], back[h], NT) for h in every]
                q_new = [mm(k_ref[heads[h], ks], back[h], NN) for h in every]
                for h in every:
                    dv_acc[heads[h], ks] += v_new[h]
                    dk_acc[heads[h], ks] += k_new[h]
                    acc_ref[h] += q_new[h]
                return 0

            lax.fori_loop(lo, hi, key_block, 0)
            for h in range(HPG):
                rows = slice(h * HD, (h + 1) * HD)
                dq_ref[rows, qs] = acc_ref[h].astype(jnp.bfloat16) * (HD ** (-0.5))

        @pl.when(hi <= lo)
        def _skip():
            dq_ref[:, qs] = jnp.zeros((HPG * HD, ABLK), jnp.bfloat16)

        return 0

    lax.fori_loop(0, ext // ABLK, query_block, 0)
    dk_ref[...] = dk_acc[...].astype(jnp.bfloat16)
    dv_ref[...] = dv_acc[...].astype(jnp.bfloat16)


def group_block(offset, rows, ext):
    return pl.BlockSpec((rows, ext), lambda g, lo, hi: (offset + g, 0))


def fixed_block(rows, ext):
    return pl.BlockSpec((rows, ext), lambda g, lo, hi: (0, 0))


def attend(lo, hi, qkv, qaug, kaug, hidden):
    ext = qkv.shape[1]
    groups = D // HD // HPG
    rows = HPG * HD
    return pl.pallas_call(
        attn_fwd_kernel,
        out_shape=(
            jax.ShapeDtypeStruct((D, ext), jnp.bfloat16),
            jax.ShapeDtypeStruct((groups, 8, ext), jnp.float32),
        ),
        grid_spec=pltpu.PrefetchScalarGridSpec(
            num_scalar_prefetch=2,
            grid=(groups,),
            in_specs=[
                group_block(0, rows, ext),
                group_block(groups, rows, ext),
                group_block(2 * groups, rows, ext),
                fixed_block(AUG, ext),
                fixed_block(AUG, ext),
                fixed_block(8, ext),
            ],
            out_specs=[
                group_block(0, rows, ext),
                pl.BlockSpec((1, 8, ext), lambda g, lo, hi: (g, 0, 0)),
            ],
            scratch_shapes=[
                pltpu.VMEM((HPG, ext, HD + AUG), jnp.bfloat16),
                pltpu.VMEM((HPG, 1, ABLK), jnp.float32),
                pltpu.VMEM((HPG, HD + AUG, ABLK), jnp.float32),
            ],
        ),
        compiler_params=pltpu.CompilerParams(vmem_limit_bytes=40 * 2**20),
        cost_estimate=pl.CostEstimate(flops=20 * 10**9, bytes_accessed=14 * 10**6, transcendentals=0),
        name="attend",
    )(lo, hi, qkv, qkv, qkv, qaug, kaug, hidden)


def attend_back(lo, hi, qkv, grads, context, logs, qaug, kaug, hidden, first, step):
    ext = qkv.shape[1]
    groups = D // HD // HPG
    rows = HPG * HD
    count = len(range(first, groups, step))
    out = jax.ShapeDtypeStruct((count * rows, ext), jnp.bfloat16)

    def taken(offset):
        return pl.BlockSpec((rows, ext), lambda g, lo, hi: (offset + first + step * g, 0))

    return pl.pallas_call(
        attn_bwd_kernel,
        out_shape=(out, out, out),
        grid_spec=pltpu.PrefetchScalarGridSpec(
            num_scalar_prefetch=2,
            grid=(count,),
            in_specs=[
                taken(0),
                taken(groups),
                taken(2 * groups),
                taken(0),
                taken(0),
                pl.BlockSpec((1, 8, ext), lambda g, lo, hi: (first + step * g, 0, 0)),
                fixed_block(AUG, ext),
                fixed_block(AUG, ext),
                fixed_block(8, ext),
            ],
            out_specs=[group_block(0, rows, ext)] * 3,
            scratch_shapes=[
                pltpu.VMEM((HPG, ext, HD + AUG), jnp.bfloat16),
                pltpu.VMEM((HPG, ext, HD), jnp.bfloat16),
                pltpu.VMEM((HPG, HD, ABLK), jnp.float32),
                pltpu.VMEM((rows, ext), jnp.float32),
                pltpu.VMEM((rows, ext), jnp.float32),
            ],
        ),
        compiler_params=pltpu.CompilerParams(vmem_limit_bytes=48 * 2**20),
        cost_estimate=pl.CostEstimate(flops=50 * 10**9, bytes_accessed=30 * 10**6, transcendentals=0),
        name="attend_back",
    )(lo, hi, qkv, qkv, qkv, grads, context, logs, qaug, kaug, hidden)


def document_plan(segment, valid, half, rows):
    length = segment.shape[0]
    ext = rows + EXT_PAD
    base = half * EXT_PAD
    position = jnp.arange(length, dtype=jnp.int32)
    documents = jnp.arange(8, dtype=jnp.int32)[:, None]
    one_hot = segment[None, :] == documents
    counts = jnp.sum(one_hot.astype(jnp.int32), axis=1, keepdims=True)
    starts = jnp.sum((segment[None, :] < documents).astype(jnp.int32), axis=1, keepdims=True)
    start = jnp.sum(jnp.where(one_hot, starts, 0), axis=0)
    end = jnp.sum(jnp.where(one_hot, starts + counts, 0), axis=0)
    crossing = (start < rows) & (end > rows)
    left = jnp.max(jnp.where(crossing, rows - start, 0))
    right = jnp.max(jnp.where(crossing, end - rows, 0))
    worker = jnp.where(left <= right, half == 1, half == 0)
    own = (position >= half * rows) & (position < (half + 1) * rows)
    handled = jnp.where(crossing, worker, own)
    cut = lambda values: lax.dynamic_slice_in_dim(values, base, ext, 0)
    handled_ext = cut(handled)
    begins = jnp.where(handled_ext, cut(start) - base, ext).reshape(-1, ABLK)
    ends = jnp.where(handled_ext, cut(end) - base, 0).reshape(-1, ABLK)
    lo = jnp.min(begins, axis=1) // ABLK
    hi = (jnp.max(ends, axis=1) + (ABLK - 1)) // ABLK
    blank = jnp.max(ends, axis=1) == 0
    lo = jnp.where(blank, 0, lo)
    hi = jnp.where(blank, 0, hi)
    hot = cut(one_hot.T).T
    masked = cut(valid) == 0
    ones = jnp.ones((1, ext), jnp.bfloat16)
    fill = jnp.zeros((AUG - 9, ext), jnp.bfloat16)
    qaug = jnp.concatenate([hot.astype(jnp.bfloat16), ones, fill], axis=0)
    kaug = jnp.concatenate(
        [
            jnp.where(hot, 0.0, neg_big).astype(jnp.bfloat16),
            jnp.where(masked[None, :], neg_big, 0.0).astype(jnp.bfloat16),
            fill,
        ],
        axis=0,
    )
    hidden = jnp.broadcast_to(masked.astype(jnp.float32)[None, :], (8, ext))
    foreign = lax.dynamic_slice_in_dim(crossing & ~worker, half * rows, rows, 0)
    return lo, hi, qaug, kaug, hidden, handled_ext, foreign


MESH = pl.DeviceIdType.MESH
CHUNKS = 3


def neighbours(z, y, core, x):
    def at(z, y, core, x):
        return {"dp": (z * 2 + y) * 2 + core, "tensor": x}

    return {
        "x": at(z, y, core, 1 - x),
        "y": at(z, 1 - y, core, x),
        "core": at(z, y, 1 - core, x),
        "up": at(jnp.minimum(z + 1, 3), y, core, x),
        "down": at(jnp.maximum(z - 1, 0), y, core, x),
    }


def greet(near, z):
    barrier = pltpu.get_barrier_semaphore()
    for name in ("x", "y", "core"):
        pl.semaphore_signal(barrier, inc=1, device_id=near[name], device_id_type=MESH)

    @pl.when(z < 3)
    def _up():
        pl.semaphore_signal(barrier, inc=1, device_id=near["up"], device_id_type=MESH)

    @pl.when(z > 0)
    def _down():
        pl.semaphore_signal(barrier, inc=1, device_id=near["down"], device_id_type=MESH)

    at_end = jnp.where((z == 0) | (z == 3), 1, 0)
    pl.semaphore_wait(barrier, 5 - at_end)


def greet_all(near, me, n_dp):
    barrier = pltpu.get_barrier_semaphore()
    pl.semaphore_signal(barrier, inc=1, device_id=near["x"], device_id_type=MESH)

    def one(i, _):
        other = {"dp": lax.rem(me + i, n_dp), "tensor": lax.axis_index("tensor")}
        pl.semaphore_signal(barrier, inc=1, device_id=other, device_id_type=MESH)
        return 0

    lax.fori_loop(1, n_dp, one, 0)
    pl.semaphore_wait(barrier, n_dp)


def gather_kernel(
    slots_ref, low_ref, mix_ref, up_ref, down_ref,
    spread_ref, dense_ref, local_sem, own_sem, post, mail, send, recv,
):
    z, y, core, x = coordinates()
    near = neighbours(z, y, core, x)
    width = D // 2
    outs = (mix_ref, up_ref, down_ref)
    me = lax.axis_index("dp")
    n_dp = low_ref.shape[0]
    greet_all(near, me, n_dp)

    def letter(to):
        return pltpu.make_async_remote_copy(
            src_ref=low_ref.at[to],
            dst_ref=spread_ref.at[pl.ds(me * CAP, CAP)],
            send_sem=post.at[to],
            recv_sem=mail.at[me],
            device_id={"dp": to, "tensor": x},
            device_id_type=MESH,
        )

    def answer(of):
        return pltpu.make_async_remote_copy(
            src_ref=low_ref.at[of],
            dst_ref=spread_ref.at[pl.ds(of * CAP, CAP)],
            send_sem=post.at[of],
            recv_sem=mail.at[of],
            device_id={"dp": of, "tensor": x},
            device_id_type=MESH,
        )

    def peer(i):
        return lax.rem(me + i, n_dp)

    def post_one(i, _):
        letter(peer(i)).start()
        return 0

    lax.fori_loop(1, n_dp, post_one, 0)
    mine = pltpu.make_async_copy(low_ref.at[me], spread_ref.at[pl.ds(me * CAP, CAP)], local_sem)
    mine.start()
    mine.wait()

    def mail_one(i, _):
        answer(peer(i)).wait_recv()
        letter(peer(i)).wait_send()
        return 0

    lax.fori_loop(1, n_dp, mail_one, 0)

    def place(p, _):
        dense_ref[p // 16, (p // 4) % 4, p % 4] = spread_ref[slots_ref[p]]
        return 0

    lax.fori_loop(0, slots_ref.shape[0], place, 0)

    def block(k, t, zz, yy, cc, part=None):
        groups = slice(None) if part is None else pl.ds(2 * part, 2)
        return outs[k].at[
            groups,
            t,
            :,
            pl.ds(pl.multiple_of((zz * 2 + yy) * 16, 16), 16),
            pl.ds(pl.multiple_of(cc * width, width), width),
        ]

    own = [
        pltpu.make_async_copy(dense_ref.at[k], block(k, x, z, y, core), own_sem.at[k])
        for k in range(CHUNKS)
    ]
    for one in own:
        one.start()

    def copy(kind, link, k, zz, t, yy, cc, part=None, fresh=False):
        view = block(k, t, zz, yy, cc, part)
        return pltpu.make_async_remote_copy(
            src_ref=dense_ref.at[k] if fresh else view,
            dst_ref=view,
            send_sem=send.at[kind, k, zz],
            recv_sem=recv.at[kind, k, zz],
            device_id=near[link],
            device_id_type=MESH,
        )

    def up(k, zz, fresh=False):
        return copy(0, "up", k, zz, x, y, core, fresh=fresh)

    def down(k, zz, fresh=False):
        return copy(1, "down", k, zz, x, y, core, fresh=fresh)

    def spread(k, zz, fresh):
        copy(2, "x", k, zz, x, y, core, fresh=fresh).start()
        copy(3, "y", k, zz, x, y, core, fresh=fresh).start()
        copy(4, "core", k, zz, x, y, core, fresh=fresh).start()

    def each(d, body):
        @pl.when((d > 0) & (z - d >= 0))
        def _below():
            for k in range(CHUNKS):
                body(k, z - d, 0)

        @pl.when((d > 0) & (z + d <= 3))
        def _above():
            for k in range(CHUNKS):
                body(k, z + d, 1)

    def each_or_own(d, body):
        each(d, body)

        @pl.when(d == 0)
        def _own():
            for k in range(CHUNKS):
                body(k, z, None)

    def begin(k):
        @pl.when(z < 3)
        def _up():
            up(k, z, True).start()

        @pl.when(z > 0)
        def _down():
            down(k, z, True).start()

        spread(k, z, True)

    def first(k, zz, side):
        if side == 0:
            up(k, zz).wait_recv()

            @pl.when(z < 3)
            def _up():
                up(k, zz).start()

        else:
            down(k, zz).wait_recv()

            @pl.when(z > 0)
            def _on():
                down(k, zz).start()

        spread(k, zz, False)

    def second(k, zz, side):
        copy(2, "x", k, zz, 1 - x, y, core).wait_recv()
        copy(5, "y", k, zz, 1 - x, y, core, 0).start()
        copy(7, "core", k, zz, 1 - x, y, core).start()
        copy(3, "y", k, zz, x, 1 - y, core).wait_recv()
        copy(6, "x", k, zz, x, 1 - y, core, 1).start()
        copy(8, "core", k, zz, x, 1 - y, core).start()

    def third(k, zz, side):
        copy(5, "y", k, zz, 1 - x, 1 - y, core, 0).wait_recv()
        copy(9, "core", k, zz, 1 - x, 1 - y, core, 0).start()
        copy(6, "x", k, zz, 1 - x, 1 - y, core, 1).wait_recv()
        copy(10, "core", k, zz, 1 - x, 1 - y, core, 1).start()

    def finish(k, zz, side):
        if side != 1:

            @pl.when(z < 3)
            def _up():
                up(k, zz).wait_send()

        if side != 0:

            @pl.when(z > 0)
            def _down():
                down(k, zz).wait_send()

        copy(2, "x", k, zz, x, y, core).wait_send()
        copy(3, "y", k, zz, x, y, core).wait_send()
        copy(5, "y", k, zz, 1 - x, y, core, 0).wait_send()
        copy(6, "x", k, zz, x, 1 - y, core, 1).wait_send()
        copy(4, "core", k, zz, x, y, core).wait_send()
        copy(7, "core", k, zz, 1 - x, y, core).wait_send()
        copy(8, "core", k, zz, x, 1 - y, core).wait_send()
        copy(9, "core", k, zz, 1 - x, 1 - y, core, 0).wait_send()
        copy(10, "core", k, zz, 1 - x, 1 - y, core, 1).wait_send()
        copy(4, "core", k, zz, x, y, 1 - core).wait_recv()
        copy(7, "core", k, zz, 1 - x, y, 1 - core).wait_recv()
        copy(8, "core", k, zz, x, 1 - y, 1 - core).wait_recv()
        copy(9, "core", k, zz, 1 - x, 1 - y, 1 - core, 0).wait_recv()
        copy(10, "core", k, zz, 1 - x, 1 - y, 1 - core, 1).wait_recv()

    for k in range(CHUNKS):
        begin(k)

    def step(d, _):
        @pl.when(d < 4)
        def _one():
            each(d, first)

        @pl.when((d >= 1) & (d < 5))
        def _two():
            each_or_own(d - 1, second)

        @pl.when(d >= 2)
        def _three():
            each_or_own(d - 2, third)

        return 0

    lax.fori_loop(1, 6, step, 0)

    def end(d, _):
        each_or_own(d, finish)
        return 0

    lax.fori_loop(0, 4, end, 0)
    for one in own:
        one.wait()


def gather_weights(slots, low):
    n_dp = low.shape[0]
    stack = jax.ShapeDtypeStruct((4, 2, 4, 128, D), low.dtype)
    return pl.pallas_call(
        gather_kernel,
        out_shape=(stack,) * 3,
        in_specs=[
            pl.BlockSpec(memory_space=pltpu.SMEM),
            pl.BlockSpec(memory_space=pl.ANY),
        ],
        out_specs=(pl.BlockSpec(memory_space=pl.ANY),) * 3,
        scratch_shapes=[
            pltpu.VMEM((n_dp * CAP, 16, D // 2), low.dtype),
            pltpu.VMEM((CHUNKS, 4, 4, 16, D // 2), low.dtype),
            pltpu.SemaphoreType.DMA,
            pltpu.SemaphoreType.DMA((CHUNKS,)),
            pltpu.SemaphoreType.DMA((n_dp,)),
            pltpu.SemaphoreType.DMA((n_dp,)),
            pltpu.SemaphoreType.DMA((11, CHUNKS, 4)),
            pltpu.SemaphoreType.DMA((11, CHUNKS, 4)),
        ],
        compiler_params=pltpu.CompilerParams(
            collective_id=1, has_side_effects=True, vmem_limit_bytes=32 * 2**20
        ),
        cost_estimate=pl.CostEstimate(flops=0, bytes_accessed=50 * 10**6, transcendentals=0),
        name="gather_weights",
    )(slots, low)


BLOCKS = 12


def reduce_kernel(
    piece_ref, vec_ref, far_qkv, far_out, far_up, far_down, near_qkv, near_out, near_up, near_down,
    out_ref, sum_ref,
    near_buf, core_in, x_in, y_in, x2_in, y2_in, line, up_in, down_in, done, parcel, vec_in, vec_out,
    near_sem, local_sem, post, mail, send, recv, vec_send, vec_recv,
):
    z, y, core, x = coordinates()
    near = neighbours(z, y, core, x)
    me = lax.axis_index("dp")
    n_dp = parcel.shape[0]
    width = D // 2
    greet_all(near, me, n_dp)

    def from_hbm(refs, i, body):
        for ref, first, count in zip(refs, (0, 3, 4, 8), (3, 1, 4, 4)):

            @pl.when((i >= first) & (i < first + count))
            def _here():
                body(ref.at[i - first])

    def remote(kind, i, link, src, dst):
        return pltpu.make_async_remote_copy(
            src_ref=src,
            dst_ref=dst,
            send_sem=send.at[kind, i],
            recv_sem=recv.at[kind, i],
            device_id=near[link],
            device_id_type=MESH,
        )

    def core_copy(i, src):
        return remote(0, i, "core", src, core_in.at[i])

    def near_copy(i, src):
        return pltpu.make_async_copy(src, near_buf.at[i], near_sem.at[i])

    def x1(i):
        return remote(1, i, "x", core_in.at[i, 1 - x, pl.ds(0, 2)], x_in.at[i])

    def y1(i):
        return remote(2, i, "y", core_in.at[i, :, pl.ds(2, 2), :, 1 - y], y_in.at[i])

    def y2(i):
        return remote(3, i, "y", x_in.at[i, :, :, 1 - y], y2_in.at[i])

    def x2(i):
        return remote(4, i, "x", y_in.at[i, 1 - x], x2_in.at[i])

    def up(i, zz):
        return remote(4 + zz, i, "up", up_in.at[i, zz], up_in.at[i, zz])

    def down(i, zz):
        return remote(8 + zz, i, "down", down_in.at[i, zz], down_in.at[i, zz])

    def load(i):
        from_hbm((far_qkv, far_out, far_up, far_down), i, lambda src: core_copy(i, src).start())
        from_hbm((near_qkv, near_out, near_up, near_down), i, lambda src: near_copy(i, src).start())

    def stage_one(i):
        near_copy(i, near_buf.at[i]).wait()
        core_copy(i, core_in.at[i]).wait_recv()

        def add(j, _):
            t, p = j // 4, j % 4
            core_in[i, t, p] = core_in[i, t, p] + near_buf[i, t, p]
            return 0

        lax.fori_loop(0, 8, add, 0)
        x1(i).start()
        y1(i).start()

    def stage_two(i):
        x1(i).wait_recv()
        y1(i).wait_recv()
        for p in range(2):
            x_in[i, p] = x_in[i, p] + core_in[i, x, p]
        for t in range(2):
            for p in range(2):
                y_in[i, t, p] = y_in[i, t, p] + core_in[i, t, 2 + p, :, y]
        y2(i).start()
        x2(i).start()

    def stage_three(i):
        y2(i).wait_recv()
        x2(i).wait_recv()
        for p in range(2):
            line[i, :, p] = x_in[i, p, :, y] + y2_in[i, p]
            line[i, :, 2 + p] = y_in[i, x, p] + x2_in[i, p]

    def stage_up(i):
        for zz in range(1, 4):

            @pl.when((z > 0) & (zz >= z))
            def _arrived():
                up(i, zz).wait_recv()

            @pl.when((z > 0) & (zz > z))
            def _add():
                up_in[i, zz] = up_in[i, zz] + line[i, zz]

            @pl.when(z == 0)
            def _first():
                up_in[i, zz] = line[i, zz]

            @pl.when(zz > z)
            def _on():
                up(i, zz).start()

    def stage_down(i):
        for zz in range(3):

            @pl.when((z < 3) & (zz <= z))
            def _arrived():
                down(i, zz).wait_recv()

            @pl.when((z < 3) & (zz < z))
            def _add():
                down_in[i, zz] = down_in[i, zz] + line[i, zz]

            @pl.when(z == 3)
            def _first():
                down_in[i, zz] = line[i, zz]

            @pl.when(zz < z)
            def _on():
                down(i, zz).start()

    def stage_last(i):
        mine = pl.ds(i * 4, 4)

        @pl.when(z == 0)
        def _bottom():
            done[mine] = line[i, 0] + down_in[i, 0]

        @pl.when((z > 0) & (z < 3))
        def _middle():
            total = line[i, z].astype(jnp.float32) + up_in[i, z].astype(jnp.float32)
            done[mine] = (total + down_in[i, z].astype(jnp.float32)).astype(jnp.bfloat16)

        @pl.when(z == 3)
        def _top():
            done[mine] = line[i, 3] + up_in[i, 3]

    def ended(i):
        core_copy(i, core_in.at[i]).wait_send()
        x1(i).wait_send()
        y1(i).wait_send()
        y2(i).wait_send()
        x2(i).wait_send()
        for zz in range(1, 4):

            @pl.when(zz > z)
            def _up():
                up(i, zz).wait_send()

        for zz in range(3):

            @pl.when(zz < z)
            def _down():
                down(i, zz).wait_send()

    z_one = z + 1 - 2 * lax.rem(z, 2)
    z_two = lax.rem(z + 2, 4)
    partners = [
        near["core"],
        near["y"],
        near["x"],
        {"dp": (z_one * 2 + y) * 2 + core, "tensor": x},
        {"dp": (z_two * 2 + y) * 2 + core, "tensor": x},
    ]

    def swap(n):
        return pltpu.make_async_remote_copy(
            src_ref=vec_out.at[n],
            dst_ref=vec_in.at[n],
            send_sem=vec_send.at[n],
            recv_sem=vec_recv.at[n],
            device_id=partners[n],
            device_id_type=MESH,
        )

    vec_out[0] = vec_ref[...]
    for i in range(3):
        load(i)

    def step(s, _):
        @pl.when(s + 3 < BLOCKS)
        def _load():
            load(s + 3)

        @pl.when(s < BLOCKS)
        def _one():
            stage_one(s)

        @pl.when((s >= 1) & (s < BLOCKS + 1))
        def _two():
            stage_two(s - 1)

        @pl.when((s >= 2) & (s < BLOCKS + 2))
        def _three():
            stage_three(s - 2)

        @pl.when((s - 3 - z >= 0) & (s - 3 - z < BLOCKS))
        def _up():
            stage_up(s - 3 - z)

        @pl.when((s - 6 + z >= 0) & (s - 6 + z < BLOCKS))
        def _down():
            stage_down(s - 6 + z)

        @pl.when(s >= 7)
        def _last():
            stage_last(s - 7)

        for n in range(5):

            @pl.when(s == n)
            def _begin():
                swap(n).start()

            @pl.when(s == n + 1)
            def _end():
                swap(n).wait()
                if n < 4:
                    vec_out[n + 1] = vec_out[n] + vec_in[n]
                else:
                    sum_ref[...] = vec_out[n] + vec_in[n]

        return 0

    lax.fori_loop(0, BLOCKS + 7, step, 0)

    def finish(i, _):
        ended(i)
        return 0

    lax.fori_loop(0, BLOCKS, finish, 0)

    done[BLOCKS * 4] = jnp.zeros((16, width), done.dtype)

    def pack(n, _):
        parcel[n // CAP, n % CAP] = done[piece_ref[n]]
        return 0

    lax.fori_loop(0, n_dp * CAP, pack, 0)

    def place(of):
        return out_ref.at[
            :,
            pl.ds(pl.multiple_of((of // 2) * 16, 16), 16),
            pl.ds(pl.multiple_of((of % 2) * width, width), width),
        ]

    def letter(to):
        return pltpu.make_async_remote_copy(
            src_ref=parcel.at[to],
            dst_ref=place(me),
            send_sem=post.at[to],
            recv_sem=mail.at[me],
            device_id={"dp": to, "tensor": x},
            device_id_type=MESH,
        )

    def answer(of):
        return pltpu.make_async_remote_copy(
            src_ref=parcel.at[of],
            dst_ref=place(of),
            send_sem=post.at[of],
            recv_sem=mail.at[of],
            device_id={"dp": of, "tensor": x},
            device_id_type=MESH,
        )

    def post_one(i, _):
        letter(lax.rem(me + i, n_dp)).start()
        return 0

    lax.fori_loop(1, n_dp, post_one, 0)
    own = pltpu.make_async_copy(parcel.at[me], place(me), local_sem)
    own.start()

    def mail_one(i, _):
        answer(lax.rem(me + i, n_dp)).wait_recv()
        letter(lax.rem(me + i, n_dp)).wait_send()
        return 0

    lax.fori_loop(1, n_dp, mail_one, 0)
    own.wait()


def reduce_grads(piece_of, vec, far, near):
    n_dp = piece_of.shape[0] // CAP
    low = jnp.bfloat16
    width = D // 2
    anywhere = pl.BlockSpec(memory_space=pl.ANY)
    vmem = pl.BlockSpec(memory_space=pltpu.VMEM)
    return pl.pallas_call(
        reduce_kernel,
        out_shape=(
            jax.ShapeDtypeStruct((CAP, 128, D), low),
            jax.ShapeDtypeStruct(vec.shape, jnp.float32),
        ),
        in_specs=[pl.BlockSpec(memory_space=pltpu.SMEM), vmem] + [anywhere] * 8,
        out_specs=(anywhere, vmem),
        scratch_shapes=[
            pltpu.VMEM((BLOCKS, 2, 4, 4, 2, 16, width), low),
            pltpu.VMEM((BLOCKS, 2, 4, 4, 2, 16, width), low),
            pltpu.VMEM((BLOCKS, 2, 4, 2, 16, width), low),
            pltpu.VMEM((BLOCKS, 2, 2, 4, 16, width), low),
            pltpu.VMEM((BLOCKS, 2, 4, 16, width), low),
            pltpu.VMEM((BLOCKS, 2, 4, 16, width), low),
            pltpu.VMEM((BLOCKS, 4, 4, 16, width), low),
            pltpu.VMEM((BLOCKS, 4, 4, 16, width), low),
            pltpu.VMEM((BLOCKS, 4, 4, 16, width), low),
            pltpu.VMEM((BLOCKS * 4 + 1, 16, width), low),
            pltpu.VMEM((n_dp, CAP, 16, width), low),
            pltpu.VMEM((5,) + vec.shape, jnp.float32),
            pltpu.VMEM((5,) + vec.shape, jnp.float32),
            pltpu.SemaphoreType.DMA((BLOCKS,)),
            pltpu.SemaphoreType.DMA,
            pltpu.SemaphoreType.DMA((n_dp,)),
            pltpu.SemaphoreType.DMA((n_dp,)),
            pltpu.SemaphoreType.DMA((11, BLOCKS)),
            pltpu.SemaphoreType.DMA((11, BLOCKS)),
            pltpu.SemaphoreType.DMA((5,)),
            pltpu.SemaphoreType.DMA((5,)),
        ],
        compiler_params=pltpu.CompilerParams(
            collective_id=2, has_side_effects=True, vmem_limit_bytes=60 * 2**20
        ),
        cost_estimate=pl.CostEstimate(flops=0, bytes_accessed=50 * 10**6, transcendentals=0),
        name="reduce_grads",
    )(piece_of, vec, *far, *near)


def gelu_pair(values):
    cdf = 0.5 * lax.erfc(values * (-(0.5**0.5)))
    density = jnp.exp(values * values * -0.5) * (0.5 / jnp.pi) ** 0.5
    return (values * cdf, cdf + values * density)


def coordinates():
    dp = lax.axis_index("dp")
    return dp // 4, (dp // 2) % 2, dp % 2, lax.axis_index("tensor")


def exchange(values, axis):
    if axis == "x":
        return lax.ppermute(values, "tensor", [(0, 1), (1, 0)])
    flip = {"core": 1, "y": 2, "z_near": 4, "z_far": 8}[axis]
    return lax.ppermute(values, "dp", [(i, i ^ flip) for i in range(lax.axis_size("dp"))])


def pick(values, index, axis):
    return lax.dynamic_index_in_dim(values, index, axis, keepdims=False)


def products(lhs, rhs, dims):
    core = lax.axis_index("dp") % 2
    width = D // 2

    def half(which):
        columns = lax.dynamic_slice_in_dim(rhs, which * width, width, 1)
        return mm(lhs, columns, dims).astype(jnp.bfloat16).reshape(-1, 2, 4, 4, 2, 16, width)

    return half(1 - core), half(core)


def on_device_rows(
    tokens,
    segment_ids,
    key_mask,
    owners,
    master_slots,
    slot_first,
    slot_second,
    vectors,
    vector_first,
    vector_second,
    out_grad,
):
    n_dp = lax.axis_size("dp")
    n_tensor = lax.axis_size("tensor")
    half = lax.axis_index("tensor")
    every = ("tensor", "dp")
    rows = tokens.shape[0]
    ext = rows + EXT_PAD
    halo = DOC_MAX // 2
    swap = [(0, 1), (1, 0)]
    edge = jnp.where(half == 0, rows - halo, 0)
    halo_at = jnp.where(half == 0, rows, EXT_PAD - halo)
    own_at = half * EXT_PAD

    def extend(own_rows, halo_rows):
        whole = jnp.zeros((ext,) + own_rows.shape[1:], own_rows.dtype)
        whole = lax.dynamic_update_slice_in_dim(whole, halo_rows, halo_at, 0)
        return lax.dynamic_update_slice_in_dim(whole, own_rows, own_at, 0)

    def own_part(values):
        return lax.dynamic_slice_in_dim(values, own_at, rows, 0)

    def halo_part(values):
        return lax.dynamic_slice_in_dim(values, halo_at, halo, 0)

    lo, hi, qaug, kaug, hidden_keys, handled, foreign = document_plan(
        segment_ids[0], key_mask[0], half, rows
    )
    halo_tokens = lax.ppermute(lax.dynamic_slice_in_dim(tokens, edge, halo, 0), "tensor", swap)
    tokens_ext = extend(tokens, halo_tokens)

    slots = slot_index(owners)
    pieces = slots.shape[0]
    piece_rows = master_slots.shape[2]
    low_slots = master_slots[0].astype(jnp.bfloat16).reshape(CAP, 8, 16, 2, D // 2)
    low_slots = low_slots.transpose(1, 3, 0, 2, 4).reshape(n_dp, CAP, 16, D // 2)
    mix_pieces = 4 * (D // n_tensor) // piece_rows
    up_pieces = (FF // n_tensor) // piece_rows
    per = mix_pieces // 4
    mix, up, down = gather_weights(slots, low_slots)
    w_qkv = mix[:3].reshape(3 * D, D)
    w_out = mix[3].reshape(D, D)
    w_up = up.reshape(FF, D)
    w_down = down.reshape(FF, D)
    bias_up = vectors[2:6].reshape(n_tensor, 4, -1).transpose(1, 0, 2).reshape(FF)

    bias_qkv = jnp.concatenate([vectors[0], jnp.zeros((D,), jnp.float32), vectors[1]])
    scale_qkv = jnp.concatenate([jnp.full((D,), HD ** (-0.5)), jnp.ones((2 * D,))])
    qkv = (
        (mm(w_qkv, tokens_ext, NT) + bias_qkv[:, None]) * scale_qkv.astype(jnp.float32)[:, None]
    ).astype(jnp.bfloat16)
    context, logs = attend(lo, hi, qkv, qaug, kaug, hidden_keys)
    attn_ext = mm(context, w_out, TN).astype(jnp.bfloat16)
    halo_attn = lax.ppermute(halo_part(attn_ext), "tensor", swap)
    attn_back = lax.dynamic_update_slice_in_dim(
        jnp.zeros((rows, D), jnp.bfloat16), halo_attn, edge, 0
    )
    attn_sum = jnp.where(foreign[:, None], attn_back, own_part(attn_ext)).astype(jnp.float32)
    residual_one = tokens.astype(jnp.float32) + (attn_sum + vectors[6])
    normal_one, inverse_one = layer_stats(residual_one)
    normed = normal_one * vectors[8] + vectors[9]
    normed_low = normed.astype(jnp.bfloat16)

    gelu, slope = gelu_pair(mm(normed_low, w_up, NT) + bias_up)
    hidden = gelu.astype(jnp.bfloat16)
    slope = slope.astype(jnp.bfloat16)
    residual_two = normed + (mm(hidden, w_down, NN) + vectors[7])
    normal_two, inverse_two = layer_stats(residual_two)
    layer_out = (normal_two * vectors[10] + vectors[11]).astype(jnp.bfloat16)
    grad_out = out_grad.astype(jnp.float32)
    grad_two = norm_back(grad_out, normal_two, inverse_two, vectors[10])
    grad_two_low = grad_two.astype(jnp.bfloat16)

    grad_pre32 = mm(grad_two_low, w_down, NT) * slope.astype(jnp.float32)
    grad_pre = grad_pre32.astype(jnp.bfloat16)
    grad_norm = grad_two + mm(grad_pre, w_up, NN)
    grad_one = norm_back(grad_norm, normal_one, inverse_one, vectors[8])
    grad_one_low = grad_one.astype(jnp.bfloat16)

    halo_grad = lax.ppermute(
        lax.dynamic_slice_in_dim(grad_one_low, edge, halo, 0), "tensor", swap
    )
    grad_ext = jnp.where(handled[:, None], extend(grad_one_low, halo_grad), 0)
    grad_context = mm(w_out, grad_ext, NT).astype(jnp.bfloat16)
    grad_q, grad_k, grad_v = attend_back(
        lo, hi, qkv, grad_context, context, logs, qaug, kaug, hidden_keys, 0, 1
    )
    grad_qkv = jnp.concatenate([grad_q, grad_k, grad_v], axis=0)
    input_ext = mm(grad_qkv, w_qkv, TN)
    halo_input = lax.ppermute(halo_part(input_ext).astype(jnp.bfloat16), "tensor", swap)
    input_back = lax.dynamic_update_slice_in_dim(
        jnp.zeros((rows, D), jnp.bfloat16), halo_input, edge, 0
    )
    input_grad = (grad_one + own_part(input_ext) + input_back.astype(jnp.float32)).astype(
        jnp.bfloat16
    )

    vector_terms = jnp.concatenate(
        [
            jnp.stack(
                [
                    jnp.sum(grad_q.astype(jnp.float32), axis=1),
                    jnp.sum(grad_v.astype(jnp.float32), axis=1),
                ]
            ),
            jnp.sum(grad_pre.astype(jnp.float32), axis=0)
            .reshape(4, n_tensor, -1)
            .transpose(1, 0, 2)
            .reshape(FF // D, D),
            jnp.stack(
                [
                    jnp.sum(grad_one, axis=0),
                    jnp.sum(grad_two, axis=0),
                    jnp.sum(grad_norm * normal_one, axis=0),
                    jnp.sum(grad_norm, axis=0),
                    jnp.sum(grad_out * normal_two, axis=0),
                    jnp.sum(grad_out, axis=0),
                ]
            ),
        ],
        axis=0,
    )
    pairs = (
        products(grad_qkv, tokens_ext, NN),
        products(context, grad_ext, NN),
        products(grad_pre, normed_low, TN),
        products(hidden, grad_two_low, TN),
    )
    piece_of = jnp.full((n_dp * CAP,), pieces, jnp.int32).at[slots].set(
        jnp.arange(pieces, dtype=jnp.int32)
    )
    own_grads, vector_grads = reduce_grads(
        piece_of,
        vector_terms,
        [pair[0] for pair in pairs],
        [pair[1] for pair in pairs],
    )
    own_grads = own_grads.astype(jnp.float32)
    slot_new, slot_first_new, slot_second_new = adam_update(
        master_slots[0], slot_first[0], slot_second[0], own_grads, rate_matrix, weight_decay
    )
    vector_new, vector_first_new, vector_second_new = adam_update(
        vectors, vector_first, vector_second, vector_grads, rate_vector, 0.0
    )
    return (
        layer_out,
        input_grad,
        slot_new[None],
        slot_first_new[None],
        slot_second_new[None],
        vector_new,
        vector_first_new,
        vector_second_new,
    )


def solution(mesh):
    placed = (
        P(("dp", "tensor"), None),
        P("dp", None),
        P("dp", None),
        P(),
        P("tensor", "dp", None, None),
        P("tensor", "dp", None, None),
        P("tensor", "dp", None, None),
        P(),
        P(),
        P(),
        P(("dp", "tensor"), None),
    )
    by_rows = mesh.shape["tensor"] == 2 and mesh.shape["dp"] == 16
    return jax.shard_map(
        on_device_rows if by_rows else on_device_generic,
        mesh=mesh,
        in_specs=placed,
        out_specs=(
            P(("dp", "tensor"), None),
            P(("dp", "tensor"), None),
            P("tensor", "dp", None, None),
            P("tensor", "dp", None, None),
            P("tensor", "dp", None, None),
            P(),
            P(),
            P(),
        ),
        check_vma=False,
    )
```

```python
import functools

import jax
import jax.numpy as jnp
from jax import lax
from jax.experimental import pallas as pl
from jax.experimental.pallas import tpu as pltpu
from jax.sharding import PartitionSpec as P

D = 1024
HD = 64
FF = 4096
QBLK = 512
STEP = 10
CAP = 6


norm_eps = 1e-05
mask_fill = -1000000000.0
beta_one = 0.5
beta_two = 0.5
rate_matrix = 0.03
rate_vector = 0.1
weight_decay = 0.01
adam_eps = 1e-08


def slot_index(owners):
    owner_of = owners[:, 0]
    positions = jnp.arange(owner_of.shape[0], dtype=jnp.int32)
    earlier = (positions[None, :] < positions[:, None]) & (owner_of[None, :] == owner_of[:, None])
    within = jnp.sum(earlier.astype(jnp.int32), axis=1)
    return owner_of * CAP + within


def layer_stats(residual):
    center = residual - jnp.mean(residual, axis=-1, keepdims=True)
    spread = jnp.mean(center * center, axis=-1, keepdims=True)
    inverse = lax.rsqrt(spread + norm_eps)
    return (center * inverse, inverse)


def norm_back(grads, normal, inverse, gains):
    scaled = grads * gains
    return inverse * (
        scaled
        - jnp.mean(scaled, axis=-1, keepdims=True)
        - normal * jnp.mean(scaled * normal, axis=-1, keepdims=True)
    )


def gelu_exact(values):
    return jax.nn.gelu(values, approximate=False)


def block_mask(segment, valid, start):
    length = segment.shape[0]
    query_pos = start + jnp.arange(QBLK, dtype=jnp.int32)
    key_pos = jnp.arange(length, dtype=jnp.int32)
    query_seg = lax.dynamic_slice_in_dim(segment, start, QBLK, 0)
    same = query_seg[:, None] == segment[None, :]
    return same & ((valid[None, :] == 1) | (query_pos[:, None] == key_pos[None, :]))


def block_scores(block_q, key_rows, segment, valid, start):
    scores = jnp.einsum("qhd,khd->hqk", block_q, key_rows, preferred_element_type=jnp.float32)
    return jnp.where(block_mask(segment, valid, start)[None], scores, mask_fill)


def attend_forward(queries, key_rows, value_rows, segment, valid):
    length = queries.shape[0]

    def one_block(index):
        start = index * QBLK
        block_q = lax.dynamic_slice_in_dim(queries, start, QBLK, 0)
        scores = block_scores(block_q, key_rows, segment, valid, start)
        row_max = jnp.max(scores, axis=2, keepdims=True)
        raised = jnp.exp(scores - row_max)
        totals = jnp.sum(raised, axis=2, keepdims=True)
        weights = (raised / totals).astype(jnp.bfloat16)
        context = jnp.einsum(
            "hqk,khd->qhd", weights, value_rows, preferred_element_type=jnp.float32
        )
        return (context, (row_max + jnp.log(totals))[:, :, 0])

    context, log_sums = lax.map(one_block, jnp.arange(length // QBLK, dtype=jnp.int32))
    return (context.reshape(length, -1), log_sums)


def attend_backward(queries, key_rows, value_rows, segment, valid, log_sums, grad_context):
    length = queries.shape[0]

    def one_block(carry, index):
        key_acc, value_acc = carry
        start = index * QBLK
        block_q = lax.dynamic_slice_in_dim(queries, start, QBLK, 0)
        block_g = lax.dynamic_slice_in_dim(grad_context, start, QBLK, 0)
        scores = block_scores(block_q, key_rows, segment, valid, start)
        weights = jnp.exp(scores - log_sums[index][:, :, None])
        value_acc = value_acc + jnp.einsum(
            "hqk,qhd->khd",
            weights.astype(jnp.bfloat16),
            block_g,
            preferred_element_type=jnp.float32,
        )
        grad_weights = jnp.einsum(
            "qhd,khd->hqk", block_g, value_rows, preferred_element_type=jnp.float32
        )
        inner = jnp.sum(weights * grad_weights, axis=2, keepdims=True)
        grad_scores = (weights * (grad_weights - inner)).astype(jnp.bfloat16)
        grad_q = jnp.einsum(
            "hqk,khd->qhd", grad_scores, key_rows, preferred_element_type=jnp.float32
        )
        key_acc = key_acc + jnp.einsum(
            "hqk,qhd->khd", grad_scores, block_q, preferred_element_type=jnp.float32
        )
        return ((key_acc, value_acc), grad_q)

    zeros_kv = jnp.zeros(key_rows.shape, jnp.float32)
    (grad_keys, grad_values), grad_queries = lax.scan(
        one_block, (zeros_kv, zeros_kv), jnp.arange(length // QBLK, dtype=jnp.int32)
    )
    return (
        grad_queries.reshape(length, -1),
        grad_keys.reshape(length, -1),
        grad_values.reshape(length, -1),
    )


def adam_update(weights, first, second, grads, rate, decay):
    first_new = beta_one * first + (1.0 - beta_one) * grads
    second_new = beta_two * second + (1.0 - beta_two) * grads * grads
    first_hat = first_new / (1.0 - beta_one**STEP)
    second_hat = second_new / (1.0 - beta_two**STEP)
    updated = weights - rate * (first_hat / (jnp.sqrt(second_hat) + adam_eps) + decay * weights)
    return (updated, first_new, second_new)


def on_device_generic(
    tokens,
    segment_ids,
    key_mask,
    owners,
    master_slots,
    slot_first,
    slot_second,
    vectors,
    vector_first,
    vector_second,
    out_grad,
):
    n_tensor = lax.axis_size("tensor")
    group = lax.axis_index("tensor")
    head_cols = D // n_tensor
    unit_cols = FF // n_tensor
    heads_here = head_cols // HD
    seq_count = segment_ids.shape[0]
    length = segment_ids.shape[1]
    query_scale = HD ** (-0.5)
    slots = slot_index(owners)
    gathered_slots = lax.all_gather(master_slots[0].astype(jnp.bfloat16), "dp", axis=0, tiled=True)
    stack = jnp.take(gathered_slots, slots, axis=0).reshape(-1, D)
    w_mix = stack[0 : 3 * head_cols]
    w_out = stack[3 * head_cols : 4 * head_cols]
    w_up = stack[4 * head_cols : 4 * head_cols + unit_cols]
    w_down = stack[4 * head_cols + unit_cols :]
    bias_query = lax.dynamic_slice_in_dim(vectors[0], group * head_cols, head_cols, 0)
    bias_value = lax.dynamic_slice_in_dim(vectors[1], group * head_cols, head_cols, 0)
    bias_up = lax.dynamic_slice_in_dim(vectors[2:6].reshape(FF), group * unit_cols, unit_cols, 0)
    gathered = lax.all_gather(tokens, "tensor", axis=0, tiled=True)
    mixed = jnp.einsum("ld,kd->lk", gathered, w_mix, preferred_element_type=jnp.float32)
    queries = ((mixed[:, :head_cols] + bias_query) * query_scale).astype(jnp.bfloat16)
    key_rows = mixed[:, head_cols : 2 * head_cols].astype(jnp.bfloat16)
    value_rows = (mixed[:, 2 * head_cols :] + bias_value).astype(jnp.bfloat16)
    head_shape = (seq_count, length, heads_here, HD)
    queries_h = queries.reshape(head_shape)
    keys_h = key_rows.reshape(head_shape)
    values_h = value_rows.reshape(head_shape)

    def forward_seq(element):
        return attend_forward(element[0], element[1], element[2], element[3], element[4])

    context, log_sums = lax.map(forward_seq, (queries_h, keys_h, values_h, segment_ids, key_mask))
    context = context.reshape(-1, head_cols).astype(jnp.bfloat16)
    attn_sum = lax.psum_scatter(
        jnp.einsum("lk,kd->ld", context, w_out, preferred_element_type=jnp.float32).astype(
            jnp.bfloat16
        ),
        "tensor",
        scatter_dimension=0,
        tiled=True,
    ).astype(jnp.float32)
    residual_one = tokens.astype(jnp.float32) + (attn_sum + vectors[6])
    normal_one, inverse_one = layer_stats(residual_one)
    normed = normal_one * vectors[8] + vectors[9]
    normed_low = normed.astype(jnp.bfloat16)
    norm_rows = lax.all_gather(normed_low, "tensor", axis=0, tiled=True)
    hidden_pre = (
        jnp.einsum("ld,kd->lk", norm_rows, w_up, preferred_element_type=jnp.float32) + bias_up
    )
    hidden_full, gelu_pull = jax.vjp(gelu_exact, hidden_pre)
    hidden = hidden_full.astype(jnp.bfloat16)
    mlp_sum = lax.psum_scatter(
        jnp.einsum("lk,kd->ld", hidden, w_down, preferred_element_type=jnp.float32).astype(
            jnp.bfloat16
        ),
        "tensor",
        scatter_dimension=0,
        tiled=True,
    ).astype(jnp.float32)
    residual_two = normed + (mlp_sum + vectors[7])
    normal_two, inverse_two = layer_stats(residual_two)
    layer_out = (normal_two * vectors[10] + vectors[11]).astype(jnp.bfloat16)
    grad_out = out_grad.astype(jnp.float32)
    grad_two = norm_back(grad_out, normal_two, inverse_two, vectors[10])
    grad_down_in = lax.all_gather(grad_two.astype(jnp.bfloat16), "tensor", axis=0, tiled=True)
    grad_hidden = jnp.einsum("ld,kd->lk", grad_down_in, w_down, preferred_element_type=jnp.float32)
    grad_w_down = jnp.einsum("lk,ld->kd", hidden, grad_down_in, preferred_element_type=jnp.float32)
    grad_pre = gelu_pull(grad_hidden)[0].astype(jnp.bfloat16)
    norm_back_rows = lax.all_gather(normed_low, "tensor", axis=0, tiled=True)
    grad_w_up = jnp.einsum(
        "lk,ld->kd", grad_pre, norm_back_rows, preferred_element_type=jnp.float32
    )
    grad_norm = grad_two + lax.psum_scatter(
        jnp.einsum("lk,kd->ld", grad_pre, w_up, preferred_element_type=jnp.float32).astype(
            jnp.bfloat16
        ),
        "tensor",
        scatter_dimension=0,
        tiled=True,
    ).astype(jnp.float32)
    grad_one = norm_back(grad_norm, normal_one, inverse_one, vectors[8])
    grad_attn_in = lax.all_gather(grad_one.astype(jnp.bfloat16), "tensor", axis=0, tiled=True)
    grad_context = jnp.einsum(
        "ld,kd->lk", grad_attn_in, w_out, preferred_element_type=jnp.float32
    ).astype(jnp.bfloat16)
    grad_w_out = jnp.einsum("lk,ld->kd", context, grad_attn_in, preferred_element_type=jnp.float32)

    def backward_seq(element):
        return attend_backward(
            element[0], element[1], element[2], element[3], element[4], element[5], element[6]
        )

    grad_q, grad_k, grad_v = lax.map(
        backward_seq,
        (
            queries_h,
            keys_h,
            values_h,
            segment_ids,
            key_mask,
            log_sums,
            grad_context.reshape(head_shape),
        ),
    )
    grad_queries = grad_q.reshape(-1, head_cols).astype(jnp.bfloat16) * query_scale
    grad_keys = grad_k.reshape(-1, head_cols).astype(jnp.bfloat16)
    grad_values = grad_v.reshape(-1, head_cols).astype(jnp.bfloat16)
    grad_mix = jnp.concatenate([grad_queries, grad_keys, grad_values], axis=1)
    mix_back_rows = lax.all_gather(tokens, "tensor", axis=0, tiled=True)
    grad_w_mix = jnp.einsum(
        "lk,ld->kd", grad_mix, mix_back_rows, preferred_element_type=jnp.float32
    )
    input_grad = (
        grad_one
        + lax.psum_scatter(
            jnp.einsum("lk,kd->ld", grad_mix, w_mix, preferred_element_type=jnp.float32).astype(
                jnp.bfloat16
            ),
            "tensor",
            scatter_dimension=0,
            tiled=True,
        ).astype(jnp.float32)
    ).astype(jnp.bfloat16)
    query_full = lax.dynamic_update_slice_in_dim(
        jnp.zeros((D,), jnp.float32),
        jnp.sum(grad_queries.astype(jnp.float32), axis=0),
        group * head_cols,
        0,
    )
    value_full = lax.dynamic_update_slice_in_dim(
        jnp.zeros((D,), jnp.float32),
        jnp.sum(grad_values.astype(jnp.float32), axis=0),
        group * head_cols,
        0,
    )
    up_full = lax.dynamic_update_slice_in_dim(
        jnp.zeros((FF,), jnp.float32),
        jnp.sum(grad_pre.astype(jnp.float32), axis=0),
        group * unit_cols,
        0,
    )
    tail_rows = jnp.stack(
        [
            jnp.sum(grad_one, axis=0),
            jnp.sum(grad_two, axis=0),
            jnp.sum(grad_norm * normal_one, axis=0),
            jnp.sum(grad_norm, axis=0),
            jnp.sum(grad_out * normal_two, axis=0),
            jnp.sum(grad_out, axis=0),
        ]
    )
    vector_terms = jnp.concatenate(
        [jnp.stack([query_full, value_full]), up_full.reshape(FF // D, D), tail_rows], axis=0
    )
    vector_grads = lax.psum(vector_terms, ("dp", "tensor"))
    grad_stack = jnp.concatenate([grad_w_mix, grad_w_out, grad_w_up, grad_w_down], axis=0)
    grad_pieces = grad_stack.reshape(slots.shape[0], -1, D)
    spread_slots = (
        jnp.zeros((lax.axis_size("dp") * CAP,) + grad_pieces.shape[1:], jnp.float32)
        .at[slots]
        .set(grad_pieces)
    )
    own_grads = lax.psum_scatter(
        spread_slots.astype(jnp.bfloat16), "dp", scatter_dimension=0, tiled=True
    ).astype(jnp.float32)
    slot_new, slot_first_new, slot_second_new = adam_update(
        master_slots[0], slot_first[0], slot_second[0], own_grads, rate_matrix, weight_decay
    )
    vector_new, vector_first_new, vector_second_new = adam_update(
        vectors, vector_first, vector_second, vector_grads, rate_vector, 0.0
    )
    return (
        layer_out,
        input_grad,
        slot_new[None],
        slot_first_new[None],
        slot_second_new[None],
        vector_new,
        vector_first_new,
        vector_second_new,
    )


DOC_MAX = 800
EXT_PAD = 512
ABLK = 256
HPG = 8
AUG = 16
neg_big = -1000000000.0
NN = (((1,), (0,)), ((), ()))
NT = (((1,), (1,)), ((), ()))
TN = (((0,), (0,)), ((), ()))


def mm(a, b, dims):
    return lax.dot_general(a, b, dims, preferred_element_type=jnp.float32)


def attn_fwd_kernel(lo_ref, hi_ref, q_ref, k_ref, v_ref, qaug_ref, kaug_ref, hid_ref, o_ref, lse_ref, kn_ref, m_ref, acc_ref):
    ext = q_ref.shape[1]
    ones = jnp.concatenate(
        [jnp.ones((1, ABLK), jnp.float32), jnp.zeros((AUG - 1, ABLK), jnp.float32)], axis=0
    ).astype(jnp.bfloat16)
    for h in range(HPG):
        rows = slice(h * HD, (h + 1) * HD)
        kn_ref[h] = jnp.concatenate([k_ref[rows, :], kaug_ref[...]], axis=0).T

    def query_block(qb, _):
        lo = lo_ref[qb]
        hi = hi_ref[qb]
        qs = pl.ds(pl.multiple_of(qb * ABLK, ABLK), ABLK)

        @pl.when(hi > lo)
        def _work():
            hidden = hid_ref[0:1, qs]
            for h in range(HPG):
                rows = slice(h * HD, (h + 1) * HD)
                q32 = q_ref[rows, qs].astype(jnp.float32)
                k32 = k_ref[rows, qs].astype(jnp.float32)
                own = jnp.sum(q32 * k32, axis=0, keepdims=True)
                m_ref[h] = jnp.where(hidden > 0.0, own, -1e30)
                acc_ref[h, 0:HD, :] = v_ref[rows, qs].astype(jnp.float32) * hidden
                acc_ref[h, HD:, :] = jnp.broadcast_to(hidden, (AUG, ABLK))

            def key_block(kb, _):
                ks = pl.ds(pl.multiple_of(kb * ABLK, ABLK), ABLK)
                heads = [slice(h * HD, (h + 1) * HD) for h in range(HPG)]
                scores = [
                    mm(kn_ref[h, ks, :], jnp.concatenate([q_ref[heads[h], qs], qaug_ref[:, qs]], axis=0), NN)
                    for h in range(HPG)
                ]
                olds = [m_ref[h] for h in range(HPG)]
                news = [
                    jnp.maximum(olds[h], jnp.max(scores[h], axis=0, keepdims=True)) for h in range(HPG)
                ]
                raised = [jnp.exp(scores[h] - news[h]).astype(jnp.bfloat16) for h in range(HPG)]
                for h in range(HPG):
                    m_ref[h] = news[h]
                    va = jnp.concatenate([v_ref[heads[h], ks], ones], axis=0)
                    acc_ref[h] = acc_ref[h] * jnp.exp(olds[h] - news[h]) + mm(va, raised[h], NN)
                return 0

            lax.fori_loop(lo, hi, key_block, 0)
            for h in range(HPG):
                rows = slice(h * HD, (h + 1) * HD)
                total = acc_ref[h, HD : HD + 1, :]
                o_ref[rows, qs] = (acc_ref[h, 0:HD, :] * (1.0 / total)).astype(jnp.bfloat16)
                lse_ref[0, h : h + 1, qs] = m_ref[h] + jnp.log(total)

        @pl.when(hi <= lo)
        def _skip():
            o_ref[:, qs] = jnp.zeros((HPG * HD, ABLK), jnp.bfloat16)
            lse_ref[0, :, qs] = jnp.zeros((8, ABLK), jnp.float32)

        return 0

    lax.fori_loop(0, ext // ABLK, query_block, 0)


def attn_bwd_kernel(
    lo_ref, hi_ref, q_ref, k_ref, v_ref, g_ref, c_ref, lse_ref, qaug_ref, kaug_ref, hid_ref,
    out_ref, kn_ref, vn_ref, acc_ref, dk_acc, dv_acc,
):
    ext = q_ref.shape[1]
    for h in range(HPG):
        rows = slice(h * HD, (h + 1) * HD)
        kn_ref[h] = jnp.concatenate([k_ref[rows, :], kaug_ref[...]], axis=0).T
        vn_ref[h] = v_ref[rows, :].T
    dk_acc[...] = jnp.zeros_like(dk_acc)
    dv_acc[...] = jnp.zeros_like(dv_acc)

    def query_block(qb, _):
        lo = lo_ref[qb]
        hi = hi_ref[qb]
        qs = pl.ds(pl.multiple_of(qb * ABLK, ABLK), ABLK)

        @pl.when(hi > lo)
        def _work():
            hidden = hid_ref[0:1, qs]
            deltas = []
            logs = []
            for h in range(HPG):
                rows = slice(h * HD, (h + 1) * HD)
                q32 = q_ref[rows, qs].astype(jnp.float32)
                k32 = k_ref[rows, qs].astype(jnp.float32)
                v32 = v_ref[rows, qs].astype(jnp.float32)
                g32 = g_ref[rows, qs].astype(jnp.float32)
                c32 = c_ref[rows, qs].astype(jnp.float32)
                delta = jnp.sum(g32 * c32, axis=0, keepdims=True)
                log = lse_ref[0, h : h + 1, qs]
                own = jnp.sum(q32 * k32, axis=0, keepdims=True)
                p_own = jnp.where(hidden > 0.0, jnp.exp(own - log), 0.0)
                d_own = p_own * (jnp.sum(g32 * v32, axis=0, keepdims=True) - delta)
                acc_ref[h] = d_own * k32
                dk_acc[rows, qs] += d_own * q32
                dv_acc[rows, qs] += p_own * g32
                deltas.append(delta)
                logs.append(log)

            def key_block(kb, _):
                ks = pl.ds(pl.multiple_of(kb * ABLK, ABLK), ABLK)
                heads = [slice(h * HD, (h + 1) * HD) for h in range(HPG)]
                every = range(HPG)
                qs_h = [q_ref[heads[h], qs] for h in every]
                gs_h = [g_ref[heads[h], qs] for h in every]
                scores = [
                    mm(kn_ref[h, ks, :], jnp.concatenate([qs_h[h], qaug_ref[:, qs]], axis=0), NN)
                    for h in every
                ]
                grads = [mm(vn_ref[h, ks, :], gs_h[h], NN) for h in every]
                weights = [jnp.exp(scores[h] - logs[h]) for h in every]
                low = [weights[h].astype(jnp.bfloat16) for h in every]
                back = [
                    (weights[h] * (grads[h] - deltas[h])).astype(jnp.bfloat16) for h in every
                ]
                v_new = [mm(gs_h[h], low[h], NT) for h in every]
                k_new = [mm(qs_h[h], back[h], NT) for h in every]
                q_new = [mm(k_ref[heads[h], ks], back[h], NN) for h in every]
                for h in every:
                    dv_acc[heads[h], ks] += v_new[h]
                    dk_acc[heads[h], ks] += k_new[h]
                    acc_ref[h] += q_new[h]
                return 0

            lax.fori_loop(lo, hi, key_block, 0)
            for h in range(HPG):
                rows = slice(h * HD, (h + 1) * HD)
                out_ref[0, rows, qs] = acc_ref[h].astype(jnp.bfloat16) * (HD ** (-0.5))

        @pl.when(hi <= lo)
        def _skip():
            out_ref[0, :, qs] = jnp.zeros((HPG * HD, ABLK), jnp.bfloat16)

        return 0

    lax.fori_loop(0, ext // ABLK, query_block, 0)
    out_ref[1] = dk_acc[...].astype(jnp.bfloat16)
    out_ref[2] = dv_acc[...].astype(jnp.bfloat16)


def group_block(offset, rows, ext):
    return pl.BlockSpec((rows, ext), lambda g, lo, hi: (offset + g, 0))


def fixed_block(rows, ext):
    return pl.BlockSpec((rows, ext), lambda g, lo, hi: (0, 0))


def attend(lo, hi, qkv, qaug, kaug, hidden):
    ext = qkv.shape[1]
    groups = D // HD // HPG
    rows = HPG * HD
    return pl.pallas_call(
        attn_fwd_kernel,
        out_shape=(
            jax.ShapeDtypeStruct((D, ext), jnp.bfloat16),
            jax.ShapeDtypeStruct((groups, 8, ext), jnp.float32),
        ),
        grid_spec=pltpu.PrefetchScalarGridSpec(
            num_scalar_prefetch=2,
            grid=(groups,),
            in_specs=[
                group_block(0, rows, ext),
                group_block(groups, rows, ext),
                group_block(2 * groups, rows, ext),
                fixed_block(AUG, ext),
                fixed_block(AUG, ext),
                fixed_block(8, ext),
            ],
            out_specs=[
                group_block(0, rows, ext),
                pl.BlockSpec((1, 8, ext), lambda g, lo, hi: (g, 0, 0)),
            ],
            scratch_shapes=[
                pltpu.VMEM((HPG, ext, HD + AUG), jnp.bfloat16),
                pltpu.VMEM((HPG, 1, ABLK), jnp.float32),
                pltpu.VMEM((HPG, HD + AUG, ABLK), jnp.float32),
            ],
        ),
        compiler_params=pltpu.CompilerParams(vmem_limit_bytes=40 * 2**20),
        cost_estimate=pl.CostEstimate(flops=20 * 10**9, bytes_accessed=14 * 10**6, transcendentals=0),
        name="attend",
    )(lo, hi, qkv, qkv, qkv, qaug, kaug, hidden)


def attend_back(lo, hi, qkv, grads, context, logs, qaug, kaug, hidden):
    ext = qkv.shape[1]
    groups = D // HD // HPG
    rows = HPG * HD
    return pl.pallas_call(
        attn_bwd_kernel,
        out_shape=jax.ShapeDtypeStruct((3, D, ext), jnp.bfloat16),
        grid_spec=pltpu.PrefetchScalarGridSpec(
            num_scalar_prefetch=2,
            grid=(groups,),
            in_specs=[
                group_block(0, rows, ext),
                group_block(groups, rows, ext),
                group_block(2 * groups, rows, ext),
                group_block(0, rows, ext),
                group_block(0, rows, ext),
                pl.BlockSpec((1, 8, ext), lambda g, lo, hi: (g, 0, 0)),
                fixed_block(AUG, ext),
                fixed_block(AUG, ext),
                fixed_block(8, ext),
            ],
            out_specs=pl.BlockSpec((3, rows, ext), lambda g, lo, hi: (0, g, 0)),
            scratch_shapes=[
                pltpu.VMEM((HPG, ext, HD + AUG), jnp.bfloat16),
                pltpu.VMEM((HPG, ext, HD), jnp.bfloat16),
                pltpu.VMEM((HPG, HD, ABLK), jnp.float32),
                pltpu.VMEM((rows, ext), jnp.float32),
                pltpu.VMEM((rows, ext), jnp.float32),
            ],
        ),
        compiler_params=pltpu.CompilerParams(vmem_limit_bytes=48 * 2**20),
        cost_estimate=pl.CostEstimate(flops=50 * 10**9, bytes_accessed=30 * 10**6, transcendentals=0),
        name="attend_back",
    )(lo, hi, qkv, qkv, qkv, grads, context, logs, qaug, kaug, hidden)


def document_plan(segment, valid, half, rows):
    length = segment.shape[0]
    ext = rows + EXT_PAD
    base = half * EXT_PAD
    position = jnp.arange(length, dtype=jnp.int32)
    documents = jnp.arange(8, dtype=jnp.int32)[:, None]
    one_hot = segment[None, :] == documents
    counts = jnp.sum(one_hot.astype(jnp.int32), axis=1, keepdims=True)
    starts = jnp.sum((segment[None, :] < documents).astype(jnp.int32), axis=1, keepdims=True)
    start = jnp.sum(jnp.where(one_hot, starts, 0), axis=0)
    end = jnp.sum(jnp.where(one_hot, starts + counts, 0), axis=0)
    crossing = (start < rows) & (end > rows)
    left = jnp.max(jnp.where(crossing, rows - start, 0))
    right = jnp.max(jnp.where(crossing, end - rows, 0))
    worker = jnp.where(left <= right, half == 1, half == 0)
    own = (position >= half * rows) & (position < (half + 1) * rows)
    handled = jnp.where(crossing, worker, own)
    cut = lambda values: lax.dynamic_slice_in_dim(values, base, ext, 0)
    handled_ext = cut(handled)
    begins = jnp.where(handled_ext, cut(start) - base, ext).reshape(-1, ABLK)
    ends = jnp.where(handled_ext, cut(end) - base, 0).reshape(-1, ABLK)
    lo = jnp.min(begins, axis=1) // ABLK
    hi = (jnp.max(ends, axis=1) + (ABLK - 1)) // ABLK
    blank = jnp.max(ends, axis=1) == 0
    lo = jnp.where(blank, 0, lo)
    hi = jnp.where(blank, 0, hi)
    hot = cut(one_hot.T).T
    masked = cut(valid) == 0
    ones = jnp.ones((1, ext), jnp.bfloat16)
    fill = jnp.zeros((AUG - 9, ext), jnp.bfloat16)
    qaug = jnp.concatenate([hot.astype(jnp.bfloat16), ones, fill], axis=0)
    kaug = jnp.concatenate(
        [
            jnp.where(hot, 0.0, neg_big).astype(jnp.bfloat16),
            jnp.where(masked[None, :], neg_big, 0.0).astype(jnp.bfloat16),
            fill,
        ],
        axis=0,
    )
    hidden = jnp.broadcast_to(masked.astype(jnp.float32)[None, :], (8, ext))
    foreign = lax.dynamic_slice_in_dim(crossing & ~worker, half * rows, rows, 0)
    return lo, hi, qaug, kaug, hidden, handled_ext, foreign


def normal_parts(values):
    bell = jnp.exp(values * values * -0.5)
    return (0.5 + 0.5 * lax.erf(values * 0.7071067811865476), bell * 0.3989422804014327)


UNITS = 1024
STRIP = 512


def up_kernel(x_ref, w_ref, bias_ref, gelu_ref, slope_ref):
    for r in range(0, x_ref.shape[0], STRIP):
        strip = slice(r, r + STRIP)
        values = mm(x_ref[strip, :], w_ref[...], NT) + bias_ref[...]
        cdf, bell = normal_parts(values)
        gelu_ref[strip, :] = (values * cdf).astype(jnp.bfloat16)
        slope_ref[strip, :] = (cdf + values * bell).astype(jnp.bfloat16)


def feed_up(rows, weights, bias):
    length = rows.shape[0]
    units = weights.shape[0]
    out = jax.ShapeDtypeStruct((length, units), jnp.bfloat16)
    columns = pl.BlockSpec((length, UNITS), lambda n: (0, n))
    return pl.pallas_call(
        up_kernel,
        out_shape=(out, out),
        grid=(units // UNITS,),
        in_specs=[
            pl.BlockSpec((length, D), lambda n: (0, 0)),
            pl.BlockSpec((UNITS, D), lambda n: (n, 0)),
            pl.BlockSpec((1, UNITS), lambda n: (0, n)),
        ],
        out_specs=(columns, columns),
        compiler_params=pltpu.CompilerParams(vmem_limit_bytes=40 * 2**20),
        cost_estimate=pl.CostEstimate(
            flops=2 * length * units * D, bytes_accessed=26 * 10**6, transcendentals=0
        ),
        name="feed_up",
    )(rows, weights, bias.reshape(1, units))


def down_back_kernel(g_ref, w_ref, slope_ref, out_ref, sum_ref):
    total = jnp.zeros((1, UNITS), jnp.float32)
    for r in range(0, g_ref.shape[0], STRIP):
        strip = slice(r, r + STRIP)
        grads = mm(g_ref[strip, :], w_ref[...], NT) * slope_ref[strip, :].astype(jnp.float32)
        low = grads.astype(jnp.bfloat16)
        out_ref[strip, :] = low
        total += jnp.sum(low.astype(jnp.float32), axis=0, keepdims=True)
    sum_ref[...] = total


def feed_down_back(grads, weights, slope):
    length = grads.shape[0]
    units = weights.shape[0]
    columns = pl.BlockSpec((length, UNITS), lambda n: (0, n))
    one_row = pl.BlockSpec((1, UNITS), lambda n: (0, n))
    return pl.pallas_call(
        down_back_kernel,
        out_shape=(
            jax.ShapeDtypeStruct((length, units), jnp.bfloat16),
            jax.ShapeDtypeStruct((1, units), jnp.float32),
        ),
        grid=(units // UNITS,),
        in_specs=[
            pl.BlockSpec((length, D), lambda n: (0, 0)),
            pl.BlockSpec((UNITS, D), lambda n: (n, 0)),
            columns,
        ],
        out_specs=(columns, one_row),
        compiler_params=pltpu.CompilerParams(vmem_limit_bytes=40 * 2**20),
        cost_estimate=pl.CostEstimate(
            flops=2 * length * units * D, bytes_accessed=26 * 10**6, transcendentals=0
        ),
        name="feed_down_back",
    )(grads, weights, slope)


MESH = pl.DeviceIdType.MESH
CHUNKS = 3


def neighbours(z, y, core, x):
    def at(z, y, core, x):
        return {"dp": (z * 2 + y) * 2 + core, "tensor": x}

    return {
        "x": at(z, y, core, 1 - x),
        "y": at(z, 1 - y, core, x),
        "core": at(z, y, 1 - core, x),
        "up": at(jnp.minimum(z + 1, 3), y, core, x),
        "down": at(jnp.maximum(z - 1, 0), y, core, x),
    }


def greet(near, z):
    barrier = pltpu.get_barrier_semaphore()
    for name in ("x", "y", "core"):
        pl.semaphore_signal(barrier, inc=1, device_id=near[name], device_id_type=MESH)

    @pl.when(z < 3)
    def _up():
        pl.semaphore_signal(barrier, inc=1, device_id=near["up"], device_id_type=MESH)

    @pl.when(z > 0)
    def _down():
        pl.semaphore_signal(barrier, inc=1, device_id=near["down"], device_id_type=MESH)

    at_end = jnp.where((z == 0) | (z == 3), 1, 0)
    pl.semaphore_wait(barrier, 5 - at_end)


def greet_all(near, me, n_dp):
    barrier = pltpu.get_barrier_semaphore()
    pl.semaphore_signal(barrier, inc=1, device_id=near["x"], device_id_type=MESH)

    def one(i, _):
        other = {"dp": lax.rem(me + i, n_dp), "tensor": lax.axis_index("tensor")}
        pl.semaphore_signal(barrier, inc=1, device_id=other, device_id_type=MESH)
        return 0

    lax.fori_loop(1, n_dp, one, 0)
    pl.semaphore_wait(barrier, n_dp)


def gather_kernel(
    slots_ref, low_ref, mix_ref, up_ref, down_ref,
    spread_ref, dense_ref, local_sem, own_sem, post, mail, send, recv,
):
    z, y, core, x = coordinates()
    near = neighbours(z, y, core, x)
    width = D // 2
    outs = (mix_ref, up_ref, down_ref)
    me = lax.axis_index("dp")
    n_dp = low_ref.shape[0]
    greet_all(near, me, n_dp)

    def letter(to):
        return pltpu.make_async_remote_copy(
            src_ref=low_ref.at[to],
            dst_ref=spread_ref.at[pl.ds(me * CAP, CAP)],
            send_sem=post.at[to],
            recv_sem=mail.at[me],
            device_id={"dp": to, "tensor": x},
            device_id_type=MESH,
        )

    def answer(of):
        return pltpu.make_async_remote_copy(
            src_ref=low_ref.at[of],
            dst_ref=spread_ref.at[pl.ds(of * CAP, CAP)],
            send_sem=post.at[of],
            recv_sem=mail.at[of],
            device_id={"dp": of, "tensor": x},
            device_id_type=MESH,
        )

    def peer(i):
        return lax.rem(me + i, n_dp)

    def post_one(i, _):
        letter(peer(i)).start()
        return 0

    lax.fori_loop(1, n_dp, post_one, 0)
    mine = pltpu.make_async_copy(low_ref.at[me], spread_ref.at[pl.ds(me * CAP, CAP)], local_sem)
    mine.start()
    mine.wait()

    def mail_one(i, _):
        answer(peer(i)).wait_recv()
        letter(peer(i)).wait_send()
        return 0

    lax.fori_loop(1, n_dp, mail_one, 0)

    def place(p, _):
        dense_ref[p // 16, (p // 4) % 4, p % 4] = spread_ref[slots_ref[p]]
        return 0

    lax.fori_loop(0, slots_ref.shape[0], place, 0)

    def block(k, t, zz, yy, cc, part=None):
        groups = slice(None) if part is None else pl.ds(2 * part, 2)
        return outs[k].at[
            groups,
            t,
            :,
            pl.ds(pl.multiple_of((zz * 2 + yy) * 16, 16), 16),
            pl.ds(pl.multiple_of(cc * width, width), width),
        ]

    own = [
        pltpu.make_async_copy(dense_ref.at[k], block(k, x, z, y, core), own_sem.at[k])
        for k in range(CHUNKS)
    ]
    for one in own:
        one.start()

    def copy(kind, link, k, zz, t, yy, cc, part=None, fresh=False):
        view = block(k, t, zz, yy, cc, part)
        return pltpu.make_async_remote_copy(
            src_ref=dense_ref.at[k] if fresh else view,
            dst_ref=view,
            send_sem=send.at[kind, k, zz],
            recv_sem=recv.at[kind, k, zz],
            device_id=near[link],
            device_id_type=MESH,
        )

    def up(k, zz, fresh=False):
        return copy(0, "up", k, zz, x, y, core, fresh=fresh)

    def down(k, zz, fresh=False):
        return copy(1, "down", k, zz, x, y, core, fresh=fresh)

    def spread(k, zz, fresh):
        copy(2, "x", k, zz, x, y, core, fresh=fresh).start()
        copy(3, "y", k, zz, x, y, core, fresh=fresh).start()
        copy(4, "core", k, zz, x, y, core, fresh=fresh).start()

    def each(d, body):
        @pl.when((d > 0) & (z - d >= 0))
        def _below():
            for k in range(CHUNKS):
                body(k, z - d, 0)

        @pl.when((d > 0) & (z + d <= 3))
        def _above():
            for k in range(CHUNKS):
                body(k, z + d, 1)

    def each_or_own(d, body):
        each(d, body)

        @pl.when(d == 0)
        def _own():
            for k in range(CHUNKS):
                body(k, z, None)

    def begin(k):
        @pl.when(z < 3)
        def _up():
            up(k, z, True).start()

        @pl.when(z > 0)
        def _down():
            down(k, z, True).start()

        spread(k, z, True)

    def first(k, zz, side):
        if side == 0:
            up(k, zz).wait_recv()

            @pl.when(z < 3)
            def _up():
                up(k, zz).start()

        else:
            down(k, zz).wait_recv()

            @pl.when(z > 0)
            def _on():
                down(k, zz).start()

        spread(k, zz, False)

    def second(k, zz, side):
        copy(2, "x", k, zz, 1 - x, y, core).wait_recv()
        copy(5, "y", k, zz, 1 - x, y, core, 0).start()
        copy(7, "core", k, zz, 1 - x, y, core).start()
        copy(3, "y", k, zz, x, 1 - y, core).wait_recv()
        copy(6, "x", k, zz, x, 1 - y, core, 1).start()
        copy(8, "core", k, zz, x, 1 - y, core).start()

    def third(k, zz, side):
        copy(5, "y", k, zz, 1 - x, 1 - y, core, 0).wait_recv()
        copy(9, "core", k, zz, 1 - x, 1 - y, core, 0).start()
        copy(6, "x", k, zz, 1 - x, 1 - y, core, 1).wait_recv()
        copy(10, "core", k, zz, 1 - x, 1 - y, core, 1).start()

    def finish(k, zz, side):
        if side != 1:

            @pl.when(z < 3)
            def _up():
                up(k, zz).wait_send()

        if side != 0:

            @pl.when(z > 0)
            def _down():
                down(k, zz).wait_send()

        copy(2, "x", k, zz, x, y, core).wait_send()
        copy(3, "y", k, zz, x, y, core).wait_send()
        copy(5, "y", k, zz, 1 - x, y, core, 0).wait_send()
        copy(6, "x", k, zz, x, 1 - y, core, 1).wait_send()
        copy(4, "core", k, zz, x, y, core).wait_send()
        copy(7, "core", k, zz, 1 - x, y, core).wait_send()
        copy(8, "core", k, zz, x, 1 - y, core).wait_send()
        copy(9, "core", k, zz, 1 - x, 1 - y, core, 0).wait_send()
        copy(10, "core", k, zz, 1 - x, 1 - y, core, 1).wait_send()
        copy(4, "core", k, zz, x, y, 1 - core).wait_recv()
        copy(7, "core", k, zz, 1 - x, y, 1 - core).wait_recv()
        copy(8, "core", k, zz, x, 1 - y, 1 - core).wait_recv()
        copy(9, "core", k, zz, 1 - x, 1 - y, 1 - core, 0).wait_recv()
        copy(10, "core", k, zz, 1 - x, 1 - y, 1 - core, 1).wait_recv()

    for k in range(CHUNKS):
        begin(k)

    def step(d, _):
        @pl.when(d < 4)
        def _one():
            each(d, first)

        @pl.when((d >= 1) & (d < 5))
        def _two():
            each_or_own(d - 1, second)

        @pl.when(d >= 2)
        def _three():
            each_or_own(d - 2, third)

        return 0

    lax.fori_loop(1, 6, step, 0)

    def end(d, _):
        each_or_own(d, finish)
        return 0

    lax.fori_loop(0, 4, end, 0)
    for one in own:
        one.wait()


def gather_weights(slots, low):
    n_dp = low.shape[0]
    stack = jax.ShapeDtypeStruct((4, 2, 4, 128, D), low.dtype)
    return pl.pallas_call(
        gather_kernel,
        out_shape=(stack,) * 3,
        in_specs=[
            pl.BlockSpec(memory_space=pltpu.SMEM),
            pl.BlockSpec(memory_space=pl.ANY),
        ],
        out_specs=(pl.BlockSpec(memory_space=pl.ANY),) * 3,
        scratch_shapes=[
            pltpu.VMEM((n_dp * CAP, 16, D // 2), low.dtype),
            pltpu.VMEM((CHUNKS, 4, 4, 16, D // 2), low.dtype),
            pltpu.SemaphoreType.DMA,
            pltpu.SemaphoreType.DMA((CHUNKS,)),
            pltpu.SemaphoreType.DMA((n_dp,)),
            pltpu.SemaphoreType.DMA((n_dp,)),
            pltpu.SemaphoreType.DMA((11, CHUNKS, 4)),
            pltpu.SemaphoreType.DMA((11, CHUNKS, 4)),
        ],
        compiler_params=pltpu.CompilerParams(
            collective_id=1, has_side_effects=True, vmem_limit_bytes=32 * 2**20
        ),
        cost_estimate=pl.CostEstimate(flops=0, bytes_accessed=50 * 10**6, transcendentals=0),
        name="gather_weights",
    )(slots, low)


BLOCKS = 12


def reduce_kernel(
    piece_ref, vec_ref, qkv_ref, ctx_ref, pre_ref, hid_ref, tok_ref, gext_ref, norm_ref, two_ref,
    out_ref, sum_ref,
    tile, tall, ext_rhs, row_rhs, far_buf, near_buf, core_in, x_in, y_in, x2_in, y2_in, line, up_in, down_in,
    done, parcel, vec_in, vec_out,
    tile_sem, rhs_sem, local_sem, post, mail, send, recv, vec_send, vec_recv,
):
    z, y, core, x = coordinates()
    near = neighbours(z, y, core, x)
    me = lax.axis_index("dp")
    n_dp = parcel.shape[0]
    width = D // 2
    rows = tile.shape[1]
    tiles = 1024 // rows

    def right(n, half):
        ref = (tok_ref, gext_ref, norm_ref, two_ref)[n]
        to = ext_rhs.at[n, half] if n < 2 else row_rhs.at[n - 2, half]
        which = 1 - core if half == 0 else core
        columns = pl.ds(pl.multiple_of(which * width, width), width)
        return pltpu.make_async_copy(ref.at[:, columns], to, rhs_sem.at[n, half])

    for n in range(4):
        for half in range(2):
            right(n, half).start()

    def fetch(n, body):
        i = n // tiles
        part = pl.ds(pl.multiple_of(lax.rem(n, tiles) * rows, rows), rows)
        slot = lax.rem(n, 2)
        ext = ext_rhs.shape[2]
        wide = tile.at[slot, :, pl.ds(0, ext)]
        sem = tile_sem.at[slot]

        @pl.when(i < 3)
        def _qkv():
            body(pltpu.make_async_copy(qkv_ref.at[i, part, :], wide, sem))

        @pl.when(i == 3)
        def _out():
            body(pltpu.make_async_copy(ctx_ref.at[part, :], wide, sem))

        def columns(first):
            start = (i - first) * 1024 + lax.rem(n, tiles) * rows
            return pl.ds(pl.multiple_of(start, rows), rows)

        @pl.when((i >= 4) & (i < 8))
        def _up():
            body(pltpu.make_async_copy(pre_ref.at[:, columns(4)], tall.at[slot], sem))

        @pl.when(i >= 8)
        def _down():
            body(pltpu.make_async_copy(hid_ref.at[:, columns(8)], tall.at[slot], sem))

    fetch(0, lambda copy: copy.start())
    greet_all(near, me, n_dp)

    def remote(kind, i, link, src, dst):
        return pltpu.make_async_remote_copy(
            src_ref=src,
            dst_ref=dst,
            send_sem=send.at[kind, i],
            recv_sem=recv.at[kind, i],
            device_id=near[link],
            device_id_type=MESH,
        )

    def core_copy(i):
        return remote(0, i, "core", far_buf.at[lax.rem(i, 2)], core_in.at[i])

    def x1(i):
        return remote(1, i, "x", core_in.at[i, 1 - x, pl.ds(0, 2)], x_in.at[i])

    def y1(i):
        return remote(2, i, "y", core_in.at[i, :, pl.ds(2, 2), :, 1 - y], y_in.at[i])

    def y2(i):
        return remote(3, i, "y", x_in.at[i, :, :, 1 - y], y2_in.at[i])

    def x2(i):
        return remote(4, i, "x", y_in.at[i, 1 - x], x2_in.at[i])

    def up(i, zz):
        return remote(4 + zz, i, "up", up_in.at[i, zz], up_in.at[i, zz])

    def down(i, zz):
        return remote(8 + zz, i, "down", down_in.at[i, zz], down_in.at[i, zz])

    def produce(i):
        ring = lax.rem(i, 2)

        for n, first in enumerate((0, 3, 4, 8)):

            @pl.when(i == first)
            def _ready():
                right(n, 0).wait()
                right(n, 1).wait()

        @pl.when(i >= 2)
        def _free():
            core_copy(i - 2).wait_send()

        def one(part, _):
            n = i * tiles + part
            slot = lax.rem(n, 2)

            @pl.when(n + 1 < BLOCKS * tiles)
            def _next():
                fetch(n + 1, lambda copy: copy.start())

            fetch(n, lambda copy: copy.wait())
            t, p = part // 2, lax.rem(part, 2) * 2

            def put(value, to):
                to[ring, t, pl.ds(p, 2)] = value.astype(jnp.bfloat16).reshape(2, 4, 2, 16, width)

            @pl.when(i < 4)
            def _wide():
                which = jnp.where(i < 3, 0, 1)
                put(mm(tile[slot], ext_rhs[which, 0], NN), far_buf)
                put(mm(tile[slot], ext_rhs[which, 1], NN), near_buf)

            @pl.when(i >= 4)
            def _tall():
                which = jnp.where(i < 8, 0, 1)
                put(mm(tall[slot], row_rhs[which, 0], TN), far_buf)
                put(mm(tall[slot], row_rhs[which, 1], TN), near_buf)

            return 0

        lax.fori_loop(0, tiles, one, 0)
        core_copy(i).start()

    def stage_one(i):
        core_copy(i).wait_recv()
        ring = lax.rem(i, 2)

        def add(j, _):
            t, p = j // 4, j % 4
            core_in[i, t, p] = core_in[i, t, p] + near_buf[ring, t, p]
            return 0

        lax.fori_loop(0, 8, add, 0)
        x1(i).start()
        y1(i).start()

    def stage_two(i):
        x1(i).wait_recv()
        y1(i).wait_recv()
        for p in range(2):
            x_in[i, p] = x_in[i, p] + core_in[i, x, p]
        for t in range(2):
            for p in range(2):
                y_in[i, t, p] = y_in[i, t, p] + core_in[i, t, 2 + p, :, y]
        y2(i).start()
        x2(i).start()

    def stage_three(i):
        y2(i).wait_recv()
        x2(i).wait_recv()
        for p in range(2):
            line[i, :, p] = x_in[i, p, :, y] + y2_in[i, p]
            line[i, :, 2 + p] = y_in[i, x, p] + x2_in[i, p]

    def stage_up(i):
        for zz in range(1, 4):

            @pl.when((z > 0) & (zz >= z))
            def _arrived():
                up(i, zz).wait_recv()

            @pl.when((z > 0) & (zz > z))
            def _add():
                up_in[i, zz] = up_in[i, zz] + line[i, zz]

            @pl.when(z == 0)
            def _first():
                up_in[i, zz] = line[i, zz]

            @pl.when(zz > z)
            def _on():
                up(i, zz).start()

    def stage_down(i):
        for zz in range(3):

            @pl.when((z < 3) & (zz <= z))
            def _arrived():
                down(i, zz).wait_recv()

            @pl.when((z < 3) & (zz < z))
            def _add():
                down_in[i, zz] = down_in[i, zz] + line[i, zz]

            @pl.when(z == 3)
            def _first():
                down_in[i, zz] = line[i, zz]

            @pl.when(zz < z)
            def _on():
                down(i, zz).start()

    def stage_last(i):
        mine = pl.ds(i * 4, 4)

        @pl.when(z == 0)
        def _bottom():
            done[mine] = line[i, 0] + down_in[i, 0]

        @pl.when((z > 0) & (z < 3))
        def _middle():
            total = line[i, z].astype(jnp.float32) + up_in[i, z].astype(jnp.float32)
            done[mine] = (total + down_in[i, z].astype(jnp.float32)).astype(jnp.bfloat16)

        @pl.when(z == 3)
        def _top():
            done[mine] = line[i, 3] + up_in[i, 3]

    def ended(i):
        @pl.when(i >= BLOCKS - 2)
        def _far():
            core_copy(i).wait_send()

        x1(i).wait_send()
        y1(i).wait_send()
        y2(i).wait_send()
        x2(i).wait_send()
        for zz in range(1, 4):

            @pl.when(zz > z)
            def _up():
                up(i, zz).wait_send()

        for zz in range(3):

            @pl.when(zz < z)
            def _down():
                down(i, zz).wait_send()

    z_one = z + 1 - 2 * lax.rem(z, 2)
    z_two = lax.rem(z + 2, 4)
    partners = [
        near["core"],
        near["y"],
        near["x"],
        {"dp": (z_one * 2 + y) * 2 + core, "tensor": x},
        {"dp": (z_two * 2 + y) * 2 + core, "tensor": x},
    ]

    def swap(n):
        return pltpu.make_async_remote_copy(
            src_ref=vec_out.at[n],
            dst_ref=vec_in.at[n],
            send_sem=vec_send.at[n],
            recv_sem=vec_recv.at[n],
            device_id=partners[n],
            device_id_type=MESH,
        )

    vec_out[0] = vec_ref[...]
    produce(0)

    def step(s, _):
        @pl.when(s + 1 < BLOCKS)
        def _produce():
            produce(s + 1)

        @pl.when(s < BLOCKS)
        def _one():
            stage_one(s)

        @pl.when((s >= 1) & (s < BLOCKS + 1))
        def _two():
            stage_two(s - 1)

        @pl.when((s >= 2) & (s < BLOCKS + 2))
        def _three():
            stage_three(s - 2)

        @pl.when((s - 3 - z >= 0) & (s - 3 - z < BLOCKS))
        def _up():
            stage_up(s - 3 - z)

        @pl.when((s - 6 + z >= 0) & (s - 6 + z < BLOCKS))
        def _down():
            stage_down(s - 6 + z)

        @pl.when(s >= 7)
        def _last():
            stage_last(s - 7)

        for n in range(5):

            @pl.when(s == n)
            def _begin():
                swap(n).start()

            @pl.when(s == n + 1)
            def _end():
                swap(n).wait()
                if n < 4:
                    vec_out[n + 1] = vec_out[n] + vec_in[n]
                else:
                    sum_ref[...] = vec_out[n] + vec_in[n]

        return 0

    lax.fori_loop(0, BLOCKS + 7, step, 0)

    def finish(i, _):
        ended(i)
        return 0

    lax.fori_loop(0, BLOCKS, finish, 0)

    done[BLOCKS * 4] = jnp.zeros((16, width), done.dtype)

    def pack(n, _):
        parcel[n // CAP, n % CAP] = done[piece_ref[n]]
        return 0

    lax.fori_loop(0, n_dp * CAP, pack, 0)

    def place(of):
        return out_ref.at[
            :,
            pl.ds(pl.multiple_of((of // 2) * 16, 16), 16),
            pl.ds(pl.multiple_of((of % 2) * width, width), width),
        ]

    def letter(to):
        return pltpu.make_async_remote_copy(
            src_ref=parcel.at[to],
            dst_ref=place(me),
            send_sem=post.at[to],
            recv_sem=mail.at[me],
            device_id={"dp": to, "tensor": x},
            device_id_type=MESH,
        )

    def answer(of):
        return pltpu.make_async_remote_copy(
            src_ref=parcel.at[of],
            dst_ref=place(of),
            send_sem=post.at[of],
            recv_sem=mail.at[of],
            device_id={"dp": of, "tensor": x},
            device_id_type=MESH,
        )

    def post_one(i, _):
        letter(lax.rem(me + i, n_dp)).start()
        return 0

    lax.fori_loop(1, n_dp, post_one, 0)
    own = pltpu.make_async_copy(parcel.at[me], place(me), local_sem)
    own.start()

    def mail_one(i, _):
        answer(lax.rem(me + i, n_dp)).wait_recv()
        letter(lax.rem(me + i, n_dp)).wait_send()
        return 0

    lax.fori_loop(1, n_dp, mail_one, 0)
    own.wait()


def reduce_grads(piece_of, vec, qkv, context, pre, hidden, tokens, ext_grads, normed, two):
    n_dp = piece_of.shape[0] // CAP
    low = jnp.bfloat16
    width = D // 2
    rows = 256
    ext = tokens.shape[0]
    length = normed.shape[0]
    anywhere = pl.BlockSpec(memory_space=pl.ANY)
    vmem = pl.BlockSpec(memory_space=pltpu.VMEM)
    return pl.pallas_call(
        reduce_kernel,
        out_shape=(
            jax.ShapeDtypeStruct((CAP, 128, D), low),
            jax.ShapeDtypeStruct(vec.shape, jnp.float32),
        ),
        in_specs=[pl.BlockSpec(memory_space=pltpu.SMEM), vmem] + [anywhere] * 8,
        out_specs=(anywhere, vmem),
        scratch_shapes=[
            pltpu.VMEM((2, rows, ext), low),
            pltpu.VMEM((2, length, rows), low),
            pltpu.VMEM((2, 2, ext, width), low),
            pltpu.VMEM((2, 2, length, width), low),
            pltpu.VMEM((2, 2, 4, 4, 2, 16, width), low),
            pltpu.VMEM((2, 2, 4, 4, 2, 16, width), low),
            pltpu.VMEM((BLOCKS, 2, 4, 4, 2, 16, width), low),
            pltpu.VMEM((BLOCKS, 2, 4, 2, 16, width), low),
            pltpu.VMEM((BLOCKS, 2, 2, 4, 16, width), low),
            pltpu.VMEM((BLOCKS, 2, 4, 16, width), low),
            pltpu.VMEM((BLOCKS, 2, 4, 16, width), low),
            pltpu.VMEM((BLOCKS, 4, 4, 16, width), low),
            pltpu.VMEM((BLOCKS, 4, 4, 16, width), low),
            pltpu.VMEM((BLOCKS, 4, 4, 16, width), low),
            pltpu.VMEM((BLOCKS * 4 + 1, 16, width), low),
            pltpu.VMEM((n_dp, CAP, 16, width), low),
            pltpu.VMEM((5,) + vec.shape, jnp.float32),
            pltpu.VMEM((5,) + vec.shape, jnp.float32),
            pltpu.SemaphoreType.DMA((2,)),
            pltpu.SemaphoreType.DMA((4, 2)),
            pltpu.SemaphoreType.DMA,
            pltpu.SemaphoreType.DMA((n_dp,)),
            pltpu.SemaphoreType.DMA((n_dp,)),
            pltpu.SemaphoreType.DMA((11, BLOCKS)),
            pltpu.SemaphoreType.DMA((11, BLOCKS)),
            pltpu.SemaphoreType.DMA((5,)),
            pltpu.SemaphoreType.DMA((5,)),
        ],
        compiler_params=pltpu.CompilerParams(
            collective_id=2, has_side_effects=True, vmem_limit_bytes=60 * 2**20
        ),
        cost_estimate=pl.CostEstimate(
            flops=31 * 10**9, bytes_accessed=50 * 10**6, transcendentals=0
        ),
        name="reduce_grads",
    )(piece_of, vec, qkv, context, pre, hidden, tokens, ext_grads, normed, two)


def coordinates():
    dp = lax.axis_index("dp")
    return dp // 4, (dp // 2) % 2, dp % 2, lax.axis_index("tensor")


def exchange(values, axis):
    if axis == "x":
        return lax.ppermute(values, "tensor", [(0, 1), (1, 0)])
    flip = {"core": 1, "y": 2, "z_near": 4, "z_far": 8}[axis]
    return lax.ppermute(values, "dp", [(i, i ^ flip) for i in range(lax.axis_size("dp"))])


def pick(values, index, axis):
    return lax.dynamic_index_in_dim(values, index, axis, keepdims=False)


def on_device_rows(
    tokens,
    segment_ids,
    key_mask,
    owners,
    master_slots,
    slot_first,
    slot_second,
    vectors,
    vector_first,
    vector_second,
    out_grad,
):
    n_dp = lax.axis_size("dp")
    n_tensor = lax.axis_size("tensor")
    half = lax.axis_index("tensor")
    every = ("tensor", "dp")
    rows = tokens.shape[0]
    ext = rows + EXT_PAD
    halo = DOC_MAX // 2
    swap = [(0, 1), (1, 0)]
    edge = jnp.where(half == 0, rows - halo, 0)
    halo_at = jnp.where(half == 0, rows, EXT_PAD - halo)
    own_at = half * EXT_PAD

    def extend(own_rows, halo_rows):
        whole = jnp.zeros((ext,) + own_rows.shape[1:], own_rows.dtype)
        whole = lax.dynamic_update_slice_in_dim(whole, halo_rows, halo_at, 0)
        return lax.dynamic_update_slice_in_dim(whole, own_rows, own_at, 0)

    def own_part(values):
        return lax.dynamic_slice_in_dim(values, own_at, rows, 0)

    def halo_part(values):
        return lax.dynamic_slice_in_dim(values, halo_at, halo, 0)

    lo, hi, qaug, kaug, hidden_keys, handled, foreign = document_plan(
        segment_ids[0], key_mask[0], half, rows
    )
    halo_tokens = lax.ppermute(lax.dynamic_slice_in_dim(tokens, edge, halo, 0), "tensor", swap)
    tokens_ext = extend(tokens, halo_tokens)

    slots = slot_index(owners)
    pieces = slots.shape[0]
    piece_rows = master_slots.shape[2]
    low_slots = master_slots[0].astype(jnp.bfloat16).reshape(CAP, 8, 16, 2, D // 2)
    low_slots = low_slots.transpose(1, 3, 0, 2, 4).reshape(n_dp, CAP, 16, D // 2)
    mix_pieces = 4 * (D // n_tensor) // piece_rows
    up_pieces = (FF // n_tensor) // piece_rows
    per = mix_pieces // 4
    mix, up, down = gather_weights(slots, low_slots)
    w_qkv = mix[:3].reshape(3 * D, D)
    w_out = mix[3].reshape(D, D)
    w_up = up.reshape(FF, D)
    w_down = down.reshape(FF, D)
    bias_up = vectors[2:6].reshape(n_tensor, 4, -1).transpose(1, 0, 2).reshape(FF)

    bias_qkv = jnp.concatenate([vectors[0], jnp.zeros((D,), jnp.float32), vectors[1]])
    scale_qkv = jnp.concatenate([jnp.full((D,), HD ** (-0.5)), jnp.ones((2 * D,))])
    qkv = (
        (mm(w_qkv, tokens_ext, NT) + bias_qkv[:, None]) * scale_qkv.astype(jnp.float32)[:, None]
    ).astype(jnp.bfloat16)
    context, logs = attend(lo, hi, qkv, qaug, kaug, hidden_keys)
    attn_ext = mm(context, w_out, TN).astype(jnp.bfloat16)
    halo_attn = lax.ppermute(halo_part(attn_ext), "tensor", swap)
    attn_back = lax.dynamic_update_slice_in_dim(
        jnp.zeros((rows, D), jnp.bfloat16), halo_attn, edge, 0
    )
    attn_sum = jnp.where(foreign[:, None], attn_back, own_part(attn_ext)).astype(jnp.float32)
    residual_one = tokens.astype(jnp.float32) + (attn_sum + vectors[6])
    normal_one, inverse_one = layer_stats(residual_one)
    normed = normal_one * vectors[8] + vectors[9]
    normed_low = normed.astype(jnp.bfloat16)

    hidden, slope = feed_up(normed_low, w_up, bias_up)
    residual_two = normed + (mm(hidden, w_down, NN) + vectors[7])
    normal_two, inverse_two = layer_stats(residual_two)
    layer_out = (normal_two * vectors[10] + vectors[11]).astype(jnp.bfloat16)
    grad_out = out_grad.astype(jnp.float32)
    grad_two = norm_back(grad_out, normal_two, inverse_two, vectors[10])
    grad_two_low = grad_two.astype(jnp.bfloat16)

    grad_pre, up_sums = feed_down_back(grad_two_low, w_down, slope)
    grad_norm = grad_two + lax.optimization_barrier(mm(grad_pre, w_up, NN))
    grad_one = norm_back(grad_norm, normal_one, inverse_one, vectors[8])
    grad_one_low = grad_one.astype(jnp.bfloat16)

    halo_grad = lax.ppermute(
        lax.dynamic_slice_in_dim(grad_one_low, edge, halo, 0), "tensor", swap
    )
    grad_ext = jnp.where(handled[:, None], extend(grad_one_low, halo_grad), 0)
    grad_context = mm(w_out, grad_ext, NT).astype(jnp.bfloat16)
    grad_qkv = attend_back(lo, hi, qkv, grad_context, context, logs, qaug, kaug, hidden_keys)
    input_ext = mm(grad_qkv.reshape(3 * D, ext), w_qkv, TN)
    halo_input = lax.ppermute(halo_part(input_ext).astype(jnp.bfloat16), "tensor", swap)
    input_back = lax.dynamic_update_slice_in_dim(
        jnp.zeros((rows, D), jnp.bfloat16), halo_input, edge, 0
    )
    input_grad = (grad_one + own_part(input_ext) + input_back.astype(jnp.float32)).astype(
        jnp.bfloat16
    )

    vector_terms = jnp.concatenate(
        [
            jnp.stack(
                [
                    jnp.sum(grad_qkv[0].astype(jnp.float32), axis=1),
                    jnp.sum(grad_qkv[2].astype(jnp.float32), axis=1),
                ]
            ),
            up_sums.reshape(4, n_tensor, -1)
            .transpose(1, 0, 2)
            .reshape(FF // D, D),
            jnp.stack(
                [
                    jnp.sum(grad_one, axis=0),
                    jnp.sum(grad_two, axis=0),
                    jnp.sum(grad_norm * normal_one, axis=0),
                    jnp.sum(grad_norm, axis=0),
                    jnp.sum(grad_out * normal_two, axis=0),
                    jnp.sum(grad_out, axis=0),
                ]
            ),
        ],
        axis=0,
    )
    piece_of = jnp.full((n_dp * CAP,), pieces, jnp.int32).at[slots].set(
        jnp.arange(pieces, dtype=jnp.int32)
    )
    own_grads, vector_grads = reduce_grads(
        piece_of,
        vector_terms,
        grad_qkv,
        context,
        grad_pre,
        hidden,
        tokens_ext,
        grad_ext,
        normed_low,
        grad_two_low,
    )
    own_grads = own_grads.astype(jnp.float32)
    slot_new, slot_first_new, slot_second_new = adam_update(
        master_slots[0], slot_first[0], slot_second[0], own_grads, rate_matrix, weight_decay
    )
    vector_new, vector_first_new, vector_second_new = adam_update(
        vectors, vector_first, vector_second, vector_grads, rate_vector, 0.0
    )
    return (
        layer_out,
        input_grad,
        slot_new[None],
        slot_first_new[None],
        slot_second_new[None],
        vector_new,
        vector_first_new,
        vector_second_new,
    )


def solution(mesh):
    placed = (
        P(("dp", "tensor"), None),
        P("dp", None),
        P("dp", None),
        P(),
        P("tensor", "dp", None, None),
        P("tensor", "dp", None, None),
        P("tensor", "dp", None, None),
        P(),
        P(),
        P(),
        P(("dp", "tensor"), None),
    )
    by_rows = mesh.shape["tensor"] == 2 and mesh.shape["dp"] == 16
    return jax.shard_map(
        on_device_rows if by_rows else on_device_generic,
        mesh=mesh,
        in_specs=placed,
        out_specs=(
            P(("dp", "tensor"), None),
            P(("dp", "tensor"), None),
            P("tensor", "dp", None, None),
            P("tensor", "dp", None, None),
            P("tensor", "dp", None, None),
            P(),
            P(),
            P(),
        ),
        check_vma=False,
    )
```

```python
import functools

import jax
import jax.numpy as jnp
from jax import lax
from jax.experimental import pallas as pl
from jax.experimental.pallas import tpu as pltpu
from jax.sharding import PartitionSpec as P

D = 1024
HD = 64
FF = 4096
QBLK = 512
STEP = 10
CAP = 6


norm_eps = 1e-05
mask_fill = -1000000000.0
beta_one = 0.5
beta_two = 0.5
rate_matrix = 0.03
rate_vector = 0.1
weight_decay = 0.01
adam_eps = 1e-08


def slot_index(owners):
    owner_of = owners[:, 0]
    positions = jnp.arange(owner_of.shape[0], dtype=jnp.int32)
    earlier = (positions[None, :] < positions[:, None]) & (owner_of[None, :] == owner_of[:, None])
    within = jnp.sum(earlier.astype(jnp.int32), axis=1)
    return owner_of * CAP + within


def layer_stats(residual):
    center = residual - jnp.mean(residual, axis=-1, keepdims=True)
    spread = jnp.mean(center * center, axis=-1, keepdims=True)
    inverse = lax.rsqrt(spread + norm_eps)
    return (center * inverse, inverse)


def norm_back(grads, normal, inverse, gains):
    scaled = grads * gains
    return inverse * (
        scaled
        - jnp.mean(scaled, axis=-1, keepdims=True)
        - normal * jnp.mean(scaled * normal, axis=-1, keepdims=True)
    )


def gelu_exact(values):
    return jax.nn.gelu(values, approximate=False)


def block_mask(segment, valid, start):
    length = segment.shape[0]
    query_pos = start + jnp.arange(QBLK, dtype=jnp.int32)
    key_pos = jnp.arange(length, dtype=jnp.int32)
    query_seg = lax.dynamic_slice_in_dim(segment, start, QBLK, 0)
    same = query_seg[:, None] == segment[None, :]
    return same & ((valid[None, :] == 1) | (query_pos[:, None] == key_pos[None, :]))


def block_scores(block_q, key_rows, segment, valid, start):
    scores = jnp.einsum("qhd,khd->hqk", block_q, key_rows, preferred_element_type=jnp.float32)
    return jnp.where(block_mask(segment, valid, start)[None], scores, mask_fill)


def attend_forward(queries, key_rows, value_rows, segment, valid):
    length = queries.shape[0]

    def one_block(index):
        start = index * QBLK
        block_q = lax.dynamic_slice_in_dim(queries, start, QBLK, 0)
        scores = block_scores(block_q, key_rows, segment, valid, start)
        row_max = jnp.max(scores, axis=2, keepdims=True)
        raised = jnp.exp(scores - row_max)
        totals = jnp.sum(raised, axis=2, keepdims=True)
        weights = (raised / totals).astype(jnp.bfloat16)
        context = jnp.einsum(
            "hqk,khd->qhd", weights, value_rows, preferred_element_type=jnp.float32
        )
        return (context, (row_max + jnp.log(totals))[:, :, 0])

    context, log_sums = lax.map(one_block, jnp.arange(length // QBLK, dtype=jnp.int32))
    return (context.reshape(length, -1), log_sums)


def attend_backward(queries, key_rows, value_rows, segment, valid, log_sums, grad_context):
    length = queries.shape[0]

    def one_block(carry, index):
        key_acc, value_acc = carry
        start = index * QBLK
        block_q = lax.dynamic_slice_in_dim(queries, start, QBLK, 0)
        block_g = lax.dynamic_slice_in_dim(grad_context, start, QBLK, 0)
        scores = block_scores(block_q, key_rows, segment, valid, start)
        weights = jnp.exp(scores - log_sums[index][:, :, None])
        value_acc = value_acc + jnp.einsum(
            "hqk,qhd->khd",
            weights.astype(jnp.bfloat16),
            block_g,
            preferred_element_type=jnp.float32,
        )
        grad_weights = jnp.einsum(
            "qhd,khd->hqk", block_g, value_rows, preferred_element_type=jnp.float32
        )
        inner = jnp.sum(weights * grad_weights, axis=2, keepdims=True)
        grad_scores = (weights * (grad_weights - inner)).astype(jnp.bfloat16)
        grad_q = jnp.einsum(
            "hqk,khd->qhd", grad_scores, key_rows, preferred_element_type=jnp.float32
        )
        key_acc = key_acc + jnp.einsum(
            "hqk,qhd->khd", grad_scores, block_q, preferred_element_type=jnp.float32
        )
        return ((key_acc, value_acc), grad_q)

    zeros_kv = jnp.zeros(key_rows.shape, jnp.float32)
    (grad_keys, grad_values), grad_queries = lax.scan(
        one_block, (zeros_kv, zeros_kv), jnp.arange(length // QBLK, dtype=jnp.int32)
    )
    return (
        grad_queries.reshape(length, -1),
        grad_keys.reshape(length, -1),
        grad_values.reshape(length, -1),
    )


def adam_update(weights, first, second, grads, rate, decay):
    first_new = beta_one * first + (1.0 - beta_one) * grads
    second_new = beta_two * second + (1.0 - beta_two) * grads * grads
    first_hat = first_new / (1.0 - beta_one**STEP)
    second_hat = second_new / (1.0 - beta_two**STEP)
    updated = weights - rate * (first_hat / (jnp.sqrt(second_hat) + adam_eps) + decay * weights)
    return (updated, first_new, second_new)


def on_device_generic(
    tokens,
    segment_ids,
    key_mask,
    owners,
    master_slots,
    slot_first,
    slot_second,
    vectors,
    vector_first,
    vector_second,
    out_grad,
):
    n_tensor = lax.axis_size("tensor")
    group = lax.axis_index("tensor")
    head_cols = D // n_tensor
    unit_cols = FF // n_tensor
    heads_here = head_cols // HD
    seq_count = segment_ids.shape[0]
    length = segment_ids.shape[1]
    query_scale = HD ** (-0.5)
    slots = slot_index(owners)
    gathered_slots = lax.all_gather(master_slots[0].astype(jnp.bfloat16), "dp", axis=0, tiled=True)
    stack = jnp.take(gathered_slots, slots, axis=0).reshape(-1, D)
    w_mix = stack[0 : 3 * head_cols]
    w_out = stack[3 * head_cols : 4 * head_cols]
    w_up = stack[4 * head_cols : 4 * head_cols + unit_cols]
    w_down = stack[4 * head_cols + unit_cols :]
    bias_query = lax.dynamic_slice_in_dim(vectors[0], group * head_cols, head_cols, 0)
    bias_value = lax.dynamic_slice_in_dim(vectors[1], group * head_cols, head_cols, 0)
    bias_up = lax.dynamic_slice_in_dim(vectors[2:6].reshape(FF), group * unit_cols, unit_cols, 0)
    gathered = lax.all_gather(tokens, "tensor", axis=0, tiled=True)
    mixed = jnp.einsum("ld,kd->lk", gathered, w_mix, preferred_element_type=jnp.float32)
    queries = ((mixed[:, :head_cols] + bias_query) * query_scale).astype(jnp.bfloat16)
    key_rows = mixed[:, head_cols : 2 * head_cols].astype(jnp.bfloat16)
    value_rows = (mixed[:, 2 * head_cols :] + bias_value).astype(jnp.bfloat16)
    head_shape = (seq_count, length, heads_here, HD)
    queries_h = queries.reshape(head_shape)
    keys_h = key_rows.reshape(head_shape)
    values_h = value_rows.reshape(head_shape)

    def forward_seq(element):
        return attend_forward(element[0], element[1], element[2], element[3], element[4])

    context, log_sums = lax.map(forward_seq, (queries_h, keys_h, values_h, segment_ids, key_mask))
    context = context.reshape(-1, head_cols).astype(jnp.bfloat16)
    attn_sum = lax.psum_scatter(
        jnp.einsum("lk,kd->ld", context, w_out, preferred_element_type=jnp.float32).astype(
            jnp.bfloat16
        ),
        "tensor",
        scatter_dimension=0,
        tiled=True,
    ).astype(jnp.float32)
    residual_one = tokens.astype(jnp.float32) + (attn_sum + vectors[6])
    normal_one, inverse_one = layer_stats(residual_one)
    normed = normal_one * vectors[8] + vectors[9]
    normed_low = normed.astype(jnp.bfloat16)
    norm_rows = lax.all_gather(normed_low, "tensor", axis=0, tiled=True)
    hidden_pre = (
        jnp.einsum("ld,kd->lk", norm_rows, w_up, preferred_element_type=jnp.float32) + bias_up
    )
    hidden_full, gelu_pull = jax.vjp(gelu_exact, hidden_pre)
    hidden = hidden_full.astype(jnp.bfloat16)
    mlp_sum = lax.psum_scatter(
        jnp.einsum("lk,kd->ld", hidden, w_down, preferred_element_type=jnp.float32).astype(
            jnp.bfloat16
        ),
        "tensor",
        scatter_dimension=0,
        tiled=True,
    ).astype(jnp.float32)
    residual_two = normed + (mlp_sum + vectors[7])
    normal_two, inverse_two = layer_stats(residual_two)
    layer_out = (normal_two * vectors[10] + vectors[11]).astype(jnp.bfloat16)
    grad_out = out_grad.astype(jnp.float32)
    grad_two = norm_back(grad_out, normal_two, inverse_two, vectors[10])
    grad_down_in = lax.all_gather(grad_two.astype(jnp.bfloat16), "tensor", axis=0, tiled=True)
    grad_hidden = jnp.einsum("ld,kd->lk", grad_down_in, w_down, preferred_element_type=jnp.float32)
    grad_w_down = jnp.einsum("lk,ld->kd", hidden, grad_down_in, preferred_element_type=jnp.float32)
    grad_pre = gelu_pull(grad_hidden)[0].astype(jnp.bfloat16)
    norm_back_rows = lax.all_gather(normed_low, "tensor", axis=0, tiled=True)
    grad_w_up = jnp.einsum(
        "lk,ld->kd", grad_pre, norm_back_rows, preferred_element_type=jnp.float32
    )
    grad_norm = grad_two + lax.psum_scatter(
        jnp.einsum("lk,kd->ld", grad_pre, w_up, preferred_element_type=jnp.float32).astype(
            jnp.bfloat16
        ),
        "tensor",
        scatter_dimension=0,
        tiled=True,
    ).astype(jnp.float32)
    grad_one = norm_back(grad_norm, normal_one, inverse_one, vectors[8])
    grad_attn_in = lax.all_gather(grad_one.astype(jnp.bfloat16), "tensor", axis=0, tiled=True)
    grad_context = jnp.einsum(
        "ld,kd->lk", grad_attn_in, w_out, preferred_element_type=jnp.float32
    ).astype(jnp.bfloat16)
    grad_w_out = jnp.einsum("lk,ld->kd", context, grad_attn_in, preferred_element_type=jnp.float32)

    def backward_seq(element):
        return attend_backward(
            element[0], element[1], element[2], element[3], element[4], element[5], element[6]
        )

    grad_q, grad_k, grad_v = lax.map(
        backward_seq,
        (
            queries_h,
            keys_h,
            values_h,
            segment_ids,
            key_mask,
            log_sums,
            grad_context.reshape(head_shape),
        ),
    )
    grad_queries = grad_q.reshape(-1, head_cols).astype(jnp.bfloat16) * query_scale
    grad_keys = grad_k.reshape(-1, head_cols).astype(jnp.bfloat16)
    grad_values = grad_v.reshape(-1, head_cols).astype(jnp.bfloat16)
    grad_mix = jnp.concatenate([grad_queries, grad_keys, grad_values], axis=1)
    mix_back_rows = lax.all_gather(tokens, "tensor", axis=0, tiled=True)
    grad_w_mix = jnp.einsum(
        "lk,ld->kd", grad_mix, mix_back_rows, preferred_element_type=jnp.float32
    )
    input_grad = (
        grad_one
        + lax.psum_scatter(
            jnp.einsum("lk,kd->ld", grad_mix, w_mix, preferred_element_type=jnp.float32).astype(
                jnp.bfloat16
            ),
            "tensor",
            scatter_dimension=0,
            tiled=True,
        ).astype(jnp.float32)
    ).astype(jnp.bfloat16)
    query_full = lax.dynamic_update_slice_in_dim(
        jnp.zeros((D,), jnp.float32),
        jnp.sum(grad_queries.astype(jnp.float32), axis=0),
        group * head_cols,
        0,
    )
    value_full = lax.dynamic_update_slice_in_dim(
        jnp.zeros((D,), jnp.float32),
        jnp.sum(grad_values.astype(jnp.float32), axis=0),
        group * head_cols,
        0,
    )
    up_full = lax.dynamic_update_slice_in_dim(
        jnp.zeros((FF,), jnp.float32),
        jnp.sum(grad_pre.astype(jnp.float32), axis=0),
        group * unit_cols,
        0,
    )
    tail_rows = jnp.stack(
        [
            jnp.sum(grad_one, axis=0),
            jnp.sum(grad_two, axis=0),
            jnp.sum(grad_norm * normal_one, axis=0),
            jnp.sum(grad_norm, axis=0),
            jnp.sum(grad_out * normal_two, axis=0),
            jnp.sum(grad_out, axis=0),
        ]
    )
    vector_terms = jnp.concatenate(
        [jnp.stack([query_full, value_full]), up_full.reshape(FF // D, D), tail_rows], axis=0
    )
    vector_grads = lax.psum(vector_terms, ("dp", "tensor"))
    grad_stack = jnp.concatenate([grad_w_mix, grad_w_out, grad_w_up, grad_w_down], axis=0)
    grad_pieces = grad_stack.reshape(slots.shape[0], -1, D)
    spread_slots = (
        jnp.zeros((lax.axis_size("dp") * CAP,) + grad_pieces.shape[1:], jnp.float32)
        .at[slots]
        .set(grad_pieces)
    )
    own_grads = lax.psum_scatter(
        spread_slots.astype(jnp.bfloat16), "dp", scatter_dimension=0, tiled=True
    ).astype(jnp.float32)
    slot_new, slot_first_new, slot_second_new = adam_update(
        master_slots[0], slot_first[0], slot_second[0], own_grads, rate_matrix, weight_decay
    )
    vector_new, vector_first_new, vector_second_new = adam_update(
        vectors, vector_first, vector_second, vector_grads, rate_vector, 0.0
    )
    return (
        layer_out,
        input_grad,
        slot_new[None],
        slot_first_new[None],
        slot_second_new[None],
        vector_new,
        vector_first_new,
        vector_second_new,
    )


DOC_MAX = 800
EXT_PAD = 512
ABLK = 256
HPG = 8
AUG = 16
neg_big = -1000000000.0
NN = (((1,), (0,)), ((), ()))
NT = (((1,), (1,)), ((), ()))
TN = (((0,), (0,)), ((), ()))


def mm(a, b, dims):
    return lax.dot_general(a, b, dims, preferred_element_type=jnp.float32)


def attn_fwd_kernel(lo_ref, hi_ref, q_ref, k_ref, v_ref, qaug_ref, kaug_ref, hid_ref, o_ref, lse_ref, kn_ref, m_ref, acc_ref):
    ext = q_ref.shape[1]
    ones = jnp.concatenate(
        [jnp.ones((1, ABLK), jnp.float32), jnp.zeros((AUG - 1, ABLK), jnp.float32)], axis=0
    ).astype(jnp.bfloat16)
    for h in range(HPG):
        rows = slice(h * HD, (h + 1) * HD)
        kn_ref[h] = jnp.concatenate([k_ref[rows, :], kaug_ref[...]], axis=0).T

    def query_block(qb, _):
        lo = lo_ref[qb]
        hi = hi_ref[qb]
        qs = pl.ds(pl.multiple_of(qb * ABLK, ABLK), ABLK)

        @pl.when(hi > lo)
        def _work():
            hidden = hid_ref[0:1, qs]
            for h in range(HPG):
                rows = slice(h * HD, (h + 1) * HD)
                q32 = q_ref[rows, qs].astype(jnp.float32)
                k32 = k_ref[rows, qs].astype(jnp.float32)
                own = jnp.sum(q32 * k32, axis=0, keepdims=True)
                m_ref[h] = jnp.where(hidden > 0.0, own, -1e30)
                acc_ref[h, 0:HD, :] = v_ref[rows, qs].astype(jnp.float32) * hidden
                acc_ref[h, HD:, :] = jnp.broadcast_to(hidden, (AUG, ABLK))

            def key_block(kb, _):
                ks = pl.ds(pl.multiple_of(kb * ABLK, ABLK), ABLK)
                heads = [slice(h * HD, (h + 1) * HD) for h in range(HPG)]
                scores = [
                    mm(kn_ref[h, ks, :], jnp.concatenate([q_ref[heads[h], qs], qaug_ref[:, qs]], axis=0), NN)
                    for h in range(HPG)
                ]
                olds = [m_ref[h] for h in range(HPG)]
                news = [
                    jnp.maximum(olds[h], jnp.max(scores[h], axis=0, keepdims=True)) for h in range(HPG)
                ]
                raised = [jnp.exp(scores[h] - news[h]).astype(jnp.bfloat16) for h in range(HPG)]
                for h in range(HPG):
                    m_ref[h] = news[h]
                    va = jnp.concatenate([v_ref[heads[h], ks], ones], axis=0)
                    acc_ref[h] = acc_ref[h] * jnp.exp(olds[h] - news[h]) + mm(va, raised[h], NN)
                return 0

            lax.fori_loop(lo, hi, key_block, 0)
            for h in range(HPG):
                rows = slice(h * HD, (h + 1) * HD)
                total = acc_ref[h, HD : HD + 1, :]
                o_ref[rows, qs] = (acc_ref[h, 0:HD, :] * (1.0 / total)).astype(jnp.bfloat16)
                lse_ref[0, h : h + 1, qs] = m_ref[h] + jnp.log(total)

        @pl.when(hi <= lo)
        def _skip():
            o_ref[:, qs] = jnp.zeros((HPG * HD, ABLK), jnp.bfloat16)
            lse_ref[0, :, qs] = jnp.zeros((8, ABLK), jnp.float32)

        return 0

    lax.fori_loop(0, ext // ABLK, query_block, 0)


def attn_bwd_kernel(
    lo_ref, hi_ref, q_ref, k_ref, v_ref, g_ref, c_ref, lse_ref, qaug_ref, kaug_ref, hid_ref,
    out_ref, kn_ref, vn_ref, acc_ref, dk_acc, dv_acc,
):
    ext = q_ref.shape[1]
    for h in range(HPG):
        rows = slice(h * HD, (h + 1) * HD)
        kn_ref[h] = jnp.concatenate([k_ref[rows, :], kaug_ref[...]], axis=0).T
        vn_ref[h] = v_ref[rows, :].T
    dk_acc[...] = jnp.zeros_like(dk_acc)
    dv_acc[...] = jnp.zeros_like(dv_acc)

    def query_block(qb, _):
        lo = lo_ref[qb]
        hi = hi_ref[qb]
        qs = pl.ds(pl.multiple_of(qb * ABLK, ABLK), ABLK)

        @pl.when(hi > lo)
        def _work():
            hidden = hid_ref[0:1, qs]
            deltas = []
            logs = []
            for h in range(HPG):
                rows = slice(h * HD, (h + 1) * HD)
                q32 = q_ref[rows, qs].astype(jnp.float32)
                k32 = k_ref[rows, qs].astype(jnp.float32)
                v32 = v_ref[rows, qs].astype(jnp.float32)
                g32 = g_ref[rows, qs].astype(jnp.float32)
                c32 = c_ref[rows, qs].astype(jnp.float32)
                delta = jnp.sum(g32 * c32, axis=0, keepdims=True)
                log = lse_ref[0, h : h + 1, qs]
                own = jnp.sum(q32 * k32, axis=0, keepdims=True)
                p_own = jnp.where(hidden > 0.0, jnp.exp(own - log), 0.0)
                d_own = p_own * (jnp.sum(g32 * v32, axis=0, keepdims=True) - delta)
                acc_ref[h] = d_own * k32
                dk_acc[rows, qs] += d_own * q32
                dv_acc[rows, qs] += p_own * g32
                deltas.append(delta)
                logs.append(log)

            def key_block(kb, _):
                ks = pl.ds(pl.multiple_of(kb * ABLK, ABLK), ABLK)
                heads = [slice(h * HD, (h + 1) * HD) for h in range(HPG)]
                every = range(HPG)
                qs_h = [q_ref[heads[h], qs] for h in every]
                gs_h = [g_ref[heads[h], qs] for h in every]
                scores = [
                    mm(kn_ref[h, ks, :], jnp.concatenate([qs_h[h], qaug_ref[:, qs]], axis=0), NN)
                    for h in every
                ]
                grads = [mm(vn_ref[h, ks, :], gs_h[h], NN) for h in every]
                weights = [jnp.exp(scores[h] - logs[h]) for h in every]
                low = [weights[h].astype(jnp.bfloat16) for h in every]
                back = [
                    (weights[h] * (grads[h] - deltas[h])).astype(jnp.bfloat16) for h in every
                ]
                v_new = [mm(gs_h[h], low[h], NT) for h in every]
                k_new = [mm(qs_h[h], back[h], NT) for h in every]
                q_new = [mm(k_ref[heads[h], ks], back[h], NN) for h in every]
                for h in every:
                    dv_acc[heads[h], ks] += v_new[h]
                    dk_acc[heads[h], ks] += k_new[h]
                    acc_ref[h] += q_new[h]
                return 0

            lax.fori_loop(lo, hi, key_block, 0)
            for h in range(HPG):
                rows = slice(h * HD, (h + 1) * HD)
                out_ref[0, rows, qs] = acc_ref[h].astype(jnp.bfloat16) * (HD ** (-0.5))

        @pl.when(hi <= lo)
        def _skip():
            out_ref[0, :, qs] = jnp.zeros((HPG * HD, ABLK), jnp.bfloat16)

        return 0

    lax.fori_loop(0, ext // ABLK, query_block, 0)
    out_ref[1] = dk_acc[...].astype(jnp.bfloat16)
    out_ref[2] = dv_acc[...].astype(jnp.bfloat16)


def group_block(offset, rows, ext):
    return pl.BlockSpec((rows, ext), lambda g, lo, hi: (offset + g, 0))


def fixed_block(rows, ext):
    return pl.BlockSpec((rows, ext), lambda g, lo, hi: (0, 0))


def attend(lo, hi, qkv, qaug, kaug, hidden):
    ext = qkv.shape[1]
    groups = D // HD // HPG
    rows = HPG * HD
    return pl.pallas_call(
        attn_fwd_kernel,
        out_shape=(
            jax.ShapeDtypeStruct((D, ext), jnp.bfloat16),
            jax.ShapeDtypeStruct((groups, 8, ext), jnp.float32),
        ),
        grid_spec=pltpu.PrefetchScalarGridSpec(
            num_scalar_prefetch=2,
            grid=(groups,),
            in_specs=[
                group_block(0, rows, ext),
                group_block(groups, rows, ext),
                group_block(2 * groups, rows, ext),
                fixed_block(AUG, ext),
                fixed_block(AUG, ext),
                fixed_block(8, ext),
            ],
            out_specs=[
                group_block(0, rows, ext),
                pl.BlockSpec((1, 8, ext), lambda g, lo, hi: (g, 0, 0)),
            ],
            scratch_shapes=[
                pltpu.VMEM((HPG, ext, HD + AUG), jnp.bfloat16),
                pltpu.VMEM((HPG, 1, ABLK), jnp.float32),
                pltpu.VMEM((HPG, HD + AUG, ABLK), jnp.float32),
            ],
        ),
        compiler_params=pltpu.CompilerParams(vmem_limit_bytes=40 * 2**20),
        cost_estimate=pl.CostEstimate(flops=20 * 10**9, bytes_accessed=14 * 10**6, transcendentals=0),
        name="attend",
    )(lo, hi, qkv, qkv, qkv, qaug, kaug, hidden)


def attend_back(lo, hi, qkv, grads, context, logs, qaug, kaug, hidden):
    ext = qkv.shape[1]
    groups = D // HD // HPG
    rows = HPG * HD
    return pl.pallas_call(
        attn_bwd_kernel,
        out_shape=jax.ShapeDtypeStruct((3, D, ext), jnp.bfloat16),
        grid_spec=pltpu.PrefetchScalarGridSpec(
            num_scalar_prefetch=2,
            grid=(groups,),
            in_specs=[
                group_block(0, rows, ext),
                group_block(groups, rows, ext),
                group_block(2 * groups, rows, ext),
                group_block(0, rows, ext),
                group_block(0, rows, ext),
                pl.BlockSpec((1, 8, ext), lambda g, lo, hi: (g, 0, 0)),
                fixed_block(AUG, ext),
                fixed_block(AUG, ext),
                fixed_block(8, ext),
            ],
            out_specs=pl.BlockSpec((3, rows, ext), lambda g, lo, hi: (0, g, 0)),
            scratch_shapes=[
                pltpu.VMEM((HPG, ext, HD + AUG), jnp.bfloat16),
                pltpu.VMEM((HPG, ext, HD), jnp.bfloat16),
                pltpu.VMEM((HPG, HD, ABLK), jnp.float32),
                pltpu.VMEM((rows, ext), jnp.float32),
                pltpu.VMEM((rows, ext), jnp.float32),
            ],
        ),
        compiler_params=pltpu.CompilerParams(vmem_limit_bytes=48 * 2**20),
        cost_estimate=pl.CostEstimate(flops=50 * 10**9, bytes_accessed=30 * 10**6, transcendentals=0),
        name="attend_back",
    )(lo, hi, qkv, qkv, qkv, grads, context, logs, qaug, kaug, hidden)


def document_plan(segment, valid, half, rows):
    length = segment.shape[0]
    ext = rows + EXT_PAD
    base = half * EXT_PAD
    position = jnp.arange(length, dtype=jnp.int32)
    documents = jnp.arange(8, dtype=jnp.int32)[:, None]
    one_hot = segment[None, :] == documents
    counts = jnp.sum(one_hot.astype(jnp.int32), axis=1, keepdims=True)
    starts = jnp.sum((segment[None, :] < documents).astype(jnp.int32), axis=1, keepdims=True)
    start = jnp.sum(jnp.where(one_hot, starts, 0), axis=0)
    end = jnp.sum(jnp.where(one_hot, starts + counts, 0), axis=0)
    crossing = (start < rows) & (end > rows)
    left = jnp.max(jnp.where(crossing, rows - start, 0))
    right = jnp.max(jnp.where(crossing, end - rows, 0))
    worker = jnp.where(left <= right, half == 1, half == 0)
    own = (position >= half * rows) & (position < (half + 1) * rows)
    handled = jnp.where(crossing, worker, own)
    cut = lambda values: lax.dynamic_slice_in_dim(values, base, ext, 0)
    handled_ext = cut(handled)
    begins = jnp.where(handled_ext, cut(start) - base, ext).reshape(-1, ABLK)
    ends = jnp.where(handled_ext, cut(end) - base, 0).reshape(-1, ABLK)
    lo = jnp.min(begins, axis=1) // ABLK
    hi = (jnp.max(ends, axis=1) + (ABLK - 1)) // ABLK
    blank = jnp.max(ends, axis=1) == 0
    lo = jnp.where(blank, 0, lo)
    hi = jnp.where(blank, 0, hi)
    hot = cut(one_hot.T).T
    masked = cut(valid) == 0
    ones = jnp.ones((1, ext), jnp.bfloat16)
    fill = jnp.zeros((AUG - 9, ext), jnp.bfloat16)
    qaug = jnp.concatenate([hot.astype(jnp.bfloat16), ones, fill], axis=0)
    kaug = jnp.concatenate(
        [
            jnp.where(hot, 0.0, neg_big).astype(jnp.bfloat16),
            jnp.where(masked[None, :], neg_big, 0.0).astype(jnp.bfloat16),
            fill,
        ],
        axis=0,
    )
    hidden = jnp.broadcast_to(masked.astype(jnp.float32)[None, :], (8, ext))
    foreign = lax.dynamic_slice_in_dim(crossing & ~worker, half * rows, rows, 0)
    return lo, hi, qaug, kaug, hidden, handled_ext, foreign


def normal_parts(values):
    bell = jnp.exp(values * values * -0.5)
    return (0.5 + 0.5 * lax.erf(values * 0.7071067811865476), bell * 0.3989422804014327)


UNITS = 1024
STRIP = 512


def up_kernel(x_ref, w_ref, bias_ref, gelu_ref, slope_ref):
    for r in range(0, x_ref.shape[0], STRIP):
        strip = slice(r, r + STRIP)
        values = mm(x_ref[strip, :], w_ref[...], NT) + bias_ref[...]
        cdf, bell = normal_parts(values)
        gelu_ref[strip, :] = (values * cdf).astype(jnp.bfloat16)
        slope_ref[strip, :] = (cdf + values * bell).astype(jnp.bfloat16)


def feed_up(rows, weights, bias):
    length = rows.shape[0]
    units = weights.shape[0]
    out = jax.ShapeDtypeStruct((length, units), jnp.bfloat16)
    columns = pl.BlockSpec((length, UNITS), lambda n: (0, n))
    return pl.pallas_call(
        up_kernel,
        out_shape=(out, out),
        grid=(units // UNITS,),
        in_specs=[
            pl.BlockSpec((length, D), lambda n: (0, 0)),
            pl.BlockSpec((UNITS, D), lambda n: (n, 0)),
            pl.BlockSpec((1, UNITS), lambda n: (0, n)),
        ],
        out_specs=(columns, columns),
        compiler_params=pltpu.CompilerParams(vmem_limit_bytes=40 * 2**20),
        cost_estimate=pl.CostEstimate(
            flops=2 * length * units * D, bytes_accessed=26 * 10**6, transcendentals=0
        ),
        name="feed_up",
    )(rows, weights, bias.reshape(1, units))


def down_back_kernel(g_ref, w_ref, slope_ref, out_ref, sum_ref):
    total = jnp.zeros((1, UNITS), jnp.float32)
    for r in range(0, g_ref.shape[0], STRIP):
        strip = slice(r, r + STRIP)
        grads = mm(g_ref[strip, :], w_ref[...], NT) * slope_ref[strip, :].astype(jnp.float32)
        low = grads.astype(jnp.bfloat16)
        out_ref[strip, :] = low
        total += jnp.sum(low.astype(jnp.float32), axis=0, keepdims=True)
    sum_ref[...] = total


def feed_down_back(grads, weights, slope):
    length = grads.shape[0]
    units = weights.shape[0]
    columns = pl.BlockSpec((length, UNITS), lambda n: (0, n))
    one_row = pl.BlockSpec((1, UNITS), lambda n: (0, n))
    return pl.pallas_call(
        down_back_kernel,
        out_shape=(
            jax.ShapeDtypeStruct((length, units), jnp.bfloat16),
            jax.ShapeDtypeStruct((1, units), jnp.float32),
        ),
        grid=(units // UNITS,),
        in_specs=[
            pl.BlockSpec((length, D), lambda n: (0, 0)),
            pl.BlockSpec((UNITS, D), lambda n: (n, 0)),
            columns,
        ],
        out_specs=(columns, one_row),
        compiler_params=pltpu.CompilerParams(vmem_limit_bytes=40 * 2**20),
        cost_estimate=pl.CostEstimate(
            flops=2 * length * units * D, bytes_accessed=26 * 10**6, transcendentals=0
        ),
        name="feed_down_back",
    )(grads, weights, slope)


MESH = pl.DeviceIdType.MESH
CHUNKS = 4
GROUPS = ((0, 3), (3, 1), (4, 4), (8, 4))
PARTS = (((0, 1), (1, 2)), ((0, 1), None), ((0, 2), (2, 2)), ((0, 2), (2, 2)))


def neighbours(z, y, core, x):
    def at(z, y, core, x):
        return {"dp": (z * 2 + y) * 2 + core, "tensor": x}

    return {
        "x": at(z, y, core, 1 - x),
        "y": at(z, 1 - y, core, x),
        "core": at(z, y, 1 - core, x),
        "up": at(jnp.minimum(z + 1, 3), y, core, x),
        "down": at(jnp.maximum(z - 1, 0), y, core, x),
    }


def greet(near, z):
    barrier = pltpu.get_barrier_semaphore()
    for name in ("x", "y", "core"):
        pl.semaphore_signal(barrier, inc=1, device_id=near[name], device_id_type=MESH)

    @pl.when(z < 3)
    def _up():
        pl.semaphore_signal(barrier, inc=1, device_id=near["up"], device_id_type=MESH)

    @pl.when(z > 0)
    def _down():
        pl.semaphore_signal(barrier, inc=1, device_id=near["down"], device_id_type=MESH)

    at_end = jnp.where((z == 0) | (z == 3), 1, 0)
    pl.semaphore_wait(barrier, 5 - at_end)


def greet_all(near, me, n_dp):
    barrier = pltpu.get_barrier_semaphore()
    pl.semaphore_signal(barrier, inc=1, device_id=near["x"], device_id_type=MESH)

    def one(i, _):
        other = {"dp": lax.rem(me + i, n_dp), "tensor": lax.axis_index("tensor")}
        pl.semaphore_signal(barrier, inc=1, device_id=other, device_id_type=MESH)
        return 0

    lax.fori_loop(1, n_dp, one, 0)
    pl.semaphore_wait(barrier, n_dp)


def gather_kernel(
    owners_ref, slots_ref, tokens_ref, qkv_ref, out_ref, up_ref, down_ref, ext_ref,
    slot_ref, low_ref, spread_ref, dense_ref, zero_ref, local_sem, own_sem, ext_sem, post, mail, send, recv, halo_send, halo_recv,
):
    z, y, core, x = coordinates()
    near = neighbours(z, y, core, x)
    width = D // 2
    me = lax.axis_index("dp")
    n_dp = low_ref.shape[0]
    for to in range(n_dp):
        lines = slice((to // 2) * 16, (to // 2) * 16 + 16)
        columns = slice((to % 2) * width, (to % 2) * width + width)
        low_ref[to] = slots_ref[:, lines, columns].astype(low_ref.dtype)
    greet_all(near, me, n_dp)

    def letter(to):
        return pltpu.make_async_remote_copy(
            src_ref=low_ref.at[to],
            dst_ref=spread_ref.at[pl.ds(me * CAP, CAP)],
            send_sem=post.at[to],
            recv_sem=mail.at[me],
            device_id={"dp": to, "tensor": x},
            device_id_type=MESH,
        )

    def answer(of):
        return pltpu.make_async_remote_copy(
            src_ref=low_ref.at[of],
            dst_ref=spread_ref.at[pl.ds(of * CAP, CAP)],
            send_sem=post.at[of],
            recv_sem=mail.at[of],
            device_id={"dp": of, "tensor": x},
            device_id_type=MESH,
        )

    def peer(i):
        return lax.rem(me + i, n_dp)

    def post_one(i, _):
        letter(peer(i)).start()
        return 0

    lax.fori_loop(1, n_dp, post_one, 0)

    rows = tokens_ref.shape[0]
    halo = DOC_MAX // 2
    blank = zero_ref.shape[0]
    zero_ref[...] = jnp.zeros_like(zero_ref)
    edge = pl.multiple_of(jnp.where(x == 0, rows - halo, 0), 16)
    there = pl.multiple_of(jnp.where(x == 0, EXT_PAD - halo, rows), 16)
    rest = pl.multiple_of(jnp.where(x == 0, rows + halo, 0), 16)
    border = pltpu.make_async_remote_copy(
        src_ref=tokens_ref.at[pl.ds(edge, halo)],
        dst_ref=ext_ref.at[pl.ds(there, halo)],
        send_sem=halo_send,
        recv_sem=halo_recv,
        device_id=near["x"],
        device_id_type=MESH,
    )
    border.start()
    inside = pltpu.make_async_copy(
        tokens_ref, ext_ref.at[pl.ds(pl.multiple_of(x * EXT_PAD, 16), rows)], ext_sem.at[0]
    )
    inside.start()
    empty = pltpu.make_async_copy(zero_ref, ext_ref.at[pl.ds(rest, blank)], ext_sem.at[1])
    empty.start()
    mine = pltpu.make_async_copy(low_ref.at[me], spread_ref.at[pl.ds(me * CAP, CAP)], local_sem)
    mine.start()
    mine.wait()

    def find(p, _):
        owner = owners_ref[p]

        def count(q, before):
            return before + jnp.where(owners_ref[q] == owner, 1, 0)

        slot_ref[p] = owner * CAP + lax.fori_loop(0, p, count, 0)
        return 0

    lax.fori_loop(0, owners_ref.shape[0], find, 0)

    def mail_one(i, _):
        answer(peer(i)).wait_recv()
        letter(peer(i)).wait_send()
        return 0

    lax.fori_loop(1, n_dp, mail_one, 0)

    def place(p, _):
        dense_ref[p // 4, p % 4] = spread_ref[slot_ref[p]]
        return 0

    lax.fori_loop(0, owners_ref.shape[0], place, 0)

    def block(k, t, zz, yy, cc, part=None):
        groups = slice(None) if part is None else pl.ds(*PARTS[k][part])
        return (qkv_ref, out_ref, up_ref, down_ref)[k].at[
            groups,
            t,
            :,
            pl.ds(pl.multiple_of((zz * 2 + yy) * 16, 16), 16),
            pl.ds(pl.multiple_of(cc * width, width), width),
        ]

    own = [
        pltpu.make_async_copy(dense_ref.at[pl.ds(*GROUPS[k])], block(k, x, z, y, core), own_sem.at[k])
        for k in range(CHUNKS)
    ]
    for one in own:
        one.start()

    def copy(kind, link, k, zz, t, yy, cc, part=None, fresh=False):
        view = block(k, t, zz, yy, cc, part)
        return pltpu.make_async_remote_copy(
            src_ref=dense_ref.at[pl.ds(*GROUPS[k])] if fresh else view,
            dst_ref=view,
            send_sem=send.at[kind, k, zz],
            recv_sem=recv.at[kind, k, zz],
            device_id=near[link],
            device_id_type=MESH,
        )

    def up(k, zz, fresh=False):
        return copy(0, "up", k, zz, x, y, core, fresh=fresh)

    def down(k, zz, fresh=False):
        return copy(1, "down", k, zz, x, y, core, fresh=fresh)

    def spread(k, zz, fresh):
        copy(2, "x", k, zz, x, y, core, fresh=fresh).start()
        copy(3, "y", k, zz, x, y, core, fresh=fresh).start()
        copy(4, "core", k, zz, x, y, core, fresh=fresh).start()

    def each(d, body):
        @pl.when((d > 0) & (z - d >= 0))
        def _below():
            for k in range(CHUNKS):
                body(k, z - d, 0)

        @pl.when((d > 0) & (z + d <= 3))
        def _above():
            for k in range(CHUNKS):
                body(k, z + d, 1)

    def each_or_own(d, body):
        each(d, body)

        @pl.when(d == 0)
        def _own():
            for k in range(CHUNKS):
                body(k, z, None)

    def begin(k):
        @pl.when(z < 3)
        def _up():
            up(k, z, True).start()

        @pl.when(z > 0)
        def _down():
            down(k, z, True).start()

        spread(k, z, True)

    def first(k, zz, side):
        if side == 0:
            up(k, zz).wait_recv()

            @pl.when(z < 3)
            def _up():
                up(k, zz).start()

        else:
            down(k, zz).wait_recv()

            @pl.when(z > 0)
            def _on():
                down(k, zz).start()

        spread(k, zz, False)

    def second(k, zz, side):
        copy(2, "x", k, zz, 1 - x, y, core).wait_recv()
        copy(5, "y", k, zz, 1 - x, y, core, 0).start()
        copy(7, "core", k, zz, 1 - x, y, core).start()
        copy(3, "y", k, zz, x, 1 - y, core).wait_recv()
        if PARTS[k][1]:
            copy(6, "x", k, zz, x, 1 - y, core, 1).start()
        copy(8, "core", k, zz, x, 1 - y, core).start()

    def third(k, zz, side):
        copy(5, "y", k, zz, 1 - x, 1 - y, core, 0).wait_recv()
        copy(9, "core", k, zz, 1 - x, 1 - y, core, 0).start()
        if PARTS[k][1]:
            copy(6, "x", k, zz, 1 - x, 1 - y, core, 1).wait_recv()
            copy(10, "core", k, zz, 1 - x, 1 - y, core, 1).start()

    def finish(k, zz, side):
        if side != 1:

            @pl.when(z < 3)
            def _up():
                up(k, zz).wait_send()

        if side != 0:

            @pl.when(z > 0)
            def _down():
                down(k, zz).wait_send()

        copy(2, "x", k, zz, x, y, core).wait_send()
        copy(3, "y", k, zz, x, y, core).wait_send()
        copy(5, "y", k, zz, 1 - x, y, core, 0).wait_send()
        if PARTS[k][1]:
            copy(6, "x", k, zz, x, 1 - y, core, 1).wait_send()
        copy(4, "core", k, zz, x, y, core).wait_send()
        copy(7, "core", k, zz, 1 - x, y, core).wait_send()
        copy(8, "core", k, zz, x, 1 - y, core).wait_send()
        copy(9, "core", k, zz, 1 - x, 1 - y, core, 0).wait_send()
        if PARTS[k][1]:
            copy(10, "core", k, zz, 1 - x, 1 - y, core, 1).wait_send()
        copy(4, "core", k, zz, x, y, 1 - core).wait_recv()
        copy(7, "core", k, zz, 1 - x, y, 1 - core).wait_recv()
        copy(8, "core", k, zz, x, 1 - y, 1 - core).wait_recv()
        copy(9, "core", k, zz, 1 - x, 1 - y, 1 - core, 0).wait_recv()
        if PARTS[k][1]:
            copy(10, "core", k, zz, 1 - x, 1 - y, 1 - core, 1).wait_recv()

    for k in range(CHUNKS):
        begin(k)

    def step(d, _):
        @pl.when(d < 4)
        def _one():
            each(d, first)

        @pl.when((d >= 1) & (d < 5))
        def _two():
            each_or_own(d - 1, second)

        @pl.when(d >= 2)
        def _three():
            each_or_own(d - 2, third)

        return 0

    lax.fori_loop(1, 6, step, 0)

    def end(d, _):
        each_or_own(d, finish)
        return 0

    lax.fori_loop(0, 4, end, 0)
    for one in own:
        one.wait()
    border.wait()
    inside.wait()
    empty.wait()


def gather_weights(owners, slots, tokens):
    n_dp = lax.axis_size("dp")
    low = jnp.bfloat16
    rows = tokens.shape[0]
    anywhere = pl.BlockSpec(memory_space=pl.ANY)
    return pl.pallas_call(
        gather_kernel,
        out_shape=tuple(
            jax.ShapeDtypeStruct((count, 2, 4, 128, D), low) for first, count in GROUPS
        )
        + (jax.ShapeDtypeStruct((rows + EXT_PAD, D), tokens.dtype),),
        in_specs=[
            pl.BlockSpec(memory_space=pltpu.SMEM),
            pl.BlockSpec(memory_space=pltpu.VMEM),
            anywhere,
        ],
        out_specs=(anywhere,) * 5,
        scratch_shapes=[
            pltpu.SMEM(owners.shape, jnp.int32),
            pltpu.VMEM((n_dp, CAP, 16, D // 2), low),
            pltpu.VMEM((n_dp * CAP, 16, D // 2), low),
            pltpu.VMEM((12, 4, 16, D // 2), low),
            pltpu.VMEM((EXT_PAD - DOC_MAX // 2, D), tokens.dtype),
            pltpu.SemaphoreType.DMA,
            pltpu.SemaphoreType.DMA((CHUNKS,)),
            pltpu.SemaphoreType.DMA((2,)),
            pltpu.SemaphoreType.DMA((n_dp,)),
            pltpu.SemaphoreType.DMA((n_dp,)),
            pltpu.SemaphoreType.DMA((11, CHUNKS, 4)),
            pltpu.SemaphoreType.DMA((11, CHUNKS, 4)),
            pltpu.SemaphoreType.DMA,
            pltpu.SemaphoreType.DMA,
        ],
        compiler_params=pltpu.CompilerParams(
            collective_id=1, has_side_effects=True, vmem_limit_bytes=32 * 2**20
        ),
        cost_estimate=pl.CostEstimate(flops=0, bytes_accessed=50 * 10**6, transcendentals=0),
        name="gather_weights",
    )(owners, slots, tokens)


BLOCKS = 12
SLICES = 2
STEPS = BLOCKS * SLICES
LAG = 2


def reduce_kernel(
    piece_ref, vec_ref, qkv_ref, ctx_ref, pre_ref, hid_ref, tok_ref, gext_ref, norm_ref, two_ref,
    out_ref, sum_ref,
    tile, tall, ext_rhs, row_rhs, far_buf, near_buf, core_in, x_in, y_in, x2_in, y2_in, line, line_in,
    done, parcel, vec_in, vec_out,
    tile_sem, rhs_sem, local_sem, post, mail, send, recv, vec_send, vec_recv,
):
    z, y, core, x = coordinates()
    near = neighbours(z, y, core, x)
    me = lax.axis_index("dp")
    n_dp = parcel.shape[1]
    half_width = D // 2
    width = half_width // SLICES
    rows = tile.shape[1]
    tiles = 1024 // rows

    def right(n, half, cut):
        ref = (tok_ref, gext_ref, norm_ref, two_ref)[n]
        to = ext_rhs.at[n, half, cut] if n < 2 else row_rhs.at[n - 2, half, cut]
        which = 1 - core if half == 0 else core
        columns = pl.ds(pl.multiple_of(which * half_width + cut * width, width), width)
        return pltpu.make_async_copy(ref.at[:, columns], to, rhs_sem.at[n, half, cut])

    for cut in range(SLICES):
        for n in range(4):
            for half in range(2):
                right(n, half, cut).start()

    def fetch(n, body):
        i = lax.rem(n // tiles, BLOCKS)
        part = pl.ds(pl.multiple_of(lax.rem(n, tiles) * rows, rows), rows)
        slot = lax.rem(n, 2)
        ext = ext_rhs.shape[3]
        wide = tile.at[slot, :, pl.ds(0, ext)]
        sem = tile_sem.at[slot]

        @pl.when(i < 3)
        def _qkv():
            body(pltpu.make_async_copy(qkv_ref.at[i, part, :], wide, sem))

        @pl.when(i == 3)
        def _out():
            body(pltpu.make_async_copy(ctx_ref.at[part, :], wide, sem))

        def columns(first):
            start = (i - first) * 1024 + lax.rem(n, tiles) * rows
            return pl.ds(pl.multiple_of(start, rows), rows)

        @pl.when((i >= 4) & (i < 8))
        def _up():
            body(pltpu.make_async_copy(pre_ref.at[:, columns(4)], tall.at[slot], sem))

        @pl.when(i >= 8)
        def _down():
            body(pltpu.make_async_copy(hid_ref.at[:, columns(8)], tall.at[slot], sem))

    fetch(0, lambda copy: copy.start())
    greet_all(near, me, n_dp)

    def remote(kind, i, link, src, dst):
        return pltpu.make_async_remote_copy(
            src_ref=src,
            dst_ref=dst,
            send_sem=send.at[kind, i],
            recv_sem=recv.at[kind, i],
            device_id=near[link],
            device_id_type=MESH,
        )

    def core_copy(i):
        return remote(0, i, "core", far_buf.at[lax.rem(i, 2)], core_in.at[i])

    def x1(i):
        return remote(1, i, "x", core_in.at[i, 1 - x, pl.ds(0, 2)], x_in.at[i])

    def y1(i):
        return remote(2, i, "y", core_in.at[i, :, pl.ds(2, 2), :, 1 - y], y_in.at[i])

    def y2(i):
        return remote(3, i, "y", x_in.at[i, :, :, 1 - y], y2_in.at[i])

    def x2(i):
        return remote(4, i, "x", y_in.at[i, 1 - x], x2_in.at[i])

    def along(i, zz):
        return pltpu.make_async_remote_copy(
            src_ref=line.at[i, zz],
            dst_ref=line_in.at[i, z],
            send_sem=send.at[5 + zz, i],
            recv_sem=recv.at[5 + z, i],
            device_id={"dp": (zz * 2 + y) * 2 + core, "tensor": x},
            device_id_type=MESH,
        )

    def arrival(i, zz):
        return pltpu.make_async_remote_copy(
            src_ref=line.at[i, zz],
            dst_ref=line_in.at[i, zz],
            send_sem=send.at[5 + zz, i],
            recv_sem=recv.at[5 + zz, i],
            device_id={"dp": (zz * 2 + y) * 2 + core, "tensor": x},
            device_id_type=MESH,
        )

    def produce(b):
        ring = lax.rem(b, 2)
        cut = b // BLOCKS
        i = lax.rem(b, BLOCKS)

        for c in range(SLICES):
            for n, first in enumerate((0, 3, 4, 8)):

                @pl.when(b == c * BLOCKS + first)
                def _ready():
                    right(n, 0, c).wait()
                    right(n, 1, c).wait()

        @pl.when(b >= 2)
        def _free():
            core_copy(b - 2).wait_send()

        def one(part, _):
            n = b * tiles + part
            slot = lax.rem(n, 2)

            @pl.when(n + 1 < STEPS * tiles)
            def _next():
                fetch(n + 1, lambda copy: copy.start())

            fetch(n, lambda copy: copy.wait())
            t, p = part // 2, lax.rem(part, 2) * 2

            def put(value, to):
                to[ring, t, pl.ds(p, 2)] = value.astype(jnp.bfloat16).reshape(2, 4, 2, 16, width)

            @pl.when(i < 4)
            def _wide():
                which = jnp.where(i < 3, 0, 1)
                put(mm(tile[slot], ext_rhs[which, 0, cut], NN), far_buf)
                put(mm(tile[slot], ext_rhs[which, 1, cut], NN), near_buf)

            @pl.when(i >= 4)
            def _tall():
                which = jnp.where(i < 8, 0, 1)
                put(mm(tall[slot], row_rhs[which, 0, cut], TN), far_buf)
                put(mm(tall[slot], row_rhs[which, 1, cut], TN), near_buf)

            return 0

        lax.fori_loop(0, tiles, one, 0)
        core_copy(b).start()

    def stage_one(i):
        core_copy(i).wait_recv()
        ring = lax.rem(i, 2)

        def add(j, _):
            t, p = j // 4, j % 4
            core_in[i, t, p] = core_in[i, t, p] + near_buf[ring, t, p]
            return 0

        lax.fori_loop(0, 8, add, 0)
        x1(i).start()
        y1(i).start()

    def stage_two(i):
        x1(i).wait_recv()
        y1(i).wait_recv()
        for p in range(2):
            x_in[i, p] = x_in[i, p] + core_in[i, x, p]
        for t in range(2):
            for p in range(2):
                y_in[i, t, p] = y_in[i, t, p] + core_in[i, t, 2 + p, :, y]
        y2(i).start()
        x2(i).start()

    def stage_three(i):
        y2(i).wait_recv()
        x2(i).wait_recv()
        for p in range(2):
            line[i, :, p] = x_in[i, p, :, y] + y2_in[i, p]
            line[i, :, 2 + p] = y_in[i, x, p] + x2_in[i, p]
        for n in range(1, 4):
            along(i, lax.rem(z + n, 4)).start()

    def stage_last(b):
        cut = b // BLOCKS
        total = line[b, z].astype(jnp.float32)
        for n in range(1, 4):
            zz = lax.rem(z + n, 4)
            arrival(b, zz).wait_recv()
            total += line_in[b, zz].astype(jnp.float32)
        done[cut, pl.ds(lax.rem(b, BLOCKS) * 4, 4)] = total.astype(jnp.bfloat16)

    def place(of, cut):
        start = (of % 2) * half_width + cut * width
        return out_ref.at[
            :,
            pl.ds(pl.multiple_of((of // 2) * 16, 16), 16),
            pl.ds(pl.multiple_of(start, width), width),
        ]

    def letter(to, cut):
        return pltpu.make_async_remote_copy(
            src_ref=parcel.at[cut, to],
            dst_ref=place(me, cut),
            send_sem=post.at[cut, to],
            recv_sem=mail.at[cut, me],
            device_id={"dp": to, "tensor": x},
            device_id_type=MESH,
        )

    def answer(of, cut):
        return pltpu.make_async_remote_copy(
            src_ref=parcel.at[cut, of],
            dst_ref=place(of, cut),
            send_sem=post.at[cut, of],
            recv_sem=mail.at[cut, of],
            device_id={"dp": of, "tensor": x},
            device_id_type=MESH,
        )

    def own_letter(cut):
        return pltpu.make_async_copy(parcel.at[cut, me], place(me, cut), local_sem.at[cut])

    def post_all(cut):
        done[cut, BLOCKS * 4] = jnp.zeros((16, width), done.dtype)

        def pack(n, _):
            parcel[cut, n // CAP, n % CAP] = done[cut, piece_ref[n]]
            return 0

        lax.fori_loop(0, n_dp * CAP, pack, 0)

        def post_one(i, _):
            letter(lax.rem(me + i, n_dp), cut).start()
            return 0

        lax.fori_loop(1, n_dp, post_one, 0)
        own_letter(cut).start()

    def ended(i):
        @pl.when(i >= STEPS - 2)
        def _far():
            core_copy(i).wait_send()

        x1(i).wait_send()
        y1(i).wait_send()
        y2(i).wait_send()
        x2(i).wait_send()
        for n in range(1, 4):
            along(i, lax.rem(z + n, 4)).wait_send()

    z_one = z + 1 - 2 * lax.rem(z, 2)
    z_two = lax.rem(z + 2, 4)
    partners = [
        near["core"],
        near["y"],
        near["x"],
        {"dp": (z_one * 2 + y) * 2 + core, "tensor": x},
        {"dp": (z_two * 2 + y) * 2 + core, "tensor": x},
    ]

    def swap(n):
        return pltpu.make_async_remote_copy(
            src_ref=vec_out.at[n],
            dst_ref=vec_in.at[n],
            send_sem=vec_send.at[n],
            recv_sem=vec_recv.at[n],
            device_id=partners[n],
            device_id_type=MESH,
        )

    vec_out[0] = vec_ref[...]
    produce(0)

    def step(s, _):
        @pl.when(s + 1 < STEPS)
        def _produce():
            produce(s + 1)

        @pl.when(s < STEPS)
        def _one():
            stage_one(s)

        @pl.when((s >= LAG) & (s < STEPS + LAG))
        def _two():
            stage_two(s - LAG)

        @pl.when((s >= 2 * LAG) & (s < STEPS + 2 * LAG))
        def _three():
            stage_three(s - 2 * LAG)

        @pl.when(s >= 3 * LAG)
        def _last():
            stage_last(s - 3 * LAG)

        for cut in range(SLICES):

            @pl.when(s - 3 * LAG == cut * BLOCKS + BLOCKS - 1)
            def _post():
                post_all(cut)

        for n in range(5):

            @pl.when(s == n)
            def _begin():
                swap(n).start()

            @pl.when(s == n + 1)
            def _end():
                swap(n).wait()
                if n < 4:
                    vec_out[n + 1] = vec_out[n] + vec_in[n]
                else:
                    sum_ref[...] = vec_out[n] + vec_in[n]

        return 0

    lax.fori_loop(0, STEPS + 3 * LAG, step, 0)

    def finish(i, _):
        ended(i)
        return 0

    lax.fori_loop(0, STEPS, finish, 0)

    def mail_one(i, _):
        for cut in range(SLICES):
            answer(lax.rem(me + i, n_dp), cut).wait_recv()
            letter(lax.rem(me + i, n_dp), cut).wait_send()
        return 0

    lax.fori_loop(1, n_dp, mail_one, 0)
    for cut in range(SLICES):
        own_letter(cut).wait()


def reduce_grads(piece_of, vec, qkv, context, pre, hidden, tokens, ext_grads, normed, two):
    n_dp = piece_of.shape[0] // CAP
    low = jnp.bfloat16
    width = D // 2 // SLICES
    rows = 256
    ext = tokens.shape[0]
    length = normed.shape[0]
    anywhere = pl.BlockSpec(memory_space=pl.ANY)
    vmem = pl.BlockSpec(memory_space=pltpu.VMEM)
    return pl.pallas_call(
        reduce_kernel,
        out_shape=(
            jax.ShapeDtypeStruct((CAP, 128, D), low),
            jax.ShapeDtypeStruct(vec.shape, jnp.float32),
        ),
        in_specs=[pl.BlockSpec(memory_space=pltpu.SMEM), vmem] + [anywhere] * 8,
        out_specs=(anywhere, vmem),
        scratch_shapes=[
            pltpu.VMEM((2, rows, ext), low),
            pltpu.VMEM((2, length, rows), low),
            pltpu.VMEM((2, 2, SLICES, ext, width), low),
            pltpu.VMEM((2, 2, SLICES, length, width), low),
            pltpu.VMEM((2, 2, 4, 4, 2, 16, width), low),
            pltpu.VMEM((2, 2, 4, 4, 2, 16, width), low),
            pltpu.VMEM((STEPS, 2, 4, 4, 2, 16, width), low),
            pltpu.VMEM((STEPS, 2, 4, 2, 16, width), low),
            pltpu.VMEM((STEPS, 2, 2, 4, 16, width), low),
            pltpu.VMEM((STEPS, 2, 4, 16, width), low),
            pltpu.VMEM((STEPS, 2, 4, 16, width), low),
            pltpu.VMEM((STEPS, 4, 4, 16, width), low),
            pltpu.VMEM((STEPS, 4, 4, 16, width), low),
            pltpu.VMEM((SLICES, BLOCKS * 4 + 1, 16, width), low),
            pltpu.VMEM((SLICES, n_dp, CAP, 16, width), low),
            pltpu.VMEM((5,) + vec.shape, jnp.float32),
            pltpu.VMEM((5,) + vec.shape, jnp.float32),
            pltpu.SemaphoreType.DMA((2,)),
            pltpu.SemaphoreType.DMA((4, 2, SLICES)),
            pltpu.SemaphoreType.DMA((SLICES,)),
            pltpu.SemaphoreType.DMA((SLICES, n_dp)),
            pltpu.SemaphoreType.DMA((SLICES, n_dp)),
            pltpu.SemaphoreType.DMA((9, STEPS)),
            pltpu.SemaphoreType.DMA((9, STEPS)),
            pltpu.SemaphoreType.DMA((5,)),
            pltpu.SemaphoreType.DMA((5,)),
        ],
        compiler_params=pltpu.CompilerParams(
            collective_id=2, has_side_effects=True, vmem_limit_bytes=60 * 2**20
        ),
        cost_estimate=pl.CostEstimate(
            flops=31 * 10**9, bytes_accessed=50 * 10**6, transcendentals=0
        ),
        name="reduce_grads",
    )(piece_of, vec, qkv, context, pre, hidden, tokens, ext_grads, normed, two)


def coordinates():
    dp = lax.axis_index("dp")
    return dp // 4, (dp // 2) % 2, dp % 2, lax.axis_index("tensor")


def exchange(values, axis):
    if axis == "x":
        return lax.ppermute(values, "tensor", [(0, 1), (1, 0)])
    flip = {"core": 1, "y": 2, "z_near": 4, "z_far": 8}[axis]
    return lax.ppermute(values, "dp", [(i, i ^ flip) for i in range(lax.axis_size("dp"))])


def pick(values, index, axis):
    return lax.dynamic_index_in_dim(values, index, axis, keepdims=False)


def on_device_rows(
    tokens,
    segment_ids,
    key_mask,
    owners,
    master_slots,
    slot_first,
    slot_second,
    vectors,
    vector_first,
    vector_second,
    out_grad,
):
    n_dp = lax.axis_size("dp")
    n_tensor = lax.axis_size("tensor")
    half = lax.axis_index("tensor")
    every = ("tensor", "dp")
    rows = tokens.shape[0]
    ext = rows + EXT_PAD
    halo = DOC_MAX // 2
    swap = [(0, 1), (1, 0)]
    edge = jnp.where(half == 0, rows - halo, 0)
    halo_at = jnp.where(half == 0, rows, EXT_PAD - halo)
    own_at = half * EXT_PAD

    def extend(own_rows, halo_rows):
        whole = jnp.zeros((ext,) + own_rows.shape[1:], own_rows.dtype)
        whole = lax.dynamic_update_slice_in_dim(whole, halo_rows, halo_at, 0)
        return lax.dynamic_update_slice_in_dim(whole, own_rows, own_at, 0)

    def own_part(values):
        return lax.dynamic_slice_in_dim(values, own_at, rows, 0)

    def halo_part(values):
        return lax.dynamic_slice_in_dim(values, halo_at, halo, 0)

    lo, hi, qaug, kaug, hidden_keys, handled, foreign = document_plan(
        segment_ids[0], key_mask[0], half, rows
    )
    slots = slot_index(owners)
    pieces = slots.shape[0]
    piece_rows = master_slots.shape[2]
    mix_pieces = 4 * (D // n_tensor) // piece_rows
    up_pieces = (FF // n_tensor) // piece_rows
    per = mix_pieces // 4
    w_qkv, w_out, w_up, w_down, tokens_ext = gather_weights(owners[:, 0], master_slots[0], tokens)
    w_qkv = w_qkv.reshape(3 * D, D)
    w_out = w_out.reshape(D, D)
    w_up = w_up.reshape(FF, D)
    w_down = w_down.reshape(FF, D)
    bias_up = vectors[2:6].reshape(n_tensor, 4, -1).transpose(1, 0, 2).reshape(FF)

    bias_qkv = jnp.concatenate([vectors[0], jnp.zeros((D,), jnp.float32), vectors[1]])
    scale_qkv = jnp.concatenate([jnp.full((D,), HD ** (-0.5)), jnp.ones((2 * D,))])
    qkv = (
        (mm(w_qkv, tokens_ext, NT) + bias_qkv[:, None]) * scale_qkv.astype(jnp.float32)[:, None]
    ).astype(jnp.bfloat16)
    context, logs = attend(lo, hi, qkv, qaug, kaug, hidden_keys)
    attn_ext = mm(context, w_out, TN).astype(jnp.bfloat16)
    halo_attn = lax.ppermute(halo_part(attn_ext), "tensor", swap)
    attn_back = lax.dynamic_update_slice_in_dim(
        jnp.zeros((rows, D), jnp.bfloat16), halo_attn, edge, 0
    )
    attn_sum = jnp.where(foreign[:, None], attn_back, own_part(attn_ext)).astype(jnp.float32)
    residual_one = tokens.astype(jnp.float32) + (attn_sum + vectors[6])
    normal_one, inverse_one = layer_stats(residual_one)
    normed = normal_one * vectors[8] + vectors[9]
    normed_low = normed.astype(jnp.bfloat16)

    hidden, slope = feed_up(normed_low, w_up, bias_up)
    residual_two = normed + (mm(hidden, w_down, NN) + vectors[7])
    normal_two, inverse_two = layer_stats(residual_two)
    layer_out = (normal_two * vectors[10] + vectors[11]).astype(jnp.bfloat16)
    grad_out = out_grad.astype(jnp.float32)
    grad_two = norm_back(grad_out, normal_two, inverse_two, vectors[10])
    grad_two_low = grad_two.astype(jnp.bfloat16)

    grad_pre, up_sums = feed_down_back(grad_two_low, w_down, slope)
    grad_norm = grad_two + lax.optimization_barrier(mm(grad_pre, w_up, NN))
    grad_one = norm_back(grad_norm, normal_one, inverse_one, vectors[8])
    grad_one_low = grad_one.astype(jnp.bfloat16)

    halo_grad = lax.ppermute(
        lax.dynamic_slice_in_dim(grad_one_low, edge, halo, 0), "tensor", swap
    )
    grad_ext = jnp.where(handled[:, None], extend(grad_one_low, halo_grad), 0)
    grad_context = mm(w_out, grad_ext, NT).astype(jnp.bfloat16)
    grad_qkv = attend_back(lo, hi, qkv, grad_context, context, logs, qaug, kaug, hidden_keys)
    input_ext = mm(grad_qkv.reshape(3 * D, ext), w_qkv, TN)
    halo_input = lax.ppermute(halo_part(input_ext).astype(jnp.bfloat16), "tensor", swap)
    input_back = lax.dynamic_update_slice_in_dim(
        jnp.zeros((rows, D), jnp.bfloat16), halo_input, edge, 0
    )
    input_grad = (grad_one + own_part(input_ext) + input_back.astype(jnp.float32)).astype(
        jnp.bfloat16
    )

    vector_terms = jnp.concatenate(
        [
            jnp.stack(
                [
                    jnp.sum(grad_qkv[0].astype(jnp.float32), axis=1),
                    jnp.sum(grad_qkv[2].astype(jnp.float32), axis=1),
                ]
            ),
            up_sums.reshape(4, n_tensor, -1)
            .transpose(1, 0, 2)
            .reshape(FF // D, D),
            jnp.stack(
                [
                    jnp.sum(grad_one, axis=0),
                    jnp.sum(grad_two, axis=0),
                    jnp.sum(grad_norm * normal_one, axis=0),
                    jnp.sum(grad_norm, axis=0),
                    jnp.sum(grad_out * normal_two, axis=0),
                    jnp.sum(grad_out, axis=0),
                ]
            ),
        ],
        axis=0,
    )
    piece_of = jnp.full((n_dp * CAP,), pieces, jnp.int32).at[slots].set(
        jnp.arange(pieces, dtype=jnp.int32)
    )
    own_grads, vector_grads = reduce_grads(
        piece_of,
        vector_terms,
        grad_qkv,
        context,
        grad_pre,
        hidden,
        tokens_ext,
        grad_ext,
        normed_low,
        grad_two_low,
    )
    own_grads = own_grads.astype(jnp.float32)
    slot_new, slot_first_new, slot_second_new = adam_update(
        master_slots[0], slot_first[0], slot_second[0], own_grads, rate_matrix, weight_decay
    )
    vector_new, vector_first_new, vector_second_new = adam_update(
        vectors, vector_first, vector_second, vector_grads, rate_vector, 0.0
    )
    return (
        layer_out,
        input_grad,
        slot_new[None],
        slot_first_new[None],
        slot_second_new[None],
        vector_new,
        vector_first_new,
        vector_second_new,
    )


def solution(mesh):
    placed = (
        P(("dp", "tensor"), None),
        P("dp", None),
        P("dp", None),
        P(),
        P("tensor", "dp", None, None),
        P("tensor", "dp", None, None),
        P("tensor", "dp", None, None),
        P(),
        P(),
        P(),
        P(("dp", "tensor"), None),
    )
    by_rows = mesh.shape["tensor"] == 2 and mesh.shape["dp"] == 16
    return jax.shard_map(
        on_device_rows if by_rows else on_device_generic,
        mesh=mesh,
        in_specs=placed,
        out_specs=(
            P(("dp", "tensor"), None),
            P(("dp", "tensor"), None),
            P("tensor", "dp", None, None),
            P("tensor", "dp", None, None),
            P("tensor", "dp", None, None),
            P(),
            P(),
            P(),
        ),
        check_vma=False,
    )
```

```python
import functools

import jax
import jax.numpy as jnp
from jax import lax
from jax.experimental import pallas as pl
from jax.experimental.pallas import tpu as pltpu
from jax.sharding import PartitionSpec as P

D = 1024
HD = 64
FF = 4096
QBLK = 512
STEP = 10
CAP = 6


norm_eps = 1e-05
mask_fill = -1000000000.0
beta_one = 0.5
beta_two = 0.5
rate_matrix = 0.03
rate_vector = 0.1
weight_decay = 0.01
adam_eps = 1e-08


def slot_index(owners):
    owner_of = owners[:, 0]
    positions = jnp.arange(owner_of.shape[0], dtype=jnp.int32)
    earlier = (positions[None, :] < positions[:, None]) & (owner_of[None, :] == owner_of[:, None])
    within = jnp.sum(earlier.astype(jnp.int32), axis=1)
    return owner_of * CAP + within


def layer_stats(residual):
    center = residual - jnp.mean(residual, axis=-1, keepdims=True)
    spread = jnp.mean(center * center, axis=-1, keepdims=True)
    inverse = lax.rsqrt(spread + norm_eps)
    return (center * inverse, inverse)


def norm_back(grads, normal, inverse, gains):
    scaled = grads * gains
    return inverse * (
        scaled
        - jnp.mean(scaled, axis=-1, keepdims=True)
        - normal * jnp.mean(scaled * normal, axis=-1, keepdims=True)
    )


def gelu_exact(values):
    return jax.nn.gelu(values, approximate=False)


def block_mask(segment, valid, start):
    length = segment.shape[0]
    query_pos = start + jnp.arange(QBLK, dtype=jnp.int32)
    key_pos = jnp.arange(length, dtype=jnp.int32)
    query_seg = lax.dynamic_slice_in_dim(segment, start, QBLK, 0)
    same = query_seg[:, None] == segment[None, :]
    return same & ((valid[None, :] == 1) | (query_pos[:, None] == key_pos[None, :]))


def block_scores(block_q, key_rows, segment, valid, start):
    scores = jnp.einsum("qhd,khd->hqk", block_q, key_rows, preferred_element_type=jnp.float32)
    return jnp.where(block_mask(segment, valid, start)[None], scores, mask_fill)


def attend_forward(queries, key_rows, value_rows, segment, valid):
    length = queries.shape[0]

    def one_block(index):
        start = index * QBLK
        block_q = lax.dynamic_slice_in_dim(queries, start, QBLK, 0)
        scores = block_scores(block_q, key_rows, segment, valid, start)
        row_max = jnp.max(scores, axis=2, keepdims=True)
        raised = jnp.exp(scores - row_max)
        totals = jnp.sum(raised, axis=2, keepdims=True)
        weights = (raised / totals).astype(jnp.bfloat16)
        context = jnp.einsum(
            "hqk,khd->qhd", weights, value_rows, preferred_element_type=jnp.float32
        )
        return (context, (row_max + jnp.log(totals))[:, :, 0])

    context, log_sums = lax.map(one_block, jnp.arange(length // QBLK, dtype=jnp.int32))
    return (context.reshape(length, -1), log_sums)


def attend_backward(queries, key_rows, value_rows, segment, valid, log_sums, grad_context):
    length = queries.shape[0]

    def one_block(carry, index):
        key_acc, value_acc = carry
        start = index * QBLK
        block_q = lax.dynamic_slice_in_dim(queries, start, QBLK, 0)
        block_g = lax.dynamic_slice_in_dim(grad_context, start, QBLK, 0)
        scores = block_scores(block_q, key_rows, segment, valid, start)
        weights = jnp.exp(scores - log_sums[index][:, :, None])
        value_acc = value_acc + jnp.einsum(
            "hqk,qhd->khd",
            weights.astype(jnp.bfloat16),
            block_g,
            preferred_element_type=jnp.float32,
        )
        grad_weights = jnp.einsum(
            "qhd,khd->hqk", block_g, value_rows, preferred_element_type=jnp.float32
        )
        inner = jnp.sum(weights * grad_weights, axis=2, keepdims=True)
        grad_scores = (weights * (grad_weights - inner)).astype(jnp.bfloat16)
        grad_q = jnp.einsum(
            "hqk,khd->qhd", grad_scores, key_rows, preferred_element_type=jnp.float32
        )
        key_acc = key_acc + jnp.einsum(
            "hqk,qhd->khd", grad_scores, block_q, preferred_element_type=jnp.float32
        )
        return ((key_acc, value_acc), grad_q)

    zeros_kv = jnp.zeros(key_rows.shape, jnp.float32)
    (grad_keys, grad_values), grad_queries = lax.scan(
        one_block, (zeros_kv, zeros_kv), jnp.arange(length // QBLK, dtype=jnp.int32)
    )
    return (
        grad_queries.reshape(length, -1),
        grad_keys.reshape(length, -1),
        grad_values.reshape(length, -1),
    )


def adam_update(weights, first, second, grads, rate, decay):
    first_new = beta_one * first + (1.0 - beta_one) * grads
    second_new = beta_two * second + (1.0 - beta_two) * grads * grads
    first_hat = first_new / (1.0 - beta_one**STEP)
    second_hat = second_new / (1.0 - beta_two**STEP)
    updated = weights - rate * (first_hat / (jnp.sqrt(second_hat) + adam_eps) + decay * weights)
    return (updated, first_new, second_new)


def on_device_generic(
    tokens,
    segment_ids,
    key_mask,
    owners,
    master_slots,
    slot_first,
    slot_second,
    vectors,
    vector_first,
    vector_second,
    out_grad,
):
    n_tensor = lax.axis_size("tensor")
    group = lax.axis_index("tensor")
    head_cols = D // n_tensor
    unit_cols = FF // n_tensor
    heads_here = head_cols // HD
    seq_count = segment_ids.shape[0]
    length = segment_ids.shape[1]
    query_scale = HD ** (-0.5)
    slots = slot_index(owners)
    gathered_slots = lax.all_gather(master_slots[0].astype(jnp.bfloat16), "dp", axis=0, tiled=True)
    stack = jnp.take(gathered_slots, slots, axis=0).reshape(-1, D)
    w_mix = stack[0 : 3 * head_cols]
    w_out = stack[3 * head_cols : 4 * head_cols]
    w_up = stack[4 * head_cols : 4 * head_cols + unit_cols]
    w_down = stack[4 * head_cols + unit_cols :]
    bias_query = lax.dynamic_slice_in_dim(vectors[0], group * head_cols, head_cols, 0)
    bias_value = lax.dynamic_slice_in_dim(vectors[1], group * head_cols, head_cols, 0)
    bias_up = lax.dynamic_slice_in_dim(vectors[2:6].reshape(FF), group * unit_cols, unit_cols, 0)
    gathered = lax.all_gather(tokens, "tensor", axis=0, tiled=True)
    mixed = jnp.einsum("ld,kd->lk", gathered, w_mix, preferred_element_type=jnp.float32)
    queries = ((mixed[:, :head_cols] + bias_query) * query_scale).astype(jnp.bfloat16)
    key_rows = mixed[:, head_cols : 2 * head_cols].astype(jnp.bfloat16)
    value_rows = (mixed[:, 2 * head_cols :] + bias_value).astype(jnp.bfloat16)
    head_shape = (seq_count, length, heads_here, HD)
    queries_h = queries.reshape(head_shape)
    keys_h = key_rows.reshape(head_shape)
    values_h = value_rows.reshape(head_shape)

    def forward_seq(element):
        return attend_forward(element[0], element[1], element[2], element[3], element[4])

    context, log_sums = lax.map(forward_seq, (queries_h, keys_h, values_h, segment_ids, key_mask))
    context = context.reshape(-1, head_cols).astype(jnp.bfloat16)
    attn_sum = lax.psum_scatter(
        jnp.einsum("lk,kd->ld", context, w_out, preferred_element_type=jnp.float32).astype(
            jnp.bfloat16
        ),
        "tensor",
        scatter_dimension=0,
        tiled=True,
    ).astype(jnp.float32)
    residual_one = tokens.astype(jnp.float32) + (attn_sum + vectors[6])
    normal_one, inverse_one = layer_stats(residual_one)
    normed = normal_one * vectors[8] + vectors[9]
    normed_low = normed.astype(jnp.bfloat16)
    norm_rows = lax.all_gather(normed_low, "tensor", axis=0, tiled=True)
    hidden_pre = (
        jnp.einsum("ld,kd->lk", norm_rows, w_up, preferred_element_type=jnp.float32) + bias_up
    )
    hidden_full, gelu_pull = jax.vjp(gelu_exact, hidden_pre)
    hidden = hidden_full.astype(jnp.bfloat16)
    mlp_sum = lax.psum_scatter(
        jnp.einsum("lk,kd->ld", hidden, w_down, preferred_element_type=jnp.float32).astype(
            jnp.bfloat16
        ),
        "tensor",
        scatter_dimension=0,
        tiled=True,
    ).astype(jnp.float32)
    residual_two = normed + (mlp_sum + vectors[7])
    normal_two, inverse_two = layer_stats(residual_two)
    layer_out = (normal_two * vectors[10] + vectors[11]).astype(jnp.bfloat16)
    grad_out = out_grad.astype(jnp.float32)
    grad_two = norm_back(grad_out, normal_two, inverse_two, vectors[10])
    grad_down_in = lax.all_gather(grad_two.astype(jnp.bfloat16), "tensor", axis=0, tiled=True)
    grad_hidden = jnp.einsum("ld,kd->lk", grad_down_in, w_down, preferred_element_type=jnp.float32)
    grad_w_down = jnp.einsum("lk,ld->kd", hidden, grad_down_in, preferred_element_type=jnp.float32)
    grad_pre = gelu_pull(grad_hidden)[0].astype(jnp.bfloat16)
    norm_back_rows = lax.all_gather(normed_low, "tensor", axis=0, tiled=True)
    grad_w_up = jnp.einsum(
        "lk,ld->kd", grad_pre, norm_back_rows, preferred_element_type=jnp.float32
    )
    grad_norm = grad_two + lax.psum_scatter(
        jnp.einsum("lk,kd->ld", grad_pre, w_up, preferred_element_type=jnp.float32).astype(
            jnp.bfloat16
        ),
        "tensor",
        scatter_dimension=0,
        tiled=True,
    ).astype(jnp.float32)
    grad_one = norm_back(grad_norm, normal_one, inverse_one, vectors[8])
    grad_attn_in = lax.all_gather(grad_one.astype(jnp.bfloat16), "tensor", axis=0, tiled=True)
    grad_context = jnp.einsum(
        "ld,kd->lk", grad_attn_in, w_out, preferred_element_type=jnp.float32
    ).astype(jnp.bfloat16)
    grad_w_out = jnp.einsum("lk,ld->kd", context, grad_attn_in, preferred_element_type=jnp.float32)

    def backward_seq(element):
        return attend_backward(
            element[0], element[1], element[2], element[3], element[4], element[5], element[6]
        )

    grad_q, grad_k, grad_v = lax.map(
        backward_seq,
        (
            queries_h,
            keys_h,
            values_h,
            segment_ids,
            key_mask,
            log_sums,
            grad_context.reshape(head_shape),
        ),
    )
    grad_queries = grad_q.reshape(-1, head_cols).astype(jnp.bfloat16) * query_scale
    grad_keys = grad_k.reshape(-1, head_cols).astype(jnp.bfloat16)
    grad_values = grad_v.reshape(-1, head_cols).astype(jnp.bfloat16)
    grad_mix = jnp.concatenate([grad_queries, grad_keys, grad_values], axis=1)
    mix_back_rows = lax.all_gather(tokens, "tensor", axis=0, tiled=True)
    grad_w_mix = jnp.einsum(
        "lk,ld->kd", grad_mix, mix_back_rows, preferred_element_type=jnp.float32
    )
    input_grad = (
        grad_one
        + lax.psum_scatter(
            jnp.einsum("lk,kd->ld", grad_mix, w_mix, preferred_element_type=jnp.float32).astype(
                jnp.bfloat16
            ),
            "tensor",
            scatter_dimension=0,
            tiled=True,
        ).astype(jnp.float32)
    ).astype(jnp.bfloat16)
    query_full = lax.dynamic_update_slice_in_dim(
        jnp.zeros((D,), jnp.float32),
        jnp.sum(grad_queries.astype(jnp.float32), axis=0),
        group * head_cols,
        0,
    )
    value_full = lax.dynamic_update_slice_in_dim(
        jnp.zeros((D,), jnp.float32),
        jnp.sum(grad_values.astype(jnp.float32), axis=0),
        group * head_cols,
        0,
    )
    up_full = lax.dynamic_update_slice_in_dim(
        jnp.zeros((FF,), jnp.float32),
        jnp.sum(grad_pre.astype(jnp.float32), axis=0),
        group * unit_cols,
        0,
    )
    tail_rows = jnp.stack(
        [
            jnp.sum(grad_one, axis=0),
            jnp.sum(grad_two, axis=0),
            jnp.sum(grad_norm * normal_one, axis=0),
            jnp.sum(grad_norm, axis=0),
            jnp.sum(grad_out * normal_two, axis=0),
            jnp.sum(grad_out, axis=0),
        ]
    )
    vector_terms = jnp.concatenate(
        [jnp.stack([query_full, value_full]), up_full.reshape(FF // D, D), tail_rows], axis=0
    )
    vector_grads = lax.psum(vector_terms, ("dp", "tensor"))
    grad_stack = jnp.concatenate([grad_w_mix, grad_w_out, grad_w_up, grad_w_down], axis=0)
    grad_pieces = grad_stack.reshape(slots.shape[0], -1, D)
    spread_slots = (
        jnp.zeros((lax.axis_size("dp") * CAP,) + grad_pieces.shape[1:], jnp.float32)
        .at[slots]
        .set(grad_pieces)
    )
    own_grads = lax.psum_scatter(
        spread_slots.astype(jnp.bfloat16), "dp", scatter_dimension=0, tiled=True
    ).astype(jnp.float32)
    slot_new, slot_first_new, slot_second_new = adam_update(
        master_slots[0], slot_first[0], slot_second[0], own_grads, rate_matrix, weight_decay
    )
    vector_new, vector_first_new, vector_second_new = adam_update(
        vectors, vector_first, vector_second, vector_grads, rate_vector, 0.0
    )
    return (
        layer_out,
        input_grad,
        slot_new[None],
        slot_first_new[None],
        slot_second_new[None],
        vector_new,
        vector_first_new,
        vector_second_new,
    )


DOC_MAX = 800
EXT_PAD = 512
ABLK = 256
FINE = 128
HPG = 8
AUG = 16
neg_big = -1000000000.0
NN = (((1,), (0,)), ((), ()))
NT = (((1,), (1,)), ((), ()))
TN = (((0,), (0,)), ((), ()))


def mm(a, b, dims):
    return lax.dot_general(a, b, dims, preferred_element_type=jnp.float32)


def attn_fwd_kernel(lo_ref, hi_ref, q_ref, k_ref, v_ref, qaug_ref, kaug_ref, hid_ref, o_ref, lse_ref, kn_ref, m_ref, acc_ref):
    ext = q_ref.shape[1]
    ones = jnp.concatenate(
        [jnp.ones((1, ABLK), jnp.float32), jnp.zeros((AUG - 1, ABLK), jnp.float32)], axis=0
    ).astype(jnp.bfloat16)
    for h in range(HPG):
        rows = slice(h * HD, (h + 1) * HD)
        kn_ref[h] = jnp.concatenate([k_ref[rows, :], kaug_ref[...]], axis=0).T

    def query_block(qb, _):
        lo = lo_ref[qb]
        hi = hi_ref[qb]
        qs = pl.ds(pl.multiple_of(qb * ABLK, ABLK), ABLK)

        @pl.when(hi > lo)
        def _work():
            hidden = hid_ref[0:1, qs]
            for h in range(HPG):
                rows = slice(h * HD, (h + 1) * HD)
                q32 = q_ref[rows, qs].astype(jnp.float32)
                k32 = k_ref[rows, qs].astype(jnp.float32)
                own = jnp.sum(q32 * k32, axis=0, keepdims=True)
                m_ref[h] = jnp.where(hidden > 0.0, own, -1e30)
                acc_ref[h, 0:HD, :] = v_ref[rows, qs].astype(jnp.float32) * hidden
                acc_ref[h, HD:, :] = jnp.broadcast_to(hidden, (AUG, ABLK))

            blocks = (hi - lo + 1) // 2
            origin = jnp.maximum(hi - 2 * blocks, 0) * FINE

            def key_block(kb, _):
                ks = pl.ds(pl.multiple_of(origin + kb * ABLK, FINE), ABLK)
                heads = [slice(h * HD, (h + 1) * HD) for h in range(HPG)]
                scores = [
                    mm(kn_ref[h, ks, :], jnp.concatenate([q_ref[heads[h], qs], qaug_ref[:, qs]], axis=0), NN)
                    for h in range(HPG)
                ]
                olds = [m_ref[h] for h in range(HPG)]
                news = [
                    jnp.maximum(olds[h], jnp.max(scores[h], axis=0, keepdims=True)) for h in range(HPG)
                ]
                raised = [jnp.exp(scores[h] - news[h]).astype(jnp.bfloat16) for h in range(HPG)]
                for h in range(HPG):
                    m_ref[h] = news[h]
                    va = jnp.concatenate([v_ref[heads[h], ks], ones], axis=0)
                    acc_ref[h] = acc_ref[h] * jnp.exp(olds[h] - news[h]) + mm(va, raised[h], NN)
                return 0

            lax.fori_loop(0, blocks, key_block, 0)
            for h in range(HPG):
                rows = slice(h * HD, (h + 1) * HD)
                total = acc_ref[h, HD : HD + 1, :]
                o_ref[rows, qs] = (acc_ref[h, 0:HD, :] * (1.0 / total)).astype(jnp.bfloat16)
                lse_ref[0, h : h + 1, qs] = m_ref[h] + jnp.log(total)

        @pl.when(hi <= lo)
        def _skip():
            o_ref[:, qs] = jnp.zeros((HPG * HD, ABLK), jnp.bfloat16)
            lse_ref[0, :, qs] = jnp.zeros((8, ABLK), jnp.float32)

        return 0

    lax.fori_loop(0, ext // ABLK, query_block, 0)


def attn_bwd_kernel(
    lo_ref, hi_ref, q_ref, k_ref, v_ref, g_ref, c_ref, lse_ref, qaug_ref, kaug_ref, hid_ref,
    out_ref, kn_ref, vn_ref, acc_ref, dk_acc, dv_acc,
):
    ext = q_ref.shape[1]
    for h in range(HPG):
        rows = slice(h * HD, (h + 1) * HD)
        kn_ref[h] = jnp.concatenate([k_ref[rows, :], kaug_ref[...]], axis=0).T
        vn_ref[h] = v_ref[rows, :].T
    dk_acc[...] = jnp.zeros_like(dk_acc)
    dv_acc[...] = jnp.zeros_like(dv_acc)

    def query_block(qb, _):
        lo = lo_ref[qb]
        hi = hi_ref[qb]
        qs = pl.ds(pl.multiple_of(qb * ABLK, ABLK), ABLK)

        @pl.when(hi > lo)
        def _work():
            hidden = hid_ref[0:1, qs]
            deltas = []
            logs = []
            for h in range(HPG):
                rows = slice(h * HD, (h + 1) * HD)
                q32 = q_ref[rows, qs].astype(jnp.float32)
                k32 = k_ref[rows, qs].astype(jnp.float32)
                v32 = v_ref[rows, qs].astype(jnp.float32)
                g32 = g_ref[rows, qs].astype(jnp.float32)
                c32 = c_ref[rows, qs].astype(jnp.float32)
                delta = jnp.sum(g32 * c32, axis=0, keepdims=True)
                log = lse_ref[0, h : h + 1, qs]
                own = jnp.sum(q32 * k32, axis=0, keepdims=True)
                p_own = jnp.where(hidden > 0.0, jnp.exp(own - log), 0.0)
                d_own = p_own * (jnp.sum(g32 * v32, axis=0, keepdims=True) - delta)
                acc_ref[h] = d_own * k32
                dk_acc[rows, qs] += d_own * q32
                dv_acc[rows, qs] += p_own * g32
                deltas.append(delta)
                logs.append(log)

            blocks = (hi - lo + 1) // 2
            origin = jnp.maximum(hi - 2 * blocks, 0) * FINE

            def key_block(kb, _):
                ks = pl.ds(pl.multiple_of(origin + kb * ABLK, FINE), ABLK)
                heads = [slice(h * HD, (h + 1) * HD) for h in range(HPG)]
                every = range(HPG)
                qs_h = [q_ref[heads[h], qs] for h in every]
                gs_h = [g_ref[heads[h], qs] for h in every]
                scores = [
                    mm(kn_ref[h, ks, :], jnp.concatenate([qs_h[h], qaug_ref[:, qs]], axis=0), NN)
                    for h in every
                ]
                grads = [mm(vn_ref[h, ks, :], gs_h[h], NN) for h in every]
                weights = [jnp.exp(scores[h] - logs[h]) for h in every]
                low = [weights[h].astype(jnp.bfloat16) for h in every]
                back = [
                    (weights[h] * (grads[h] - deltas[h])).astype(jnp.bfloat16) for h in every
                ]
                v_new = [mm(gs_h[h], low[h], NT) for h in every]
                k_new = [mm(qs_h[h], back[h], NT) for h in every]
                q_new = [mm(k_ref[heads[h], ks], back[h], NN) for h in every]
                for h in every:
                    dv_acc[heads[h], ks] += v_new[h]
                    dk_acc[heads[h], ks] += k_new[h]
                    acc_ref[h] += q_new[h]
                return 0

            lax.fori_loop(0, blocks, key_block, 0)
            for h in range(HPG):
                rows = slice(h * HD, (h + 1) * HD)
                out_ref[0, rows, qs] = acc_ref[h].astype(jnp.bfloat16) * (HD ** (-0.5))

        @pl.when(hi <= lo)
        def _skip():
            out_ref[0, :, qs] = jnp.zeros((HPG * HD, ABLK), jnp.bfloat16)

        return 0

    lax.fori_loop(0, ext // ABLK, query_block, 0)
    out_ref[1] = dk_acc[...].astype(jnp.bfloat16)
    out_ref[2] = dv_acc[...].astype(jnp.bfloat16)


def group_block(offset, rows, ext):
    return pl.BlockSpec((rows, ext), lambda g, lo, hi: (offset + g, 0))


def fixed_block(rows, ext):
    return pl.BlockSpec((rows, ext), lambda g, lo, hi: (0, 0))


def attend(lo, hi, qkv, qaug, kaug, hidden):
    ext = qkv.shape[1]
    groups = D // HD // HPG
    rows = HPG * HD
    return pl.pallas_call(
        attn_fwd_kernel,
        out_shape=(
            jax.ShapeDtypeStruct((D, ext), jnp.bfloat16),
            jax.ShapeDtypeStruct((groups, 8, ext), jnp.float32),
        ),
        grid_spec=pltpu.PrefetchScalarGridSpec(
            num_scalar_prefetch=2,
            grid=(groups,),
            in_specs=[
                group_block(0, rows, ext),
                group_block(groups, rows, ext),
                group_block(2 * groups, rows, ext),
                fixed_block(AUG, ext),
                fixed_block(AUG, ext),
                fixed_block(8, ext),
            ],
            out_specs=[
                group_block(0, rows, ext),
                pl.BlockSpec((1, 8, ext), lambda g, lo, hi: (g, 0, 0)),
            ],
            scratch_shapes=[
                pltpu.VMEM((HPG, ext, HD + AUG), jnp.bfloat16),
                pltpu.VMEM((HPG, 1, ABLK), jnp.float32),
                pltpu.VMEM((HPG, HD + AUG, ABLK), jnp.float32),
            ],
        ),
        compiler_params=pltpu.CompilerParams(vmem_limit_bytes=40 * 2**20),
        cost_estimate=pl.CostEstimate(flops=20 * 10**9, bytes_accessed=14 * 10**6, transcendentals=0),
        name="attend",
    )(lo, hi, qkv, qkv, qkv, qaug, kaug, hidden)


def attend_back(lo, hi, qkv, grads, context, logs, qaug, kaug, hidden):
    ext = qkv.shape[1]
    groups = D // HD // HPG
    rows = HPG * HD
    return pl.pallas_call(
        attn_bwd_kernel,
        out_shape=jax.ShapeDtypeStruct((3, D, ext), jnp.bfloat16),
        grid_spec=pltpu.PrefetchScalarGridSpec(
            num_scalar_prefetch=2,
            grid=(groups,),
            in_specs=[
                group_block(0, rows, ext),
                group_block(groups, rows, ext),
                group_block(2 * groups, rows, ext),
                group_block(0, rows, ext),
                group_block(0, rows, ext),
                pl.BlockSpec((1, 8, ext), lambda g, lo, hi: (g, 0, 0)),
                fixed_block(AUG, ext),
                fixed_block(AUG, ext),
                fixed_block(8, ext),
            ],
            out_specs=pl.BlockSpec((3, rows, ext), lambda g, lo, hi: (0, g, 0)),
            scratch_shapes=[
                pltpu.VMEM((HPG, ext, HD + AUG), jnp.bfloat16),
                pltpu.VMEM((HPG, ext, HD), jnp.bfloat16),
                pltpu.VMEM((HPG, HD, ABLK), jnp.float32),
                pltpu.VMEM((rows, ext), jnp.float32),
                pltpu.VMEM((rows, ext), jnp.float32),
            ],
        ),
        compiler_params=pltpu.CompilerParams(vmem_limit_bytes=48 * 2**20),
        cost_estimate=pl.CostEstimate(flops=50 * 10**9, bytes_accessed=30 * 10**6, transcendentals=0),
        name="attend_back",
    )(lo, hi, qkv, qkv, qkv, grads, context, logs, qaug, kaug, hidden)


def document_plan(segment, valid, half, rows):
    length = segment.shape[0]
    ext = rows + EXT_PAD
    base = half * EXT_PAD
    position = jnp.arange(length, dtype=jnp.int32)
    documents = jnp.arange(8, dtype=jnp.int32)[:, None]
    one_hot = segment[None, :] == documents
    counts = jnp.sum(one_hot.astype(jnp.int32), axis=1, keepdims=True)
    starts = jnp.sum((segment[None, :] < documents).astype(jnp.int32), axis=1, keepdims=True)
    start = jnp.sum(jnp.where(one_hot, starts, 0), axis=0)
    end = jnp.sum(jnp.where(one_hot, starts + counts, 0), axis=0)
    crossing = (start < rows) & (end > rows)
    left = jnp.max(jnp.where(crossing, rows - start, 0))
    right = jnp.max(jnp.where(crossing, end - rows, 0))
    in_left = position < rows
    work = jnp.where(crossing, 0, end - start)
    left_work = jnp.sum(jnp.where(in_left, work, 0))
    right_work = jnp.sum(jnp.where(in_left, 0, work))
    both_fit = (left <= DOC_MAX // 2) & (right <= DOC_MAX // 2)
    second = jnp.where(both_fit, right_work <= left_work, left <= right)
    worker = jnp.where(second, half == 1, half == 0)
    own = (position >= half * rows) & (position < (half + 1) * rows)
    handled = jnp.where(crossing, worker, own)
    cut = lambda values: lax.dynamic_slice_in_dim(values, base, ext, 0)
    handled_ext = cut(handled)
    begins = jnp.where(handled_ext, cut(start) - base, ext).reshape(-1, ABLK)
    ends = jnp.where(handled_ext, cut(end) - base, 0).reshape(-1, ABLK)
    lo = jnp.min(begins, axis=1) // FINE
    hi = (jnp.max(ends, axis=1) + (FINE - 1)) // FINE
    blank = jnp.max(ends, axis=1) == 0
    lo = jnp.where(blank, 0, lo)
    hi = jnp.where(blank, 0, hi)
    hot = cut(one_hot.T).T
    masked = cut(valid) == 0
    ones = jnp.ones((1, ext), jnp.bfloat16)
    fill = jnp.zeros((AUG - 9, ext), jnp.bfloat16)
    qaug = jnp.concatenate([hot.astype(jnp.bfloat16), ones, fill], axis=0)
    kaug = jnp.concatenate(
        [
            jnp.where(hot, 0.0, neg_big).astype(jnp.bfloat16),
            jnp.where(masked[None, :], neg_big, 0.0).astype(jnp.bfloat16),
            fill,
        ],
        axis=0,
    )
    hidden = jnp.broadcast_to(masked.astype(jnp.float32)[None, :], (8, ext))
    foreign = lax.dynamic_slice_in_dim(crossing & ~worker, half * rows, rows, 0)
    return lo, hi, qaug, kaug, hidden, handled_ext, foreign


def normal_parts(values):
    bell = jnp.exp(values * values * -0.5)
    return (0.5 + 0.5 * lax.erf(values * 0.7071067811865476), bell * 0.3989422804014327)


UNITS = 1024
STRIP = 512


def up_kernel(x_ref, w_ref, bias_ref, gelu_ref, slope_ref):
    for r in range(0, x_ref.shape[0], STRIP):
        strip = slice(r, r + STRIP)
        values = mm(x_ref[strip, :], w_ref[...], NT) + bias_ref[...]
        cdf, bell = normal_parts(values)
        gelu_ref[strip, :] = (values * cdf).astype(jnp.bfloat16)
        slope_ref[strip, :] = (cdf + values * bell).astype(jnp.bfloat16)


def feed_up(rows, weights, bias):
    length = rows.shape[0]
    units = weights.shape[0]
    out = jax.ShapeDtypeStruct((length, units), jnp.bfloat16)
    columns = pl.BlockSpec((length, UNITS), lambda n: (0, n))
    return pl.pallas_call(
        up_kernel,
        out_shape=(out, out),
        grid=(units // UNITS,),
        in_specs=[
            pl.BlockSpec((length, D), lambda n: (0, 0)),
            pl.BlockSpec((UNITS, D), lambda n: (n, 0)),
            pl.BlockSpec((1, UNITS), lambda n: (0, n)),
        ],
        out_specs=(columns, columns),
        compiler_params=pltpu.CompilerParams(vmem_limit_bytes=40 * 2**20),
        cost_estimate=pl.CostEstimate(
            flops=2 * length * units * D, bytes_accessed=26 * 10**6, transcendentals=0
        ),
        name="feed_up",
    )(rows, weights, bias.reshape(1, units))


def down_back_kernel(g_ref, w_ref, slope_ref, out_ref, sum_ref):
    total = jnp.zeros((1, UNITS), jnp.float32)
    for r in range(0, g_ref.shape[0], STRIP):
        strip = slice(r, r + STRIP)
        grads = mm(g_ref[strip, :], w_ref[...], NT) * slope_ref[strip, :].astype(jnp.float32)
        low = grads.astype(jnp.bfloat16)
        out_ref[strip, :] = low
        total += jnp.sum(low.astype(jnp.float32), axis=0, keepdims=True)
    sum_ref[...] = total


def feed_down_back(grads, weights, slope):
    length = grads.shape[0]
    units = weights.shape[0]
    columns = pl.BlockSpec((length, UNITS), lambda n: (0, n))
    one_row = pl.BlockSpec((1, UNITS), lambda n: (0, n))
    return pl.pallas_call(
        down_back_kernel,
        out_shape=(
            jax.ShapeDtypeStruct((length, units), jnp.bfloat16),
            jax.ShapeDtypeStruct((1, units), jnp.float32),
        ),
        grid=(units // UNITS,),
        in_specs=[
            pl.BlockSpec((length, D), lambda n: (0, 0)),
            pl.BlockSpec((UNITS, D), lambda n: (n, 0)),
            columns,
        ],
        out_specs=(columns, one_row),
        compiler_params=pltpu.CompilerParams(vmem_limit_bytes=40 * 2**20),
        cost_estimate=pl.CostEstimate(
            flops=2 * length * units * D, bytes_accessed=26 * 10**6, transcendentals=0
        ),
        name="feed_down_back",
    )(grads, weights, slope)


MESH = pl.DeviceIdType.MESH
CHUNKS = 3
GROUPS = ((0, 3), (3, 1), (4, 4))
PARTS = (((0, 1), (1, 2)), ((0, 1), None), ((0, 2), (2, 2)))


def neighbours(z, y, core, x):
    def at(z, y, core, x):
        return {"dp": (z * 2 + y) * 2 + core, "tensor": x}

    return {
        "x": at(z, y, core, 1 - x),
        "y": at(z, 1 - y, core, x),
        "core": at(z, y, 1 - core, x),
        "up": at(jnp.minimum(z + 1, 3), y, core, x),
        "down": at(jnp.maximum(z - 1, 0), y, core, x),
    }


def greet(near, z):
    barrier = pltpu.get_barrier_semaphore()
    for name in ("x", "y", "core"):
        pl.semaphore_signal(barrier, inc=1, device_id=near[name], device_id_type=MESH)

    @pl.when(z < 3)
    def _up():
        pl.semaphore_signal(barrier, inc=1, device_id=near["up"], device_id_type=MESH)

    @pl.when(z > 0)
    def _down():
        pl.semaphore_signal(barrier, inc=1, device_id=near["down"], device_id_type=MESH)

    at_end = jnp.where((z == 0) | (z == 3), 1, 0)
    pl.semaphore_wait(barrier, 5 - at_end)


def greet_all(near, me, n_dp):
    barrier = pltpu.get_barrier_semaphore()
    pl.semaphore_signal(barrier, inc=1, device_id=near["x"], device_id_type=MESH)

    def one(i, _):
        other = {"dp": lax.rem(me + i, n_dp), "tensor": lax.axis_index("tensor")}
        pl.semaphore_signal(barrier, inc=1, device_id=other, device_id_type=MESH)
        return 0

    lax.fori_loop(1, n_dp, one, 0)
    pl.semaphore_wait(barrier, n_dp)


def gather_kernel(
    owners_ref, slots_ref, tokens_ref, qkv_ref, out_ref, up_ref, down_ref, ext_ref,
    slot_ref, low_ref, spread_ref, dense_ref, zero_ref, local_sem, own_sem, ext_sem, post, mail, send, recv, halo_send, halo_recv,
):
    z, y, core, x = coordinates()
    near = neighbours(z, y, core, x)
    width = D // 2
    me = lax.axis_index("dp")
    n_dp = low_ref.shape[0]
    for to in range(n_dp):
        lines = slice((to // 2) * 16, (to // 2) * 16 + 16)
        columns = slice((to % 2) * width, (to % 2) * width + width)
        low_ref[to] = slots_ref[:, lines, columns].astype(low_ref.dtype)
    greet_all(near, me, n_dp)

    def letter(to):
        return pltpu.make_async_remote_copy(
            src_ref=low_ref.at[to],
            dst_ref=spread_ref.at[pl.ds(me * CAP, CAP)],
            send_sem=post.at[to],
            recv_sem=mail.at[me],
            device_id={"dp": to, "tensor": x},
            device_id_type=MESH,
        )

    def answer(of):
        return pltpu.make_async_remote_copy(
            src_ref=low_ref.at[of],
            dst_ref=spread_ref.at[pl.ds(of * CAP, CAP)],
            send_sem=post.at[of],
            recv_sem=mail.at[of],
            device_id={"dp": of, "tensor": x},
            device_id_type=MESH,
        )

    def peer(i):
        return lax.rem(me + i, n_dp)

    def post_one(i, _):
        letter(peer(i)).start()
        return 0

    lax.fori_loop(1, n_dp, post_one, 0)

    rows = tokens_ref.shape[0]
    halo = DOC_MAX // 2
    blank = zero_ref.shape[0]
    zero_ref[...] = jnp.zeros_like(zero_ref)
    edge = pl.multiple_of(jnp.where(x == 0, rows - halo, 0), 16)
    there = pl.multiple_of(jnp.where(x == 0, EXT_PAD - halo, rows), 16)
    rest = pl.multiple_of(jnp.where(x == 0, rows + halo, 0), 16)
    border = pltpu.make_async_remote_copy(
        src_ref=tokens_ref.at[pl.ds(edge, halo)],
        dst_ref=ext_ref.at[pl.ds(there, halo)],
        send_sem=halo_send,
        recv_sem=halo_recv,
        device_id=near["x"],
        device_id_type=MESH,
    )
    border.start()
    inside = pltpu.make_async_copy(
        tokens_ref, ext_ref.at[pl.ds(pl.multiple_of(x * EXT_PAD, 16), rows)], ext_sem.at[0]
    )
    inside.start()
    empty = pltpu.make_async_copy(zero_ref, ext_ref.at[pl.ds(rest, blank)], ext_sem.at[1])
    empty.start()
    mine = pltpu.make_async_copy(low_ref.at[me], spread_ref.at[pl.ds(me * CAP, CAP)], local_sem)
    mine.start()
    mine.wait()

    def find(p, _):
        owner = owners_ref[p]

        def count(q, before):
            return before + jnp.where(owners_ref[q] == owner, 1, 0)

        slot_ref[p] = owner * CAP + lax.fori_loop(0, p, count, 0)
        return 0

    lax.fori_loop(0, owners_ref.shape[0], find, 0)

    def mail_one(i, _):
        answer(peer(i)).wait_recv()
        letter(peer(i)).wait_send()
        return 0

    lax.fori_loop(1, n_dp, mail_one, 0)

    def place(p, _):
        dense_ref[p // 4, p % 4] = spread_ref[slot_ref[p]]
        return 0

    lax.fori_loop(0, owners_ref.shape[0], place, 0)
    rest_groups = pl.ds(GROUPS[-1][0] + GROUPS[-1][1], 4)
    later = pltpu.make_async_copy(dense_ref.at[rest_groups], down_ref, local_sem)
    later.start()
    later.wait()

    def block(k, t, zz, yy, cc, part=None):
        groups = slice(None) if part is None else pl.ds(*PARTS[k][part])
        return (qkv_ref, out_ref, up_ref)[k].at[
            groups,
            t,
            :,
            pl.ds(pl.multiple_of((zz * 2 + yy) * 16, 16), 16),
            pl.ds(pl.multiple_of(cc * width, width), width),
        ]

    own = [
        pltpu.make_async_copy(dense_ref.at[pl.ds(*GROUPS[k])], block(k, x, z, y, core), own_sem.at[k])
        for k in range(CHUNKS)
    ]
    for one in own:
        one.start()

    def copy(kind, link, k, zz, t, yy, cc, part=None, fresh=False):
        view = block(k, t, zz, yy, cc, part)
        return pltpu.make_async_remote_copy(
            src_ref=dense_ref.at[pl.ds(*GROUPS[k])] if fresh else view,
            dst_ref=view,
            send_sem=send.at[kind, k, zz],
            recv_sem=recv.at[kind, k, zz],
            device_id=near[link],
            device_id_type=MESH,
        )

    def up(k, zz, fresh=False):
        return copy(0, "up", k, zz, x, y, core, fresh=fresh)

    def down(k, zz, fresh=False):
        return copy(1, "down", k, zz, x, y, core, fresh=fresh)

    def spread(k, zz, fresh):
        copy(2, "x", k, zz, x, y, core, fresh=fresh).start()
        copy(3, "y", k, zz, x, y, core, fresh=fresh).start()
        copy(4, "core", k, zz, x, y, core, fresh=fresh).start()

    def each(d, body):
        @pl.when((d > 0) & (z - d >= 0))
        def _below():
            for k in range(CHUNKS):
                body(k, z - d, 0)

        @pl.when((d > 0) & (z + d <= 3))
        def _above():
            for k in range(CHUNKS):
                body(k, z + d, 1)

    def each_or_own(d, body):
        each(d, body)

        @pl.when(d == 0)
        def _own():
            for k in range(CHUNKS):
                body(k, z, None)

    def begin(k):
        @pl.when(z < 3)
        def _up():
            up(k, z, True).start()

        @pl.when(z > 0)
        def _down():
            down(k, z, True).start()

        spread(k, z, True)

    def first(k, zz, side):
        if side == 0:
            up(k, zz).wait_recv()

            @pl.when(z < 3)
            def _up():
                up(k, zz).start()

        else:
            down(k, zz).wait_recv()

            @pl.when(z > 0)
            def _on():
                down(k, zz).start()

        spread(k, zz, False)

    def second(k, zz, side):
        copy(2, "x", k, zz, 1 - x, y, core).wait_recv()
        copy(5, "y", k, zz, 1 - x, y, core, 0).start()
        copy(7, "core", k, zz, 1 - x, y, core).start()
        copy(3, "y", k, zz, x, 1 - y, core).wait_recv()
        if PARTS[k][1]:
            copy(6, "x", k, zz, x, 1 - y, core, 1).start()
        copy(8, "core", k, zz, x, 1 - y, core).start()

    def third(k, zz, side):
        copy(5, "y", k, zz, 1 - x, 1 - y, core, 0).wait_recv()
        copy(9, "core", k, zz, 1 - x, 1 - y, core, 0).start()
        if PARTS[k][1]:
            copy(6, "x", k, zz, 1 - x, 1 - y, core, 1).wait_recv()
            copy(10, "core", k, zz, 1 - x, 1 - y, core, 1).start()

    def finish(k, zz, side):
        if side != 1:

            @pl.when(z < 3)
            def _up():
                up(k, zz).wait_send()

        if side != 0:

            @pl.when(z > 0)
            def _down():
                down(k, zz).wait_send()

        copy(2, "x", k, zz, x, y, core).wait_send()
        copy(3, "y", k, zz, x, y, core).wait_send()
        copy(5, "y", k, zz, 1 - x, y, core, 0).wait_send()
        if PARTS[k][1]:
            copy(6, "x", k, zz, x, 1 - y, core, 1).wait_send()
        copy(4, "core", k, zz, x, y, core).wait_send()
        copy(7, "core", k, zz, 1 - x, y, core).wait_send()
        copy(8, "core", k, zz, x, 1 - y, core).wait_send()
        copy(9, "core", k, zz, 1 - x, 1 - y, core, 0).wait_send()
        if PARTS[k][1]:
            copy(10, "core", k, zz, 1 - x, 1 - y, core, 1).wait_send()
        copy(4, "core", k, zz, x, y, 1 - core).wait_recv()
        copy(7, "core", k, zz, 1 - x, y, 1 - core).wait_recv()
        copy(8, "core", k, zz, x, 1 - y, 1 - core).wait_recv()
        copy(9, "core", k, zz, 1 - x, 1 - y, 1 - core, 0).wait_recv()
        if PARTS[k][1]:
            copy(10, "core", k, zz, 1 - x, 1 - y, 1 - core, 1).wait_recv()

    for k in range(CHUNKS):
        begin(k)

    def step(d, _):
        @pl.when(d < 4)
        def _one():
            each(d, first)

        @pl.when((d >= 1) & (d < 5))
        def _two():
            each_or_own(d - 1, second)

        @pl.when(d >= 2)
        def _three():
            each_or_own(d - 2, third)

        return 0

    lax.fori_loop(1, 6, step, 0)

    def end(d, _):
        each_or_own(d, finish)
        return 0

    lax.fori_loop(0, 4, end, 0)
    for one in own:
        one.wait()
    border.wait()
    inside.wait()
    empty.wait()


def gather_weights(owners, slots, tokens):
    n_dp = lax.axis_size("dp")
    low = jnp.bfloat16
    rows = tokens.shape[0]
    anywhere = pl.BlockSpec(memory_space=pl.ANY)
    return pl.pallas_call(
        gather_kernel,
        out_shape=tuple(
            jax.ShapeDtypeStruct((count, 2, 4, 128, D), low) for first, count in GROUPS
        )
        + (
            jax.ShapeDtypeStruct((4, 4, 16, D // 2), low),
            jax.ShapeDtypeStruct((rows + EXT_PAD, D), tokens.dtype),
        ),
        in_specs=[
            pl.BlockSpec(memory_space=pltpu.SMEM),
            pl.BlockSpec(memory_space=pltpu.VMEM),
            anywhere,
        ],
        out_specs=(anywhere,) * 5,
        scratch_shapes=[
            pltpu.SMEM(owners.shape, jnp.int32),
            pltpu.VMEM((n_dp, CAP, 16, D // 2), low),
            pltpu.VMEM((n_dp * CAP, 16, D // 2), low),
            pltpu.VMEM((12, 4, 16, D // 2), low),
            pltpu.VMEM((EXT_PAD - DOC_MAX // 2, D), tokens.dtype),
            pltpu.SemaphoreType.DMA,
            pltpu.SemaphoreType.DMA((CHUNKS,)),
            pltpu.SemaphoreType.DMA((2,)),
            pltpu.SemaphoreType.DMA((n_dp,)),
            pltpu.SemaphoreType.DMA((n_dp,)),
            pltpu.SemaphoreType.DMA((11, CHUNKS, 4)),
            pltpu.SemaphoreType.DMA((11, CHUNKS, 4)),
            pltpu.SemaphoreType.DMA,
            pltpu.SemaphoreType.DMA,
        ],
        compiler_params=pltpu.CompilerParams(
            collective_id=1, has_side_effects=True, vmem_limit_bytes=32 * 2**20
        ),
        cost_estimate=pl.CostEstimate(flops=0, bytes_accessed=50 * 10**6, transcendentals=0),
        name="gather_weights",
    )(owners, slots, tokens)


def stack_kernel(parts_ref, out_ref):
    for p in range(4):
        for line in range(8):
            for half in range(2):
                columns = slice(half * (D // 2), (half + 1) * (D // 2))
                out_ref[0, 0, p, line, :, columns] = parts_ref[0, line, half, 0, p]


def stack_chunks(parts):
    return pl.pallas_call(
        stack_kernel,
        out_shape=jax.ShapeDtypeStruct((4, 2, 4, 8, 16, D), parts.dtype),
        grid=(4, 2),
        in_specs=[
            pl.BlockSpec((1, 8, 2, 1, 4, 16, D // 2), lambda m, t: (t, 0, 0, m, 0, 0, 0)),
        ],
        out_specs=pl.BlockSpec((1, 1, 4, 8, 16, D), lambda m, t: (m, t, 0, 0, 0, 0)),
        cost_estimate=pl.CostEstimate(flops=0, bytes_accessed=17 * 10**6, transcendentals=0),
        name="stack_chunks",
    )(parts)


BLOCKS = 12
SLICES = 2
STEPS = BLOCKS * SLICES
LAG = 2


def reduce_kernel(
    piece_ref, vec_ref, qkv_ref, ctx_ref, pre_ref, hid_ref, tok_ref, gext_ref, norm_ref, two_ref,
    out_ref, sum_ref,
    tile, tall, ext_rhs, row_rhs, far_buf, near_buf, core_in, x_in, y_in, x2_in, y2_in, line, line_in,
    done, parcel, vec_in, vec_out,
    tile_sem, rhs_sem, local_sem, post, mail, send, recv, vec_send, vec_recv,
):
    z, y, core, x = coordinates()
    near = neighbours(z, y, core, x)
    me = lax.axis_index("dp")
    n_dp = parcel.shape[1]
    half_width = D // 2
    width = half_width // SLICES
    rows = tile.shape[1]
    tiles = 1024 // rows

    def right(n, half, cut):
        ref = (tok_ref, gext_ref, norm_ref, two_ref)[n]
        to = ext_rhs.at[n, half, cut] if n < 2 else row_rhs.at[n - 2, half, cut]
        which = 1 - core if half == 0 else core
        columns = pl.ds(pl.multiple_of(which * half_width + cut * width, width), width)
        return pltpu.make_async_copy(ref.at[:, columns], to, rhs_sem.at[n, half, cut])

    for cut in range(SLICES):
        for n in range(4):
            for half in range(2):
                right(n, half, cut).start()

    def fetch(n, body):
        i = lax.rem(n // tiles, BLOCKS)
        part = pl.ds(pl.multiple_of(lax.rem(n, tiles) * rows, rows), rows)
        slot = lax.rem(n, 2)
        ext = ext_rhs.shape[3]
        wide = tile.at[slot, :, pl.ds(0, ext)]
        sem = tile_sem.at[slot]

        @pl.when(i < 3)
        def _qkv():
            body(pltpu.make_async_copy(qkv_ref.at[i, part, :], wide, sem))

        @pl.when(i == 3)
        def _out():
            body(pltpu.make_async_copy(ctx_ref.at[part, :], wide, sem))

        def columns(first):
            start = (i - first) * 1024 + lax.rem(n, tiles) * rows
            return pl.ds(pl.multiple_of(start, rows), rows)

        @pl.when((i >= 4) & (i < 8))
        def _up():
            body(pltpu.make_async_copy(pre_ref.at[:, columns(4)], tall.at[slot], sem))

        @pl.when(i >= 8)
        def _down():
            body(pltpu.make_async_copy(hid_ref.at[:, columns(8)], tall.at[slot], sem))

    fetch(0, lambda copy: copy.start())
    greet_all(near, me, n_dp)

    def remote(kind, i, link, src, dst):
        return pltpu.make_async_remote_copy(
            src_ref=src,
            dst_ref=dst,
            send_sem=send.at[kind, i],
            recv_sem=recv.at[kind, i],
            device_id=near[link],
            device_id_type=MESH,
        )

    def core_copy(i):
        return remote(0, i, "core", far_buf.at[lax.rem(i, 2)], core_in.at[i])

    def x1(i):
        return remote(1, i, "x", core_in.at[i, 1 - x, pl.ds(0, 2)], x_in.at[i])

    def y1(i):
        return remote(2, i, "y", core_in.at[i, :, pl.ds(2, 2), :, 1 - y], y_in.at[i])

    def y2(i):
        return remote(3, i, "y", x_in.at[i, :, :, 1 - y], y2_in.at[i])

    def x2(i):
        return remote(4, i, "x", y_in.at[i, 1 - x], x2_in.at[i])

    def along(i, zz):
        return pltpu.make_async_remote_copy(
            src_ref=line.at[i, zz],
            dst_ref=line_in.at[i, z],
            send_sem=send.at[5 + zz, i],
            recv_sem=recv.at[5 + z, i],
            device_id={"dp": (zz * 2 + y) * 2 + core, "tensor": x},
            device_id_type=MESH,
        )

    def arrival(i, zz):
        return pltpu.make_async_remote_copy(
            src_ref=line.at[i, zz],
            dst_ref=line_in.at[i, zz],
            send_sem=send.at[5 + zz, i],
            recv_sem=recv.at[5 + zz, i],
            device_id={"dp": (zz * 2 + y) * 2 + core, "tensor": x},
            device_id_type=MESH,
        )

    def produce(b):
        ring = lax.rem(b, 2)
        cut = b // BLOCKS
        i = lax.rem(b, BLOCKS)

        for c in range(SLICES):
            for n, first in enumerate((0, 3, 4, 8)):

                @pl.when(b == c * BLOCKS + first)
                def _ready():
                    right(n, 0, c).wait()
                    right(n, 1, c).wait()

        @pl.when(b >= 2)
        def _free():
            core_copy(b - 2).wait_send()

        def one(part, _):
            n = b * tiles + part
            slot = lax.rem(n, 2)

            @pl.when(n + 1 < STEPS * tiles)
            def _next():
                fetch(n + 1, lambda copy: copy.start())

            fetch(n, lambda copy: copy.wait())
            t, p = part // 2, lax.rem(part, 2) * 2

            def put(value, to):
                to[ring, t, pl.ds(p, 2)] = value.astype(jnp.bfloat16).reshape(2, 4, 2, 16, width)

            @pl.when(i < 4)
            def _wide():
                which = jnp.where(i < 3, 0, 1)
                put(mm(tile[slot], ext_rhs[which, 0, cut], NN), far_buf)
                put(mm(tile[slot], ext_rhs[which, 1, cut], NN), near_buf)

            @pl.when(i >= 4)
            def _tall():
                which = jnp.where(i < 8, 0, 1)
                put(mm(tall[slot], row_rhs[which, 0, cut], TN), far_buf)
                put(mm(tall[slot], row_rhs[which, 1, cut], TN), near_buf)

            return 0

        lax.fori_loop(0, tiles, one, 0)
        core_copy(b).start()

    def stage_one(i):
        core_copy(i).wait_recv()
        ring = lax.rem(i, 2)

        def add(j, _):
            t, p = j // 4, j % 4
            core_in[i, t, p] = core_in[i, t, p] + near_buf[ring, t, p]
            return 0

        lax.fori_loop(0, 8, add, 0)
        x1(i).start()
        y1(i).start()

    def stage_two(i):
        x1(i).wait_recv()
        y1(i).wait_recv()
        for p in range(2):
            x_in[i, p] = x_in[i, p] + core_in[i, x, p]
        for t in range(2):
            for p in range(2):
                y_in[i, t, p] = y_in[i, t, p] + core_in[i, t, 2 + p, :, y]
        y2(i).start()
        x2(i).start()

    def stage_three(i):
        y2(i).wait_recv()
        x2(i).wait_recv()
        for p in range(2):
            line[i, :, p] = x_in[i, p, :, y] + y2_in[i, p]
            line[i, :, 2 + p] = y_in[i, x, p] + x2_in[i, p]
        for n in range(1, 4):
            along(i, lax.rem(z + n, 4)).start()

    def stage_last(b):
        cut = b // BLOCKS
        total = line[b, z].astype(jnp.float32)
        for n in range(1, 4):
            zz = lax.rem(z + n, 4)
            arrival(b, zz).wait_recv()
            total += line_in[b, zz].astype(jnp.float32)
        done[cut, pl.ds(lax.rem(b, BLOCKS) * 4, 4)] = total.astype(jnp.bfloat16)

    def place(of, cut):
        start = (of % 2) * half_width + cut * width
        return out_ref.at[
            :,
            pl.ds(pl.multiple_of((of // 2) * 16, 16), 16),
            pl.ds(pl.multiple_of(start, width), width),
        ]

    def letter(to, cut):
        return pltpu.make_async_remote_copy(
            src_ref=parcel.at[cut, to],
            dst_ref=place(me, cut),
            send_sem=post.at[cut, to],
            recv_sem=mail.at[cut, me],
            device_id={"dp": to, "tensor": x},
            device_id_type=MESH,
        )

    def answer(of, cut):
        return pltpu.make_async_remote_copy(
            src_ref=parcel.at[cut, of],
            dst_ref=place(of, cut),
            send_sem=post.at[cut, of],
            recv_sem=mail.at[cut, of],
            device_id={"dp": of, "tensor": x},
            device_id_type=MESH,
        )

    def own_letter(cut):
        return pltpu.make_async_copy(parcel.at[cut, me], place(me, cut), local_sem.at[cut])

    def post_all(cut):
        done[cut, BLOCKS * 4] = jnp.zeros((16, width), done.dtype)

        def pack(n, _):
            parcel[cut, n // CAP, n % CAP] = done[cut, piece_ref[n]]
            return 0

        lax.fori_loop(0, n_dp * CAP, pack, 0)

        def post_one(i, _):
            letter(lax.rem(me + i, n_dp), cut).start()
            return 0

        lax.fori_loop(1, n_dp, post_one, 0)
        own_letter(cut).start()

    def ended(i):
        @pl.when(i >= STEPS - 2)
        def _far():
            core_copy(i).wait_send()

        x1(i).wait_send()
        y1(i).wait_send()
        y2(i).wait_send()
        x2(i).wait_send()
        for n in range(1, 4):
            along(i, lax.rem(z + n, 4)).wait_send()

    z_one = z + 1 - 2 * lax.rem(z, 2)
    z_two = lax.rem(z + 2, 4)
    partners = [
        near["core"],
        near["y"],
        near["x"],
        {"dp": (z_one * 2 + y) * 2 + core, "tensor": x},
        {"dp": (z_two * 2 + y) * 2 + core, "tensor": x},
    ]

    def swap(n):
        return pltpu.make_async_remote_copy(
            src_ref=vec_out.at[n],
            dst_ref=vec_in.at[n],
            send_sem=vec_send.at[n],
            recv_sem=vec_recv.at[n],
            device_id=partners[n],
            device_id_type=MESH,
        )

    vec_out[0] = vec_ref[...]
    produce(0)

    def step(s, _):
        @pl.when(s + 1 < STEPS)
        def _produce():
            produce(s + 1)

        @pl.when(s < STEPS)
        def _one():
            stage_one(s)

        @pl.when((s >= LAG) & (s < STEPS + LAG))
        def _two():
            stage_two(s - LAG)

        @pl.when((s >= 2 * LAG) & (s < STEPS + 2 * LAG))
        def _three():
            stage_three(s - 2 * LAG)

        @pl.when(s >= 3 * LAG)
        def _last():
            stage_last(s - 3 * LAG)

        for cut in range(SLICES):

            @pl.when(s - 3 * LAG == cut * BLOCKS + BLOCKS - 1)
            def _post():
                post_all(cut)

        for n in range(5):

            @pl.when(s == n)
            def _begin():
                swap(n).start()

            @pl.when(s == n + 1)
            def _end():
                swap(n).wait()
                if n < 4:
                    vec_out[n + 1] = vec_out[n] + vec_in[n]
                else:
                    sum_ref[...] = vec_out[n] + vec_in[n]

        return 0

    lax.fori_loop(0, STEPS + 3 * LAG, step, 0)

    def finish(i, _):
        ended(i)
        return 0

    lax.fori_loop(0, STEPS, finish, 0)

    def mail_one(i, _):
        for cut in range(SLICES):
            answer(lax.rem(me + i, n_dp), cut).wait_recv()
            letter(lax.rem(me + i, n_dp), cut).wait_send()
        return 0

    lax.fori_loop(1, n_dp, mail_one, 0)
    for cut in range(SLICES):
        own_letter(cut).wait()


def reduce_grads(piece_of, vec, qkv, context, pre, hidden, tokens, ext_grads, normed, two):
    n_dp = piece_of.shape[0] // CAP
    low = jnp.bfloat16
    width = D // 2 // SLICES
    rows = 256
    ext = tokens.shape[0]
    length = normed.shape[0]
    anywhere = pl.BlockSpec(memory_space=pl.ANY)
    vmem = pl.BlockSpec(memory_space=pltpu.VMEM)
    return pl.pallas_call(
        reduce_kernel,
        out_shape=(
            jax.ShapeDtypeStruct((CAP, 128, D), low),
            jax.ShapeDtypeStruct(vec.shape, jnp.float32),
        ),
        in_specs=[pl.BlockSpec(memory_space=pltpu.SMEM), vmem] + [anywhere] * 8,
        out_specs=(anywhere, vmem),
        scratch_shapes=[
            pltpu.VMEM((2, rows, ext), low),
            pltpu.VMEM((2, length, rows), low),
            pltpu.VMEM((2, 2, SLICES, ext, width), low),
            pltpu.VMEM((2, 2, SLICES, length, width), low),
            pltpu.VMEM((2, 2, 4, 4, 2, 16, width), low),
            pltpu.VMEM((2, 2, 4, 4, 2, 16, width), low),
            pltpu.VMEM((STEPS, 2, 4, 4, 2, 16, width), low),
            pltpu.VMEM((STEPS, 2, 4, 2, 16, width), low),
            pltpu.VMEM((STEPS, 2, 2, 4, 16, width), low),
            pltpu.VMEM((STEPS, 2, 4, 16, width), low),
            pltpu.VMEM((STEPS, 2, 4, 16, width), low),
            pltpu.VMEM((STEPS, 4, 4, 16, width), low),
            pltpu.VMEM((STEPS, 4, 4, 16, width), low),
            pltpu.VMEM((SLICES, BLOCKS * 4 + 1, 16, width), low),
            pltpu.VMEM((SLICES, n_dp, CAP, 16, width), low),
            pltpu.VMEM((5,) + vec.shape, jnp.float32),
            pltpu.VMEM((5,) + vec.shape, jnp.float32),
            pltpu.SemaphoreType.DMA((2,)),
            pltpu.SemaphoreType.DMA((4, 2, SLICES)),
            pltpu.SemaphoreType.DMA((SLICES,)),
            pltpu.SemaphoreType.DMA((SLICES, n_dp)),
            pltpu.SemaphoreType.DMA((SLICES, n_dp)),
            pltpu.SemaphoreType.DMA((9, STEPS)),
            pltpu.SemaphoreType.DMA((9, STEPS)),
            pltpu.SemaphoreType.DMA((5,)),
            pltpu.SemaphoreType.DMA((5,)),
        ],
        compiler_params=pltpu.CompilerParams(
            collective_id=2, has_side_effects=True, vmem_limit_bytes=60 * 2**20
        ),
        cost_estimate=pl.CostEstimate(
            flops=31 * 10**9, bytes_accessed=50 * 10**6, transcendentals=0
        ),
        name="reduce_grads",
    )(piece_of, vec, qkv, context, pre, hidden, tokens, ext_grads, normed, two)


def coordinates():
    dp = lax.axis_index("dp")
    return dp // 4, (dp // 2) % 2, dp % 2, lax.axis_index("tensor")


def exchange(values, axis):
    if axis == "x":
        return lax.ppermute(values, "tensor", [(0, 1), (1, 0)])
    flip = {"core": 1, "y": 2, "z_near": 4, "z_far": 8}[axis]
    return lax.ppermute(values, "dp", [(i, i ^ flip) for i in range(lax.axis_size("dp"))])


def pick(values, index, axis):
    return lax.dynamic_index_in_dim(values, index, axis, keepdims=False)


def on_device_rows(
    tokens,
    segment_ids,
    key_mask,
    owners,
    master_slots,
    slot_first,
    slot_second,
    vectors,
    vector_first,
    vector_second,
    out_grad,
):
    n_dp = lax.axis_size("dp")
    n_tensor = lax.axis_size("tensor")
    half = lax.axis_index("tensor")
    every = ("tensor", "dp")
    rows = tokens.shape[0]
    ext = rows + EXT_PAD
    halo = DOC_MAX // 2
    swap = [(0, 1), (1, 0)]
    edge = jnp.where(half == 0, rows - halo, 0)
    halo_at = jnp.where(half == 0, rows, EXT_PAD - halo)
    own_at = half * EXT_PAD

    def extend(own_rows, halo_rows):
        whole = jnp.zeros((ext,) + own_rows.shape[1:], own_rows.dtype)
        whole = lax.dynamic_update_slice_in_dim(whole, halo_rows, halo_at, 0)
        return lax.dynamic_update_slice_in_dim(whole, own_rows, own_at, 0)

    def own_part(values):
        return lax.dynamic_slice_in_dim(values, own_at, rows, 0)

    def halo_part(values):
        return lax.dynamic_slice_in_dim(values, halo_at, halo, 0)

    lo, hi, qaug, kaug, hidden_keys, handled, foreign = document_plan(
        segment_ids[0], key_mask[0], half, rows
    )
    slots = slot_index(owners)
    pieces = slots.shape[0]
    piece_rows = master_slots.shape[2]
    mix_pieces = 4 * (D // n_tensor) // piece_rows
    up_pieces = (FF // n_tensor) // piece_rows
    per = mix_pieces // 4
    w_qkv, w_out, w_up, down_chunk, tokens_ext = gather_weights(owners[:, 0], master_slots[0], tokens)
    w_qkv = w_qkv.reshape(3 * D, D)
    w_out = w_out.reshape(D, D)
    w_up = w_up.reshape(FF, D)
    down_chunks = lax.all_gather(down_chunk, every, axis=0, tiled=False)
    w_down = stack_chunks(down_chunks.reshape((n_tensor, 8, 2) + down_chunk.shape)).reshape(FF, D)
    bias_up = vectors[2:6].reshape(n_tensor, 4, -1).transpose(1, 0, 2).reshape(FF)

    bias_qkv = jnp.concatenate([vectors[0], jnp.zeros((D,), jnp.float32), vectors[1]])
    scale_qkv = jnp.concatenate([jnp.full((D,), HD ** (-0.5)), jnp.ones((2 * D,))])
    qkv = (
        (mm(w_qkv, tokens_ext, NT) + bias_qkv[:, None]) * scale_qkv.astype(jnp.float32)[:, None]
    ).astype(jnp.bfloat16)
    context, logs = attend(lo, hi, qkv, qaug, kaug, hidden_keys)
    attn_ext = mm(context, w_out, TN).astype(jnp.bfloat16)
    halo_attn = lax.ppermute(halo_part(attn_ext), "tensor", swap)
    attn_back = lax.dynamic_update_slice_in_dim(
        jnp.zeros((rows, D), jnp.bfloat16), halo_attn, edge, 0
    )
    attn_sum = jnp.where(foreign[:, None], attn_back, own_part(attn_ext)).astype(jnp.float32)
    residual_one = tokens.astype(jnp.float32) + (attn_sum + vectors[6])
    normal_one, inverse_one = layer_stats(residual_one)
    normed = normal_one * vectors[8] + vectors[9]
    normed_low = normed.astype(jnp.bfloat16)

    hidden, slope = feed_up(normed_low, w_up, bias_up)
    residual_two = normed + (mm(hidden, w_down, NN) + vectors[7])
    normal_two, inverse_two = layer_stats(residual_two)
    layer_out = (normal_two * vectors[10] + vectors[11]).astype(jnp.bfloat16)
    grad_out = out_grad.astype(jnp.float32)
    grad_two = norm_back(grad_out, normal_two, inverse_two, vectors[10])
    grad_two_low = grad_two.astype(jnp.bfloat16)

    grad_pre, up_sums = feed_down_back(grad_two_low, w_down, slope)
    grad_norm = grad_two + lax.optimization_barrier(mm(grad_pre, w_up, NN))
    grad_one = norm_back(grad_norm, normal_one, inverse_one, vectors[8])
    grad_one_low = grad_one.astype(jnp.bfloat16)

    halo_grad = lax.ppermute(
        lax.dynamic_slice_in_dim(grad_one_low, edge, halo, 0), "tensor", swap
    )
    grad_ext = jnp.where(handled[:, None], extend(grad_one_low, halo_grad), 0)
    grad_context = mm(w_out, grad_ext, NT).astype(jnp.bfloat16)
    grad_qkv = attend_back(lo, hi, qkv, grad_context, context, logs, qaug, kaug, hidden_keys)
    input_ext = mm(grad_qkv.reshape(3 * D, ext), w_qkv, TN)
    halo_input = lax.ppermute(halo_part(input_ext).astype(jnp.bfloat16), "tensor", swap)
    input_back = lax.dynamic_update_slice_in_dim(
        jnp.zeros((rows, D), jnp.bfloat16), halo_input, edge, 0
    )
    input_grad = (grad_one + own_part(input_ext) + input_back.astype(jnp.float32)).astype(
        jnp.bfloat16
    )

    vector_terms = jnp.concatenate(
        [
            jnp.stack(
                [
                    jnp.sum(grad_qkv[0].astype(jnp.float32), axis=1),
                    jnp.sum(grad_qkv[2].astype(jnp.float32), axis=1),
                ]
            ),
            up_sums.reshape(4, n_tensor, -1)
            .transpose(1, 0, 2)
            .reshape(FF // D, D),
            jnp.stack(
                [
                    jnp.sum(grad_one, axis=0),
                    jnp.sum(grad_two, axis=0),
                    jnp.sum(grad_norm * normal_one, axis=0),
                    jnp.sum(grad_norm, axis=0),
                    jnp.sum(grad_out * normal_two, axis=0),
                    jnp.sum(grad_out, axis=0),
                ]
            ),
        ],
        axis=0,
    )
    piece_of = jnp.full((n_dp * CAP,), pieces, jnp.int32).at[slots].set(
        jnp.arange(pieces, dtype=jnp.int32)
    )
    own_grads, vector_grads = reduce_grads(
        piece_of,
        vector_terms,
        grad_qkv,
        context,
        grad_pre,
        hidden,
        tokens_ext,
        grad_ext,
        normed_low,
        grad_two_low,
    )
    own_grads = own_grads.astype(jnp.float32)
    slot_new, slot_first_new, slot_second_new = adam_update(
        master_slots[0], slot_first[0], slot_second[0], own_grads, rate_matrix, weight_decay
    )
    vector_new, vector_first_new, vector_second_new = adam_update(
        vectors, vector_first, vector_second, vector_grads, rate_vector, 0.0
    )
    return (
        layer_out,
        input_grad,
        slot_new[None],
        slot_first_new[None],
        slot_second_new[None],
        vector_new,
        vector_first_new,
        vector_second_new,
    )


def solution(mesh):
    placed = (
        P(("dp", "tensor"), None),
        P("dp", None),
        P("dp", None),
        P(),
        P("tensor", "dp", None, None),
        P("tensor", "dp", None, None),
        P("tensor", "dp", None, None),
        P(),
        P(),
        P(),
        P(("dp", "tensor"), None),
    )
    by_rows = mesh.shape["tensor"] == 2 and mesh.shape["dp"] == 16
    return jax.shard_map(
        on_device_rows if by_rows else on_device_generic,
        mesh=mesh,
        in_specs=placed,
        out_specs=(
            P(("dp", "tensor"), None),
            P(("dp", "tensor"), None),
            P("tensor", "dp", None, None),
            P("tensor", "dp", None, None),
            P("tensor", "dp", None, None),
            P(),
            P(),
            P(),
        ),
        check_vma=False,
    )
```

```python
import functools

import jax
import jax.numpy as jnp
from jax import lax
from jax.experimental import pallas as pl
from jax.experimental.pallas import tpu as pltpu
from jax.sharding import PartitionSpec as P

D = 1024
HD = 64
FF = 4096
QBLK = 512
STEP = 10
CAP = 6


norm_eps = 1e-05
mask_fill = -1000000000.0
beta_one = 0.5
beta_two = 0.5
rate_matrix = 0.03
rate_vector = 0.1
weight_decay = 0.01
adam_eps = 1e-08


def slot_index(owners):
    owner_of = owners[:, 0]
    positions = jnp.arange(owner_of.shape[0], dtype=jnp.int32)
    earlier = (positions[None, :] < positions[:, None]) & (owner_of[None, :] == owner_of[:, None])
    within = jnp.sum(earlier.astype(jnp.int32), axis=1)
    return owner_of * CAP + within


def layer_stats(residual):
    center = residual - jnp.mean(residual, axis=-1, keepdims=True)
    spread = jnp.mean(center * center, axis=-1, keepdims=True)
    inverse = lax.rsqrt(spread + norm_eps)
    return (center * inverse, inverse)


def norm_back(grads, normal, inverse, gains):
    scaled = grads * gains
    return inverse * (
        scaled
        - jnp.mean(scaled, axis=-1, keepdims=True)
        - normal * jnp.mean(scaled * normal, axis=-1, keepdims=True)
    )


def gelu_exact(values):
    return jax.nn.gelu(values, approximate=False)


def block_mask(segment, valid, start):
    length = segment.shape[0]
    query_pos = start + jnp.arange(QBLK, dtype=jnp.int32)
    key_pos = jnp.arange(length, dtype=jnp.int32)
    query_seg = lax.dynamic_slice_in_dim(segment, start, QBLK, 0)
    same = query_seg[:, None] == segment[None, :]
    return same & ((valid[None, :] == 1) | (query_pos[:, None] == key_pos[None, :]))


def block_scores(block_q, key_rows, segment, valid, start):
    scores = jnp.einsum("qhd,khd->hqk", block_q, key_rows, preferred_element_type=jnp.float32)
    return jnp.where(block_mask(segment, valid, start)[None], scores, mask_fill)


def attend_forward(queries, key_rows, value_rows, segment, valid):
    length = queries.shape[0]

    def one_block(index):
        start = index * QBLK
        block_q = lax.dynamic_slice_in_dim(queries, start, QBLK, 0)
        scores = block_scores(block_q, key_rows, segment, valid, start)
        row_max = jnp.max(scores, axis=2, keepdims=True)
        raised = jnp.exp(scores - row_max)
        totals = jnp.sum(raised, axis=2, keepdims=True)
        weights = (raised / totals).astype(jnp.bfloat16)
        context = jnp.einsum(
            "hqk,khd->qhd", weights, value_rows, preferred_element_type=jnp.float32
        )
        return (context, (row_max + jnp.log(totals))[:, :, 0])

    context, log_sums = lax.map(one_block, jnp.arange(length // QBLK, dtype=jnp.int32))
    return (context.reshape(length, -1), log_sums)


def attend_backward(queries, key_rows, value_rows, segment, valid, log_sums, grad_context):
    length = queries.shape[0]

    def one_block(carry, index):
        key_acc, value_acc = carry
        start = index * QBLK
        block_q = lax.dynamic_slice_in_dim(queries, start, QBLK, 0)
        block_g = lax.dynamic_slice_in_dim(grad_context, start, QBLK, 0)
        scores = block_scores(block_q, key_rows, segment, valid, start)
        weights = jnp.exp(scores - log_sums[index][:, :, None])
        value_acc = value_acc + jnp.einsum(
            "hqk,qhd->khd",
            weights.astype(jnp.bfloat16),
            block_g,
            preferred_element_type=jnp.float32,
        )
        grad_weights = jnp.einsum(
            "qhd,khd->hqk", block_g, value_rows, preferred_element_type=jnp.float32
        )
        inner = jnp.sum(weights * grad_weights, axis=2, keepdims=True)
        grad_scores = (weights * (grad_weights - inner)).astype(jnp.bfloat16)
        grad_q = jnp.einsum(
            "hqk,khd->qhd", grad_scores, key_rows, preferred_element_type=jnp.float32
        )
        key_acc = key_acc + jnp.einsum(
            "hqk,qhd->khd", grad_scores, block_q, preferred_element_type=jnp.float32
        )
        return ((key_acc, value_acc), grad_q)

    zeros_kv = jnp.zeros(key_rows.shape, jnp.float32)
    (grad_keys, grad_values), grad_queries = lax.scan(
        one_block, (zeros_kv, zeros_kv), jnp.arange(length // QBLK, dtype=jnp.int32)
    )
    return (
        grad_queries.reshape(length, -1),
        grad_keys.reshape(length, -1),
        grad_values.reshape(length, -1),
    )


def adam_update(weights, first, second, grads, rate, decay):
    first_new = beta_one * first + (1.0 - beta_one) * grads
    second_new = beta_two * second + (1.0 - beta_two) * grads * grads
    first_hat = first_new / (1.0 - beta_one**STEP)
    second_hat = second_new / (1.0 - beta_two**STEP)
    updated = weights - rate * (first_hat / (jnp.sqrt(second_hat) + adam_eps) + decay * weights)
    return (updated, first_new, second_new)


def on_device_generic(
    tokens,
    segment_ids,
    key_mask,
    owners,
    master_slots,
    slot_first,
    slot_second,
    vectors,
    vector_first,
    vector_second,
    out_grad,
):
    n_tensor = lax.axis_size("tensor")
    group = lax.axis_index("tensor")
    head_cols = D // n_tensor
    unit_cols = FF // n_tensor
    heads_here = head_cols // HD
    seq_count = segment_ids.shape[0]
    length = segment_ids.shape[1]
    query_scale = HD ** (-0.5)
    slots = slot_index(owners)
    gathered_slots = lax.all_gather(master_slots[0].astype(jnp.bfloat16), "dp", axis=0, tiled=True)
    stack = jnp.take(gathered_slots, slots, axis=0).reshape(-1, D)
    w_mix = stack[0 : 3 * head_cols]
    w_out = stack[3 * head_cols : 4 * head_cols]
    w_up = stack[4 * head_cols : 4 * head_cols + unit_cols]
    w_down = stack[4 * head_cols + unit_cols :]
    bias_query = lax.dynamic_slice_in_dim(vectors[0], group * head_cols, head_cols, 0)
    bias_value = lax.dynamic_slice_in_dim(vectors[1], group * head_cols, head_cols, 0)
    bias_up = lax.dynamic_slice_in_dim(vectors[2:6].reshape(FF), group * unit_cols, unit_cols, 0)
    gathered = lax.all_gather(tokens, "tensor", axis=0, tiled=True)
    mixed = jnp.einsum("ld,kd->lk", gathered, w_mix, preferred_element_type=jnp.float32)
    queries = ((mixed[:, :head_cols] + bias_query) * query_scale).astype(jnp.bfloat16)
    key_rows = mixed[:, head_cols : 2 * head_cols].astype(jnp.bfloat16)
    value_rows = (mixed[:, 2 * head_cols :] + bias_value).astype(jnp.bfloat16)
    head_shape = (seq_count, length, heads_here, HD)
    queries_h = queries.reshape(head_shape)
    keys_h = key_rows.reshape(head_shape)
    values_h = value_rows.reshape(head_shape)

    def forward_seq(element):
        return attend_forward(element[0], element[1], element[2], element[3], element[4])

    context, log_sums = lax.map(forward_seq, (queries_h, keys_h, values_h, segment_ids, key_mask))
    context = context.reshape(-1, head_cols).astype(jnp.bfloat16)
    attn_sum = lax.psum_scatter(
        jnp.einsum("lk,kd->ld", context, w_out, preferred_element_type=jnp.float32).astype(
            jnp.bfloat16
        ),
        "tensor",
        scatter_dimension=0,
        tiled=True,
    ).astype(jnp.float32)
    residual_one = tokens.astype(jnp.float32) + (attn_sum + vectors[6])
    normal_one, inverse_one = layer_stats(residual_one)
    normed = normal_one * vectors[8] + vectors[9]
    normed_low = normed.astype(jnp.bfloat16)
    norm_rows = lax.all_gather(normed_low, "tensor", axis=0, tiled=True)
    hidden_pre = (
        jnp.einsum("ld,kd->lk", norm_rows, w_up, preferred_element_type=jnp.float32) + bias_up
    )
    hidden_full, gelu_pull = jax.vjp(gelu_exact, hidden_pre)
    hidden = hidden_full.astype(jnp.bfloat16)
    mlp_sum = lax.psum_scatter(
        jnp.einsum("lk,kd->ld", hidden, w_down, preferred_element_type=jnp.float32).astype(
            jnp.bfloat16
        ),
        "tensor",
        scatter_dimension=0,
        tiled=True,
    ).astype(jnp.float32)
    residual_two = normed + (mlp_sum + vectors[7])
    normal_two, inverse_two = layer_stats(residual_two)
    layer_out = (normal_two * vectors[10] + vectors[11]).astype(jnp.bfloat16)
    grad_out = out_grad.astype(jnp.float32)
    grad_two = norm_back(grad_out, normal_two, inverse_two, vectors[10])
    grad_down_in = lax.all_gather(grad_two.astype(jnp.bfloat16), "tensor", axis=0, tiled=True)
    grad_hidden = jnp.einsum("ld,kd->lk", grad_down_in, w_down, preferred_element_type=jnp.float32)
    grad_w_down = jnp.einsum("lk,ld->kd", hidden, grad_down_in, preferred_element_type=jnp.float32)
    grad_pre = gelu_pull(grad_hidden)[0].astype(jnp.bfloat16)
    norm_back_rows = lax.all_gather(normed_low, "tensor", axis=0, tiled=True)
    grad_w_up = jnp.einsum(
        "lk,ld->kd", grad_pre, norm_back_rows, preferred_element_type=jnp.float32
    )
    grad_norm = grad_two + lax.psum_scatter(
        jnp.einsum("lk,kd->ld", grad_pre, w_up, preferred_element_type=jnp.float32).astype(
            jnp.bfloat16
        ),
        "tensor",
        scatter_dimension=0,
        tiled=True,
    ).astype(jnp.float32)
    grad_one = norm_back(grad_norm, normal_one, inverse_one, vectors[8])
    grad_attn_in = lax.all_gather(grad_one.astype(jnp.bfloat16), "tensor", axis=0, tiled=True)
    grad_context = jnp.einsum(
        "ld,kd->lk", grad_attn_in, w_out, preferred_element_type=jnp.float32
    ).astype(jnp.bfloat16)
    grad_w_out = jnp.einsum("lk,ld->kd", context, grad_attn_in, preferred_element_type=jnp.float32)

    def backward_seq(element):
        return attend_backward(
            element[0], element[1], element[2], element[3], element[4], element[5], element[6]
        )

    grad_q, grad_k, grad_v = lax.map(
        backward_seq,
        (
            queries_h,
            keys_h,
            values_h,
            segment_ids,
            key_mask,
            log_sums,
            grad_context.reshape(head_shape),
        ),
    )
    grad_queries = grad_q.reshape(-1, head_cols).astype(jnp.bfloat16) * query_scale
    grad_keys = grad_k.reshape(-1, head_cols).astype(jnp.bfloat16)
    grad_values = grad_v.reshape(-1, head_cols).astype(jnp.bfloat16)
    grad_mix = jnp.concatenate([grad_queries, grad_keys, grad_values], axis=1)
    mix_back_rows = lax.all_gather(tokens, "tensor", axis=0, tiled=True)
    grad_w_mix = jnp.einsum(
        "lk,ld->kd", grad_mix, mix_back_rows, preferred_element_type=jnp.float32
    )
    input_grad = (
        grad_one
        + lax.psum_scatter(
            jnp.einsum("lk,kd->ld", grad_mix, w_mix, preferred_element_type=jnp.float32).astype(
                jnp.bfloat16
            ),
            "tensor",
            scatter_dimension=0,
            tiled=True,
        ).astype(jnp.float32)
    ).astype(jnp.bfloat16)
    query_full = lax.dynamic_update_slice_in_dim(
        jnp.zeros((D,), jnp.float32),
        jnp.sum(grad_queries.astype(jnp.float32), axis=0),
        group * head_cols,
        0,
    )
    value_full = lax.dynamic_update_slice_in_dim(
        jnp.zeros((D,), jnp.float32),
        jnp.sum(grad_values.astype(jnp.float32), axis=0),
        group * head_cols,
        0,
    )
    up_full = lax.dynamic_update_slice_in_dim(
        jnp.zeros((FF,), jnp.float32),
        jnp.sum(grad_pre.astype(jnp.float32), axis=0),
        group * unit_cols,
        0,
    )
    tail_rows = jnp.stack(
        [
            jnp.sum(grad_one, axis=0),
            jnp.sum(grad_two, axis=0),
            jnp.sum(grad_norm * normal_one, axis=0),
            jnp.sum(grad_norm, axis=0),
            jnp.sum(grad_out * normal_two, axis=0),
            jnp.sum(grad_out, axis=0),
        ]
    )
    vector_terms = jnp.concatenate(
        [jnp.stack([query_full, value_full]), up_full.reshape(FF // D, D), tail_rows], axis=0
    )
    vector_grads = lax.psum(vector_terms, ("dp", "tensor"))
    grad_stack = jnp.concatenate([grad_w_mix, grad_w_out, grad_w_up, grad_w_down], axis=0)
    grad_pieces = grad_stack.reshape(slots.shape[0], -1, D)
    spread_slots = (
        jnp.zeros((lax.axis_size("dp") * CAP,) + grad_pieces.shape[1:], jnp.float32)
        .at[slots]
        .set(grad_pieces)
    )
    own_grads = lax.psum_scatter(
        spread_slots.astype(jnp.bfloat16), "dp", scatter_dimension=0, tiled=True
    ).astype(jnp.float32)
    slot_new, slot_first_new, slot_second_new = adam_update(
        master_slots[0], slot_first[0], slot_second[0], own_grads, rate_matrix, weight_decay
    )
    vector_new, vector_first_new, vector_second_new = adam_update(
        vectors, vector_first, vector_second, vector_grads, rate_vector, 0.0
    )
    return (
        layer_out,
        input_grad,
        slot_new[None],
        slot_first_new[None],
        slot_second_new[None],
        vector_new,
        vector_first_new,
        vector_second_new,
    )


DOC_MAX = 800
EXT_PAD = 512
ABLK = 256
FINE = 128
HPG = 8
AUG = 16
neg_big = -1000000000.0
NN = (((1,), (0,)), ((), ()))
NT = (((1,), (1,)), ((), ()))
TN = (((0,), (0,)), ((), ()))


def mm(a, b, dims):
    return lax.dot_general(a, b, dims, preferred_element_type=jnp.float32)


def attn_fwd_kernel(lo_ref, hi_ref, q_ref, k_ref, v_ref, qaug_ref, kaug_ref, hid_ref, o_ref, lse_ref, kn_ref, m_ref, acc_ref):
    ext = q_ref.shape[1]
    ones = jnp.concatenate(
        [jnp.ones((1, ABLK), jnp.float32), jnp.zeros((AUG - 1, ABLK), jnp.float32)], axis=0
    ).astype(jnp.bfloat16)
    for h in range(HPG):
        rows = slice(h * HD, (h + 1) * HD)
        kn_ref[h] = jnp.concatenate([k_ref[rows, :], kaug_ref[...]], axis=0).T

    def query_block(qb, _):
        lo = lo_ref[qb]
        hi = hi_ref[qb]
        qs = pl.ds(pl.multiple_of(qb * ABLK, ABLK), ABLK)

        @pl.when(hi > lo)
        def _work():
            hidden = hid_ref[0:1, qs]
            for h in range(HPG):
                rows = slice(h * HD, (h + 1) * HD)
                q32 = q_ref[rows, qs].astype(jnp.float32)
                k32 = k_ref[rows, qs].astype(jnp.float32)
                own = jnp.sum(q32 * k32, axis=0, keepdims=True)
                m_ref[h] = jnp.where(hidden > 0.0, own, -1e30)
                acc_ref[h, 0:HD, :] = v_ref[rows, qs].astype(jnp.float32) * hidden
                acc_ref[h, HD:, :] = jnp.broadcast_to(hidden, (AUG, ABLK))

            blocks = (hi - lo + 1) // 2
            origin = jnp.maximum(hi - 2 * blocks, 0) * FINE

            def key_block(kb, _):
                ks = pl.ds(pl.multiple_of(origin + kb * ABLK, FINE), ABLK)
                heads = [slice(h * HD, (h + 1) * HD) for h in range(HPG)]
                scores = [
                    mm(kn_ref[h, ks, :], jnp.concatenate([q_ref[heads[h], qs], qaug_ref[:, qs]], axis=0), NN)
                    for h in range(HPG)
                ]
                olds = [m_ref[h] for h in range(HPG)]
                news = [
                    jnp.maximum(olds[h], jnp.max(scores[h], axis=0, keepdims=True)) for h in range(HPG)
                ]
                raised = [jnp.exp(scores[h] - news[h]).astype(jnp.bfloat16) for h in range(HPG)]
                for h in range(HPG):
                    m_ref[h] = news[h]
                    va = jnp.concatenate([v_ref[heads[h], ks], ones], axis=0)
                    acc_ref[h] = acc_ref[h] * jnp.exp(olds[h] - news[h]) + mm(va, raised[h], NN)
                return 0

            lax.fori_loop(0, blocks, key_block, 0)
            for h in range(HPG):
                rows = slice(h * HD, (h + 1) * HD)
                total = acc_ref[h, HD : HD + 1, :]
                o_ref[rows, qs] = (acc_ref[h, 0:HD, :] * (1.0 / total)).astype(jnp.bfloat16)
                lse_ref[0, h : h + 1, qs] = m_ref[h] + jnp.log(total)

        @pl.when(hi <= lo)
        def _skip():
            o_ref[:, qs] = jnp.zeros((HPG * HD, ABLK), jnp.bfloat16)
            lse_ref[0, :, qs] = jnp.zeros((8, ABLK), jnp.float32)

        return 0

    lax.fori_loop(0, ext // ABLK, query_block, 0)


def attn_bwd_kernel(
    lo_ref, hi_ref, q_ref, k_ref, v_ref, g_ref, c_ref, lse_ref, qaug_ref, kaug_ref, hid_ref,
    out_ref, sums_ref, kn_ref, vn_ref, acc_ref, dk_acc, dv_acc,
):
    ext = q_ref.shape[1]
    for h in range(HPG):
        rows = slice(h * HD, (h + 1) * HD)
        kn_ref[h] = jnp.concatenate([k_ref[rows, :], kaug_ref[...]], axis=0).T
        vn_ref[h] = v_ref[rows, :].T
    dk_acc[...] = jnp.zeros_like(dk_acc)
    dv_acc[...] = jnp.zeros_like(dv_acc)

    def query_block(qb, _):
        lo = lo_ref[qb]
        hi = hi_ref[qb]
        qs = pl.ds(pl.multiple_of(qb * ABLK, ABLK), ABLK)

        @pl.when(hi > lo)
        def _work():
            hidden = hid_ref[0:1, qs]
            deltas = []
            logs = []
            for h in range(HPG):
                rows = slice(h * HD, (h + 1) * HD)
                q32 = q_ref[rows, qs].astype(jnp.float32)
                k32 = k_ref[rows, qs].astype(jnp.float32)
                v32 = v_ref[rows, qs].astype(jnp.float32)
                g32 = g_ref[rows, qs].astype(jnp.float32)
                c32 = c_ref[rows, qs].astype(jnp.float32)
                delta = jnp.sum(g32 * c32, axis=0, keepdims=True)
                log = lse_ref[0, h : h + 1, qs]
                own = jnp.sum(q32 * k32, axis=0, keepdims=True)
                p_own = jnp.where(hidden > 0.0, jnp.exp(own - log), 0.0)
                d_own = p_own * (jnp.sum(g32 * v32, axis=0, keepdims=True) - delta)
                acc_ref[h] = d_own * k32
                dk_acc[rows, qs] += d_own * q32
                dv_acc[rows, qs] += p_own * g32
                deltas.append(delta)
                logs.append(log)

            blocks = (hi - lo + 1) // 2
            origin = jnp.maximum(hi - 2 * blocks, 0) * FINE

            def key_block(kb, _):
                ks = pl.ds(pl.multiple_of(origin + kb * ABLK, FINE), ABLK)
                heads = [slice(h * HD, (h + 1) * HD) for h in range(HPG)]
                every = range(HPG)
                qs_h = [q_ref[heads[h], qs] for h in every]
                gs_h = [g_ref[heads[h], qs] for h in every]
                scores = [
                    mm(kn_ref[h, ks, :], jnp.concatenate([qs_h[h], qaug_ref[:, qs]], axis=0), NN)
                    for h in every
                ]
                grads = [mm(vn_ref[h, ks, :], gs_h[h], NN) for h in every]
                weights = [jnp.exp(scores[h] - logs[h]) for h in every]
                low = [weights[h].astype(jnp.bfloat16) for h in every]
                back = [
                    (weights[h] * (grads[h] - deltas[h])).astype(jnp.bfloat16) for h in every
                ]
                v_new = [mm(gs_h[h], low[h], NT) for h in every]
                k_new = [mm(qs_h[h], back[h], NT) for h in every]
                q_new = [mm(k_ref[heads[h], ks], back[h], NN) for h in every]
                for h in every:
                    dv_acc[heads[h], ks] += v_new[h]
                    dk_acc[heads[h], ks] += k_new[h]
                    acc_ref[h] += q_new[h]
                return 0

            lax.fori_loop(0, blocks, key_block, 0)
            for h in range(HPG):
                rows = slice(h * HD, (h + 1) * HD)
                out_ref[0, rows, qs] = acc_ref[h].astype(jnp.bfloat16) * (HD ** (-0.5))

        @pl.when(hi <= lo)
        def _skip():
            out_ref[0, :, qs] = jnp.zeros((HPG * HD, ABLK), jnp.bfloat16)

        return 0

    lax.fori_loop(0, ext // ABLK, query_block, 0)
    out_ref[1] = dk_acc[...].astype(jnp.bfloat16)
    out_ref[2] = dv_acc[...].astype(jnp.bfloat16)
    for n in range(2):
        total = jnp.sum(out_ref[2 * n].astype(jnp.float32), axis=1, keepdims=True)
        sums_ref[n] = jnp.broadcast_to(total, sums_ref.shape[1:])


def group_block(offset, rows, ext):
    return pl.BlockSpec((rows, ext), lambda g, lo, hi: (offset + g, 0))


def fixed_block(rows, ext):
    return pl.BlockSpec((rows, ext), lambda g, lo, hi: (0, 0))


def attend(lo, hi, qkv, qaug, kaug, hidden):
    ext = qkv.shape[1]
    groups = D // HD // HPG
    rows = HPG * HD
    return pl.pallas_call(
        attn_fwd_kernel,
        out_shape=(
            jax.ShapeDtypeStruct((D, ext), jnp.bfloat16),
            jax.ShapeDtypeStruct((groups, 8, ext), jnp.float32),
        ),
        grid_spec=pltpu.PrefetchScalarGridSpec(
            num_scalar_prefetch=2,
            grid=(groups,),
            in_specs=[
                group_block(0, rows, ext),
                group_block(groups, rows, ext),
                group_block(2 * groups, rows, ext),
                fixed_block(AUG, ext),
                fixed_block(AUG, ext),
                fixed_block(8, ext),
            ],
            out_specs=[
                group_block(0, rows, ext),
                pl.BlockSpec((1, 8, ext), lambda g, lo, hi: (g, 0, 0)),
            ],
            scratch_shapes=[
                pltpu.VMEM((HPG, ext, HD + AUG), jnp.bfloat16),
                pltpu.VMEM((HPG, 1, ABLK), jnp.float32),
                pltpu.VMEM((HPG, HD + AUG, ABLK), jnp.float32),
            ],
        ),
        compiler_params=pltpu.CompilerParams(vmem_limit_bytes=40 * 2**20),
        cost_estimate=pl.CostEstimate(flops=20 * 10**9, bytes_accessed=14 * 10**6, transcendentals=0),
        name="attend",
    )(lo, hi, qkv, qkv, qkv, qaug, kaug, hidden)


def attend_back(lo, hi, qkv, grads, context, logs, qaug, kaug, hidden):
    ext = qkv.shape[1]
    groups = D // HD // HPG
    rows = HPG * HD
    return pl.pallas_call(
        attn_bwd_kernel,
        out_shape=(
            jax.ShapeDtypeStruct((3, D, ext), jnp.bfloat16),
            jax.ShapeDtypeStruct((2, D, 128), jnp.float32),
        ),
        grid_spec=pltpu.PrefetchScalarGridSpec(
            num_scalar_prefetch=2,
            grid=(groups,),
            in_specs=[
                group_block(0, rows, ext),
                group_block(groups, rows, ext),
                group_block(2 * groups, rows, ext),
                group_block(0, rows, ext),
                group_block(0, rows, ext),
                pl.BlockSpec((1, 8, ext), lambda g, lo, hi: (g, 0, 0)),
                fixed_block(AUG, ext),
                fixed_block(AUG, ext),
                fixed_block(8, ext),
            ],
            out_specs=(
                pl.BlockSpec((3, rows, ext), lambda g, lo, hi: (0, g, 0)),
                pl.BlockSpec((2, rows, 128), lambda g, lo, hi: (0, g, 0)),
            ),
            scratch_shapes=[
                pltpu.VMEM((HPG, ext, HD + AUG), jnp.bfloat16),
                pltpu.VMEM((HPG, ext, HD), jnp.bfloat16),
                pltpu.VMEM((HPG, HD, ABLK), jnp.float32),
                pltpu.VMEM((rows, ext), jnp.float32),
                pltpu.VMEM((rows, ext), jnp.float32),
            ],
        ),
        compiler_params=pltpu.CompilerParams(vmem_limit_bytes=48 * 2**20),
        cost_estimate=pl.CostEstimate(flops=50 * 10**9, bytes_accessed=30 * 10**6, transcendentals=0),
        name="attend_back",
    )(lo, hi, qkv, qkv, qkv, grads, context, logs, qaug, kaug, hidden)


def document_plan(segment, valid, half, rows):
    length = segment.shape[0]
    ext = rows + EXT_PAD
    base = half * EXT_PAD
    position = jnp.arange(length, dtype=jnp.int32)
    documents = jnp.arange(8, dtype=jnp.int32)[:, None]
    one_hot = segment[None, :] == documents
    counts = jnp.sum(one_hot.astype(jnp.int32), axis=1, keepdims=True)
    starts = jnp.sum((segment[None, :] < documents).astype(jnp.int32), axis=1, keepdims=True)
    start = jnp.sum(jnp.where(one_hot, starts, 0), axis=0)
    end = jnp.sum(jnp.where(one_hot, starts + counts, 0), axis=0)
    crossing = (start < rows) & (end > rows)
    left = jnp.max(jnp.where(crossing, rows - start, 0))
    right = jnp.max(jnp.where(crossing, end - rows, 0))
    in_left = position < rows
    work = jnp.where(crossing, 0, end - start)
    left_work = jnp.sum(jnp.where(in_left, work, 0))
    right_work = jnp.sum(jnp.where(in_left, 0, work))
    both_fit = (left <= DOC_MAX // 2) & (right <= DOC_MAX // 2)
    second = jnp.where(both_fit, right_work <= left_work, left <= right)
    worker = jnp.where(second, half == 1, half == 0)
    own = (position >= half * rows) & (position < (half + 1) * rows)
    handled = jnp.where(crossing, worker, own)
    cut = lambda values: lax.dynamic_slice_in_dim(values, base, ext, 0)
    handled_ext = cut(handled)
    begins = jnp.where(handled_ext, cut(start) - base, ext).reshape(-1, ABLK)
    ends = jnp.where(handled_ext, cut(end) - base, 0).reshape(-1, ABLK)
    lo = jnp.min(begins, axis=1) // FINE
    hi = (jnp.max(ends, axis=1) + (FINE - 1)) // FINE
    blank = jnp.max(ends, axis=1) == 0
    lo = jnp.where(blank, 0, lo)
    hi = jnp.where(blank, 0, hi)
    hot = cut(one_hot.T).T
    masked = cut(valid) == 0
    ones = jnp.ones((1, ext), jnp.bfloat16)
    fill = jnp.zeros((AUG - 9, ext), jnp.bfloat16)
    qaug = jnp.concatenate([hot.astype(jnp.bfloat16), ones, fill], axis=0)
    kaug = jnp.concatenate(
        [
            jnp.where(hot, 0.0, neg_big).astype(jnp.bfloat16),
            jnp.where(masked[None, :], neg_big, 0.0).astype(jnp.bfloat16),
            fill,
        ],
        axis=0,
    )
    hidden = jnp.broadcast_to(masked.astype(jnp.float32)[None, :], (8, ext))
    foreign = lax.dynamic_slice_in_dim(crossing & ~worker, half * rows, rows, 0)
    return lo, hi, qaug, kaug, hidden, handled_ext, foreign


def normal_parts(values):
    bell = jnp.exp(values * values * -0.5)
    return (0.5 + 0.5 * lax.erf(values * 0.7071067811865476), bell * 0.3989422804014327)


UNITS = 1024
STRIP = 512


def up_kernel(x_ref, w_ref, bias_ref, gelu_ref, slope_ref):
    for r in range(0, x_ref.shape[0], STRIP):
        strip = slice(r, r + STRIP)
        values = mm(x_ref[strip, :], w_ref[...], NT) + bias_ref[...]
        cdf, bell = normal_parts(values)
        gelu_ref[strip, :] = (values * cdf).astype(jnp.bfloat16)
        slope_ref[strip, :] = (cdf + values * bell).astype(jnp.bfloat16)


def feed_up(rows, weights, bias):
    length = rows.shape[0]
    units = weights.shape[0]
    out = jax.ShapeDtypeStruct((length, units), jnp.bfloat16)
    columns = pl.BlockSpec((length, UNITS), lambda n: (0, n))
    return pl.pallas_call(
        up_kernel,
        out_shape=(out, out),
        grid=(units // UNITS,),
        in_specs=[
            pl.BlockSpec((length, D), lambda n: (0, 0)),
            pl.BlockSpec((UNITS, D), lambda n: (n, 0)),
            pl.BlockSpec((1, UNITS), lambda n: (0, n)),
        ],
        out_specs=(columns, columns),
        compiler_params=pltpu.CompilerParams(vmem_limit_bytes=60 * 2**20),
        cost_estimate=pl.CostEstimate(
            flops=2 * length * units * D, bytes_accessed=26 * 10**6, transcendentals=0
        ),
        name="feed_up",
    )(rows, weights, bias.reshape(1, units))


def down_back_kernel(g_ref, w_ref, slope_ref, out_ref, sum_ref):
    total = jnp.zeros((1, UNITS), jnp.float32)
    for r in range(0, g_ref.shape[0], STRIP):
        strip = slice(r, r + STRIP)
        grads = mm(g_ref[strip, :], w_ref[...], NT) * slope_ref[strip, :].astype(jnp.float32)
        low = grads.astype(jnp.bfloat16)
        out_ref[strip, :] = low
        total += jnp.sum(low.astype(jnp.float32), axis=0, keepdims=True)
    sum_ref[...] = total


def feed_down_back(grads, weights, slope):
    length = grads.shape[0]
    units = weights.shape[0]
    columns = pl.BlockSpec((length, UNITS), lambda n: (0, n))
    one_row = pl.BlockSpec((1, UNITS), lambda n: (0, n))
    return pl.pallas_call(
        down_back_kernel,
        out_shape=(
            jax.ShapeDtypeStruct((length, units), jnp.bfloat16),
            jax.ShapeDtypeStruct((1, units), jnp.float32),
        ),
        grid=(units // UNITS,),
        in_specs=[
            pl.BlockSpec((length, D), lambda n: (0, 0)),
            pl.BlockSpec((UNITS, D), lambda n: (n, 0)),
            columns,
        ],
        out_specs=(columns, one_row),
        compiler_params=pltpu.CompilerParams(vmem_limit_bytes=40 * 2**20),
        cost_estimate=pl.CostEstimate(
            flops=2 * length * units * D, bytes_accessed=26 * 10**6, transcendentals=0
        ),
        name="feed_down_back",
    )(grads, weights, slope)


MESH = pl.DeviceIdType.MESH
CHUNKS = 3
GROUPS = ((0, 3), (3, 1), (4, 4))
PARTS = (((0, 1), (1, 2)), ((0, 1), None), ((0, 2), (2, 2)))


def neighbours(z, y, core, x):
    def at(z, y, core, x):
        return {"dp": (z * 2 + y) * 2 + core, "tensor": x}

    return {
        "x": at(z, y, core, 1 - x),
        "y": at(z, 1 - y, core, x),
        "core": at(z, y, 1 - core, x),
        "up": at(jnp.minimum(z + 1, 3), y, core, x),
        "down": at(jnp.maximum(z - 1, 0), y, core, x),
    }


def greet(near, z):
    barrier = pltpu.get_barrier_semaphore()
    for name in ("x", "y", "core"):
        pl.semaphore_signal(barrier, inc=1, device_id=near[name], device_id_type=MESH)

    @pl.when(z < 3)
    def _up():
        pl.semaphore_signal(barrier, inc=1, device_id=near["up"], device_id_type=MESH)

    @pl.when(z > 0)
    def _down():
        pl.semaphore_signal(barrier, inc=1, device_id=near["down"], device_id_type=MESH)

    at_end = jnp.where((z == 0) | (z == 3), 1, 0)
    pl.semaphore_wait(barrier, 5 - at_end)


def greet_all(near, me, n_dp):
    barrier = pltpu.get_barrier_semaphore()
    pl.semaphore_signal(barrier, inc=1, device_id=near["x"], device_id_type=MESH)

    def one(i, _):
        other = {"dp": lax.rem(me + i, n_dp), "tensor": lax.axis_index("tensor")}
        pl.semaphore_signal(barrier, inc=1, device_id=other, device_id_type=MESH)
        return 0

    lax.fori_loop(1, n_dp, one, 0)
    pl.semaphore_wait(barrier, n_dp)


def gather_kernel(
    owners_ref, slots_ref, tokens_ref, qkv_ref, out_ref, up_ref, down_ref, ext_ref,
    slot_ref, low_ref, spread_ref, dense_ref, zero_ref, local_sem, own_sem, ext_sem, post, mail, send, recv, halo_send, halo_recv,
):
    z, y, core, x = coordinates()
    near = neighbours(z, y, core, x)
    width = D // 2
    me = lax.axis_index("dp")
    n_dp = low_ref.shape[0]
    for to in range(n_dp):
        lines = slice((to // 2) * 16, (to // 2) * 16 + 16)
        columns = slice((to % 2) * width, (to % 2) * width + width)
        low_ref[to] = slots_ref[:, lines, columns].astype(low_ref.dtype)
    greet_all(near, me, n_dp)

    def letter(to):
        return pltpu.make_async_remote_copy(
            src_ref=low_ref.at[to],
            dst_ref=spread_ref.at[pl.ds(me * CAP, CAP)],
            send_sem=post.at[to],
            recv_sem=mail.at[me],
            device_id={"dp": to, "tensor": x},
            device_id_type=MESH,
        )

    def answer(of):
        return pltpu.make_async_remote_copy(
            src_ref=low_ref.at[of],
            dst_ref=spread_ref.at[pl.ds(of * CAP, CAP)],
            send_sem=post.at[of],
            recv_sem=mail.at[of],
            device_id={"dp": of, "tensor": x},
            device_id_type=MESH,
        )

    def peer(i):
        return lax.rem(me + i, n_dp)

    def post_one(i, _):
        letter(peer(i)).start()
        return 0

    lax.fori_loop(1, n_dp, post_one, 0)

    rows = tokens_ref.shape[0]
    halo = DOC_MAX // 2
    blank = zero_ref.shape[0]
    zero_ref[...] = jnp.zeros_like(zero_ref)
    edge = pl.multiple_of(jnp.where(x == 0, rows - halo, 0), 16)
    there = pl.multiple_of(jnp.where(x == 0, EXT_PAD - halo, rows), 16)
    rest = pl.multiple_of(jnp.where(x == 0, rows + halo, 0), 16)
    border = pltpu.make_async_remote_copy(
        src_ref=tokens_ref.at[pl.ds(edge, halo)],
        dst_ref=ext_ref.at[pl.ds(there, halo)],
        send_sem=halo_send,
        recv_sem=halo_recv,
        device_id=near["x"],
        device_id_type=MESH,
    )
    border.start()
    inside = pltpu.make_async_copy(
        tokens_ref, ext_ref.at[pl.ds(pl.multiple_of(x * EXT_PAD, 16), rows)], ext_sem.at[0]
    )
    inside.start()
    empty = pltpu.make_async_copy(zero_ref, ext_ref.at[pl.ds(rest, blank)], ext_sem.at[1])
    empty.start()
    mine = pltpu.make_async_copy(low_ref.at[me], spread_ref.at[pl.ds(me * CAP, CAP)], local_sem)
    mine.start()
    mine.wait()

    def find(p, _):
        owner = owners_ref[p]

        def count(q, before):
            return before + jnp.where(owners_ref[q] == owner, 1, 0)

        slot_ref[p] = owner * CAP + lax.fori_loop(0, p, count, 0)
        return 0

    lax.fori_loop(0, owners_ref.shape[0], find, 0)

    def mail_one(i, _):
        answer(peer(i)).wait_recv()
        letter(peer(i)).wait_send()
        return 0

    lax.fori_loop(1, n_dp, mail_one, 0)

    def place(p, _):
        dense_ref[p // 4, p % 4] = spread_ref[slot_ref[p]]
        return 0

    lax.fori_loop(0, owners_ref.shape[0], place, 0)
    rest_groups = pl.ds(GROUPS[-1][0] + GROUPS[-1][1], 4)
    later = pltpu.make_async_copy(dense_ref.at[rest_groups], down_ref, local_sem)
    later.start()
    later.wait()

    def block(k, t, zz, yy, cc, part=None):
        groups = slice(None) if part is None else pl.ds(*PARTS[k][part])
        return (qkv_ref, out_ref, up_ref)[k].at[
            groups,
            t,
            :,
            pl.ds(pl.multiple_of((zz * 2 + yy) * 16, 16), 16),
            pl.ds(pl.multiple_of(cc * width, width), width),
        ]

    own = [
        pltpu.make_async_copy(dense_ref.at[pl.ds(*GROUPS[k])], block(k, x, z, y, core), own_sem.at[k])
        for k in range(CHUNKS)
    ]
    for one in own:
        one.start()

    def copy(kind, link, k, zz, t, yy, cc, part=None, fresh=False):
        view = block(k, t, zz, yy, cc, part)
        return pltpu.make_async_remote_copy(
            src_ref=dense_ref.at[pl.ds(*GROUPS[k])] if fresh else view,
            dst_ref=view,
            send_sem=send.at[kind, k, zz],
            recv_sem=recv.at[kind, k, zz],
            device_id=near[link],
            device_id_type=MESH,
        )

    def up(k, zz, fresh=False):
        return copy(0, "up", k, zz, x, y, core, fresh=fresh)

    def down(k, zz, fresh=False):
        return copy(1, "down", k, zz, x, y, core, fresh=fresh)

    def spread(k, zz, fresh):
        copy(2, "x", k, zz, x, y, core, fresh=fresh).start()
        copy(3, "y", k, zz, x, y, core, fresh=fresh).start()
        copy(4, "core", k, zz, x, y, core, fresh=fresh).start()

    def each(d, body):
        @pl.when((d > 0) & (z - d >= 0))
        def _below():
            for k in range(CHUNKS):
                body(k, z - d, 0)

        @pl.when((d > 0) & (z + d <= 3))
        def _above():
            for k in range(CHUNKS):
                body(k, z + d, 1)

    def each_or_own(d, body):
        each(d, body)

        @pl.when(d == 0)
        def _own():
            for k in range(CHUNKS):
                body(k, z, None)

    def begin(k):
        @pl.when(z < 3)
        def _up():
            up(k, z, True).start()

        @pl.when(z > 0)
        def _down():
            down(k, z, True).start()

        spread(k, z, True)

    def first(k, zz, side):
        if side == 0:
            up(k, zz).wait_recv()

            @pl.when(z < 3)
            def _up():
                up(k, zz).start()

        else:
            down(k, zz).wait_recv()

            @pl.when(z > 0)
            def _on():
                down(k, zz).start()

        spread(k, zz, False)

    def second(k, zz, side):
        copy(2, "x", k, zz, 1 - x, y, core).wait_recv()
        copy(5, "y", k, zz, 1 - x, y, core, 0).start()
        copy(7, "core", k, zz, 1 - x, y, core).start()
        copy(3, "y", k, zz, x, 1 - y, core).wait_recv()
        if PARTS[k][1]:
            copy(6, "x", k, zz, x, 1 - y, core, 1).start()
        copy(8, "core", k, zz, x, 1 - y, core).start()

    def third(k, zz, side):
        copy(5, "y", k, zz, 1 - x, 1 - y, core, 0).wait_recv()
        copy(9, "core", k, zz, 1 - x, 1 - y, core, 0).start()
        if PARTS[k][1]:
            copy(6, "x", k, zz, 1 - x, 1 - y, core, 1).wait_recv()
            copy(10, "core", k, zz, 1 - x, 1 - y, core, 1).start()

    def finish(k, zz, side):
        if side != 1:

            @pl.when(z < 3)
            def _up():
                up(k, zz).wait_send()

        if side != 0:

            @pl.when(z > 0)
            def _down():
                down(k, zz).wait_send()

        copy(2, "x", k, zz, x, y, core).wait_send()
        copy(3, "y", k, zz, x, y, core).wait_send()
        copy(5, "y", k, zz, 1 - x, y, core, 0).wait_send()
        if PARTS[k][1]:
            copy(6, "x", k, zz, x, 1 - y, core, 1).wait_send()
        copy(4, "core", k, zz, x, y, core).wait_send()
        copy(7, "core", k, zz, 1 - x, y, core).wait_send()
        copy(8, "core", k, zz, x, 1 - y, core).wait_send()
        copy(9, "core", k, zz, 1 - x, 1 - y, core, 0).wait_send()
        if PARTS[k][1]:
            copy(10, "core", k, zz, 1 - x, 1 - y, core, 1).wait_send()
        copy(4, "core", k, zz, x, y, 1 - core).wait_recv()
        copy(7, "core", k, zz, 1 - x, y, 1 - core).wait_recv()
        copy(8, "core", k, zz, x, 1 - y, 1 - core).wait_recv()
        copy(9, "core", k, zz, 1 - x, 1 - y, 1 - core, 0).wait_recv()
        if PARTS[k][1]:
            copy(10, "core", k, zz, 1 - x, 1 - y, 1 - core, 1).wait_recv()

    for k in range(CHUNKS):
        begin(k)

    def step(d, _):
        @pl.when(d < 4)
        def _one():
            each(d, first)

        @pl.when((d >= 1) & (d < 5))
        def _two():
            each_or_own(d - 1, second)

        @pl.when(d >= 2)
        def _three():
            each_or_own(d - 2, third)

        return 0

    lax.fori_loop(1, 6, step, 0)

    def end(d, _):
        each_or_own(d, finish)
        return 0

    lax.fori_loop(0, 4, end, 0)
    for one in own:
        one.wait()
    border.wait()
    inside.wait()
    empty.wait()


def gather_weights(owners, slots, tokens):
    n_dp = lax.axis_size("dp")
    low = jnp.bfloat16
    rows = tokens.shape[0]
    anywhere = pl.BlockSpec(memory_space=pl.ANY)
    return pl.pallas_call(
        gather_kernel,
        out_shape=tuple(
            jax.ShapeDtypeStruct((count, 2, 4, 128, D), low) for first, count in GROUPS
        )
        + (
            jax.ShapeDtypeStruct((4, 4, 16, D // 2), low),
            jax.ShapeDtypeStruct((rows + EXT_PAD, D), tokens.dtype),
        ),
        in_specs=[
            pl.BlockSpec(memory_space=pltpu.SMEM),
            pl.BlockSpec(memory_space=pltpu.VMEM),
            anywhere,
        ],
        out_specs=(anywhere,) * 5,
        scratch_shapes=[
            pltpu.SMEM(owners.shape, jnp.int32),
            pltpu.VMEM((n_dp, CAP, 16, D // 2), low),
            pltpu.VMEM((n_dp * CAP, 16, D // 2), low),
            pltpu.VMEM((12, 4, 16, D // 2), low),
            pltpu.VMEM((EXT_PAD - DOC_MAX // 2, D), tokens.dtype),
            pltpu.SemaphoreType.DMA,
            pltpu.SemaphoreType.DMA((CHUNKS,)),
            pltpu.SemaphoreType.DMA((2,)),
            pltpu.SemaphoreType.DMA((n_dp,)),
            pltpu.SemaphoreType.DMA((n_dp,)),
            pltpu.SemaphoreType.DMA((11, CHUNKS, 4)),
            pltpu.SemaphoreType.DMA((11, CHUNKS, 4)),
            pltpu.SemaphoreType.DMA,
            pltpu.SemaphoreType.DMA,
        ],
        compiler_params=pltpu.CompilerParams(
            collective_id=1, has_side_effects=True, vmem_limit_bytes=60 * 2**20
        ),
        cost_estimate=pl.CostEstimate(flops=0, bytes_accessed=50 * 10**6, transcendentals=0),
        name="gather_weights",
    )(owners, slots, tokens)


def stack_kernel(parts_ref, out_ref):
    for p in range(4):
        for line in range(8):
            for half in range(2):
                columns = slice(half * (D // 2), (half + 1) * (D // 2))
                out_ref[0, 0, p, line, :, columns] = parts_ref[0, line, half, 0, p]


def stack_chunks(parts):
    return pl.pallas_call(
        stack_kernel,
        out_shape=jax.ShapeDtypeStruct((4, 2, 4, 8, 16, D), parts.dtype),
        grid=(4, 2),
        in_specs=[
            pl.BlockSpec((1, 8, 2, 1, 4, 16, D // 2), lambda m, t: (t, 0, 0, m, 0, 0, 0)),
        ],
        out_specs=pl.BlockSpec((1, 1, 4, 8, 16, D), lambda m, t: (m, t, 0, 0, 0, 0)),
        compiler_params=pltpu.CompilerParams(vmem_limit_bytes=60 * 2**20),
        cost_estimate=pl.CostEstimate(flops=0, bytes_accessed=17 * 10**6, transcendentals=0),
        name="stack_chunks",
    )(parts)


BLOCKS = 12
SLICES = 2
STEPS = BLOCKS * SLICES
LAG = 2


def reduce_kernel(
    piece_ref, vec_ref, qkv_ref, ctx_ref, pre_ref, hid_ref, tok_ref, gext_ref, norm_ref, two_ref, weight_ref,
    out_ref, sum_ref, input_ref, border_ref,
    weight_buf, strip, strip_out, weight_sem, strip_sem, strip_out_sem, border_send, border_recv,
    tile, tall, ext_rhs, row_rhs, far_buf, near_buf, core_in, x_in, y_in, x2_in, y2_in, line, line_in,
    done, parcel, vec_in, vec_out,
    tile_sem, rhs_sem, local_sem, post, mail, send, recv, vec_send, vec_recv,
):
    z, y, core, x = coordinates()
    near = neighbours(z, y, core, x)
    me = lax.axis_index("dp")
    n_dp = parcel.shape[1]
    half_width = D // 2
    width = half_width // SLICES
    rows = tile.shape[1]
    tiles = 1024 // rows

    def right(n, half, cut):
        ref = (tok_ref, gext_ref, norm_ref, two_ref)[n]
        to = ext_rhs.at[n, half, cut] if n < 2 else row_rhs.at[n - 2, half, cut]
        which = 1 - core if half == 0 else core
        columns = pl.ds(pl.multiple_of(which * half_width + cut * width, width), width)
        return pltpu.make_async_copy(ref.at[:, columns], to, rhs_sem.at[n, half, cut])

    for cut in range(SLICES):
        for n in range(4):
            for half in range(2):
                right(n, half, cut).start()

    def fetch(n, body):
        i = lax.rem(n // tiles, BLOCKS)
        part = pl.ds(pl.multiple_of(lax.rem(n, tiles) * rows, rows), rows)
        slot = lax.rem(n, 2)
        ext = ext_rhs.shape[3]
        wide = tile.at[slot, :, pl.ds(0, ext)]
        sem = tile_sem.at[slot]

        @pl.when(i < 3)
        def _qkv():
            body(pltpu.make_async_copy(qkv_ref.at[i, part, :], wide, sem))

        @pl.when(i == 3)
        def _out():
            body(pltpu.make_async_copy(ctx_ref.at[part, :], wide, sem))

        def columns(first):
            start = (i - first) * 1024 + lax.rem(n, tiles) * rows
            return pl.ds(pl.multiple_of(start, rows), rows)

        @pl.when((i >= 4) & (i < 8))
        def _up():
            body(pltpu.make_async_copy(pre_ref.at[:, columns(4)], tall.at[slot], sem))

        @pl.when(i >= 8)
        def _down():
            body(pltpu.make_async_copy(hid_ref.at[:, columns(8)], tall.at[slot], sem))

    strip_rows = strip.shape[3]
    strips = qkv_ref.shape[2] // strip_rows
    weight_copy = pltpu.make_async_copy(weight_ref, weight_buf, weight_sem)
    weight_copy.start()

    def strip_copy(r):
        slot = lax.rem(r, 2)
        here = pl.ds(pl.multiple_of(r * strip_rows, strip_rows), strip_rows)
        return pltpu.make_async_copy(qkv_ref.at[:, :, here], strip.at[slot], strip_sem.at[slot])

    def strip_done(r):
        slot = lax.rem(r, 2)
        here = pl.ds(pl.multiple_of(r * strip_rows, strip_rows), strip_rows)
        return pltpu.make_async_copy(strip_out.at[slot], input_ref.at[here], strip_out_sem.at[slot])

    def input_strip(r):
        slot = lax.rem(r, 2)

        @pl.when(r + 1 < strips)
        def _next():
            strip_copy(r + 1).start()

        @pl.when(r >= 2)
        def _free():
            strip_done(r - 2).wait()

        strip_copy(r).wait()
        total = mm(strip[slot, 0], weight_buf[0], TN)
        total += mm(strip[slot, 1], weight_buf[1], TN)
        total += mm(strip[slot, 2], weight_buf[2], TN)
        strip_out[slot] = total.astype(jnp.bfloat16)
        strip_done(r).start()

    halo = border_ref.shape[0]
    border_at = pl.multiple_of(jnp.where(x == 0, input_ref.shape[0] - EXT_PAD, EXT_PAD - halo), 16)
    border = pltpu.make_async_remote_copy(
        src_ref=input_ref.at[pl.ds(border_at, halo)],
        dst_ref=border_ref,
        send_sem=border_send,
        recv_sem=border_recv,
        device_id=near["x"],
        device_id_type=MESH,
    )
    strip_copy(0).start()
    fetch(0, lambda copy: copy.start())
    greet_all(near, me, n_dp)

    def remote(kind, i, link, src, dst):
        return pltpu.make_async_remote_copy(
            src_ref=src,
            dst_ref=dst,
            send_sem=send.at[kind, i],
            recv_sem=recv.at[kind, i],
            device_id=near[link],
            device_id_type=MESH,
        )

    def core_copy(i):
        return remote(0, i, "core", far_buf.at[lax.rem(i, 2)], core_in.at[i])

    def x1(i):
        return remote(1, i, "x", core_in.at[i, 1 - x, pl.ds(0, 2)], x_in.at[i])

    def y1(i):
        return remote(2, i, "y", core_in.at[i, :, pl.ds(2, 2), :, 1 - y], y_in.at[i])

    def y2(i):
        return remote(3, i, "y", x_in.at[i, :, :, 1 - y], y2_in.at[i])

    def x2(i):
        return remote(4, i, "x", y_in.at[i, 1 - x], x2_in.at[i])

    def along(i, zz):
        return pltpu.make_async_remote_copy(
            src_ref=line.at[i, zz],
            dst_ref=line_in.at[i, z],
            send_sem=send.at[5 + zz, i],
            recv_sem=recv.at[5 + z, i],
            device_id={"dp": (zz * 2 + y) * 2 + core, "tensor": x},
            device_id_type=MESH,
        )

    def arrival(i, zz):
        return pltpu.make_async_remote_copy(
            src_ref=line.at[i, zz],
            dst_ref=line_in.at[i, zz],
            send_sem=send.at[5 + zz, i],
            recv_sem=recv.at[5 + zz, i],
            device_id={"dp": (zz * 2 + y) * 2 + core, "tensor": x},
            device_id_type=MESH,
        )

    def produce(b):
        ring = lax.rem(b, 2)
        cut = b // BLOCKS
        i = lax.rem(b, BLOCKS)

        for c in range(SLICES):
            for n, first in enumerate((0, 3, 4, 8)):

                @pl.when(b == c * BLOCKS + first)
                def _ready():
                    right(n, 0, c).wait()
                    right(n, 1, c).wait()

        @pl.when(b >= 2)
        def _free():
            core_copy(b - 2).wait_send()

        def one(part, _):
            n = b * tiles + part
            slot = lax.rem(n, 2)

            @pl.when(n + 1 < STEPS * tiles)
            def _next():
                fetch(n + 1, lambda copy: copy.start())

            fetch(n, lambda copy: copy.wait())
            t, p = part // 2, lax.rem(part, 2) * 2

            def put(value, to):
                to[ring, t, pl.ds(p, 2)] = value.astype(jnp.bfloat16).reshape(2, 4, 2, 16, width)

            @pl.when(i < 4)
            def _wide():
                which = jnp.where(i < 3, 0, 1)
                put(mm(tile[slot], ext_rhs[which, 0, cut], NN), far_buf)
                put(mm(tile[slot], ext_rhs[which, 1, cut], NN), near_buf)

            @pl.when(i >= 4)
            def _tall():
                which = jnp.where(i < 8, 0, 1)
                put(mm(tall[slot], row_rhs[which, 0, cut], TN), far_buf)
                put(mm(tall[slot], row_rhs[which, 1, cut], TN), near_buf)

            return 0

        lax.fori_loop(0, tiles, one, 0)
        core_copy(b).start()

    def stage_one(i):
        core_copy(i).wait_recv()
        ring = lax.rem(i, 2)

        def add(j, _):
            t, p = j // 4, j % 4
            core_in[i, t, p] = core_in[i, t, p] + near_buf[ring, t, p]
            return 0

        lax.fori_loop(0, 8, add, 0)
        x1(i).start()
        y1(i).start()

    def stage_two(i):
        x1(i).wait_recv()
        y1(i).wait_recv()
        for p in range(2):
            x_in[i, p] = x_in[i, p] + core_in[i, x, p]
        for t in range(2):
            for p in range(2):
                y_in[i, t, p] = y_in[i, t, p] + core_in[i, t, 2 + p, :, y]
        y2(i).start()
        x2(i).start()

    def stage_three(i):
        y2(i).wait_recv()
        x2(i).wait_recv()
        for p in range(2):
            line[i, :, p] = x_in[i, p, :, y] + y2_in[i, p]
            line[i, :, 2 + p] = y_in[i, x, p] + x2_in[i, p]
        for n in range(1, 4):
            along(i, lax.rem(z + n, 4)).start()

    def stage_last(b):
        cut = b // BLOCKS
        total = line[b, z].astype(jnp.float32)
        for n in range(1, 4):
            zz = lax.rem(z + n, 4)
            arrival(b, zz).wait_recv()
            total += line_in[b, zz].astype(jnp.float32)
        done[cut, pl.ds(lax.rem(b, BLOCKS) * 4, 4)] = total.astype(jnp.bfloat16)

    def place(of, cut):
        start = (of % 2) * half_width + cut * width
        return out_ref.at[
            :,
            pl.ds(pl.multiple_of((of // 2) * 16, 16), 16),
            pl.ds(pl.multiple_of(start, width), width),
        ]

    def letter(to, cut):
        return pltpu.make_async_remote_copy(
            src_ref=parcel.at[cut, to],
            dst_ref=place(me, cut),
            send_sem=post.at[cut, to],
            recv_sem=mail.at[cut, me],
            device_id={"dp": to, "tensor": x},
            device_id_type=MESH,
        )

    def answer(of, cut):
        return pltpu.make_async_remote_copy(
            src_ref=parcel.at[cut, of],
            dst_ref=place(of, cut),
            send_sem=post.at[cut, of],
            recv_sem=mail.at[cut, of],
            device_id={"dp": of, "tensor": x},
            device_id_type=MESH,
        )

    def own_letter(cut):
        return pltpu.make_async_copy(parcel.at[cut, me], place(me, cut), local_sem.at[cut])

    def post_all(cut):
        done[cut, BLOCKS * 4] = jnp.zeros((16, width), done.dtype)

        def pack(n, _):
            parcel[cut, n // CAP, n % CAP] = done[cut, piece_ref[n]]
            return 0

        lax.fori_loop(0, n_dp * CAP, pack, 0)

        def post_one(i, _):
            letter(lax.rem(me + i, n_dp), cut).start()
            return 0

        lax.fori_loop(1, n_dp, post_one, 0)
        own_letter(cut).start()

    def ended(i):
        @pl.when(i >= STEPS - 2)
        def _far():
            core_copy(i).wait_send()

        x1(i).wait_send()
        y1(i).wait_send()
        y2(i).wait_send()
        x2(i).wait_send()
        for n in range(1, 4):
            along(i, lax.rem(z + n, 4)).wait_send()

    z_one = z + 1 - 2 * lax.rem(z, 2)
    z_two = lax.rem(z + 2, 4)
    partners = [
        near["core"],
        near["y"],
        near["x"],
        {"dp": (z_one * 2 + y) * 2 + core, "tensor": x},
        {"dp": (z_two * 2 + y) * 2 + core, "tensor": x},
    ]

    def swap(n):
        return pltpu.make_async_remote_copy(
            src_ref=vec_out.at[n],
            dst_ref=vec_in.at[n],
            send_sem=vec_send.at[n],
            recv_sem=vec_recv.at[n],
            device_id=partners[n],
            device_id_type=MESH,
        )

    vec_out[0] = vec_ref[...]
    produce(0)

    def step(s, _):
        @pl.when(s + 1 < STEPS)
        def _produce():
            produce(s + 1)

        @pl.when(s < STEPS)
        def _one():
            stage_one(s)

        @pl.when((s >= LAG) & (s < STEPS + LAG))
        def _two():
            stage_two(s - LAG)

        @pl.when((s >= 2 * LAG) & (s < STEPS + 2 * LAG))
        def _three():
            stage_three(s - 2 * LAG)

        @pl.when(s == 2)
        def _weights():
            weight_copy.wait()

        @pl.when((s >= 2) & (s < 2 + 3 * strips) & (lax.rem(s, 3) == 2))
        def _input():
            input_strip(s // 3)

        @pl.when(s == 2 + 3 * strips)
        def _border():
            strip_done(strips - 2).wait()
            strip_done(strips - 1).wait()
            border.start()

        @pl.when(s >= 3 * LAG)
        def _last():
            stage_last(s - 3 * LAG)

        for cut in range(SLICES):

            @pl.when(s - 3 * LAG == cut * BLOCKS + BLOCKS - 1)
            def _post():
                post_all(cut)

        for n in range(5):

            @pl.when(s == n)
            def _begin():
                swap(n).start()

            @pl.when(s == n + 1)
            def _end():
                swap(n).wait()
                if n < 4:
                    vec_out[n + 1] = vec_out[n] + vec_in[n]
                else:
                    sum_ref[...] = vec_out[n] + vec_in[n]

        return 0

    lax.fori_loop(0, STEPS + 3 * LAG, step, 0)

    def finish(i, _):
        ended(i)
        return 0

    lax.fori_loop(0, STEPS, finish, 0)

    def mail_one(i, _):
        for cut in range(SLICES):
            answer(lax.rem(me + i, n_dp), cut).wait_recv()
            letter(lax.rem(me + i, n_dp), cut).wait_send()
        return 0

    lax.fori_loop(1, n_dp, mail_one, 0)
    for cut in range(SLICES):
        own_letter(cut).wait()
    border.wait()


def reduce_grads(piece_of, vec, qkv, context, pre, hidden, tokens, ext_grads, normed, two, weights):
    n_dp = piece_of.shape[0] // CAP
    low = jnp.bfloat16
    width = D // 2 // SLICES
    rows = 256
    ext = tokens.shape[0]
    length = normed.shape[0]
    anywhere = pl.BlockSpec(memory_space=pl.ANY)
    vmem = pl.BlockSpec(memory_space=pltpu.VMEM)
    return pl.pallas_call(
        reduce_kernel,
        out_shape=(
            jax.ShapeDtypeStruct((CAP, 128, D), low),
            jax.ShapeDtypeStruct(vec.shape, jnp.float32),
            jax.ShapeDtypeStruct((ext, D), low),
            jax.ShapeDtypeStruct((DOC_MAX // 2, D), low),
        ),
        in_specs=[pl.BlockSpec(memory_space=pltpu.SMEM), vmem] + [anywhere] * 9,
        out_specs=(anywhere, vmem, anywhere, anywhere),
        scratch_shapes=[
            pltpu.VMEM((3, D, D), low),
            pltpu.VMEM((2, 3, D, 256), low),
            pltpu.VMEM((2, 256, D), low),
            pltpu.SemaphoreType.DMA,
            pltpu.SemaphoreType.DMA((2,)),
            pltpu.SemaphoreType.DMA((2,)),
            pltpu.SemaphoreType.DMA,
            pltpu.SemaphoreType.DMA,
            pltpu.VMEM((2, rows, ext), low),
            pltpu.VMEM((2, length, rows), low),
            pltpu.VMEM((2, 2, SLICES, ext, width), low),
            pltpu.VMEM((2, 2, SLICES, length, width), low),
            pltpu.VMEM((2, 2, 4, 4, 2, 16, width), low),
            pltpu.VMEM((2, 2, 4, 4, 2, 16, width), low),
            pltpu.VMEM((STEPS, 2, 4, 4, 2, 16, width), low),
            pltpu.VMEM((STEPS, 2, 4, 2, 16, width), low),
            pltpu.VMEM((STEPS, 2, 2, 4, 16, width), low),
            pltpu.VMEM((STEPS, 2, 4, 16, width), low),
            pltpu.VMEM((STEPS, 2, 4, 16, width), low),
            pltpu.VMEM((STEPS, 4, 4, 16, width), low),
            pltpu.VMEM((STEPS, 4, 4, 16, width), low),
            pltpu.VMEM((SLICES, BLOCKS * 4 + 1, 16, width), low),
            pltpu.VMEM((SLICES, n_dp, CAP, 16, width), low),
            pltpu.VMEM((5,) + vec.shape, jnp.float32),
            pltpu.VMEM((5,) + vec.shape, jnp.float32),
            pltpu.SemaphoreType.DMA((2,)),
            pltpu.SemaphoreType.DMA((4, 2, SLICES)),
            pltpu.SemaphoreType.DMA((SLICES,)),
            pltpu.SemaphoreType.DMA((SLICES, n_dp)),
            pltpu.SemaphoreType.DMA((SLICES, n_dp)),
            pltpu.SemaphoreType.DMA((9, STEPS)),
            pltpu.SemaphoreType.DMA((9, STEPS)),
            pltpu.SemaphoreType.DMA((5,)),
            pltpu.SemaphoreType.DMA((5,)),
        ],
        compiler_params=pltpu.CompilerParams(
            collective_id=2, has_side_effects=True, vmem_limit_bytes=60 * 2**20
        ),
        cost_estimate=pl.CostEstimate(
            flops=41 * 10**9, bytes_accessed=50 * 10**6, transcendentals=0
        ),
        name="reduce_grads",
    )(piece_of, vec, qkv, context, pre, hidden, tokens, ext_grads, normed, two, weights)


def coordinates():
    dp = lax.axis_index("dp")
    return dp // 4, (dp // 2) % 2, dp % 2, lax.axis_index("tensor")


def exchange(values, axis):
    if axis == "x":
        return lax.ppermute(values, "tensor", [(0, 1), (1, 0)])
    flip = {"core": 1, "y": 2, "z_near": 4, "z_far": 8}[axis]
    return lax.ppermute(values, "dp", [(i, i ^ flip) for i in range(lax.axis_size("dp"))])


def pick(values, index, axis):
    return lax.dynamic_index_in_dim(values, index, axis, keepdims=False)


def on_device_rows(
    tokens,
    segment_ids,
    key_mask,
    owners,
    master_slots,
    slot_first,
    slot_second,
    vectors,
    vector_first,
    vector_second,
    out_grad,
):
    n_dp = lax.axis_size("dp")
    n_tensor = lax.axis_size("tensor")
    half = lax.axis_index("tensor")
    every = ("tensor", "dp")
    rows = tokens.shape[0]
    ext = rows + EXT_PAD
    halo = DOC_MAX // 2
    swap = [(0, 1), (1, 0)]
    edge = jnp.where(half == 0, rows - halo, 0)
    halo_at = jnp.where(half == 0, rows, EXT_PAD - halo)
    own_at = half * EXT_PAD

    def extend(own_rows, halo_rows):
        whole = jnp.zeros((ext,) + own_rows.shape[1:], own_rows.dtype)
        whole = lax.dynamic_update_slice_in_dim(whole, halo_rows, halo_at, 0)
        return lax.dynamic_update_slice_in_dim(whole, own_rows, own_at, 0)

    def own_part(values):
        return lax.dynamic_slice_in_dim(values, own_at, rows, 0)

    def halo_part(values):
        return lax.dynamic_slice_in_dim(values, halo_at, halo, 0)

    lo, hi, qaug, kaug, hidden_keys, handled, foreign = document_plan(
        segment_ids[0], key_mask[0], half, rows
    )
    slots = slot_index(owners)
    pieces = slots.shape[0]
    piece_rows = master_slots.shape[2]
    mix_pieces = 4 * (D // n_tensor) // piece_rows
    up_pieces = (FF // n_tensor) // piece_rows
    per = mix_pieces // 4
    w_qkv, w_out, w_up, down_chunk, tokens_ext = gather_weights(owners[:, 0], master_slots[0], tokens)
    w_qkv = w_qkv.reshape(3 * D, D)
    w_out = w_out.reshape(D, D)
    w_up = w_up.reshape(FF, D)
    down_chunks = lax.all_gather(down_chunk, every, axis=0, tiled=False)
    w_down = stack_chunks(down_chunks.reshape((n_tensor, 8, 2) + down_chunk.shape)).reshape(FF, D)
    bias_up = vectors[2:6].reshape(n_tensor, 4, -1).transpose(1, 0, 2).reshape(FF)

    bias_qkv = jnp.concatenate([vectors[0], jnp.zeros((D,), jnp.float32), vectors[1]])
    scale_qkv = jnp.concatenate([jnp.full((D,), HD ** (-0.5)), jnp.ones((2 * D,))])
    qkv = (
        (mm(w_qkv, tokens_ext, NT) + bias_qkv[:, None]) * scale_qkv.astype(jnp.float32)[:, None]
    ).astype(jnp.bfloat16)
    context, logs = attend(lo, hi, qkv, qaug, kaug, hidden_keys)
    attn_ext = mm(context, w_out, TN).astype(jnp.bfloat16)
    halo_attn = lax.ppermute(halo_part(attn_ext), "tensor", swap)
    attn_back = lax.dynamic_update_slice_in_dim(
        jnp.zeros((rows, D), jnp.bfloat16), halo_attn, edge, 0
    )
    attn_sum = jnp.where(foreign[:, None], attn_back, own_part(attn_ext)).astype(jnp.float32)
    residual_one = tokens.astype(jnp.float32) + (attn_sum + vectors[6])
    normal_one, inverse_one = layer_stats(residual_one)
    normed = normal_one * vectors[8] + vectors[9]
    normed_low = normed.astype(jnp.bfloat16)

    hidden, slope = feed_up(normed_low, w_up, bias_up)
    residual_two = normed + (mm(hidden, w_down, NN) + vectors[7])
    normal_two, inverse_two = layer_stats(residual_two)
    layer_out = (normal_two * vectors[10] + vectors[11]).astype(jnp.bfloat16)
    grad_out = out_grad.astype(jnp.float32)
    grad_two = norm_back(grad_out, normal_two, inverse_two, vectors[10])
    grad_two_low = grad_two.astype(jnp.bfloat16)

    grad_pre, up_sums = feed_down_back(grad_two_low, w_down, slope)
    grad_norm = grad_two + lax.optimization_barrier(mm(grad_pre, w_up, NN))
    grad_one = norm_back(grad_norm, normal_one, inverse_one, vectors[8])
    grad_one_low = grad_one.astype(jnp.bfloat16)

    halo_grad = lax.ppermute(
        lax.dynamic_slice_in_dim(grad_one_low, edge, halo, 0), "tensor", swap
    )
    grad_ext = jnp.where(handled[:, None], extend(grad_one_low, halo_grad), 0)
    grad_context = mm(w_out, grad_ext, NT).astype(jnp.bfloat16)
    grad_qkv, qkv_sums = attend_back(
        lo, hi, qkv, grad_context, context, logs, qaug, kaug, hidden_keys
    )

    vector_terms = jnp.concatenate(
        [
            qkv_sums[:, :, 0],
            up_sums.reshape(4, n_tensor, -1)
            .transpose(1, 0, 2)
            .reshape(FF // D, D),
            jnp.stack(
                [
                    jnp.sum(grad_one, axis=0),
                    jnp.sum(grad_two, axis=0),
                    jnp.sum(grad_norm * normal_one, axis=0),
                    jnp.sum(grad_norm, axis=0),
                    jnp.sum(grad_out * normal_two, axis=0),
                    jnp.sum(grad_out, axis=0),
                ]
            ),
        ],
        axis=0,
    )
    piece_of = jnp.full((n_dp * CAP,), pieces, jnp.int32).at[slots].set(
        jnp.arange(pieces, dtype=jnp.int32)
    )
    own_grads, vector_grads, input_ext, halo_input = reduce_grads(
        piece_of,
        vector_terms,
        grad_qkv,
        context,
        grad_pre,
        hidden,
        tokens_ext,
        grad_ext,
        normed_low,
        grad_two_low,
        w_qkv.reshape(3, D, D),
    )
    own_grads = own_grads.astype(jnp.float32)
    input_back = lax.dynamic_update_slice_in_dim(
        jnp.zeros((rows, D), jnp.bfloat16), halo_input, edge, 0
    )
    input_grad = (
        grad_one + own_part(input_ext).astype(jnp.float32) + input_back.astype(jnp.float32)
    ).astype(jnp.bfloat16)
    slot_new, slot_first_new, slot_second_new = adam_update(
        master_slots[0], slot_first[0], slot_second[0], own_grads, rate_matrix, weight_decay
    )
    vector_new, vector_first_new, vector_second_new = adam_update(
        vectors, vector_first, vector_second, vector_grads, rate_vector, 0.0
    )
    return (
        layer_out,
        input_grad,
        slot_new[None],
        slot_first_new[None],
        slot_second_new[None],
        vector_new,
        vector_first_new,
        vector_second_new,
    )


def solution(mesh):
    placed = (
        P(("dp", "tensor"), None),
        P("dp", None),
        P("dp", None),
        P(),
        P("tensor", "dp", None, None),
        P("tensor", "dp", None, None),
        P("tensor", "dp", None, None),
        P(),
        P(),
        P(),
        P(("dp", "tensor"), None),
    )
    by_rows = mesh.shape["tensor"] == 2 and mesh.shape["dp"] == 16
    return jax.shard_map(
        on_device_rows if by_rows else on_device_generic,
        mesh=mesh,
        in_specs=placed,
        out_specs=(
            P(("dp", "tensor"), None),
            P(("dp", "tensor"), None),
            P("tensor", "dp", None, None),
            P("tensor", "dp", None, None),
            P("tensor", "dp", None, None),
            P(),
            P(),
            P(),
        ),
        check_vma=False,
    )
```

```python
import functools

import jax
import jax.numpy as jnp
from jax import lax
from jax.experimental import pallas as pl
from jax.experimental.pallas import tpu as pltpu
from jax.sharding import PartitionSpec as P

D = 1024
HD = 64
FF = 4096
QBLK = 512
STEP = 10
CAP = 6


norm_eps = 1e-05
mask_fill = -1000000000.0
beta_one = 0.5
beta_two = 0.5
rate_matrix = 0.03
rate_vector = 0.1
weight_decay = 0.01
adam_eps = 1e-08


def slot_index(owners):
    owner_of = owners[:, 0]
    positions = jnp.arange(owner_of.shape[0], dtype=jnp.int32)
    earlier = (positions[None, :] < positions[:, None]) & (owner_of[None, :] == owner_of[:, None])
    within = jnp.sum(earlier.astype(jnp.int32), axis=1)
    return owner_of * CAP + within


def layer_stats(residual):
    center = residual - jnp.mean(residual, axis=-1, keepdims=True)
    spread = jnp.mean(center * center, axis=-1, keepdims=True)
    inverse = lax.rsqrt(spread + norm_eps)
    return (center * inverse, inverse)


def norm_back(grads, normal, inverse, gains):
    scaled = grads * gains
    return inverse * (
        scaled
        - jnp.mean(scaled, axis=-1, keepdims=True)
        - normal * jnp.mean(scaled * normal, axis=-1, keepdims=True)
    )


def gelu_exact(values):
    return jax.nn.gelu(values, approximate=False)


def block_mask(segment, valid, start):
    length = segment.shape[0]
    query_pos = start + jnp.arange(QBLK, dtype=jnp.int32)
    key_pos = jnp.arange(length, dtype=jnp.int32)
    query_seg = lax.dynamic_slice_in_dim(segment, start, QBLK, 0)
    same = query_seg[:, None] == segment[None, :]
    return same & ((valid[None, :] == 1) | (query_pos[:, None] == key_pos[None, :]))


def block_scores(block_q, key_rows, segment, valid, start):
    scores = jnp.einsum("qhd,khd->hqk", block_q, key_rows, preferred_element_type=jnp.float32)
    return jnp.where(block_mask(segment, valid, start)[None], scores, mask_fill)


def attend_forward(queries, key_rows, value_rows, segment, valid):
    length = queries.shape[0]

    def one_block(index):
        start = index * QBLK
        block_q = lax.dynamic_slice_in_dim(queries, start, QBLK, 0)
        scores = block_scores(block_q, key_rows, segment, valid, start)
        row_max = jnp.max(scores, axis=2, keepdims=True)
        raised = jnp.exp(scores - row_max)
        totals = jnp.sum(raised, axis=2, keepdims=True)
        weights = (raised / totals).astype(jnp.bfloat16)
        context = jnp.einsum(
            "hqk,khd->qhd", weights, value_rows, preferred_element_type=jnp.float32
        )
        return (context, (row_max + jnp.log(totals))[:, :, 0])

    context, log_sums = lax.map(one_block, jnp.arange(length // QBLK, dtype=jnp.int32))
    return (context.reshape(length, -1), log_sums)


def attend_backward(queries, key_rows, value_rows, segment, valid, log_sums, grad_context):
    length = queries.shape[0]

    def one_block(carry, index):
        key_acc, value_acc = carry
        start = index * QBLK
        block_q = lax.dynamic_slice_in_dim(queries, start, QBLK, 0)
        block_g = lax.dynamic_slice_in_dim(grad_context, start, QBLK, 0)
        scores = block_scores(block_q, key_rows, segment, valid, start)
        weights = jnp.exp(scores - log_sums[index][:, :, None])
        value_acc = value_acc + jnp.einsum(
            "hqk,qhd->khd",
            weights.astype(jnp.bfloat16),
            block_g,
            preferred_element_type=jnp.float32,
        )
        grad_weights = jnp.einsum(
            "qhd,khd->hqk", block_g, value_rows, preferred_element_type=jnp.float32
        )
        inner = jnp.sum(weights * grad_weights, axis=2, keepdims=True)
        grad_scores = (weights * (grad_weights - inner)).astype(jnp.bfloat16)
        grad_q = jnp.einsum(
            "hqk,khd->qhd", grad_scores, key_rows, preferred_element_type=jnp.float32
        )
        key_acc = key_acc + jnp.einsum(
            "hqk,qhd->khd", grad_scores, block_q, preferred_element_type=jnp.float32
        )
        return ((key_acc, value_acc), grad_q)

    zeros_kv = jnp.zeros(key_rows.shape, jnp.float32)
    (grad_keys, grad_values), grad_queries = lax.scan(
        one_block, (zeros_kv, zeros_kv), jnp.arange(length // QBLK, dtype=jnp.int32)
    )
    return (
        grad_queries.reshape(length, -1),
        grad_keys.reshape(length, -1),
        grad_values.reshape(length, -1),
    )


def adam_update(weights, first, second, grads, rate, decay):
    first_new = beta_one * first + (1.0 - beta_one) * grads
    second_new = beta_two * second + (1.0 - beta_two) * grads * grads
    first_hat = first_new / (1.0 - beta_one**STEP)
    second_hat = second_new / (1.0 - beta_two**STEP)
    updated = weights - rate * (first_hat / (jnp.sqrt(second_hat) + adam_eps) + decay * weights)
    return (updated, first_new, second_new)


def on_device_generic(
    tokens,
    segment_ids,
    key_mask,
    owners,
    master_slots,
    slot_first,
    slot_second,
    vectors,
    vector_first,
    vector_second,
    out_grad,
):
    n_tensor = lax.axis_size("tensor")
    group = lax.axis_index("tensor")
    head_cols = D // n_tensor
    unit_cols = FF // n_tensor
    heads_here = head_cols // HD
    seq_count = segment_ids.shape[0]
    length = segment_ids.shape[1]
    query_scale = HD ** (-0.5)
    slots = slot_index(owners)
    gathered_slots = lax.all_gather(master_slots[0].astype(jnp.bfloat16), "dp", axis=0, tiled=True)
    stack = jnp.take(gathered_slots, slots, axis=0).reshape(-1, D)
    w_mix = stack[0 : 3 * head_cols]
    w_out = stack[3 * head_cols : 4 * head_cols]
    w_up = stack[4 * head_cols : 4 * head_cols + unit_cols]
    w_down = stack[4 * head_cols + unit_cols :]
    bias_query = lax.dynamic_slice_in_dim(vectors[0], group * head_cols, head_cols, 0)
    bias_value = lax.dynamic_slice_in_dim(vectors[1], group * head_cols, head_cols, 0)
    bias_up = lax.dynamic_slice_in_dim(vectors[2:6].reshape(FF), group * unit_cols, unit_cols, 0)
    gathered = lax.all_gather(tokens, "tensor", axis=0, tiled=True)
    mixed = jnp.einsum("ld,kd->lk", gathered, w_mix, preferred_element_type=jnp.float32)
    queries = ((mixed[:, :head_cols] + bias_query) * query_scale).astype(jnp.bfloat16)
    key_rows = mixed[:, head_cols : 2 * head_cols].astype(jnp.bfloat16)
    value_rows = (mixed[:, 2 * head_cols :] + bias_value).astype(jnp.bfloat16)
    head_shape = (seq_count, length, heads_here, HD)
    queries_h = queries.reshape(head_shape)
    keys_h = key_rows.reshape(head_shape)
    values_h = value_rows.reshape(head_shape)

    def forward_seq(element):
        return attend_forward(element[0], element[1], element[2], element[3], element[4])

    context, log_sums = lax.map(forward_seq, (queries_h, keys_h, values_h, segment_ids, key_mask))
    context = context.reshape(-1, head_cols).astype(jnp.bfloat16)
    attn_sum = lax.psum_scatter(
        jnp.einsum("lk,kd->ld", context, w_out, preferred_element_type=jnp.float32).astype(
            jnp.bfloat16
        ),
        "tensor",
        scatter_dimension=0,
        tiled=True,
    ).astype(jnp.float32)
    residual_one = tokens.astype(jnp.float32) + (attn_sum + vectors[6])
    normal_one, inverse_one = layer_stats(residual_one)
    normed = normal_one * vectors[8] + vectors[9]
    normed_low = normed.astype(jnp.bfloat16)
    norm_rows = lax.all_gather(normed_low, "tensor", axis=0, tiled=True)
    hidden_pre = (
        jnp.einsum("ld,kd->lk", norm_rows, w_up, preferred_element_type=jnp.float32) + bias_up
    )
    hidden_full, gelu_pull = jax.vjp(gelu_exact, hidden_pre)
    hidden = hidden_full.astype(jnp.bfloat16)
    mlp_sum = lax.psum_scatter(
        jnp.einsum("lk,kd->ld", hidden, w_down, preferred_element_type=jnp.float32).astype(
            jnp.bfloat16
        ),
        "tensor",
        scatter_dimension=0,
        tiled=True,
    ).astype(jnp.float32)
    residual_two = normed + (mlp_sum + vectors[7])
    normal_two, inverse_two = layer_stats(residual_two)
    layer_out = (normal_two * vectors[10] + vectors[11]).astype(jnp.bfloat16)
    grad_out = out_grad.astype(jnp.float32)
    grad_two = norm_back(grad_out, normal_two, inverse_two, vectors[10])
    grad_down_in = lax.all_gather(grad_two.astype(jnp.bfloat16), "tensor", axis=0, tiled=True)
    grad_hidden = jnp.einsum("ld,kd->lk", grad_down_in, w_down, preferred_element_type=jnp.float32)
    grad_w_down = jnp.einsum("lk,ld->kd", hidden, grad_down_in, preferred_element_type=jnp.float32)
    grad_pre = gelu_pull(grad_hidden)[0].astype(jnp.bfloat16)
    norm_back_rows = lax.all_gather(normed_low, "tensor", axis=0, tiled=True)
    grad_w_up = jnp.einsum(
        "lk,ld->kd", grad_pre, norm_back_rows, preferred_element_type=jnp.float32
    )
    grad_norm = grad_two + lax.psum_scatter(
        jnp.einsum("lk,kd->ld", grad_pre, w_up, preferred_element_type=jnp.float32).astype(
            jnp.bfloat16
        ),
        "tensor",
        scatter_dimension=0,
        tiled=True,
    ).astype(jnp.float32)
    grad_one = norm_back(grad_norm, normal_one, inverse_one, vectors[8])
    grad_attn_in = lax.all_gather(grad_one.astype(jnp.bfloat16), "tensor", axis=0, tiled=True)
    grad_context = jnp.einsum(
        "ld,kd->lk", grad_attn_in, w_out, preferred_element_type=jnp.float32
    ).astype(jnp.bfloat16)
    grad_w_out = jnp.einsum("lk,ld->kd", context, grad_attn_in, preferred_element_type=jnp.float32)

    def backward_seq(element):
        return attend_backward(
            element[0], element[1], element[2], element[3], element[4], element[5], element[6]
        )

    grad_q, grad_k, grad_v = lax.map(
        backward_seq,
        (
            queries_h,
            keys_h,
            values_h,
            segment_ids,
            key_mask,
            log_sums,
            grad_context.reshape(head_shape),
        ),
    )
    grad_queries = grad_q.reshape(-1, head_cols).astype(jnp.bfloat16) * query_scale
    grad_keys = grad_k.reshape(-1, head_cols).astype(jnp.bfloat16)
    grad_values = grad_v.reshape(-1, head_cols).astype(jnp.bfloat16)
    grad_mix = jnp.concatenate([grad_queries, grad_keys, grad_values], axis=1)
    mix_back_rows = lax.all_gather(tokens, "tensor", axis=0, tiled=True)
    grad_w_mix = jnp.einsum(
        "lk,ld->kd", grad_mix, mix_back_rows, preferred_element_type=jnp.float32
    )
    input_grad = (
        grad_one
        + lax.psum_scatter(
            jnp.einsum("lk,kd->ld", grad_mix, w_mix, preferred_element_type=jnp.float32).astype(
                jnp.bfloat16
            ),
            "tensor",
            scatter_dimension=0,
            tiled=True,
        ).astype(jnp.float32)
    ).astype(jnp.bfloat16)
    query_full = lax.dynamic_update_slice_in_dim(
        jnp.zeros((D,), jnp.float32),
        jnp.sum(grad_queries.astype(jnp.float32), axis=0),
        group * head_cols,
        0,
    )
    value_full = lax.dynamic_update_slice_in_dim(
        jnp.zeros((D,), jnp.float32),
        jnp.sum(grad_values.astype(jnp.float32), axis=0),
        group * head_cols,
        0,
    )
    up_full = lax.dynamic_update_slice_in_dim(
        jnp.zeros((FF,), jnp.float32),
        jnp.sum(grad_pre.astype(jnp.float32), axis=0),
        group * unit_cols,
        0,
    )
    tail_rows = jnp.stack(
        [
            jnp.sum(grad_one, axis=0),
            jnp.sum(grad_two, axis=0),
            jnp.sum(grad_norm * normal_one, axis=0),
            jnp.sum(grad_norm, axis=0),
            jnp.sum(grad_out * normal_two, axis=0),
            jnp.sum(grad_out, axis=0),
        ]
    )
    vector_terms = jnp.concatenate(
        [jnp.stack([query_full, value_full]), up_full.reshape(FF // D, D), tail_rows], axis=0
    )
    vector_grads = lax.psum(vector_terms, ("dp", "tensor"))
    grad_stack = jnp.concatenate([grad_w_mix, grad_w_out, grad_w_up, grad_w_down], axis=0)
    grad_pieces = grad_stack.reshape(slots.shape[0], -1, D)
    spread_slots = (
        jnp.zeros((lax.axis_size("dp") * CAP,) + grad_pieces.shape[1:], jnp.float32)
        .at[slots]
        .set(grad_pieces)
    )
    own_grads = lax.psum_scatter(
        spread_slots.astype(jnp.bfloat16), "dp", scatter_dimension=0, tiled=True
    ).astype(jnp.float32)
    slot_new, slot_first_new, slot_second_new = adam_update(
        master_slots[0], slot_first[0], slot_second[0], own_grads, rate_matrix, weight_decay
    )
    vector_new, vector_first_new, vector_second_new = adam_update(
        vectors, vector_first, vector_second, vector_grads, rate_vector, 0.0
    )
    return (
        layer_out,
        input_grad,
        slot_new[None],
        slot_first_new[None],
        slot_second_new[None],
        vector_new,
        vector_first_new,
        vector_second_new,
    )


DOC_MAX = 800
ABLK = 256
FINE = 128
HPG = 8
AUG = 16
neg_big = -1000000000.0
NN = (((1,), (0,)), ((), ()))
NT = (((1,), (1,)), ((), ()))
TN = (((0,), (0,)), ((), ()))


def mm(a, b, dims):
    return lax.dot_general(a, b, dims, preferred_element_type=jnp.float32)


def attn_fwd_kernel(lo_ref, hi_ref, q_ref, k_ref, v_ref, qaug_ref, kaug_ref, hid_ref, o_ref, lse_ref, kn_ref, m_ref, acc_ref):
    ext = q_ref.shape[1]
    ones = jnp.concatenate(
        [jnp.ones((1, ABLK), jnp.float32), jnp.zeros((AUG - 1, ABLK), jnp.float32)], axis=0
    ).astype(jnp.bfloat16)
    for h in range(HPG):
        rows = slice(h * HD, (h + 1) * HD)
        kn_ref[h] = jnp.concatenate([k_ref[rows, :], kaug_ref[...]], axis=0).T

    def query_block(qb, _):
        lo = lo_ref[qb]
        hi = hi_ref[qb]
        qs = pl.ds(pl.multiple_of(qb * ABLK, ABLK), ABLK)

        @pl.when(hi > lo)
        def _work():
            hidden = hid_ref[0:1, qs]
            for h in range(HPG):
                rows = slice(h * HD, (h + 1) * HD)
                q32 = q_ref[rows, qs].astype(jnp.float32)
                k32 = k_ref[rows, qs].astype(jnp.float32)
                own = jnp.sum(q32 * k32, axis=0, keepdims=True)
                m_ref[h] = jnp.where(hidden > 0.0, own, -1e30)
                acc_ref[h, 0:HD, :] = v_ref[rows, qs].astype(jnp.float32) * hidden
                acc_ref[h, HD:, :] = jnp.broadcast_to(hidden, (AUG, ABLK))

            blocks = (hi - lo + 1) // 2
            origin = jnp.maximum(hi - 2 * blocks, 0) * FINE

            def key_block(kb, _):
                ks = pl.ds(pl.multiple_of(origin + kb * ABLK, FINE), ABLK)
                heads = [slice(h * HD, (h + 1) * HD) for h in range(HPG)]
                scores = [
                    mm(kn_ref[h, ks, :], jnp.concatenate([q_ref[heads[h], qs], qaug_ref[:, qs]], axis=0), NN)
                    for h in range(HPG)
                ]
                olds = [m_ref[h] for h in range(HPG)]
                news = [
                    jnp.maximum(olds[h], jnp.max(scores[h], axis=0, keepdims=True)) for h in range(HPG)
                ]
                raised = [jnp.exp(scores[h] - news[h]).astype(jnp.bfloat16) for h in range(HPG)]
                for h in range(HPG):
                    m_ref[h] = news[h]
                    va = jnp.concatenate([v_ref[heads[h], ks], ones], axis=0)
                    acc_ref[h] = acc_ref[h] * jnp.exp(olds[h] - news[h]) + mm(va, raised[h], NN)
                return 0

            lax.fori_loop(0, blocks, key_block, 0)
            for h in range(HPG):
                rows = slice(h * HD, (h + 1) * HD)
                total = acc_ref[h, HD : HD + 1, :]
                o_ref[rows, qs] = (acc_ref[h, 0:HD, :] * (1.0 / total)).astype(jnp.bfloat16)
                lse_ref[0, h : h + 1, qs] = m_ref[h] + jnp.log(total)

        @pl.when(hi <= lo)
        def _skip():
            o_ref[:, qs] = jnp.zeros((HPG * HD, ABLK), jnp.bfloat16)
            lse_ref[0, :, qs] = jnp.zeros((8, ABLK), jnp.float32)

        return 0

    lax.fori_loop(0, ext // ABLK, query_block, 0)


def attn_bwd_kernel(
    lo_ref, hi_ref, q_ref, k_ref, v_ref, g_ref, c_ref, lse_ref, qaug_ref, kaug_ref, hid_ref,
    out_ref, sums_ref, kn_ref, vn_ref, acc_ref, dk_acc, dv_acc,
):
    ext = q_ref.shape[1]
    for h in range(HPG):
        rows = slice(h * HD, (h + 1) * HD)
        kn_ref[h] = jnp.concatenate([k_ref[rows, :], kaug_ref[...]], axis=0).T
        vn_ref[h] = v_ref[rows, :].T
    dk_acc[...] = jnp.zeros_like(dk_acc)
    dv_acc[...] = jnp.zeros_like(dv_acc)

    def query_block(qb, _):
        lo = lo_ref[qb]
        hi = hi_ref[qb]
        qs = pl.ds(pl.multiple_of(qb * ABLK, ABLK), ABLK)

        @pl.when(hi > lo)
        def _work():
            hidden = hid_ref[0:1, qs]
            deltas = []
            logs = []
            for h in range(HPG):
                rows = slice(h * HD, (h + 1) * HD)
                q32 = q_ref[rows, qs].astype(jnp.float32)
                k32 = k_ref[rows, qs].astype(jnp.float32)
                v32 = v_ref[rows, qs].astype(jnp.float32)
                g32 = g_ref[rows, qs].astype(jnp.float32)
                c32 = c_ref[rows, qs].astype(jnp.float32)
                delta = jnp.sum(g32 * c32, axis=0, keepdims=True)
                log = lse_ref[0, h : h + 1, qs]
                own = jnp.sum(q32 * k32, axis=0, keepdims=True)
                p_own = jnp.where(hidden > 0.0, jnp.exp(own - log), 0.0)
                d_own = p_own * (jnp.sum(g32 * v32, axis=0, keepdims=True) - delta)
                acc_ref[h] = d_own * k32
                dk_acc[rows, qs] += d_own * q32
                dv_acc[rows, qs] += p_own * g32
                deltas.append(delta)
                logs.append(log)

            blocks = (hi - lo + 1) // 2
            origin = jnp.maximum(hi - 2 * blocks, 0) * FINE

            def key_block(kb, _):
                ks = pl.ds(pl.multiple_of(origin + kb * ABLK, FINE), ABLK)
                heads = [slice(h * HD, (h + 1) * HD) for h in range(HPG)]
                every = range(HPG)
                qs_h = [q_ref[heads[h], qs] for h in every]
                gs_h = [g_ref[heads[h], qs] for h in every]
                scores = [
                    mm(kn_ref[h, ks, :], jnp.concatenate([qs_h[h], qaug_ref[:, qs]], axis=0), NN)
                    for h in every
                ]
                grads = [mm(vn_ref[h, ks, :], gs_h[h], NN) for h in every]
                weights = [jnp.exp(scores[h] - logs[h]) for h in every]
                low = [weights[h].astype(jnp.bfloat16) for h in every]
                back = [
                    (weights[h] * (grads[h] - deltas[h])).astype(jnp.bfloat16) for h in every
                ]
                v_new = [mm(gs_h[h], low[h], NT) for h in every]
                k_new = [mm(qs_h[h], back[h], NT) for h in every]
                q_new = [mm(k_ref[heads[h], ks], back[h], NN) for h in every]
                for h in every:
                    dv_acc[heads[h], ks] += v_new[h]
                    dk_acc[heads[h], ks] += k_new[h]
                    acc_ref[h] += q_new[h]
                return 0

            lax.fori_loop(0, blocks, key_block, 0)
            for h in range(HPG):
                rows = slice(h * HD, (h + 1) * HD)
                out_ref[0, rows, qs] = acc_ref[h].astype(jnp.bfloat16) * (HD ** (-0.5))

        @pl.when(hi <= lo)
        def _skip():
            out_ref[0, :, qs] = jnp.zeros((HPG * HD, ABLK), jnp.bfloat16)

        return 0

    lax.fori_loop(0, ext // ABLK, query_block, 0)
    out_ref[1] = dk_acc[...].astype(jnp.bfloat16)
    out_ref[2] = dv_acc[...].astype(jnp.bfloat16)
    for n in range(2):
        total = jnp.sum(out_ref[2 * n].astype(jnp.float32), axis=1, keepdims=True)
        sums_ref[n] = jnp.broadcast_to(total, sums_ref.shape[1:])


def group_block(offset, rows, ext):
    return pl.BlockSpec((rows, ext), lambda g, lo, hi: (offset + g, 0))


def fixed_block(rows, ext):
    return pl.BlockSpec((rows, ext), lambda g, lo, hi: (0, 0))


def attend(lo, hi, qkv, qaug, kaug, hidden):
    ext = qkv.shape[1]
    groups = D // HD // HPG
    rows = HPG * HD
    return pl.pallas_call(
        attn_fwd_kernel,
        out_shape=(
            jax.ShapeDtypeStruct((D, ext), jnp.bfloat16),
            jax.ShapeDtypeStruct((groups, 8, ext), jnp.float32),
        ),
        grid_spec=pltpu.PrefetchScalarGridSpec(
            num_scalar_prefetch=2,
            grid=(groups,),
            in_specs=[
                group_block(0, rows, ext),
                group_block(groups, rows, ext),
                group_block(2 * groups, rows, ext),
                fixed_block(AUG, ext),
                fixed_block(AUG, ext),
                fixed_block(8, ext),
            ],
            out_specs=[
                group_block(0, rows, ext),
                pl.BlockSpec((1, 8, ext), lambda g, lo, hi: (g, 0, 0)),
            ],
            scratch_shapes=[
                pltpu.VMEM((HPG, ext, HD + AUG), jnp.bfloat16),
                pltpu.VMEM((HPG, 1, ABLK), jnp.float32),
                pltpu.VMEM((HPG, HD + AUG, ABLK), jnp.float32),
            ],
        ),
        compiler_params=pltpu.CompilerParams(vmem_limit_bytes=40 * 2**20),
        cost_estimate=pl.CostEstimate(flops=20 * 10**9, bytes_accessed=14 * 10**6, transcendentals=0),
        name="attend",
    )(lo, hi, qkv, qkv, qkv, qaug, kaug, hidden)


def attend_back(lo, hi, qkv, grads, context, logs, qaug, kaug, hidden):
    ext = qkv.shape[1]
    groups = D // HD // HPG
    rows = HPG * HD
    return pl.pallas_call(
        attn_bwd_kernel,
        out_shape=(
            jax.ShapeDtypeStruct((3, D, ext), jnp.bfloat16),
            jax.ShapeDtypeStruct((2, D, 128), jnp.float32),
        ),
        grid_spec=pltpu.PrefetchScalarGridSpec(
            num_scalar_prefetch=2,
            grid=(groups,),
            in_specs=[
                group_block(0, rows, ext),
                group_block(groups, rows, ext),
                group_block(2 * groups, rows, ext),
                group_block(0, rows, ext),
                group_block(0, rows, ext),
                pl.BlockSpec((1, 8, ext), lambda g, lo, hi: (g, 0, 0)),
                fixed_block(AUG, ext),
                fixed_block(AUG, ext),
                fixed_block(8, ext),
            ],
            out_specs=(
                pl.BlockSpec((3, rows, ext), lambda g, lo, hi: (0, g, 0)),
                pl.BlockSpec((2, rows, 128), lambda g, lo, hi: (0, g, 0)),
            ),
            scratch_shapes=[
                pltpu.VMEM((HPG, ext, HD + AUG), jnp.bfloat16),
                pltpu.VMEM((HPG, ext, HD), jnp.bfloat16),
                pltpu.VMEM((HPG, HD, ABLK), jnp.float32),
                pltpu.VMEM((rows, ext), jnp.float32),
                pltpu.VMEM((rows, ext), jnp.float32),
            ],
        ),
        compiler_params=pltpu.CompilerParams(vmem_limit_bytes=56 * 2**20),
        cost_estimate=pl.CostEstimate(flops=50 * 10**9, bytes_accessed=30 * 10**6, transcendentals=0),
        name="attend_back",
    )(lo, hi, qkv, qkv, qkv, grads, context, logs, qaug, kaug, hidden)


def document_plan(segment, valid, half, rows):
    length = segment.shape[0]
    position = jnp.arange(length, dtype=jnp.int32)
    documents = jnp.arange(8, dtype=jnp.int32)[:, None]
    hot = segment[None, :] == documents
    counts = jnp.sum(hot.astype(jnp.int32), axis=1, keepdims=True)
    starts = jnp.sum((segment[None, :] < documents).astype(jnp.int32), axis=1, keepdims=True)
    start = jnp.sum(jnp.where(hot, starts, 0), axis=0)
    end = jnp.sum(jnp.where(hot, starts + counts, 0), axis=0)
    own = (position >= half * rows) & (position < (half + 1) * rows)
    begins = jnp.where(own, start, length).reshape(-1, ABLK)
    ends = jnp.where(own, end, 0).reshape(-1, ABLK)
    hi = (jnp.max(ends, axis=1) + (FINE - 1)) // FINE
    lo = jnp.where(hi == 0, 0, jnp.min(begins, axis=1) // FINE)
    masked = valid == 0
    ones = jnp.ones((1, length), jnp.bfloat16)
    fill = jnp.zeros((AUG - 9, length), jnp.bfloat16)
    qaug = jnp.concatenate([hot.astype(jnp.bfloat16), ones, fill], axis=0)
    kaug = jnp.concatenate(
        [
            jnp.where(hot, 0.0, neg_big).astype(jnp.bfloat16),
            jnp.where(masked[None, :], neg_big, 0.0).astype(jnp.bfloat16),
            fill,
        ],
        axis=0,
    )
    hidden = jnp.broadcast_to(masked.astype(jnp.float32)[None, :], (8, length))
    return lo, hi, qaug, kaug, hidden


def normal_parts(values):
    bell = jnp.exp(values * values * -0.5)
    return (0.5 + 0.5 * lax.erf(values * 0.7071067811865476), bell * 0.3989422804014327)


UNITS = 1024
STRIP = 512


def up_kernel(x_ref, w_ref, bias_ref, gelu_ref, slope_ref):
    for r in range(0, x_ref.shape[0], STRIP):
        strip = slice(r, r + STRIP)
        values = mm(x_ref[strip, :], w_ref[...], NT) + bias_ref[...]
        cdf, bell = normal_parts(values)
        gelu_ref[strip, :] = (values * cdf).astype(jnp.bfloat16)
        slope_ref[strip, :] = (cdf + values * bell).astype(jnp.bfloat16)


def feed_up(rows, weights, bias):
    length = rows.shape[0]
    units = weights.shape[0]
    out = jax.ShapeDtypeStruct((length, units), jnp.bfloat16)
    columns = pl.BlockSpec((length, UNITS), lambda n: (0, n))
    return pl.pallas_call(
        up_kernel,
        out_shape=(out, out),
        grid=(units // UNITS,),
        in_specs=[
            pl.BlockSpec((length, D), lambda n: (0, 0)),
            pl.BlockSpec((UNITS, D), lambda n: (n, 0)),
            pl.BlockSpec((1, UNITS), lambda n: (0, n)),
        ],
        out_specs=(columns, columns),
        compiler_params=pltpu.CompilerParams(vmem_limit_bytes=60 * 2**20),
        cost_estimate=pl.CostEstimate(
            flops=2 * length * units * D, bytes_accessed=26 * 10**6, transcendentals=0
        ),
        name="feed_up",
    )(rows, weights, bias.reshape(1, units))


def down_back_kernel(g_ref, w_ref, slope_ref, out_ref, sum_ref):
    total = jnp.zeros((1, UNITS), jnp.float32)
    for r in range(0, g_ref.shape[0], STRIP):
        strip = slice(r, r + STRIP)
        grads = mm(g_ref[strip, :], w_ref[...], NT) * slope_ref[strip, :].astype(jnp.float32)
        low = grads.astype(jnp.bfloat16)
        out_ref[strip, :] = low
        total += jnp.sum(low.astype(jnp.float32), axis=0, keepdims=True)
    sum_ref[...] = total


def feed_down_back(grads, weights, slope):
    length = grads.shape[0]
    units = weights.shape[0]
    columns = pl.BlockSpec((length, UNITS), lambda n: (0, n))
    one_row = pl.BlockSpec((1, UNITS), lambda n: (0, n))
    return pl.pallas_call(
        down_back_kernel,
        out_shape=(
            jax.ShapeDtypeStruct((length, units), jnp.bfloat16),
            jax.ShapeDtypeStruct((1, units), jnp.float32),
        ),
        grid=(units // UNITS,),
        in_specs=[
            pl.BlockSpec((length, D), lambda n: (0, 0)),
            pl.BlockSpec((UNITS, D), lambda n: (n, 0)),
            columns,
        ],
        out_specs=(columns, one_row),
        compiler_params=pltpu.CompilerParams(vmem_limit_bytes=40 * 2**20),
        cost_estimate=pl.CostEstimate(
            flops=2 * length * units * D, bytes_accessed=26 * 10**6, transcendentals=0
        ),
        name="feed_down_back",
    )(grads, weights, slope)


MESH = pl.DeviceIdType.MESH
CHUNKS = 3
GROUPS = ((0, 3), (3, 1), (4, 4))
PARTS = (((0, 1), (1, 2)), ((0, 1), None), ((0, 2), (2, 2)))


def neighbours(z, y, core, x):
    def at(z, y, core, x):
        return {"dp": (z * 2 + y) * 2 + core, "tensor": x}

    return {
        "x": at(z, y, core, 1 - x),
        "y": at(z, 1 - y, core, x),
        "core": at(z, y, 1 - core, x),
        "up": at(jnp.minimum(z + 1, 3), y, core, x),
        "down": at(jnp.maximum(z - 1, 0), y, core, x),
    }


def greet(near, z):
    barrier = pltpu.get_barrier_semaphore()
    for name in ("x", "y", "core"):
        pl.semaphore_signal(barrier, inc=1, device_id=near[name], device_id_type=MESH)

    @pl.when(z < 3)
    def _up():
        pl.semaphore_signal(barrier, inc=1, device_id=near["up"], device_id_type=MESH)

    @pl.when(z > 0)
    def _down():
        pl.semaphore_signal(barrier, inc=1, device_id=near["down"], device_id_type=MESH)

    at_end = jnp.where((z == 0) | (z == 3), 1, 0)
    pl.semaphore_wait(barrier, 5 - at_end)


def greet_all(near, me, n_dp):
    barrier = pltpu.get_barrier_semaphore()
    pl.semaphore_signal(barrier, inc=1, device_id=near["x"], device_id_type=MESH)

    def one(i, _):
        other = {"dp": lax.rem(me + i, n_dp), "tensor": lax.axis_index("tensor")}
        pl.semaphore_signal(barrier, inc=1, device_id=other, device_id_type=MESH)
        return 0

    lax.fori_loop(1, n_dp, one, 0)
    pl.semaphore_wait(barrier, n_dp)


def gather_kernel(
    owners_ref, slots_ref, tokens_ref, qkv_ref, out_ref, up_ref, down_ref, ext_ref,
    slot_ref, low_ref, spread_ref, dense_ref, zero_ref, local_sem, own_sem, ext_sem, post, mail, send, recv, halo_send, halo_recv,
):
    z, y, core, x = coordinates()
    near = neighbours(z, y, core, x)
    width = D // 2
    me = lax.axis_index("dp")
    n_dp = low_ref.shape[0]
    for to in range(n_dp):
        lines = slice((to // 2) * 16, (to // 2) * 16 + 16)
        columns = slice((to % 2) * width, (to % 2) * width + width)
        low_ref[to] = slots_ref[:, lines, columns].astype(low_ref.dtype)
    greet_all(near, me, n_dp)

    def letter(to):
        return pltpu.make_async_remote_copy(
            src_ref=low_ref.at[to],
            dst_ref=spread_ref.at[pl.ds(me * CAP, CAP)],
            send_sem=post.at[to],
            recv_sem=mail.at[me],
            device_id={"dp": to, "tensor": x},
            device_id_type=MESH,
        )

    def answer(of):
        return pltpu.make_async_remote_copy(
            src_ref=low_ref.at[of],
            dst_ref=spread_ref.at[pl.ds(of * CAP, CAP)],
            send_sem=post.at[of],
            recv_sem=mail.at[of],
            device_id={"dp": of, "tensor": x},
            device_id_type=MESH,
        )

    def peer(i):
        return lax.rem(me + i, n_dp)

    def post_one(i, _):
        letter(peer(i)).start()
        return 0

    lax.fori_loop(1, n_dp, post_one, 0)

    rows = tokens_ref.shape[0]
    halo = DOC_MAX
    blank = zero_ref.shape[0]
    zero_ref[...] = jnp.zeros_like(zero_ref)
    edge = pl.multiple_of(jnp.where(x == 0, rows - halo, 0), 16)
    there = pl.multiple_of(jnp.where(x == 0, rows - halo, rows), 16)
    rest = pl.multiple_of(jnp.where(x == 0, rows + halo, 0), 16)
    border = pltpu.make_async_remote_copy(
        src_ref=tokens_ref.at[pl.ds(edge, halo)],
        dst_ref=ext_ref.at[pl.ds(there, halo)],
        send_sem=halo_send,
        recv_sem=halo_recv,
        device_id=near["x"],
        device_id_type=MESH,
    )
    border.start()
    inside = pltpu.make_async_copy(
        tokens_ref, ext_ref.at[pl.ds(pl.multiple_of(x * rows, 16), rows)], ext_sem.at[0]
    )
    inside.start()
    empty = pltpu.make_async_copy(zero_ref, ext_ref.at[pl.ds(rest, blank)], ext_sem.at[1])
    empty.start()
    mine = pltpu.make_async_copy(low_ref.at[me], spread_ref.at[pl.ds(me * CAP, CAP)], local_sem)
    mine.start()
    mine.wait()

    def find(p, _):
        owner = owners_ref[p]

        def count(q, before):
            return before + jnp.where(owners_ref[q] == owner, 1, 0)

        slot_ref[p] = owner * CAP + lax.fori_loop(0, p, count, 0)
        return 0

    lax.fori_loop(0, owners_ref.shape[0], find, 0)

    def mail_one(i, _):
        answer(peer(i)).wait_recv()
        letter(peer(i)).wait_send()
        return 0

    lax.fori_loop(1, n_dp, mail_one, 0)

    def place(p, _):
        dense_ref[p // 4, p % 4] = spread_ref[slot_ref[p]]
        return 0

    lax.fori_loop(0, owners_ref.shape[0], place, 0)
    rest_groups = pl.ds(GROUPS[-1][0] + GROUPS[-1][1], 4)
    later = pltpu.make_async_copy(dense_ref.at[rest_groups], down_ref, local_sem)
    later.start()
    later.wait()

    def block(k, t, zz, yy, cc, part=None):
        groups = slice(None) if part is None else pl.ds(*PARTS[k][part])
        return (qkv_ref, out_ref, up_ref)[k].at[
            groups,
            t,
            :,
            pl.ds(pl.multiple_of((zz * 2 + yy) * 16, 16), 16),
            pl.ds(pl.multiple_of(cc * width, width), width),
        ]

    own = [
        pltpu.make_async_copy(dense_ref.at[pl.ds(*GROUPS[k])], block(k, x, z, y, core), own_sem.at[k])
        for k in range(CHUNKS)
    ]
    for one in own:
        one.start()

    def copy(kind, link, k, zz, t, yy, cc, part=None, fresh=False):
        view = block(k, t, zz, yy, cc, part)
        return pltpu.make_async_remote_copy(
            src_ref=dense_ref.at[pl.ds(*GROUPS[k])] if fresh else view,
            dst_ref=view,
            send_sem=send.at[kind, k, zz],
            recv_sem=recv.at[kind, k, zz],
            device_id=near[link],
            device_id_type=MESH,
        )

    def up(k, zz, fresh=False):
        return copy(0, "up", k, zz, x, y, core, fresh=fresh)

    def down(k, zz, fresh=False):
        return copy(1, "down", k, zz, x, y, core, fresh=fresh)

    def spread(k, zz, fresh):
        copy(2, "x", k, zz, x, y, core, fresh=fresh).start()
        copy(3, "y", k, zz, x, y, core, fresh=fresh).start()
        copy(4, "core", k, zz, x, y, core, fresh=fresh).start()

    def each(d, body):
        @pl.when((d > 0) & (z - d >= 0))
        def _below():
            for k in range(CHUNKS):
                body(k, z - d, 0)

        @pl.when((d > 0) & (z + d <= 3))
        def _above():
            for k in range(CHUNKS):
                body(k, z + d, 1)

    def each_or_own(d, body):
        each(d, body)

        @pl.when(d == 0)
        def _own():
            for k in range(CHUNKS):
                body(k, z, None)

    def begin(k):
        @pl.when(z < 3)
        def _up():
            up(k, z, True).start()

        @pl.when(z > 0)
        def _down():
            down(k, z, True).start()

        spread(k, z, True)

    def first(k, zz, side):
        if side == 0:
            up(k, zz).wait_recv()

            @pl.when(z < 3)
            def _up():
                up(k, zz).start()

        else:
            down(k, zz).wait_recv()

            @pl.when(z > 0)
            def _on():
                down(k, zz).start()

        spread(k, zz, False)

    def second(k, zz, side):
        copy(2, "x", k, zz, 1 - x, y, core).wait_recv()
        copy(5, "y", k, zz, 1 - x, y, core, 0).start()
        copy(7, "core", k, zz, 1 - x, y, core).start()
        copy(3, "y", k, zz, x, 1 - y, core).wait_recv()
        if PARTS[k][1]:
            copy(6, "x", k, zz, x, 1 - y, core, 1).start()
        copy(8, "core", k, zz, x, 1 - y, core).start()

    def third(k, zz, side):
        copy(5, "y", k, zz, 1 - x, 1 - y, core, 0).wait_recv()
        copy(9, "core", k, zz, 1 - x, 1 - y, core, 0).start()
        if PARTS[k][1]:
            copy(6, "x", k, zz, 1 - x, 1 - y, core, 1).wait_recv()
            copy(10, "core", k, zz, 1 - x, 1 - y, core, 1).start()

    def finish(k, zz, side):
        if side != 1:

            @pl.when(z < 3)
            def _up():
                up(k, zz).wait_send()

        if side != 0:

            @pl.when(z > 0)
            def _down():
                down(k, zz).wait_send()

        copy(2, "x", k, zz, x, y, core).wait_send()
        copy(3, "y", k, zz, x, y, core).wait_send()
        copy(5, "y", k, zz, 1 - x, y, core, 0).wait_send()
        if PARTS[k][1]:
            copy(6, "x", k, zz, x, 1 - y, core, 1).wait_send()
        copy(4, "core", k, zz, x, y, core).wait_send()
        copy(7, "core", k, zz, 1 - x, y, core).wait_send()
        copy(8, "core", k, zz, x, 1 - y, core).wait_send()
        copy(9, "core", k, zz, 1 - x, 1 - y, core, 0).wait_send()
        if PARTS[k][1]:
            copy(10, "core", k, zz, 1 - x, 1 - y, core, 1).wait_send()
        copy(4, "core", k, zz, x, y, 1 - core).wait_recv()
        copy(7, "core", k, zz, 1 - x, y, 1 - core).wait_recv()
        copy(8, "core", k, zz, x, 1 - y, 1 - core).wait_recv()
        copy(9, "core", k, zz, 1 - x, 1 - y, 1 - core, 0).wait_recv()
        if PARTS[k][1]:
            copy(10, "core", k, zz, 1 - x, 1 - y, 1 - core, 1).wait_recv()

    for k in range(CHUNKS):
        begin(k)

    def step(d, _):
        @pl.when(d < 4)
        def _one():
            each(d, first)

        @pl.when((d >= 1) & (d < 5))
        def _two():
            each_or_own(d - 1, second)

        @pl.when(d >= 2)
        def _three():
            each_or_own(d - 2, third)

        return 0

    lax.fori_loop(1, 6, step, 0)

    def end(d, _):
        each_or_own(d, finish)
        return 0

    lax.fori_loop(0, 4, end, 0)
    for one in own:
        one.wait()
    border.wait()
    inside.wait()
    empty.wait()


def gather_weights(owners, slots, tokens):
    n_dp = lax.axis_size("dp")
    low = jnp.bfloat16
    rows = tokens.shape[0]
    anywhere = pl.BlockSpec(memory_space=pl.ANY)
    return pl.pallas_call(
        gather_kernel,
        out_shape=tuple(
            jax.ShapeDtypeStruct((count, 2, 4, 128, D), low) for first, count in GROUPS
        )
        + (
            jax.ShapeDtypeStruct((4, 4, 16, D // 2), low),
            jax.ShapeDtypeStruct((2 * rows, D), tokens.dtype),
        ),
        in_specs=[
            pl.BlockSpec(memory_space=pltpu.SMEM),
            pl.BlockSpec(memory_space=pltpu.VMEM),
            anywhere,
        ],
        out_specs=(anywhere,) * 5,
        scratch_shapes=[
            pltpu.SMEM(owners.shape, jnp.int32),
            pltpu.VMEM((n_dp, CAP, 16, D // 2), low),
            pltpu.VMEM((n_dp * CAP, 16, D // 2), low),
            pltpu.VMEM((12, 4, 16, D // 2), low),
            pltpu.VMEM((rows - DOC_MAX, D), tokens.dtype),
            pltpu.SemaphoreType.DMA,
            pltpu.SemaphoreType.DMA((CHUNKS,)),
            pltpu.SemaphoreType.DMA((2,)),
            pltpu.SemaphoreType.DMA((n_dp,)),
            pltpu.SemaphoreType.DMA((n_dp,)),
            pltpu.SemaphoreType.DMA((11, CHUNKS, 4)),
            pltpu.SemaphoreType.DMA((11, CHUNKS, 4)),
            pltpu.SemaphoreType.DMA,
            pltpu.SemaphoreType.DMA,
        ],
        compiler_params=pltpu.CompilerParams(
            collective_id=1, has_side_effects=True, vmem_limit_bytes=60 * 2**20
        ),
        cost_estimate=pl.CostEstimate(flops=0, bytes_accessed=50 * 10**6, transcendentals=0),
        name="gather_weights",
    )(owners, slots, tokens)


def stack_kernel(parts_ref, out_ref):
    for p in range(4):
        for line in range(8):
            for half in range(2):
                columns = slice(half * (D // 2), (half + 1) * (D // 2))
                out_ref[0, 0, p, line, :, columns] = parts_ref[0, line, half, 0, p]


def stack_chunks(parts):
    return pl.pallas_call(
        stack_kernel,
        out_shape=jax.ShapeDtypeStruct((4, 2, 4, 8, 16, D), parts.dtype),
        grid=(4, 2),
        in_specs=[
            pl.BlockSpec((1, 8, 2, 1, 4, 16, D // 2), lambda m, t: (t, 0, 0, m, 0, 0, 0)),
        ],
        out_specs=pl.BlockSpec((1, 1, 4, 8, 16, D), lambda m, t: (m, t, 0, 0, 0, 0)),
        compiler_params=pltpu.CompilerParams(vmem_limit_bytes=60 * 2**20),
        cost_estimate=pl.CostEstimate(flops=0, bytes_accessed=17 * 10**6, transcendentals=0),
        name="stack_chunks",
    )(parts)


BLOCKS = 12
SLICES = 2
STEPS = BLOCKS * SLICES
LAG = 2


def reduce_kernel(
    piece_ref, vec_ref, qkv_ref, ctx_ref, pre_ref, hid_ref, tok_ref, gext_ref, norm_ref, two_ref, weight_ref,
    out_ref, sum_ref, input_ref, border_ref,
    weight_buf, strip, strip_out, weight_sem, strip_sem, strip_out_sem, border_send, border_recv,
    tile, tall, ext_rhs, row_rhs, far_buf, near_buf, core_in, x_in, y_in, x2_in, y2_in, line, line_in,
    done, parcel, vec_in, vec_out,
    tile_sem, rhs_sem, local_sem, post, mail, send, recv, vec_send, vec_recv,
):
    z, y, core, x = coordinates()
    near = neighbours(z, y, core, x)
    me = lax.axis_index("dp")
    n_dp = parcel.shape[1]
    half_width = D // 2
    width = half_width // SLICES
    rows = tile.shape[1]
    tiles = 1024 // rows

    def right(n, half, cut):
        ref = (tok_ref, gext_ref, norm_ref, two_ref)[n]
        to = ext_rhs.at[n, half, cut] if n < 2 else row_rhs.at[n - 2, half, cut]
        which = 1 - core if half == 0 else core
        columns = pl.ds(pl.multiple_of(which * half_width + cut * width, width), width)
        return pltpu.make_async_copy(ref.at[:, columns], to, rhs_sem.at[n, half, cut])

    for cut in range(SLICES):
        for n in range(4):
            for half in range(2):
                right(n, half, cut).start()

    def fetch(n, body):
        i = lax.rem(n // tiles, BLOCKS)
        part = pl.ds(pl.multiple_of(lax.rem(n, tiles) * rows, rows), rows)
        slot = lax.rem(n, 2)
        ext = ext_rhs.shape[3]
        wide = tile.at[slot]
        near_half = tile.at[slot, :, pl.ds(0, ext // 2)]
        own = pl.ds(pl.multiple_of(x * (ext // 2), 128), ext // 2)
        sem = tile_sem.at[slot]

        @pl.when(i == 0)
        def _q():
            body(pltpu.make_async_copy(qkv_ref.at[0, part, own], near_half, sem))

        @pl.when((i == 1) | (i == 2))
        def _kv():
            body(pltpu.make_async_copy(qkv_ref.at[i, part, :], wide, sem))

        @pl.when(i == 3)
        def _out():
            body(pltpu.make_async_copy(ctx_ref.at[part, own], near_half, sem))

        def columns(first):
            start = (i - first) * 1024 + lax.rem(n, tiles) * rows
            return pl.ds(pl.multiple_of(start, rows), rows)

        @pl.when((i >= 4) & (i < 8))
        def _up():
            body(pltpu.make_async_copy(pre_ref.at[:, columns(4)], tall.at[slot], sem))

        @pl.when(i >= 8)
        def _down():
            body(pltpu.make_async_copy(hid_ref.at[:, columns(8)], tall.at[slot], sem))

    strip_rows = strip.shape[3]
    strips = qkv_ref.shape[2] // strip_rows
    weight_copy = pltpu.make_async_copy(weight_ref, weight_buf, weight_sem)
    weight_copy.start()

    def strip_at(r):
        other = lax.rem(r + (1 - x) * (strips // 2), strips)
        return pl.ds(pl.multiple_of(other * strip_rows, strip_rows), strip_rows)

    def strip_copy(r):
        slot = lax.rem(r, 2)
        here = strip_at(r)
        return pltpu.make_async_copy(qkv_ref.at[:, :, here], strip.at[slot], strip_sem.at[slot])

    def strip_done(r):
        slot = lax.rem(r, 2)
        here = strip_at(r)
        return pltpu.make_async_copy(strip_out.at[slot], input_ref.at[here], strip_out_sem.at[slot])

    def input_strip(r):
        slot = lax.rem(r, 2)

        @pl.when(r + 1 < strips)
        def _next():
            strip_copy(r + 1).start()

        @pl.when(r >= 2)
        def _free():
            strip_done(r - 2).wait()

        strip_copy(r).wait()
        mine = lax.rem(r + (1 - x) * (strips // 2), strips) // (strips // 2) == x

        @pl.when(mine)
        def _own():
            total = mm(strip[slot, 0], weight_buf[0], TN)
            total += mm(strip[slot, 1], weight_buf[1], TN)
            total += mm(strip[slot, 2], weight_buf[2], TN)
            strip_out[slot] = total.astype(jnp.bfloat16)

        @pl.when(jnp.logical_not(mine))
        def _other():
            total = mm(strip[slot, 1], weight_buf[1], TN)
            total += mm(strip[slot, 2], weight_buf[2], TN)
            strip_out[slot] = total.astype(jnp.bfloat16)

        strip_done(r).start()

    halo = border_ref.shape[0]
    middle = input_ref.shape[0] // 2
    border_at = pl.multiple_of(jnp.where(x == 0, middle, middle - halo), 16)
    border = pltpu.make_async_remote_copy(
        src_ref=input_ref.at[pl.ds(border_at, halo)],
        dst_ref=border_ref,
        send_sem=border_send,
        recv_sem=border_recv,
        device_id=near["x"],
        device_id_type=MESH,
    )
    strip_copy(0).start()
    fetch(0, lambda copy: copy.start())
    greet_all(near, me, n_dp)

    def remote(kind, i, link, src, dst):
        return pltpu.make_async_remote_copy(
            src_ref=src,
            dst_ref=dst,
            send_sem=send.at[kind, i],
            recv_sem=recv.at[kind, i],
            device_id=near[link],
            device_id_type=MESH,
        )

    def core_copy(i):
        return remote(0, i, "core", far_buf.at[lax.rem(i, 2)], core_in.at[i])

    def x1(i):
        return remote(1, i, "x", core_in.at[i, 1 - x, pl.ds(0, 2)], x_in.at[i])

    def y1(i):
        return remote(2, i, "y", core_in.at[i, :, pl.ds(2, 2), :, 1 - y], y_in.at[i])

    def y2(i):
        return remote(3, i, "y", x_in.at[i, :, :, 1 - y], y2_in.at[i])

    def x2(i):
        return remote(4, i, "x", y_in.at[i, 1 - x], x2_in.at[i])

    def along(i, zz):
        return pltpu.make_async_remote_copy(
            src_ref=line.at[i, zz],
            dst_ref=line_in.at[i, z],
            send_sem=send.at[5 + zz, i],
            recv_sem=recv.at[5 + z, i],
            device_id={"dp": (zz * 2 + y) * 2 + core, "tensor": x},
            device_id_type=MESH,
        )

    def arrival(i, zz):
        return pltpu.make_async_remote_copy(
            src_ref=line.at[i, zz],
            dst_ref=line_in.at[i, zz],
            send_sem=send.at[5 + zz, i],
            recv_sem=recv.at[5 + zz, i],
            device_id={"dp": (zz * 2 + y) * 2 + core, "tensor": x},
            device_id_type=MESH,
        )

    def produce(b):
        ring = lax.rem(b, 2)
        cut = b // BLOCKS
        i = lax.rem(b, BLOCKS)

        for c in range(SLICES):
            for n, first in enumerate((0, 3, 4, 8)):

                @pl.when(b == c * BLOCKS + first)
                def _ready():
                    right(n, 0, c).wait()
                    right(n, 1, c).wait()

        @pl.when(b >= 2)
        def _free():
            core_copy(b - 2).wait_send()

        def one(part, _):
            n = b * tiles + part
            slot = lax.rem(n, 2)

            @pl.when(n + 1 < STEPS * tiles)
            def _next():
                fetch(n + 1, lambda copy: copy.start())

            fetch(n, lambda copy: copy.wait())
            t, p = part // 2, lax.rem(part, 2) * 2

            def put(value, to):
                to[ring, t, pl.ds(p, 2)] = value.astype(jnp.bfloat16).reshape(2, 4, 2, 16, width)

            @pl.when((i == 1) | (i == 2))
            def _wide():
                put(mm(tile[slot], ext_rhs[0, 0, cut], NN), far_buf)
                put(mm(tile[slot], ext_rhs[0, 1, cut], NN), near_buf)

            @pl.when((i == 0) | (i == 3))
            def _own():
                which = jnp.where(i == 0, 0, 1)
                length = ext_rhs.shape[3] // 2
                own = pl.ds(pl.multiple_of(x * length, length), length)
                left = tile[slot, :, 0:length]
                put(mm(left, ext_rhs[which, 0, cut, own], NN), far_buf)
                put(mm(left, ext_rhs[which, 1, cut, own], NN), near_buf)

            @pl.when(i >= 4)
            def _tall():
                which = jnp.where(i < 8, 0, 1)
                put(mm(tall[slot], row_rhs[which, 0, cut], TN), far_buf)
                put(mm(tall[slot], row_rhs[which, 1, cut], TN), near_buf)

            return 0

        lax.fori_loop(0, tiles, one, 0)
        core_copy(b).start()

    def stage_one(i):
        core_copy(i).wait_recv()
        ring = lax.rem(i, 2)

        def add(j, _):
            t, p = j // 4, j % 4
            core_in[i, t, p] = core_in[i, t, p] + near_buf[ring, t, p]
            return 0

        lax.fori_loop(0, 8, add, 0)
        x1(i).start()
        y1(i).start()

    def stage_two(i):
        x1(i).wait_recv()
        y1(i).wait_recv()
        for p in range(2):
            x_in[i, p] = x_in[i, p] + core_in[i, x, p]
        for t in range(2):
            for p in range(2):
                y_in[i, t, p] = y_in[i, t, p] + core_in[i, t, 2 + p, :, y]
        y2(i).start()
        x2(i).start()

    def stage_three(i):
        y2(i).wait_recv()
        x2(i).wait_recv()
        for p in range(2):
            line[i, :, p] = x_in[i, p, :, y] + y2_in[i, p]
            line[i, :, 2 + p] = y_in[i, x, p] + x2_in[i, p]
        for n in range(1, 4):
            along(i, lax.rem(z + n, 4)).start()

    def stage_last(b):
        cut = b // BLOCKS
        total = line[b, z].astype(jnp.float32)
        for n in range(1, 4):
            zz = lax.rem(z + n, 4)
            arrival(b, zz).wait_recv()
            total += line_in[b, zz].astype(jnp.float32)
        done[cut, pl.ds(lax.rem(b, BLOCKS) * 4, 4)] = total.astype(jnp.bfloat16)

    def place(of, cut):
        start = (of % 2) * half_width + cut * width
        return out_ref.at[
            :,
            pl.ds(pl.multiple_of((of // 2) * 16, 16), 16),
            pl.ds(pl.multiple_of(start, width), width),
        ]

    def letter(to, cut):
        return pltpu.make_async_remote_copy(
            src_ref=parcel.at[cut, to],
            dst_ref=place(me, cut),
            send_sem=post.at[cut, to],
            recv_sem=mail.at[cut, me],
            device_id={"dp": to, "tensor": x},
            device_id_type=MESH,
        )

    def answer(of, cut):
        return pltpu.make_async_remote_copy(
            src_ref=parcel.at[cut, of],
            dst_ref=place(of, cut),
            send_sem=post.at[cut, of],
            recv_sem=mail.at[cut, of],
            device_id={"dp": of, "tensor": x},
            device_id_type=MESH,
        )

    def own_letter(cut):
        return pltpu.make_async_copy(parcel.at[cut, me], place(me, cut), local_sem.at[cut])

    def post_all(cut):
        done[cut, BLOCKS * 4] = jnp.zeros((16, width), done.dtype)

        def pack(n, _):
            parcel[cut, n // CAP, n % CAP] = done[cut, piece_ref[n]]
            return 0

        lax.fori_loop(0, n_dp * CAP, pack, 0)

        def post_one(i, _):
            letter(lax.rem(me + i, n_dp), cut).start()
            return 0

        lax.fori_loop(1, n_dp, post_one, 0)
        own_letter(cut).start()

    def ended(i):
        @pl.when(i >= STEPS - 2)
        def _far():
            core_copy(i).wait_send()

        x1(i).wait_send()
        y1(i).wait_send()
        y2(i).wait_send()
        x2(i).wait_send()
        for n in range(1, 4):
            along(i, lax.rem(z + n, 4)).wait_send()

    z_one = z + 1 - 2 * lax.rem(z, 2)
    z_two = lax.rem(z + 2, 4)
    partners = [
        near["core"],
        near["y"],
        near["x"],
        {"dp": (z_one * 2 + y) * 2 + core, "tensor": x},
        {"dp": (z_two * 2 + y) * 2 + core, "tensor": x},
    ]

    def swap(n):
        return pltpu.make_async_remote_copy(
            src_ref=vec_out.at[n],
            dst_ref=vec_in.at[n],
            send_sem=vec_send.at[n],
            recv_sem=vec_recv.at[n],
            device_id=partners[n],
            device_id_type=MESH,
        )

    vec_out[0] = vec_ref[...]
    produce(0)

    def step(s, _):
        @pl.when(s + 1 < STEPS)
        def _produce():
            produce(s + 1)

        @pl.when(s < STEPS)
        def _one():
            stage_one(s)

        @pl.when((s >= LAG) & (s < STEPS + LAG))
        def _two():
            stage_two(s - LAG)

        @pl.when((s >= 2 * LAG) & (s < STEPS + 2 * LAG))
        def _three():
            stage_three(s - 2 * LAG)

        @pl.when(s == 2)
        def _weights():
            weight_copy.wait()

        @pl.when((s >= 2) & (s < 2 + 3 * strips) & (lax.rem(s, 3) == 2))
        def _input():
            input_strip(s // 3)

        @pl.when(s == STEPS + LAG)
        def _border():
            strip_done(strips - 2).wait()
            strip_done(strips - 1).wait()
            border.start()

        @pl.when(s >= 3 * LAG)
        def _last():
            stage_last(s - 3 * LAG)

        for cut in range(SLICES):

            @pl.when(s - 3 * LAG == cut * BLOCKS + BLOCKS - 1)
            def _post():
                post_all(cut)

        for n in range(5):

            @pl.when(s == n)
            def _begin():
                swap(n).start()

            @pl.when(s == n + 1)
            def _end():
                swap(n).wait()
                if n < 4:
                    vec_out[n + 1] = vec_out[n] + vec_in[n]
                else:
                    sum_ref[...] = vec_out[n] + vec_in[n]

        return 0

    lax.fori_loop(0, STEPS + 3 * LAG, step, 0)

    def finish(i, _):
        ended(i)
        return 0

    lax.fori_loop(0, STEPS, finish, 0)

    def mail_one(i, _):
        for cut in range(SLICES):
            answer(lax.rem(me + i, n_dp), cut).wait_recv()
            letter(lax.rem(me + i, n_dp), cut).wait_send()
        return 0

    lax.fori_loop(1, n_dp, mail_one, 0)
    for cut in range(SLICES):
        own_letter(cut).wait()
    border.wait()


def reduce_grads(piece_of, vec, qkv, context, pre, hidden, tokens, ext_grads, normed, two, weights):
    n_dp = piece_of.shape[0] // CAP
    low = jnp.bfloat16
    width = D // 2 // SLICES
    rows = 256
    ext = tokens.shape[0]
    length = normed.shape[0]
    anywhere = pl.BlockSpec(memory_space=pl.ANY)
    vmem = pl.BlockSpec(memory_space=pltpu.VMEM)
    return pl.pallas_call(
        reduce_kernel,
        out_shape=(
            jax.ShapeDtypeStruct((CAP, 128, D), low),
            jax.ShapeDtypeStruct(vec.shape, jnp.float32),
            jax.ShapeDtypeStruct((ext, D), low),
            jax.ShapeDtypeStruct((DOC_MAX, D), low),
        ),
        in_specs=[pl.BlockSpec(memory_space=pltpu.SMEM), vmem] + [anywhere] * 9,
        out_specs=(anywhere, vmem, anywhere, anywhere),
        scratch_shapes=[
            pltpu.VMEM((3, D, D), low),
            pltpu.VMEM((2, 3, D, 256), low),
            pltpu.VMEM((2, 256, D), low),
            pltpu.SemaphoreType.DMA,
            pltpu.SemaphoreType.DMA((2,)),
            pltpu.SemaphoreType.DMA((2,)),
            pltpu.SemaphoreType.DMA,
            pltpu.SemaphoreType.DMA,
            pltpu.VMEM((2, rows, ext), low),
            pltpu.VMEM((2, length, rows), low),
            pltpu.VMEM((2, 2, SLICES, ext, width), low),
            pltpu.VMEM((2, 2, SLICES, length, width), low),
            pltpu.VMEM((2, 2, 4, 4, 2, 16, width), low),
            pltpu.VMEM((2, 2, 4, 4, 2, 16, width), low),
            pltpu.VMEM((STEPS, 2, 4, 4, 2, 16, width), low),
            pltpu.VMEM((STEPS, 2, 4, 2, 16, width), low),
            pltpu.VMEM((STEPS, 2, 2, 4, 16, width), low),
            pltpu.VMEM((STEPS, 2, 4, 16, width), low),
            pltpu.VMEM((STEPS, 2, 4, 16, width), low),
            pltpu.VMEM((STEPS, 4, 4, 16, width), low),
            pltpu.VMEM((STEPS, 4, 4, 16, width), low),
            pltpu.VMEM((SLICES, BLOCKS * 4 + 1, 16, width), low),
            pltpu.VMEM((SLICES, n_dp, CAP, 16, width), low),
            pltpu.VMEM((5,) + vec.shape, jnp.float32),
            pltpu.VMEM((5,) + vec.shape, jnp.float32),
            pltpu.SemaphoreType.DMA((2,)),
            pltpu.SemaphoreType.DMA((4, 2, SLICES)),
            pltpu.SemaphoreType.DMA((SLICES,)),
            pltpu.SemaphoreType.DMA((SLICES, n_dp)),
            pltpu.SemaphoreType.DMA((SLICES, n_dp)),
            pltpu.SemaphoreType.DMA((9, STEPS)),
            pltpu.SemaphoreType.DMA((9, STEPS)),
            pltpu.SemaphoreType.DMA((5,)),
            pltpu.SemaphoreType.DMA((5,)),
        ],
        compiler_params=pltpu.CompilerParams(
            collective_id=2, has_side_effects=True, vmem_limit_bytes=63 * 2**20
        ),
        cost_estimate=pl.CostEstimate(
            flops=41 * 10**9, bytes_accessed=50 * 10**6, transcendentals=0
        ),
        name="reduce_grads",
    )(piece_of, vec, qkv, context, pre, hidden, tokens, ext_grads, normed, two, weights)


def coordinates():
    dp = lax.axis_index("dp")
    return dp // 4, (dp // 2) % 2, dp % 2, lax.axis_index("tensor")


def exchange(values, axis):
    if axis == "x":
        return lax.ppermute(values, "tensor", [(0, 1), (1, 0)])
    flip = {"core": 1, "y": 2, "z_near": 4, "z_far": 8}[axis]
    return lax.ppermute(values, "dp", [(i, i ^ flip) for i in range(lax.axis_size("dp"))])


def pick(values, index, axis):
    return lax.dynamic_index_in_dim(values, index, axis, keepdims=False)


def on_device_rows(
    tokens,
    segment_ids,
    key_mask,
    owners,
    master_slots,
    slot_first,
    slot_second,
    vectors,
    vector_first,
    vector_second,
    out_grad,
):
    n_dp = lax.axis_size("dp")
    n_tensor = lax.axis_size("tensor")
    half = lax.axis_index("tensor")
    every = ("tensor", "dp")
    rows = tokens.shape[0]
    ext = 2 * rows
    own_at = half * rows
    lo, hi, qaug, kaug, hidden_keys = document_plan(segment_ids[0], key_mask[0], half, rows)
    slots = slot_index(owners)
    pieces = slots.shape[0]
    piece_rows = master_slots.shape[2]
    mix_pieces = 4 * (D // n_tensor) // piece_rows
    up_pieces = (FF // n_tensor) // piece_rows
    per = mix_pieces // 4
    w_qkv, w_out, w_up, down_chunk, tokens_ext = gather_weights(owners[:, 0], master_slots[0], tokens)
    w_qkv = w_qkv.reshape(3 * D, D)
    w_out = w_out.reshape(D, D)
    w_up = w_up.reshape(FF, D)
    down_chunks = lax.all_gather(down_chunk, every, axis=0, tiled=False)
    w_down = stack_chunks(down_chunks.reshape((n_tensor, 8, 2) + down_chunk.shape)).reshape(FF, D)
    bias_up = vectors[2:6].reshape(n_tensor, 4, -1).transpose(1, 0, 2).reshape(FF)

    bias_qkv = jnp.concatenate([vectors[0], jnp.zeros((D,), jnp.float32), vectors[1]])
    scale_qkv = jnp.concatenate([jnp.full((D,), HD ** (-0.5)), jnp.ones((2 * D,))])
    qkv = (
        (mm(w_qkv, tokens_ext, NT) + bias_qkv[:, None]) * scale_qkv.astype(jnp.float32)[:, None]
    ).astype(jnp.bfloat16)
    context, logs = attend(lo, hi, qkv, qaug, kaug, hidden_keys)
    own_context = lax.dynamic_slice_in_dim(context, own_at, rows, 1)
    attn_sum = mm(own_context, w_out, TN).astype(jnp.bfloat16).astype(jnp.float32)
    residual_one = tokens.astype(jnp.float32) + (attn_sum + vectors[6])
    normal_one, inverse_one = layer_stats(residual_one)
    normed = normal_one * vectors[8] + vectors[9]
    normed_low = normed.astype(jnp.bfloat16)

    hidden, slope = feed_up(normed_low, w_up, bias_up)
    residual_two = normed + (mm(hidden, w_down, NN) + vectors[7])
    normal_two, inverse_two = layer_stats(residual_two)
    layer_out = (normal_two * vectors[10] + vectors[11]).astype(jnp.bfloat16)
    grad_out = out_grad.astype(jnp.float32)
    grad_two = norm_back(grad_out, normal_two, inverse_two, vectors[10])
    grad_two_low = grad_two.astype(jnp.bfloat16)

    grad_pre, up_sums = feed_down_back(grad_two_low, w_down, slope)
    grad_norm = grad_two + lax.optimization_barrier(mm(grad_pre, w_up, NN))
    grad_one = norm_back(grad_norm, normal_one, inverse_one, vectors[8])
    grad_one_low = grad_one.astype(jnp.bfloat16)

    grad_ext = lax.dynamic_update_slice_in_dim(
        jnp.zeros((ext, D), jnp.bfloat16), grad_one_low, own_at, 0
    )
    grad_context = lax.dynamic_update_slice_in_dim(
        jnp.zeros((D, ext), jnp.bfloat16),
        mm(w_out, grad_one_low, NT).astype(jnp.bfloat16),
        own_at,
        1,
    )
    grad_qkv, qkv_sums = attend_back(
        lo, hi, qkv, grad_context, context, logs, qaug, kaug, hidden_keys
    )

    vector_terms = jnp.concatenate(
        [
            qkv_sums[:, :, 0],
            up_sums.reshape(4, n_tensor, -1)
            .transpose(1, 0, 2)
            .reshape(FF // D, D),
            jnp.stack(
                [
                    jnp.sum(grad_one, axis=0),
                    jnp.sum(grad_two, axis=0),
                    jnp.sum(grad_norm * normal_one, axis=0),
                    jnp.sum(grad_norm, axis=0),
                    jnp.sum(grad_out * normal_two, axis=0),
                    jnp.sum(grad_out, axis=0),
                ]
            ),
        ],
        axis=0,
    )
    piece_of = jnp.full((n_dp * CAP,), pieces, jnp.int32).at[slots].set(
        jnp.arange(pieces, dtype=jnp.int32)
    )
    own_grads, vector_grads, input_ext, halo_input = reduce_grads(
        piece_of,
        vector_terms,
        grad_qkv,
        context,
        grad_pre,
        hidden,
        tokens_ext,
        grad_ext,
        normed_low,
        grad_two_low,
        w_qkv.reshape(3, D, D),
    )
    own_grads = own_grads.astype(jnp.float32)
    input_back = lax.dynamic_update_slice_in_dim(
        jnp.zeros((rows, D), jnp.bfloat16),
        halo_input,
        jnp.where(half == 0, rows - DOC_MAX, 0),
        0,
    )
    input_grad = (
        grad_one + lax.dynamic_slice_in_dim(input_ext, own_at, rows, 0).astype(jnp.float32) + input_back.astype(jnp.float32)
    ).astype(jnp.bfloat16)
    slot_new, slot_first_new, slot_second_new = adam_update(
        master_slots[0], slot_first[0], slot_second[0], own_grads, rate_matrix, weight_decay
    )
    vector_new, vector_first_new, vector_second_new = adam_update(
        vectors, vector_first, vector_second, vector_grads, rate_vector, 0.0
    )
    return (
        layer_out,
        input_grad,
        slot_new[None],
        slot_first_new[None],
        slot_second_new[None],
        vector_new,
        vector_first_new,
        vector_second_new,
    )


def solution(mesh):
    placed = (
        P(("dp", "tensor"), None),
        P("dp", None),
        P("dp", None),
        P(),
        P("tensor", "dp", None, None),
        P("tensor", "dp", None, None),
        P("tensor", "dp", None, None),
        P(),
        P(),
        P(),
        P(("dp", "tensor"), None),
    )
    by_rows = mesh.shape["tensor"] == 2 and mesh.shape["dp"] == 16
    return jax.shard_map(
        on_device_rows if by_rows else on_device_generic,
        mesh=mesh,
        in_specs=placed,
        out_specs=(
            P(("dp", "tensor"), None),
            P(("dp", "tensor"), None),
            P("tensor", "dp", None, None),
            P("tensor", "dp", None, None),
            P("tensor", "dp", None, None),
            P(),
            P(),
            P(),
        ),
        check_vma=False,
    )
```

```python
import functools

import jax
import jax.numpy as jnp
from jax import lax
from jax.experimental import pallas as pl
from jax.experimental.pallas import tpu as pltpu
from jax.sharding import PartitionSpec as P

D = 1024
HD = 64
FF = 4096
QBLK = 512
STEP = 10
CAP = 6


norm_eps = 1e-05
mask_fill = -1000000000.0
beta_one = 0.5
beta_two = 0.5
rate_matrix = 0.03
rate_vector = 0.1
weight_decay = 0.01
adam_eps = 1e-08


def slot_index(owners):
    owner_of = owners[:, 0]
    positions = jnp.arange(owner_of.shape[0], dtype=jnp.int32)
    earlier = (positions[None, :] < positions[:, None]) & (owner_of[None, :] == owner_of[:, None])
    within = jnp.sum(earlier.astype(jnp.int32), axis=1)
    return owner_of * CAP + within


def layer_stats(residual):
    center = residual - jnp.mean(residual, axis=-1, keepdims=True)
    spread = jnp.mean(center * center, axis=-1, keepdims=True)
    inverse = lax.rsqrt(spread + norm_eps)
    return (center * inverse, inverse)


def norm_back(grads, normal, inverse, gains):
    scaled = grads * gains
    return inverse * (
        scaled
        - jnp.mean(scaled, axis=-1, keepdims=True)
        - normal * jnp.mean(scaled * normal, axis=-1, keepdims=True)
    )


def gelu_exact(values):
    return jax.nn.gelu(values, approximate=False)


def block_mask(segment, valid, start):
    length = segment.shape[0]
    query_pos = start + jnp.arange(QBLK, dtype=jnp.int32)
    key_pos = jnp.arange(length, dtype=jnp.int32)
    query_seg = lax.dynamic_slice_in_dim(segment, start, QBLK, 0)
    same = query_seg[:, None] == segment[None, :]
    return same & ((valid[None, :] == 1) | (query_pos[:, None] == key_pos[None, :]))


def block_scores(block_q, key_rows, segment, valid, start):
    scores = jnp.einsum("qhd,khd->hqk", block_q, key_rows, preferred_element_type=jnp.float32)
    return jnp.where(block_mask(segment, valid, start)[None], scores, mask_fill)


def attend_forward(queries, key_rows, value_rows, segment, valid):
    length = queries.shape[0]

    def one_block(index):
        start = index * QBLK
        block_q = lax.dynamic_slice_in_dim(queries, start, QBLK, 0)
        scores = block_scores(block_q, key_rows, segment, valid, start)
        row_max = jnp.max(scores, axis=2, keepdims=True)
        raised = jnp.exp(scores - row_max)
        totals = jnp.sum(raised, axis=2, keepdims=True)
        weights = (raised / totals).astype(jnp.bfloat16)
        context = jnp.einsum(
            "hqk,khd->qhd", weights, value_rows, preferred_element_type=jnp.float32
        )
        return (context, (row_max + jnp.log(totals))[:, :, 0])

    context, log_sums = lax.map(one_block, jnp.arange(length // QBLK, dtype=jnp.int32))
    return (context.reshape(length, -1), log_sums)


def attend_backward(queries, key_rows, value_rows, segment, valid, log_sums, grad_context):
    length = queries.shape[0]

    def one_block(carry, index):
        key_acc, value_acc = carry
        start = index * QBLK
        block_q = lax.dynamic_slice_in_dim(queries, start, QBLK, 0)
        block_g = lax.dynamic_slice_in_dim(grad_context, start, QBLK, 0)
        scores = block_scores(block_q, key_rows, segment, valid, start)
        weights = jnp.exp(scores - log_sums[index][:, :, None])
        value_acc = value_acc + jnp.einsum(
            "hqk,qhd->khd",
            weights.astype(jnp.bfloat16),
            block_g,
            preferred_element_type=jnp.float32,
        )
        grad_weights = jnp.einsum(
            "qhd,khd->hqk", block_g, value_rows, preferred_element_type=jnp.float32
        )
        inner = jnp.sum(weights * grad_weights, axis=2, keepdims=True)
        grad_scores = (weights * (grad_weights - inner)).astype(jnp.bfloat16)
        grad_q = jnp.einsum(
            "hqk,khd->qhd", grad_scores, key_rows, preferred_element_type=jnp.float32
        )
        key_acc = key_acc + jnp.einsum(
            "hqk,qhd->khd", grad_scores, block_q, preferred_element_type=jnp.float32
        )
        return ((key_acc, value_acc), grad_q)

    zeros_kv = jnp.zeros(key_rows.shape, jnp.float32)
    (grad_keys, grad_values), grad_queries = lax.scan(
        one_block, (zeros_kv, zeros_kv), jnp.arange(length // QBLK, dtype=jnp.int32)
    )
    return (
        grad_queries.reshape(length, -1),
        grad_keys.reshape(length, -1),
        grad_values.reshape(length, -1),
    )


def adam_update(weights, first, second, grads, rate, decay):
    first_new = beta_one * first + (1.0 - beta_one) * grads
    second_new = beta_two * second + (1.0 - beta_two) * grads * grads
    first_hat = first_new / (1.0 - beta_one**STEP)
    second_hat = second_new / (1.0 - beta_two**STEP)
    updated = weights - rate * (first_hat / (jnp.sqrt(second_hat) + adam_eps) + decay * weights)
    return (updated, first_new, second_new)


def on_device_generic(
    tokens,
    segment_ids,
    key_mask,
    owners,
    master_slots,
    slot_first,
    slot_second,
    vectors,
    vector_first,
    vector_second,
    out_grad,
):
    n_tensor = lax.axis_size("tensor")
    group = lax.axis_index("tensor")
    head_cols = D // n_tensor
    unit_cols = FF // n_tensor
    heads_here = head_cols // HD
    seq_count = segment_ids.shape[0]
    length = segment_ids.shape[1]
    query_scale = HD ** (-0.5)
    slots = slot_index(owners)
    gathered_slots = lax.all_gather(master_slots[0].astype(jnp.bfloat16), "dp", axis=0, tiled=True)
    stack = jnp.take(gathered_slots, slots, axis=0).reshape(-1, D)
    w_mix = stack[0 : 3 * head_cols]
    w_out = stack[3 * head_cols : 4 * head_cols]
    w_up = stack[4 * head_cols : 4 * head_cols + unit_cols]
    w_down = stack[4 * head_cols + unit_cols :]
    bias_query = lax.dynamic_slice_in_dim(vectors[0], group * head_cols, head_cols, 0)
    bias_value = lax.dynamic_slice_in_dim(vectors[1], group * head_cols, head_cols, 0)
    bias_up = lax.dynamic_slice_in_dim(vectors[2:6].reshape(FF), group * unit_cols, unit_cols, 0)
    gathered = lax.all_gather(tokens, "tensor", axis=0, tiled=True)
    mixed = jnp.einsum("ld,kd->lk", gathered, w_mix, preferred_element_type=jnp.float32)
    queries = ((mixed[:, :head_cols] + bias_query) * query_scale).astype(jnp.bfloat16)
    key_rows = mixed[:, head_cols : 2 * head_cols].astype(jnp.bfloat16)
    value_rows = (mixed[:, 2 * head_cols :] + bias_value).astype(jnp.bfloat16)
    head_shape = (seq_count, length, heads_here, HD)
    queries_h = queries.reshape(head_shape)
    keys_h = key_rows.reshape(head_shape)
    values_h = value_rows.reshape(head_shape)

    def forward_seq(element):
        return attend_forward(element[0], element[1], element[2], element[3], element[4])

    context, log_sums = lax.map(forward_seq, (queries_h, keys_h, values_h, segment_ids, key_mask))
    context = context.reshape(-1, head_cols).astype(jnp.bfloat16)
    attn_sum = lax.psum_scatter(
        jnp.einsum("lk,kd->ld", context, w_out, preferred_element_type=jnp.float32).astype(
            jnp.bfloat16
        ),
        "tensor",
        scatter_dimension=0,
        tiled=True,
    ).astype(jnp.float32)
    residual_one = tokens.astype(jnp.float32) + (attn_sum + vectors[6])
    normal_one, inverse_one = layer_stats(residual_one)
    normed = normal_one * vectors[8] + vectors[9]
    normed_low = normed.astype(jnp.bfloat16)
    norm_rows = lax.all_gather(normed_low, "tensor", axis=0, tiled=True)
    hidden_pre = (
        jnp.einsum("ld,kd->lk", norm_rows, w_up, preferred_element_type=jnp.float32) + bias_up
    )
    hidden_full, gelu_pull = jax.vjp(gelu_exact, hidden_pre)
    hidden = hidden_full.astype(jnp.bfloat16)
    mlp_sum = lax.psum_scatter(
        jnp.einsum("lk,kd->ld", hidden, w_down, preferred_element_type=jnp.float32).astype(
            jnp.bfloat16
        ),
        "tensor",
        scatter_dimension=0,
        tiled=True,
    ).astype(jnp.float32)
    residual_two = normed + (mlp_sum + vectors[7])
    normal_two, inverse_two = layer_stats(residual_two)
    layer_out = (normal_two * vectors[10] + vectors[11]).astype(jnp.bfloat16)
    grad_out = out_grad.astype(jnp.float32)
    grad_two = norm_back(grad_out, normal_two, inverse_two, vectors[10])
    grad_down_in = lax.all_gather(grad_two.astype(jnp.bfloat16), "tensor", axis=0, tiled=True)
    grad_hidden = jnp.einsum("ld,kd->lk", grad_down_in, w_down, preferred_element_type=jnp.float32)
    grad_w_down = jnp.einsum("lk,ld->kd", hidden, grad_down_in, preferred_element_type=jnp.float32)
    grad_pre = gelu_pull(grad_hidden)[0].astype(jnp.bfloat16)
    norm_back_rows = lax.all_gather(normed_low, "tensor", axis=0, tiled=True)
    grad_w_up = jnp.einsum(
        "lk,ld->kd", grad_pre, norm_back_rows, preferred_element_type=jnp.float32
    )
    grad_norm = grad_two + lax.psum_scatter(
        jnp.einsum("lk,kd->ld", grad_pre, w_up, preferred_element_type=jnp.float32).astype(
            jnp.bfloat16
        ),
        "tensor",
        scatter_dimension=0,
        tiled=True,
    ).astype(jnp.float32)
    grad_one = norm_back(grad_norm, normal_one, inverse_one, vectors[8])
    grad_attn_in = lax.all_gather(grad_one.astype(jnp.bfloat16), "tensor", axis=0, tiled=True)
    grad_context = jnp.einsum(
        "ld,kd->lk", grad_attn_in, w_out, preferred_element_type=jnp.float32
    ).astype(jnp.bfloat16)
    grad_w_out = jnp.einsum("lk,ld->kd", context, grad_attn_in, preferred_element_type=jnp.float32)

    def backward_seq(element):
        return attend_backward(
            element[0], element[1], element[2], element[3], element[4], element[5], element[6]
        )

    grad_q, grad_k, grad_v = lax.map(
        backward_seq,
        (
            queries_h,
            keys_h,
            values_h,
            segment_ids,
            key_mask,
            log_sums,
            grad_context.reshape(head_shape),
        ),
    )
    grad_queries = grad_q.reshape(-1, head_cols).astype(jnp.bfloat16) * query_scale
    grad_keys = grad_k.reshape(-1, head_cols).astype(jnp.bfloat16)
    grad_values = grad_v.reshape(-1, head_cols).astype(jnp.bfloat16)
    grad_mix = jnp.concatenate([grad_queries, grad_keys, grad_values], axis=1)
    mix_back_rows = lax.all_gather(tokens, "tensor", axis=0, tiled=True)
    grad_w_mix = jnp.einsum(
        "lk,ld->kd", grad_mix, mix_back_rows, preferred_element_type=jnp.float32
    )
    input_grad = (
        grad_one
        + lax.psum_scatter(
            jnp.einsum("lk,kd->ld", grad_mix, w_mix, preferred_element_type=jnp.float32).astype(
                jnp.bfloat16
            ),
            "tensor",
            scatter_dimension=0,
            tiled=True,
        ).astype(jnp.float32)
    ).astype(jnp.bfloat16)
    query_full = lax.dynamic_update_slice_in_dim(
        jnp.zeros((D,), jnp.float32),
        jnp.sum(grad_queries.astype(jnp.float32), axis=0),
        group * head_cols,
        0,
    )
    value_full = lax.dynamic_update_slice_in_dim(
        jnp.zeros((D,), jnp.float32),
        jnp.sum(grad_values.astype(jnp.float32), axis=0),
        group * head_cols,
        0,
    )
    up_full = lax.dynamic_update_slice_in_dim(
        jnp.zeros((FF,), jnp.float32),
        jnp.sum(grad_pre.astype(jnp.float32), axis=0),
        group * unit_cols,
        0,
    )
    tail_rows = jnp.stack(
        [
            jnp.sum(grad_one, axis=0),
            jnp.sum(grad_two, axis=0),
            jnp.sum(grad_norm * normal_one, axis=0),
            jnp.sum(grad_norm, axis=0),
            jnp.sum(grad_out * normal_two, axis=0),
            jnp.sum(grad_out, axis=0),
        ]
    )
    vector_terms = jnp.concatenate(
        [jnp.stack([query_full, value_full]), up_full.reshape(FF // D, D), tail_rows], axis=0
    )
    vector_grads = lax.psum(vector_terms, ("dp", "tensor"))
    grad_stack = jnp.concatenate([grad_w_mix, grad_w_out, grad_w_up, grad_w_down], axis=0)
    grad_pieces = grad_stack.reshape(slots.shape[0], -1, D)
    spread_slots = (
        jnp.zeros((lax.axis_size("dp") * CAP,) + grad_pieces.shape[1:], jnp.float32)
        .at[slots]
        .set(grad_pieces)
    )
    own_grads = lax.psum_scatter(
        spread_slots.astype(jnp.bfloat16), "dp", scatter_dimension=0, tiled=True
    ).astype(jnp.float32)
    slot_new, slot_first_new, slot_second_new = adam_update(
        master_slots[0], slot_first[0], slot_second[0], own_grads, rate_matrix, weight_decay
    )
    vector_new, vector_first_new, vector_second_new = adam_update(
        vectors, vector_first, vector_second, vector_grads, rate_vector, 0.0
    )
    return (
        layer_out,
        input_grad,
        slot_new[None],
        slot_first_new[None],
        slot_second_new[None],
        vector_new,
        vector_first_new,
        vector_second_new,
    )


DOC_MAX = 800
ABLK = 256
FINE = 128
HPG = 8
AUG = 16
neg_big = -1000000000.0
NN = (((1,), (0,)), ((), ()))
NT = (((1,), (1,)), ((), ()))
TN = (((0,), (0,)), ((), ()))


def mm(a, b, dims):
    return lax.dot_general(a, b, dims, preferred_element_type=jnp.float32)


def attn_fwd_kernel(lo_ref, hi_ref, q_ref, k_ref, v_ref, qaug_ref, kaug_ref, hid_ref, o_ref, lse_ref, kn_ref, m_ref, acc_ref):
    ext = q_ref.shape[1]
    ones = jnp.concatenate(
        [jnp.ones((1, ABLK), jnp.float32), jnp.zeros((AUG - 1, ABLK), jnp.float32)], axis=0
    ).astype(jnp.bfloat16)
    for h in range(HPG):
        rows = slice(h * HD, (h + 1) * HD)
        kn_ref[h] = jnp.concatenate([k_ref[rows, :], kaug_ref[...]], axis=0).T

    def query_block(qb, _):
        lo = lo_ref[qb]
        hi = hi_ref[qb]
        qs = pl.ds(pl.multiple_of(qb * ABLK, ABLK), ABLK)

        @pl.when(hi > lo)
        def _work():
            hidden = hid_ref[0:1, qs]
            for h in range(HPG):
                rows = slice(h * HD, (h + 1) * HD)
                q32 = q_ref[rows, qs].astype(jnp.float32)
                k32 = k_ref[rows, qs].astype(jnp.float32)
                own = jnp.sum(q32 * k32, axis=0, keepdims=True)
                m_ref[h] = jnp.where(hidden > 0.0, own, -1e30)
                acc_ref[h, 0:HD, :] = v_ref[rows, qs].astype(jnp.float32) * hidden
                acc_ref[h, HD:, :] = jnp.broadcast_to(hidden, (AUG, ABLK))

            blocks = (hi - lo + 1) // 2
            origin = jnp.maximum(hi - 2 * blocks, 0) * FINE

            def key_block(kb, _):
                ks = pl.ds(pl.multiple_of(origin + kb * ABLK, FINE), ABLK)
                heads = [slice(h * HD, (h + 1) * HD) for h in range(HPG)]
                scores = [
                    mm(kn_ref[h, ks, :], jnp.concatenate([q_ref[heads[h], qs], qaug_ref[:, qs]], axis=0), NN)
                    for h in range(HPG)
                ]
                olds = [m_ref[h] for h in range(HPG)]
                news = [
                    jnp.maximum(olds[h], jnp.max(scores[h], axis=0, keepdims=True)) for h in range(HPG)
                ]
                raised = [jnp.exp(scores[h] - news[h]).astype(jnp.bfloat16) for h in range(HPG)]
                for h in range(HPG):
                    m_ref[h] = news[h]
                    va = jnp.concatenate([v_ref[heads[h], ks], ones], axis=0)
                    acc_ref[h] = acc_ref[h] * jnp.exp(olds[h] - news[h]) + mm(va, raised[h], NN)
                return 0

            lax.fori_loop(0, blocks, key_block, 0)
            for h in range(HPG):
                rows = slice(h * HD, (h + 1) * HD)
                total = acc_ref[h, HD : HD + 1, :]
                o_ref[rows, qs] = (acc_ref[h, 0:HD, :] * (1.0 / total)).astype(jnp.bfloat16)
                lse_ref[0, h : h + 1, qs] = m_ref[h] + jnp.log(total)

        @pl.when(hi <= lo)
        def _skip():
            o_ref[:, qs] = jnp.zeros((HPG * HD, ABLK), jnp.bfloat16)
            lse_ref[0, :, qs] = jnp.zeros((8, ABLK), jnp.float32)

        return 0

    lax.fori_loop(0, ext // ABLK, query_block, 0)


def attn_bwd_kernel(
    lo_ref, hi_ref, q_ref, k_ref, v_ref, g_ref, c_ref, lse_ref, qaug_ref, kaug_ref, hid_ref,
    out_ref, sums_ref, kn_ref, vn_ref, acc_ref, dk_acc, dv_acc,
):
    ext = q_ref.shape[1]
    for h in range(HPG):
        rows = slice(h * HD, (h + 1) * HD)
        kn_ref[h] = jnp.concatenate([k_ref[rows, :], kaug_ref[...]], axis=0).T
        vn_ref[h] = v_ref[rows, :].T
    dk_acc[...] = jnp.zeros_like(dk_acc)
    dv_acc[...] = jnp.zeros_like(dv_acc)

    def query_block(qb, _):
        lo = lo_ref[qb]
        hi = hi_ref[qb]
        qs = pl.ds(pl.multiple_of(qb * ABLK, ABLK), ABLK)

        @pl.when(hi > lo)
        def _work():
            hidden = hid_ref[0:1, qs]
            deltas = []
            logs = []
            for h in range(HPG):
                rows = slice(h * HD, (h + 1) * HD)
                q32 = q_ref[rows, qs].astype(jnp.float32)
                k32 = k_ref[rows, qs].astype(jnp.float32)
                v32 = v_ref[rows, qs].astype(jnp.float32)
                g32 = g_ref[rows, qs].astype(jnp.float32)
                c32 = c_ref[rows, qs].astype(jnp.float32)
                delta = jnp.sum(g32 * c32, axis=0, keepdims=True)
                log = lse_ref[0, h : h + 1, qs]
                own = jnp.sum(q32 * k32, axis=0, keepdims=True)
                p_own = jnp.where(hidden > 0.0, jnp.exp(own - log), 0.0)
                d_own = p_own * (jnp.sum(g32 * v32, axis=0, keepdims=True) - delta)
                acc_ref[h] = d_own * k32
                dk_acc[rows, qs] += d_own * q32
                dv_acc[rows, qs] += p_own * g32
                deltas.append(delta)
                logs.append(log)

            blocks = (hi - lo + 1) // 2
            origin = jnp.maximum(hi - 2 * blocks, 0) * FINE

            def key_block(kb, _):
                ks = pl.ds(pl.multiple_of(origin + kb * ABLK, FINE), ABLK)
                heads = [slice(h * HD, (h + 1) * HD) for h in range(HPG)]
                every = range(HPG)
                qs_h = [q_ref[heads[h], qs] for h in every]
                gs_h = [g_ref[heads[h], qs] for h in every]
                scores = [
                    mm(kn_ref[h, ks, :], jnp.concatenate([qs_h[h], qaug_ref[:, qs]], axis=0), NN)
                    for h in every
                ]
                grads = [mm(vn_ref[h, ks, :], gs_h[h], NN) for h in every]
                weights = [jnp.exp(scores[h] - logs[h]) for h in every]
                low = [weights[h].astype(jnp.bfloat16) for h in every]
                back = [
                    (weights[h] * (grads[h] - deltas[h])).astype(jnp.bfloat16) for h in every
                ]
                v_new = [mm(gs_h[h], low[h], NT) for h in every]
                k_new = [mm(qs_h[h], back[h], NT) for h in every]
                q_new = [mm(k_ref[heads[h], ks], back[h], NN) for h in every]
                for h in every:
                    dv_acc[heads[h], ks] += v_new[h]
                    dk_acc[heads[h], ks] += k_new[h]
                    acc_ref[h] += q_new[h]
                return 0

            lax.fori_loop(0, blocks, key_block, 0)
            for h in range(HPG):
                rows = slice(h * HD, (h + 1) * HD)
                out_ref[0, rows, qs] = acc_ref[h].astype(jnp.bfloat16) * (HD ** (-0.5))

        @pl.when(hi <= lo)
        def _skip():
            out_ref[0, :, qs] = jnp.zeros((HPG * HD, ABLK), jnp.bfloat16)

        return 0

    lax.fori_loop(0, ext // ABLK, query_block, 0)
    out_ref[1] = dk_acc[...].astype(jnp.bfloat16)
    out_ref[2] = dv_acc[...].astype(jnp.bfloat16)
    for n in range(2):
        total = jnp.sum(out_ref[2 * n].astype(jnp.float32), axis=1, keepdims=True)
        sums_ref[n] = jnp.broadcast_to(total, sums_ref.shape[1:])


def group_block(offset, rows, ext):
    return pl.BlockSpec((rows, ext), lambda g, lo, hi: (offset + g, 0))


def fixed_block(rows, ext):
    return pl.BlockSpec((rows, ext), lambda g, lo, hi: (0, 0))


def attend(lo, hi, qkv, qaug, kaug, hidden):
    ext = qkv.shape[1]
    groups = D // HD // HPG
    rows = HPG * HD
    return pl.pallas_call(
        attn_fwd_kernel,
        out_shape=(
            jax.ShapeDtypeStruct((D, ext), jnp.bfloat16),
            jax.ShapeDtypeStruct((groups, 8, ext), jnp.float32),
        ),
        grid_spec=pltpu.PrefetchScalarGridSpec(
            num_scalar_prefetch=2,
            grid=(groups,),
            in_specs=[
                group_block(0, rows, ext),
                group_block(groups, rows, ext),
                group_block(2 * groups, rows, ext),
                fixed_block(AUG, ext),
                fixed_block(AUG, ext),
                fixed_block(8, ext),
            ],
            out_specs=[
                group_block(0, rows, ext),
                pl.BlockSpec((1, 8, ext), lambda g, lo, hi: (g, 0, 0)),
            ],
            scratch_shapes=[
                pltpu.VMEM((HPG, ext, HD + AUG), jnp.bfloat16),
                pltpu.VMEM((HPG, 1, ABLK), jnp.float32),
                pltpu.VMEM((HPG, HD + AUG, ABLK), jnp.float32),
            ],
        ),
        compiler_params=pltpu.CompilerParams(vmem_limit_bytes=40 * 2**20),
        cost_estimate=pl.CostEstimate(flops=20 * 10**9, bytes_accessed=14 * 10**6, transcendentals=0),
        name="attend",
    )(lo, hi, qkv, qkv, qkv, qaug, kaug, hidden)


def attend_back(lo, hi, qkv, grads, context, logs, qaug, kaug, hidden):
    ext = qkv.shape[1]
    groups = D // HD // HPG
    rows = HPG * HD
    return pl.pallas_call(
        attn_bwd_kernel,
        out_shape=(
            jax.ShapeDtypeStruct((3, D, ext), jnp.bfloat16),
            jax.ShapeDtypeStruct((2, D, 128), jnp.float32),
        ),
        grid_spec=pltpu.PrefetchScalarGridSpec(
            num_scalar_prefetch=2,
            grid=(groups,),
            in_specs=[
                group_block(0, rows, ext),
                group_block(groups, rows, ext),
                group_block(2 * groups, rows, ext),
                group_block(0, rows, ext),
                group_block(0, rows, ext),
                pl.BlockSpec((1, 8, ext), lambda g, lo, hi: (g, 0, 0)),
                fixed_block(AUG, ext),
                fixed_block(AUG, ext),
                fixed_block(8, ext),
            ],
            out_specs=(
                pl.BlockSpec((3, rows, ext), lambda g, lo, hi: (0, g, 0)),
                pl.BlockSpec((2, rows, 128), lambda g, lo, hi: (0, g, 0)),
            ),
            scratch_shapes=[
                pltpu.VMEM((HPG, ext, HD + AUG), jnp.bfloat16),
                pltpu.VMEM((HPG, ext, HD), jnp.bfloat16),
                pltpu.VMEM((HPG, HD, ABLK), jnp.float32),
                pltpu.VMEM((rows, ext), jnp.float32),
                pltpu.VMEM((rows, ext), jnp.float32),
            ],
        ),
        compiler_params=pltpu.CompilerParams(vmem_limit_bytes=56 * 2**20),
        cost_estimate=pl.CostEstimate(flops=50 * 10**9, bytes_accessed=30 * 10**6, transcendentals=0),
        name="attend_back",
    )(lo, hi, qkv, qkv, qkv, grads, context, logs, qaug, kaug, hidden)


def document_plan(segment, valid, half, rows):
    length = segment.shape[0]
    position = jnp.arange(length, dtype=jnp.int32)
    documents = jnp.arange(8, dtype=jnp.int32)[:, None]
    hot = segment[None, :] == documents
    counts = jnp.sum(hot.astype(jnp.int32), axis=1, keepdims=True)
    starts = jnp.sum((segment[None, :] < documents).astype(jnp.int32), axis=1, keepdims=True)
    start = jnp.sum(jnp.where(hot, starts, 0), axis=0)
    end = jnp.sum(jnp.where(hot, starts + counts, 0), axis=0)
    own = (position >= half * rows) & (position < (half + 1) * rows)
    begins = jnp.where(own, start, length).reshape(-1, ABLK)
    ends = jnp.where(own, end, 0).reshape(-1, ABLK)
    hi = (jnp.max(ends, axis=1) + (FINE - 1)) // FINE
    lo = jnp.where(hi == 0, 0, jnp.min(begins, axis=1) // FINE)
    masked = valid == 0
    ones = jnp.ones((1, length), jnp.bfloat16)
    fill = jnp.zeros((AUG - 9, length), jnp.bfloat16)
    qaug = jnp.concatenate([hot.astype(jnp.bfloat16), ones, fill], axis=0)
    kaug = jnp.concatenate(
        [
            jnp.where(hot, 0.0, neg_big).astype(jnp.bfloat16),
            jnp.where(masked[None, :], neg_big, 0.0).astype(jnp.bfloat16),
            fill,
        ],
        axis=0,
    )
    hidden = jnp.broadcast_to(masked.astype(jnp.float32)[None, :], (8, length))
    return lo, hi, qaug, kaug, hidden


def normal_parts(values):
    bell = jnp.exp(values * values * -0.5)
    return (0.5 + 0.5 * lax.erf(values * 0.7071067811865476), bell * 0.3989422804014327)


UNITS = 1024
STRIP = 512


def up_kernel(x_ref, w_ref, bias_ref, gelu_ref, slope_ref):
    for r in range(0, x_ref.shape[0], STRIP):
        strip = slice(r, r + STRIP)
        values = mm(x_ref[strip, :], w_ref[...], NT) + bias_ref[...]
        cdf, bell = normal_parts(values)
        gelu_ref[strip, :] = (values * cdf).astype(jnp.bfloat16)
        slope_ref[strip, :] = (cdf + values * bell).astype(jnp.bfloat16)


def feed_up(rows, weights, bias):
    length = rows.shape[0]
    units = weights.shape[0]
    out = jax.ShapeDtypeStruct((length, units), jnp.bfloat16)
    columns = pl.BlockSpec((length, UNITS), lambda n: (0, n))
    return pl.pallas_call(
        up_kernel,
        out_shape=(out, out),
        grid=(units // UNITS,),
        in_specs=[
            pl.BlockSpec((length, D), lambda n: (0, 0)),
            pl.BlockSpec((UNITS, D), lambda n: (n, 0)),
            pl.BlockSpec((1, UNITS), lambda n: (0, n)),
        ],
        out_specs=(columns, columns),
        compiler_params=pltpu.CompilerParams(vmem_limit_bytes=60 * 2**20),
        cost_estimate=pl.CostEstimate(
            flops=2 * length * units * D, bytes_accessed=26 * 10**6, transcendentals=0
        ),
        name="feed_up",
    )(rows, weights, bias.reshape(1, units))


def down_back_kernel(g_ref, w_ref, slope_ref, out_ref, sum_ref):
    total = jnp.zeros((1, UNITS), jnp.float32)
    for r in range(0, g_ref.shape[0], STRIP):
        strip = slice(r, r + STRIP)
        grads = mm(g_ref[strip, :], w_ref[...], NT) * slope_ref[strip, :].astype(jnp.float32)
        low = grads.astype(jnp.bfloat16)
        out_ref[strip, :] = low
        total += jnp.sum(low.astype(jnp.float32), axis=0, keepdims=True)
    sum_ref[...] = total


def feed_down_back(grads, weights, slope):
    length = grads.shape[0]
    units = weights.shape[0]
    columns = pl.BlockSpec((length, UNITS), lambda n: (0, n))
    one_row = pl.BlockSpec((1, UNITS), lambda n: (0, n))
    return pl.pallas_call(
        down_back_kernel,
        out_shape=(
            jax.ShapeDtypeStruct((length, units), jnp.bfloat16),
            jax.ShapeDtypeStruct((1, units), jnp.float32),
        ),
        grid=(units // UNITS,),
        in_specs=[
            pl.BlockSpec((length, D), lambda n: (0, 0)),
            pl.BlockSpec((UNITS, D), lambda n: (n, 0)),
            columns,
        ],
        out_specs=(columns, one_row),
        compiler_params=pltpu.CompilerParams(vmem_limit_bytes=40 * 2**20),
        cost_estimate=pl.CostEstimate(
            flops=2 * length * units * D, bytes_accessed=26 * 10**6, transcendentals=0
        ),
        name="feed_down_back",
    )(grads, weights, slope)


MESH = pl.DeviceIdType.MESH
CHUNKS = 3
GROUPS = ((0, 3), (3, 1), (4, 4))
PARTS = (((0, 1), (1, 2)), ((0, 1), None), ((0, 2), (2, 2)))


def neighbours(z, y, core, x):
    def at(z, y, core, x):
        return {"dp": (z * 2 + y) * 2 + core, "tensor": x}

    return {
        "x": at(z, y, core, 1 - x),
        "y": at(z, 1 - y, core, x),
        "core": at(z, y, 1 - core, x),
        "up": at(jnp.minimum(z + 1, 3), y, core, x),
        "down": at(jnp.maximum(z - 1, 0), y, core, x),
    }


def greet(near, z):
    barrier = pltpu.get_barrier_semaphore()
    for name in ("x", "y", "core"):
        pl.semaphore_signal(barrier, inc=1, device_id=near[name], device_id_type=MESH)

    @pl.when(z < 3)
    def _up():
        pl.semaphore_signal(barrier, inc=1, device_id=near["up"], device_id_type=MESH)

    @pl.when(z > 0)
    def _down():
        pl.semaphore_signal(barrier, inc=1, device_id=near["down"], device_id_type=MESH)

    at_end = jnp.where((z == 0) | (z == 3), 1, 0)
    pl.semaphore_wait(barrier, 5 - at_end)


def greet_all(near, me, n_dp):
    barrier = pltpu.get_barrier_semaphore()
    pl.semaphore_signal(barrier, inc=1, device_id=near["x"], device_id_type=MESH)

    def one(i, _):
        other = {"dp": lax.rem(me + i, n_dp), "tensor": lax.axis_index("tensor")}
        pl.semaphore_signal(barrier, inc=1, device_id=other, device_id_type=MESH)
        return 0

    lax.fori_loop(1, n_dp, one, 0)
    pl.semaphore_wait(barrier, n_dp)


def gather_kernel(
    owners_ref, slots_ref, tokens_ref, qkv_ref, out_ref, up_ref, down_ref, ext_ref,
    slot_ref, low_ref, spread_ref, dense_ref, zero_ref, local_sem, own_sem, ext_sem, post, mail, send, recv, halo_send, halo_recv,
):
    z, y, core, x = coordinates()
    near = neighbours(z, y, core, x)
    width = D // 2
    me = lax.axis_index("dp")
    n_dp = low_ref.shape[0]
    for to in range(n_dp):
        lines = slice((to // 2) * 16, (to // 2) * 16 + 16)
        columns = slice((to % 2) * width, (to % 2) * width + width)
        low_ref[to] = slots_ref[:, lines, columns].astype(low_ref.dtype)
    greet_all(near, me, n_dp)

    def letter(to):
        return pltpu.make_async_remote_copy(
            src_ref=low_ref.at[to],
            dst_ref=spread_ref.at[pl.ds(me * CAP, CAP)],
            send_sem=post.at[to],
            recv_sem=mail.at[me],
            device_id={"dp": to, "tensor": x},
            device_id_type=MESH,
        )

    def answer(of):
        return pltpu.make_async_remote_copy(
            src_ref=low_ref.at[of],
            dst_ref=spread_ref.at[pl.ds(of * CAP, CAP)],
            send_sem=post.at[of],
            recv_sem=mail.at[of],
            device_id={"dp": of, "tensor": x},
            device_id_type=MESH,
        )

    def peer(i):
        return lax.rem(me + i, n_dp)

    def post_one(i, _):
        letter(peer(i)).start()
        return 0

    lax.fori_loop(1, n_dp, post_one, 0)

    rows = tokens_ref.shape[0]
    halo = DOC_MAX
    blank = zero_ref.shape[0]
    zero_ref[...] = jnp.zeros_like(zero_ref)
    edge = pl.multiple_of(jnp.where(x == 0, rows - halo, 0), 16)
    there = pl.multiple_of(jnp.where(x == 0, rows - halo, rows), 16)
    rest = pl.multiple_of(jnp.where(x == 0, rows + halo, 0), 16)
    border = pltpu.make_async_remote_copy(
        src_ref=tokens_ref.at[pl.ds(edge, halo)],
        dst_ref=ext_ref.at[pl.ds(there, halo)],
        send_sem=halo_send,
        recv_sem=halo_recv,
        device_id=near["x"],
        device_id_type=MESH,
    )
    border.start()
    inside = pltpu.make_async_copy(
        tokens_ref, ext_ref.at[pl.ds(pl.multiple_of(x * rows, 16), rows)], ext_sem.at[0]
    )
    inside.start()
    empty = pltpu.make_async_copy(zero_ref, ext_ref.at[pl.ds(rest, blank)], ext_sem.at[1])
    empty.start()
    mine = pltpu.make_async_copy(low_ref.at[me], spread_ref.at[pl.ds(me * CAP, CAP)], local_sem)
    mine.start()
    mine.wait()

    def find(p, _):
        owner = owners_ref[p]

        def count(q, before):
            return before + jnp.where(owners_ref[q] == owner, 1, 0)

        slot_ref[p] = owner * CAP + lax.fori_loop(0, p, count, 0)
        return 0

    lax.fori_loop(0, owners_ref.shape[0], find, 0)

    def mail_one(i, _):
        answer(peer(i)).wait_recv()
        letter(peer(i)).wait_send()
        return 0

    lax.fori_loop(1, n_dp, mail_one, 0)

    def place(p, _):
        dense_ref[p // 4, p % 4] = spread_ref[slot_ref[p]]
        return 0

    lax.fori_loop(0, owners_ref.shape[0], place, 0)
    rest_groups = pl.ds(GROUPS[-1][0] + GROUPS[-1][1], 4)
    later = pltpu.make_async_copy(dense_ref.at[rest_groups], down_ref, local_sem)
    later.start()
    later.wait()

    def block(k, t, zz, yy, cc, part=None):
        groups = slice(None) if part is None else pl.ds(*PARTS[k][part])
        return (qkv_ref, out_ref, up_ref)[k].at[
            groups,
            t,
            :,
            pl.ds(pl.multiple_of((zz * 2 + yy) * 16, 16), 16),
            pl.ds(pl.multiple_of(cc * width, width), width),
        ]

    own = [
        pltpu.make_async_copy(dense_ref.at[pl.ds(*GROUPS[k])], block(k, x, z, y, core), own_sem.at[k])
        for k in range(CHUNKS)
    ]
    for one in own:
        one.start()

    def copy(kind, link, k, zz, t, yy, cc, part=None, fresh=False):
        view = block(k, t, zz, yy, cc, part)
        return pltpu.make_async_remote_copy(
            src_ref=dense_ref.at[pl.ds(*GROUPS[k])] if fresh else view,
            dst_ref=view,
            send_sem=send.at[kind, k, zz],
            recv_sem=recv.at[kind, k, zz],
            device_id=near[link],
            device_id_type=MESH,
        )

    def up(k, zz, fresh=False):
        return copy(0, "up", k, zz, x, y, core, fresh=fresh)

    def down(k, zz, fresh=False):
        return copy(1, "down", k, zz, x, y, core, fresh=fresh)

    def spread(k, zz, fresh):
        copy(2, "x", k, zz, x, y, core, fresh=fresh).start()
        copy(3, "y", k, zz, x, y, core, fresh=fresh).start()
        copy(4, "core", k, zz, x, y, core, fresh=fresh).start()

    def each(d, body):
        @pl.when((d > 0) & (z - d >= 0))
        def _below():
            for k in range(CHUNKS):
                body(k, z - d, 0)

        @pl.when((d > 0) & (z + d <= 3))
        def _above():
            for k in range(CHUNKS):
                body(k, z + d, 1)

    def each_or_own(d, body):
        each(d, body)

        @pl.when(d == 0)
        def _own():
            for k in range(CHUNKS):
                body(k, z, None)

    def begin(k):
        @pl.when(z < 3)
        def _up():
            up(k, z, True).start()

        @pl.when(z > 0)
        def _down():
            down(k, z, True).start()

        spread(k, z, True)

    def first(k, zz, side):
        if side == 0:
            up(k, zz).wait_recv()

            @pl.when(z < 3)
            def _up():
                up(k, zz).start()

        else:
            down(k, zz).wait_recv()

            @pl.when(z > 0)
            def _on():
                down(k, zz).start()

        spread(k, zz, False)

    def second(k, zz, side):
        copy(2, "x", k, zz, 1 - x, y, core).wait_recv()
        copy(5, "y", k, zz, 1 - x, y, core, 0).start()
        copy(7, "core", k, zz, 1 - x, y, core).start()
        copy(3, "y", k, zz, x, 1 - y, core).wait_recv()
        if PARTS[k][1]:
            copy(6, "x", k, zz, x, 1 - y, core, 1).start()
        copy(8, "core", k, zz, x, 1 - y, core).start()

    def third(k, zz, side):
        copy(5, "y", k, zz, 1 - x, 1 - y, core, 0).wait_recv()
        copy(9, "core", k, zz, 1 - x, 1 - y, core, 0).start()
        if PARTS[k][1]:
            copy(6, "x", k, zz, 1 - x, 1 - y, core, 1).wait_recv()
            copy(10, "core", k, zz, 1 - x, 1 - y, core, 1).start()

    def finish(k, zz, side):
        if side != 1:

            @pl.when(z < 3)
            def _up():
                up(k, zz).wait_send()

        if side != 0:

            @pl.when(z > 0)
            def _down():
                down(k, zz).wait_send()

        copy(2, "x", k, zz, x, y, core).wait_send()
        copy(3, "y", k, zz, x, y, core).wait_send()
        copy(5, "y", k, zz, 1 - x, y, core, 0).wait_send()
        if PARTS[k][1]:
            copy(6, "x", k, zz, x, 1 - y, core, 1).wait_send()
        copy(4, "core", k, zz, x, y, core).wait_send()
        copy(7, "core", k, zz, 1 - x, y, core).wait_send()
        copy(8, "core", k, zz, x, 1 - y, core).wait_send()
        copy(9, "core", k, zz, 1 - x, 1 - y, core, 0).wait_send()
        if PARTS[k][1]:
            copy(10, "core", k, zz, 1 - x, 1 - y, core, 1).wait_send()
        copy(4, "core", k, zz, x, y, 1 - core).wait_recv()
        copy(7, "core", k, zz, 1 - x, y, 1 - core).wait_recv()
        copy(8, "core", k, zz, x, 1 - y, 1 - core).wait_recv()
        copy(9, "core", k, zz, 1 - x, 1 - y, 1 - core, 0).wait_recv()
        if PARTS[k][1]:
            copy(10, "core", k, zz, 1 - x, 1 - y, 1 - core, 1).wait_recv()

    for k in range(CHUNKS):
        begin(k)

    def step(d, _):
        @pl.when(d < 4)
        def _one():
            each(d, first)

        @pl.when((d >= 1) & (d < 5))
        def _two():
            each_or_own(d - 1, second)

        @pl.when(d >= 2)
        def _three():
            each_or_own(d - 2, third)

        return 0

    lax.fori_loop(1, 6, step, 0)

    def end(d, _):
        each_or_own(d, finish)
        return 0

    lax.fori_loop(0, 4, end, 0)
    for one in own:
        one.wait()
    border.wait()
    inside.wait()
    empty.wait()


def gather_weights(owners, slots, tokens):
    n_dp = lax.axis_size("dp")
    low = jnp.bfloat16
    rows = tokens.shape[0]
    anywhere = pl.BlockSpec(memory_space=pl.ANY)
    return pl.pallas_call(
        gather_kernel,
        out_shape=tuple(
            jax.ShapeDtypeStruct((count, 2, 4, 128, D), low) for first, count in GROUPS
        )
        + (
            jax.ShapeDtypeStruct((4, 4, 16, D // 2), low),
            jax.ShapeDtypeStruct((2 * rows, D), tokens.dtype),
        ),
        in_specs=[
            pl.BlockSpec(memory_space=pltpu.SMEM),
            pl.BlockSpec(memory_space=pltpu.VMEM),
            anywhere,
        ],
        out_specs=(anywhere,) * 5,
        scratch_shapes=[
            pltpu.SMEM(owners.shape, jnp.int32),
            pltpu.VMEM((n_dp, CAP, 16, D // 2), low),
            pltpu.VMEM((n_dp * CAP, 16, D // 2), low),
            pltpu.VMEM((12, 4, 16, D // 2), low),
            pltpu.VMEM((rows - DOC_MAX, D), tokens.dtype),
            pltpu.SemaphoreType.DMA,
            pltpu.SemaphoreType.DMA((CHUNKS,)),
            pltpu.SemaphoreType.DMA((2,)),
            pltpu.SemaphoreType.DMA((n_dp,)),
            pltpu.SemaphoreType.DMA((n_dp,)),
            pltpu.SemaphoreType.DMA((11, CHUNKS, 4)),
            pltpu.SemaphoreType.DMA((11, CHUNKS, 4)),
            pltpu.SemaphoreType.DMA,
            pltpu.SemaphoreType.DMA,
        ],
        compiler_params=pltpu.CompilerParams(
            collective_id=1, has_side_effects=True, vmem_limit_bytes=60 * 2**20
        ),
        cost_estimate=pl.CostEstimate(flops=0, bytes_accessed=50 * 10**6, transcendentals=0),
        name="gather_weights",
    )(owners, slots, tokens)


def stack_kernel(parts_ref, out_ref):
    for p in range(4):
        for line in range(8):
            for half in range(2):
                columns = slice(half * (D // 2), (half + 1) * (D // 2))
                out_ref[0, 0, p, line, :, columns] = parts_ref[0, line, half, 0, p]


def stack_chunks(parts):
    return pl.pallas_call(
        stack_kernel,
        out_shape=jax.ShapeDtypeStruct((4, 2, 4, 8, 16, D), parts.dtype),
        grid=(4, 2),
        in_specs=[
            pl.BlockSpec((1, 8, 2, 1, 4, 16, D // 2), lambda m, t: (t, 0, 0, m, 0, 0, 0)),
        ],
        out_specs=pl.BlockSpec((1, 1, 4, 8, 16, D), lambda m, t: (m, t, 0, 0, 0, 0)),
        compiler_params=pltpu.CompilerParams(vmem_limit_bytes=60 * 2**20),
        cost_estimate=pl.CostEstimate(flops=0, bytes_accessed=17 * 10**6, transcendentals=0),
        name="stack_chunks",
    )(parts)


BLOCKS = 12
SLICES = 2
STEPS = BLOCKS * SLICES
LAG = 3


def reduce_kernel(
    piece_ref, vec_ref, qkv_ref, ctx_ref, pre_ref, hid_ref, tok_ref, gext_ref, norm_ref, two_ref, weight_ref,
    out_ref, sum_ref, input_ref, border_ref,
    weight_buf, strip, strip_out, weight_sem, strip_sem, strip_out_sem, border_send, border_recv,
    tile, tall, ext_rhs, row_rhs, far_buf, near_buf, core_in, x_in, y_in, x2_in, y2_in, line, line_in,
    done, parcel, vec_in, vec_out,
    tile_sem, rhs_sem, local_sem, post, mail, send, recv, vec_send, vec_recv,
):
    z, y, core, x = coordinates()
    near = neighbours(z, y, core, x)
    me = lax.axis_index("dp")
    n_dp = parcel.shape[1]
    half_width = D // 2
    width = half_width // SLICES
    rows = tile.shape[1]
    tiles = 1024 // rows

    def right(n, half, cut):
        ref = (tok_ref, gext_ref, norm_ref, two_ref)[n]
        to = ext_rhs.at[n, half, cut] if n < 2 else row_rhs.at[n - 2, half, cut]
        which = 1 - core if half == 0 else core
        columns = pl.ds(pl.multiple_of(which * half_width + cut * width, width), width)
        return pltpu.make_async_copy(ref.at[:, columns], to, rhs_sem.at[n, half, cut])

    for cut in range(SLICES):
        for n in range(4):
            for half in range(2):
                right(n, half, cut).start()

    def fetch(n, body):
        i = lax.rem(n // tiles, BLOCKS)
        part = pl.ds(pl.multiple_of(lax.rem(n, tiles) * rows, rows), rows)
        slot = lax.rem(n, 2)
        ext = ext_rhs.shape[3]
        wide = tile.at[slot]
        near_half = tile.at[slot, :, pl.ds(0, ext // 2)]
        own = pl.ds(pl.multiple_of(x * (ext // 2), 128), ext // 2)
        sem = tile_sem.at[slot]

        @pl.when(i == 0)
        def _q():
            body(pltpu.make_async_copy(qkv_ref.at[0, part, own], near_half, sem))

        @pl.when((i == 1) | (i == 2))
        def _kv():
            body(pltpu.make_async_copy(qkv_ref.at[i, part, :], wide, sem))

        @pl.when(i == 3)
        def _out():
            body(pltpu.make_async_copy(ctx_ref.at[part, own], near_half, sem))

        def columns(first):
            start = (i - first) * 1024 + lax.rem(n, tiles) * rows
            return pl.ds(pl.multiple_of(start, rows), rows)

        @pl.when((i >= 4) & (i < 8))
        def _up():
            body(pltpu.make_async_copy(pre_ref.at[:, columns(4)], tall.at[slot], sem))

        @pl.when(i >= 8)
        def _down():
            body(pltpu.make_async_copy(hid_ref.at[:, columns(8)], tall.at[slot], sem))

    strip_rows = strip.shape[3]
    strips = qkv_ref.shape[2] // strip_rows
    weight_copy = pltpu.make_async_copy(weight_ref, weight_buf, weight_sem)
    weight_copy.start()

    def strip_at(r):
        other = lax.rem(r + (1 - x) * (strips // 2), strips)
        return pl.ds(pl.multiple_of(other * strip_rows, strip_rows), strip_rows)

    def strip_copy(r):
        slot = lax.rem(r, 2)
        here = strip_at(r)
        return pltpu.make_async_copy(qkv_ref.at[:, :, here], strip.at[slot], strip_sem.at[slot])

    def strip_done(r):
        slot = lax.rem(r, 2)
        here = strip_at(r)
        return pltpu.make_async_copy(strip_out.at[slot], input_ref.at[here], strip_out_sem.at[slot])

    def input_strip(r):
        slot = lax.rem(r, 2)

        @pl.when(r + 1 < strips)
        def _next():
            strip_copy(r + 1).start()

        @pl.when(r >= 2)
        def _free():
            strip_done(r - 2).wait()

        strip_copy(r).wait()
        mine = lax.rem(r + (1 - x) * (strips // 2), strips) // (strips // 2) == x

        @pl.when(mine)
        def _own():
            total = mm(strip[slot, 0], weight_buf[0], TN)
            total += mm(strip[slot, 1], weight_buf[1], TN)
            total += mm(strip[slot, 2], weight_buf[2], TN)
            strip_out[slot] = total.astype(jnp.bfloat16)

        @pl.when(jnp.logical_not(mine))
        def _other():
            total = mm(strip[slot, 1], weight_buf[1], TN)
            total += mm(strip[slot, 2], weight_buf[2], TN)
            strip_out[slot] = total.astype(jnp.bfloat16)

        strip_done(r).start()

    halo = border_ref.shape[0]
    middle = input_ref.shape[0] // 2
    border_at = pl.multiple_of(jnp.where(x == 0, middle, middle - halo), 16)
    border = pltpu.make_async_remote_copy(
        src_ref=input_ref.at[pl.ds(border_at, halo)],
        dst_ref=border_ref,
        send_sem=border_send,
        recv_sem=border_recv,
        device_id=near["x"],
        device_id_type=MESH,
    )
    strip_copy(0).start()
    fetch(0, lambda copy: copy.start())
    greet_all(near, me, n_dp)

    def remote(kind, i, link, src, dst):
        return pltpu.make_async_remote_copy(
            src_ref=src,
            dst_ref=dst,
            send_sem=send.at[kind, i],
            recv_sem=recv.at[kind, i],
            device_id=near[link],
            device_id_type=MESH,
        )

    def core_copy(i):
        return remote(0, i, "core", far_buf.at[lax.rem(i, 2)], core_in.at[i])

    def x1(i):
        return remote(1, i, "x", core_in.at[i, 1 - x, pl.ds(0, 2)], x_in.at[i])

    def y1(i):
        return remote(2, i, "y", core_in.at[i, :, pl.ds(2, 2), :, 1 - y], y_in.at[i])

    def y2(i):
        return remote(3, i, "y", x_in.at[i, :, :, 1 - y], y2_in.at[i])

    def x2(i):
        return remote(4, i, "x", y_in.at[i, 1 - x], x2_in.at[i])

    def along(i, zz):
        return pltpu.make_async_remote_copy(
            src_ref=line.at[i, zz],
            dst_ref=line_in.at[i, z],
            send_sem=send.at[5 + zz, i],
            recv_sem=recv.at[5 + z, i],
            device_id={"dp": (zz * 2 + y) * 2 + core, "tensor": x},
            device_id_type=MESH,
        )

    def arrival(i, zz):
        return pltpu.make_async_remote_copy(
            src_ref=line.at[i, zz],
            dst_ref=line_in.at[i, zz],
            send_sem=send.at[5 + zz, i],
            recv_sem=recv.at[5 + zz, i],
            device_id={"dp": (zz * 2 + y) * 2 + core, "tensor": x},
            device_id_type=MESH,
        )

    def produce(b):
        ring = lax.rem(b, 2)
        cut = b // BLOCKS
        i = lax.rem(b, BLOCKS)

        for c in range(SLICES):
            for n, first in enumerate((0, 3, 4, 8)):

                @pl.when(b == c * BLOCKS + first)
                def _ready():
                    right(n, 0, c).wait()
                    right(n, 1, c).wait()

        @pl.when(b >= 2)
        def _free():
            core_copy(b - 2).wait_send()

        def one(part, _):
            n = b * tiles + part
            slot = lax.rem(n, 2)

            @pl.when(n + 1 < STEPS * tiles)
            def _next():
                fetch(n + 1, lambda copy: copy.start())

            fetch(n, lambda copy: copy.wait())
            t, p = part // 2, lax.rem(part, 2) * 2

            def put(value, to):
                to[ring, t, pl.ds(p, 2)] = value.astype(jnp.bfloat16).reshape(2, 4, 2, 16, width)

            @pl.when((i == 1) | (i == 2))
            def _wide():
                put(mm(tile[slot], ext_rhs[0, 0, cut], NN), far_buf)
                put(mm(tile[slot], ext_rhs[0, 1, cut], NN), near_buf)

            @pl.when((i == 0) | (i == 3))
            def _own():
                which = jnp.where(i == 0, 0, 1)
                length = ext_rhs.shape[3] // 2
                own = pl.ds(pl.multiple_of(x * length, length), length)
                left = tile[slot, :, 0:length]
                put(mm(left, ext_rhs[which, 0, cut, own], NN), far_buf)
                put(mm(left, ext_rhs[which, 1, cut, own], NN), near_buf)

            @pl.when(i >= 4)
            def _tall():
                which = jnp.where(i < 8, 0, 1)
                put(mm(tall[slot], row_rhs[which, 0, cut], TN), far_buf)
                put(mm(tall[slot], row_rhs[which, 1, cut], TN), near_buf)

            return 0

        lax.fori_loop(0, tiles, one, 0)
        core_copy(b).start()

    def stage_one(i):
        core_copy(i).wait_recv()
        ring = lax.rem(i, 2)

        def add(j, _):
            t, p = j // 4, j % 4
            core_in[i, t, p] = core_in[i, t, p] + near_buf[ring, t, p]
            return 0

        lax.fori_loop(0, 8, add, 0)
        x1(i).start()
        y1(i).start()

    def stage_two(i):
        x1(i).wait_recv()
        y1(i).wait_recv()
        for p in range(2):
            x_in[i, p] = x_in[i, p] + core_in[i, x, p]
        for t in range(2):
            for p in range(2):
                y_in[i, t, p] = y_in[i, t, p] + core_in[i, t, 2 + p, :, y]
        y2(i).start()
        x2(i).start()

    def stage_three(i):
        y2(i).wait_recv()
        x2(i).wait_recv()
        for p in range(2):
            line[i, :, p] = x_in[i, p, :, y] + y2_in[i, p]
            line[i, :, 2 + p] = y_in[i, x, p] + x2_in[i, p]
        for n in range(1, 4):
            along(i, lax.rem(z + n, 4)).start()

    def stage_last(b):
        cut = b // BLOCKS
        total = line[b, z].astype(jnp.float32)
        for n in range(1, 4):
            zz = lax.rem(z + n, 4)
            arrival(b, zz).wait_recv()
            total += line_in[b, zz].astype(jnp.float32)
        done[cut, pl.ds(lax.rem(b, BLOCKS) * 4, 4)] = total.astype(jnp.bfloat16)

    def place(of, cut):
        start = (of % 2) * half_width + cut * width
        return out_ref.at[
            :,
            pl.ds(pl.multiple_of((of // 2) * 16, 16), 16),
            pl.ds(pl.multiple_of(start, width), width),
        ]

    def letter(to, cut):
        return pltpu.make_async_remote_copy(
            src_ref=parcel.at[cut, to],
            dst_ref=place(me, cut),
            send_sem=post.at[cut, to],
            recv_sem=mail.at[cut, me],
            device_id={"dp": to, "tensor": x},
            device_id_type=MESH,
        )

    def answer(of, cut):
        return pltpu.make_async_remote_copy(
            src_ref=parcel.at[cut, of],
            dst_ref=place(of, cut),
            send_sem=post.at[cut, of],
            recv_sem=mail.at[cut, of],
            device_id={"dp": of, "tensor": x},
            device_id_type=MESH,
        )

    def own_letter(cut):
        return pltpu.make_async_copy(parcel.at[cut, me], place(me, cut), local_sem.at[cut])

    def post_all(cut):
        done[cut, BLOCKS * 4] = jnp.zeros((16, width), done.dtype)

        def pack(n, _):
            parcel[cut, n // CAP, n % CAP] = done[cut, piece_ref[n]]
            return 0

        lax.fori_loop(0, n_dp * CAP, pack, 0)

        def post_one(i, _):
            letter(lax.rem(me + i, n_dp), cut).start()
            return 0

        lax.fori_loop(1, n_dp, post_one, 0)
        own_letter(cut).start()

    def ended(i):
        @pl.when(i >= STEPS - 2)
        def _far():
            core_copy(i).wait_send()

        x1(i).wait_send()
        y1(i).wait_send()
        y2(i).wait_send()
        x2(i).wait_send()
        for n in range(1, 4):
            along(i, lax.rem(z + n, 4)).wait_send()

    z_one = z + 1 - 2 * lax.rem(z, 2)
    z_two = lax.rem(z + 2, 4)
    partners = [
        near["core"],
        near["y"],
        near["x"],
        {"dp": (z_one * 2 + y) * 2 + core, "tensor": x},
        {"dp": (z_two * 2 + y) * 2 + core, "tensor": x},
    ]

    def swap(n):
        return pltpu.make_async_remote_copy(
            src_ref=vec_out.at[n],
            dst_ref=vec_in.at[n],
            send_sem=vec_send.at[n],
            recv_sem=vec_recv.at[n],
            device_id=partners[n],
            device_id_type=MESH,
        )

    vec_out[0] = vec_ref[...]
    produce(0)

    def step(s, _):
        @pl.when(s + 1 < STEPS)
        def _produce():
            produce(s + 1)

        @pl.when(s < STEPS)
        def _one():
            stage_one(s)

        @pl.when((s >= LAG) & (s < STEPS + LAG))
        def _two():
            stage_two(s - LAG)

        @pl.when((s >= 2 * LAG) & (s < STEPS + 2 * LAG))
        def _three():
            stage_three(s - 2 * LAG)

        @pl.when(s == 2)
        def _weights():
            weight_copy.wait()

        @pl.when((s >= 2) & (s < 2 + 3 * strips) & (lax.rem(s, 3) == 2))
        def _input():
            input_strip(s // 3)

        @pl.when(s == STEPS + LAG)
        def _border():
            strip_done(strips - 2).wait()
            strip_done(strips - 1).wait()
            border.start()

        @pl.when(s >= 3 * LAG)
        def _last():
            stage_last(s - 3 * LAG)

        for cut in range(SLICES):

            @pl.when(s - 3 * LAG == cut * BLOCKS + BLOCKS - 1)
            def _post():
                post_all(cut)

        for n in range(5):

            @pl.when(s == n)
            def _begin():
                swap(n).start()

            @pl.when(s == n + 1)
            def _end():
                swap(n).wait()
                if n < 4:
                    vec_out[n + 1] = vec_out[n] + vec_in[n]
                else:
                    sum_ref[...] = vec_out[n] + vec_in[n]

        return 0

    lax.fori_loop(0, STEPS + 3 * LAG, step, 0)

    def finish(i, _):
        ended(i)
        return 0

    lax.fori_loop(0, STEPS, finish, 0)

    def mail_one(i, _):
        for cut in range(SLICES):
            answer(lax.rem(me + i, n_dp), cut).wait_recv()
            letter(lax.rem(me + i, n_dp), cut).wait_send()
        return 0

    lax.fori_loop(1, n_dp, mail_one, 0)
    for cut in range(SLICES):
        own_letter(cut).wait()
    border.wait()


def reduce_grads(piece_of, vec, qkv, context, pre, hidden, tokens, ext_grads, normed, two, weights):
    n_dp = piece_of.shape[0] // CAP
    low = jnp.bfloat16
    width = D // 2 // SLICES
    rows = 256
    ext = tokens.shape[0]
    length = normed.shape[0]
    anywhere = pl.BlockSpec(memory_space=pl.ANY)
    vmem = pl.BlockSpec(memory_space=pltpu.VMEM)
    return pl.pallas_call(
        reduce_kernel,
        out_shape=(
            jax.ShapeDtypeStruct((CAP, 128, D), low),
            jax.ShapeDtypeStruct(vec.shape, jnp.float32),
            jax.ShapeDtypeStruct((ext, D), low),
            jax.ShapeDtypeStruct((DOC_MAX, D), low),
        ),
        in_specs=[pl.BlockSpec(memory_space=pltpu.SMEM), vmem] + [anywhere] * 9,
        out_specs=(anywhere, vmem, anywhere, anywhere),
        scratch_shapes=[
            pltpu.VMEM((3, D, D), low),
            pltpu.VMEM((2, 3, D, 256), low),
            pltpu.VMEM((2, 256, D), low),
            pltpu.SemaphoreType.DMA,
            pltpu.SemaphoreType.DMA((2,)),
            pltpu.SemaphoreType.DMA((2,)),
            pltpu.SemaphoreType.DMA,
            pltpu.SemaphoreType.DMA,
            pltpu.VMEM((2, rows, ext), low),
            pltpu.VMEM((2, length, rows), low),
            pltpu.VMEM((2, 2, SLICES, ext, width), low),
            pltpu.VMEM((2, 2, SLICES, length, width), low),
            pltpu.VMEM((2, 2, 4, 4, 2, 16, width), low),
            pltpu.VMEM((2, 2, 4, 4, 2, 16, width), low),
            pltpu.VMEM((STEPS, 2, 4, 4, 2, 16, width), low),
            pltpu.VMEM((STEPS, 2, 4, 2, 16, width), low),
            pltpu.VMEM((STEPS, 2, 2, 4, 16, width), low),
            pltpu.VMEM((STEPS, 2, 4, 16, width), low),
            pltpu.VMEM((STEPS, 2, 4, 16, width), low),
            pltpu.VMEM((STEPS, 4, 4, 16, width), low),
            pltpu.VMEM((STEPS, 4, 4, 16, width), low),
            pltpu.VMEM((SLICES, BLOCKS * 4 + 1, 16, width), low),
            pltpu.VMEM((SLICES, n_dp, CAP, 16, width), low),
            pltpu.VMEM((5,) + vec.shape, jnp.float32),
            pltpu.VMEM((5,) + vec.shape, jnp.float32),
            pltpu.SemaphoreType.DMA((2,)),
            pltpu.SemaphoreType.DMA((4, 2, SLICES)),
            pltpu.SemaphoreType.DMA((SLICES,)),
            pltpu.SemaphoreType.DMA((SLICES, n_dp)),
            pltpu.SemaphoreType.DMA((SLICES, n_dp)),
            pltpu.SemaphoreType.DMA((9, STEPS)),
            pltpu.SemaphoreType.DMA((9, STEPS)),
            pltpu.SemaphoreType.DMA((5,)),
            pltpu.SemaphoreType.DMA((5,)),
        ],
        compiler_params=pltpu.CompilerParams(
            collective_id=2, has_side_effects=True, vmem_limit_bytes=63 * 2**20
        ),
        cost_estimate=pl.CostEstimate(
            flops=41 * 10**9, bytes_accessed=50 * 10**6, transcendentals=0
        ),
        name="reduce_grads",
    )(piece_of, vec, qkv, context, pre, hidden, tokens, ext_grads, normed, two, weights)


def coordinates():
    dp = lax.axis_index("dp")
    return dp // 4, (dp // 2) % 2, dp % 2, lax.axis_index("tensor")


def exchange(values, axis):
    if axis == "x":
        return lax.ppermute(values, "tensor", [(0, 1), (1, 0)])
    flip = {"core": 1, "y": 2, "z_near": 4, "z_far": 8}[axis]
    return lax.ppermute(values, "dp", [(i, i ^ flip) for i in range(lax.axis_size("dp"))])


def pick(values, index, axis):
    return lax.dynamic_index_in_dim(values, index, axis, keepdims=False)


def on_device_rows(
    tokens,
    segment_ids,
    key_mask,
    owners,
    master_slots,
    slot_first,
    slot_second,
    vectors,
    vector_first,
    vector_second,
    out_grad,
):
    n_dp = lax.axis_size("dp")
    n_tensor = lax.axis_size("tensor")
    half = lax.axis_index("tensor")
    every = ("tensor", "dp")
    rows = tokens.shape[0]
    ext = 2 * rows
    own_at = half * rows
    lo, hi, qaug, kaug, hidden_keys = document_plan(segment_ids[0], key_mask[0], half, rows)
    slots = slot_index(owners)
    pieces = slots.shape[0]
    piece_rows = master_slots.shape[2]
    mix_pieces = 4 * (D // n_tensor) // piece_rows
    up_pieces = (FF // n_tensor) // piece_rows
    per = mix_pieces // 4
    w_qkv, w_out, w_up, down_chunk, tokens_ext = gather_weights(owners[:, 0], master_slots[0], tokens)
    w_qkv = w_qkv.reshape(3 * D, D)
    w_out = w_out.reshape(D, D)
    w_up = w_up.reshape(FF, D)
    down_chunks = lax.all_gather(down_chunk, every, axis=0, tiled=False)
    w_down = stack_chunks(down_chunks.reshape((n_tensor, 8, 2) + down_chunk.shape)).reshape(FF, D)
    bias_up = vectors[2:6].reshape(n_tensor, 4, -1).transpose(1, 0, 2).reshape(FF)

    bias_qkv = jnp.concatenate([vectors[0], jnp.zeros((D,), jnp.float32), vectors[1]])
    scale_qkv = jnp.concatenate([jnp.full((D,), HD ** (-0.5)), jnp.ones((2 * D,))])
    qkv = (
        (mm(w_qkv, tokens_ext, NT) + bias_qkv[:, None]) * scale_qkv.astype(jnp.float32)[:, None]
    ).astype(jnp.bfloat16)
    context, logs = attend(lo, hi, qkv, qaug, kaug, hidden_keys)
    own_context = lax.dynamic_slice_in_dim(context, own_at, rows, 1)
    attn_sum = mm(own_context, w_out, TN).astype(jnp.bfloat16).astype(jnp.float32)
    residual_one = tokens.astype(jnp.float32) + (attn_sum + vectors[6])
    normal_one, inverse_one = layer_stats(residual_one)
    normed = normal_one * vectors[8] + vectors[9]
    normed_low = normed.astype(jnp.bfloat16)

    hidden, slope = feed_up(normed_low, w_up, bias_up)
    residual_two = normed + (mm(hidden, w_down, NN) + vectors[7])
    normal_two, inverse_two = layer_stats(residual_two)
    layer_out = (normal_two * vectors[10] + vectors[11]).astype(jnp.bfloat16)
    grad_out = out_grad.astype(jnp.float32)
    grad_two = norm_back(grad_out, normal_two, inverse_two, vectors[10])
    grad_two_low = grad_two.astype(jnp.bfloat16)

    grad_pre, up_sums = feed_down_back(grad_two_low, w_down, slope)
    grad_norm = grad_two + lax.optimization_barrier(mm(grad_pre, w_up, NN))
    grad_one = norm_back(grad_norm, normal_one, inverse_one, vectors[8])
    grad_one_low = grad_one.astype(jnp.bfloat16)

    grad_ext = lax.dynamic_update_slice_in_dim(
        jnp.zeros((ext, D), jnp.bfloat16), grad_one_low, own_at, 0
    )
    grad_context = lax.dynamic_update_slice_in_dim(
        jnp.zeros((D, ext), jnp.bfloat16),
        mm(w_out, grad_one_low, NT).astype(jnp.bfloat16),
        own_at,
        1,
    )
    grad_qkv, qkv_sums = attend_back(
        lo, hi, qkv, grad_context, context, logs, qaug, kaug, hidden_keys
    )

    vector_terms = jnp.concatenate(
        [
            qkv_sums[:, :, 0],
            up_sums.reshape(4, n_tensor, -1)
            .transpose(1, 0, 2)
            .reshape(FF // D, D),
            jnp.stack(
                [
                    jnp.sum(grad_one, axis=0),
                    jnp.sum(grad_two, axis=0),
                    jnp.sum(grad_norm * normal_one, axis=0),
                    jnp.sum(grad_norm, axis=0),
                    jnp.sum(grad_out * normal_two, axis=0),
                    jnp.sum(grad_out, axis=0),
                ]
            ),
        ],
        axis=0,
    )
    piece_of = jnp.full((n_dp * CAP,), pieces, jnp.int32).at[slots].set(
        jnp.arange(pieces, dtype=jnp.int32)
    )
    own_grads, vector_grads, input_ext, halo_input = reduce_grads(
        piece_of,
        vector_terms,
        grad_qkv,
        context,
        grad_pre,
        hidden,
        tokens_ext,
        grad_ext,
        normed_low,
        grad_two_low,
        w_qkv.reshape(3, D, D),
    )
    own_grads = own_grads.astype(jnp.float32)
    input_back = lax.dynamic_update_slice_in_dim(
        jnp.zeros((rows, D), jnp.bfloat16),
        halo_input,
        jnp.where(half == 0, rows - DOC_MAX, 0),
        0,
    )
    input_grad = (
        grad_one + lax.dynamic_slice_in_dim(input_ext, own_at, rows, 0).astype(jnp.float32) + input_back.astype(jnp.float32)
    ).astype(jnp.bfloat16)
    slot_new, slot_first_new, slot_second_new = adam_update(
        master_slots[0], slot_first[0], slot_second[0], own_grads, rate_matrix, weight_decay
    )
    vector_new, vector_first_new, vector_second_new = adam_update(
        vectors, vector_first, vector_second, vector_grads, rate_vector, 0.0
    )
    return (
        layer_out,
        input_grad,
        slot_new[None],
        slot_first_new[None],
        slot_second_new[None],
        vector_new,
        vector_first_new,
        vector_second_new,
    )


def solution(mesh):
    placed = (
        P(("dp", "tensor"), None),
        P("dp", None),
        P("dp", None),
        P(),
        P("tensor", "dp", None, None),
        P("tensor", "dp", None, None),
        P("tensor", "dp", None, None),
        P(),
        P(),
        P(),
        P(("dp", "tensor"), None),
    )
    by_rows = mesh.shape["tensor"] == 2 and mesh.shape["dp"] == 16
    return jax.shard_map(
        on_device_rows if by_rows else on_device_generic,
        mesh=mesh,
        in_specs=placed,
        out_specs=(
            P(("dp", "tensor"), None),
            P(("dp", "tensor"), None),
            P("tensor", "dp", None, None),
            P("tensor", "dp", None, None),
            P("tensor", "dp", None, None),
            P(),
            P(),
            P(),
        ),
        check_vma=False,
    )
```
